32 devices in a mesh: groups: 2 (over x), tensor: 16 (over z, y, core).
Axes of the slice: x: 2, y: 2, z: 4, core: 2. Of those that a mesh axis runs over, the one named last changes fastest.
Arguments:
- tokens: bfloat16 [512, 8192], P(('groups', 'tensor')), parts along dimension 0, may hold values from -6 to 6
- gate_weight: bfloat16 [8192, 16384], P(None, 'tensor'), may hold values from -0.0625 to 0.0625
- up_weight: bfloat16 [8192, 16384], P(None, 'tensor'), may hold values from -0.0625 to 0.0625
- adapter_down_weight: bfloat16 [32, 64, 8192], P(('groups', 'tensor')), parts along dimension 0, may hold values from -0.0625 to 0.0625
- adapter_up_weight: bfloat16 [32, 64, 16384], P(('groups', 'tensor')), parts along dimension 0, may hold values from -0.75 to 0.75
- row_adapter: int32 [512], P('groups'), parts along dimension 0, may hold values from 0 to 15, as said below
- sorted_rows: int32 [512], P('groups'), parts along dimension 0, may hold values from 0 to 255, as said below
- segment_count: int32 [32], P('groups'), parts along dimension 0, may hold values from 1 to 64, as said below
Outputs:
- hidden: bfloat16 [512, 16384], P('groups', 'tensor'), parts along dimension 0
The draws below stay inside these ranges and needn't reach their ends.
There are 2 independent parts, one for each index of `groups`. The reference program is written for one: setup_inputs(seed, part) draws one part's arguments, and reference() takes and returns one part's arrays. A program takes and returns all parts, laid end to end along the dimension named above; an argument that names none is the same for every part. Nothing has to cross between parts.
Inputs may be any that keep to these rules, and one draw needn't show every extreme that they name: Row r uses adapter row_adapter[r]; adapter j is used by segment_count[j] rows. `sorted_rows`: a permutation of the rows; the rows of adapter j stand at positions seg_start[j] to seg_start[j] + segment_count[j] - 1. `segment_count`: the counts sum to 256; some adapter has exactly 64 rows.
All inputs are finite; a program needn't handle non-finite values.
Results may differ from the reference program's by a relative error of at most 0.0036.
Values may be sent and summed in bfloat16 or wider, within the bound.
No kernel may reach another device: no remote copies, remote signals or barrier semaphores. Data moves between devices by JAX's collectives and lax.ppermute only.
A program may use at most 128 MiB of HBM per device.

```python
import jax
import jax.numpy as jnp
from jax import lax

MODEL_WIDTH = 8192
HIDDEN_UNITS = 16384
ADAPTER_RANK = 64
ROW_DEV = 16
ROWS = 256
ADAPTER_TOTAL = 16
ROWS_PER_LIMIT = 64


def segment_plan(key):
    rank_key = jax.random.fold_in(key, 11)
    shift_key = jax.random.fold_in(key, 12)
    order_key = jax.random.fold_in(key, 13)
    per_device = ROW_DEV
    ranking = jax.random.permutation(rank_key, ADAPTER_TOTAL).astype(jnp.int32)
    places = jnp.arange(ADAPTER_TOTAL, dtype=jnp.int32)
    baseline = jnp.where(places == 0, 4 * per_device, jnp.where(places <= 6, per_device // 2, per_device))
    offsets = places - 7
    partner = jnp.clip(7 + 2 * (offsets // 2), 0, ADAPTER_TOTAL - 1)
    shifts = jax.random.randint(shift_key, (ADAPTER_TOTAL,), -(per_device // 2), per_device // 2 + 1)
    paired = (offsets >= 0) & ((offsets % 2 == 1) | (offsets + 1 < ADAPTER_TOTAL - 7))
    moved_rows = jnp.where(offsets % 2 == 0, shifts[partner], -shifts[partner])
    profile = (baseline + jnp.where(paired, moved_rows, 0)).astype(jnp.int32)
    counts = jnp.zeros((ADAPTER_TOTAL,), jnp.int32).at[ranking].set(profile)
    segment_ends = jnp.cumsum(counts).astype(jnp.int32)
    positions = jnp.arange(ROWS, dtype=jnp.int32)
    sorted_adapter = jnp.sum((positions[:, None] >= segment_ends[None, :]).astype(jnp.int32), axis=1)
    sorted_rows = jax.random.permutation(order_key, ROWS).astype(jnp.int32)
    row_adapter = jnp.zeros((ROWS,), jnp.int32).at[sorted_rows].set(sorted_adapter.astype(jnp.int32))
    return (row_adapter, sorted_rows, counts)


def draw_row_adapter(key, part):
    return segment_plan(key)[0]


def draw_sorted_rows(key, part):
    return segment_plan(key)[1]


def draw_segment_count(key, part):
    return segment_plan(key)[2]


def levels(key, shape, split, low, top_value):
    def one(axis_at, blocks):
        steps = jax.random.uniform(jax.random.fold_in(jax.random.fold_in(key, 6), axis_at), (blocks,), jnp.float32, low / len(split), top_value / len(split))
        return jnp.repeat(jnp.exp(steps), shape[axis_at] // blocks).reshape((-1,) + (1,) * (len(shape) - axis_at - 1))

    level = one(*split[0])
    for cut in split[1:]:
        level = level * one(*cut)
    return level


def scatter_about(key, extent, spread, bound, shards=(), held_as=jnp.bfloat16):
    level = levels(key, extent, shards, -0.22, 0.18) if shards else 1.0
    values = jax.random.normal(key, extent, jnp.float32) * spread * level
    return jnp.minimum(jnp.maximum(values, -bound), bound).astype(held_as)


def setup_inputs(seed: int = 0, part: int = 0) -> dict:
    keys = jax.random.split(jax.random.key(seed), 9)
    own_keys = jax.random.split(jax.random.fold_in(keys[8], part), 9)
    tokens = scatter_about(own_keys[0], (ROWS, MODEL_WIDTH), 1.0, 6.0, ((0, 16),))
    gate_weight = scatter_about(keys[1], (MODEL_WIDTH, HIDDEN_UNITS), MODEL_WIDTH ** -0.5, 0.0625, ((1, 16),))
    up_weight = scatter_about(keys[2], (MODEL_WIDTH, HIDDEN_UNITS), MODEL_WIDTH ** -0.5, 0.0625, ((1, 16),))
    adapter_down_weight = scatter_about(own_keys[3], (ADAPTER_TOTAL, ADAPTER_RANK, MODEL_WIDTH), MODEL_WIDTH ** -0.5, 0.0625, ((0, 16),))
    adapter_up_weight = scatter_about(own_keys[4], (ADAPTER_TOTAL, ADAPTER_RANK, HIDDEN_UNITS), ADAPTER_RANK ** -0.5, 0.75, ((0, 16),))
    row_adapter = draw_row_adapter(jax.random.fold_in(jax.random.fold_in(keys[8], part), 71), part)
    sorted_rows = draw_sorted_rows(jax.random.fold_in(jax.random.fold_in(keys[8], part), 71), part)
    segment_count = draw_segment_count(jax.random.fold_in(jax.random.fold_in(keys[8], part), 71), part)
    return {"tokens": tokens, "gate_weight": gate_weight, "up_weight": up_weight, "adapter_down_weight": adapter_down_weight, "adapter_up_weight": adapter_up_weight, "row_adapter": row_adapter, "sorted_rows": sorted_rows, "segment_count": segment_count}


ADAPTER_SCALE = 0.5


def reference(tokens, gate_weight, up_weight, adapter_down_weight, adapter_up_weight, row_adapter, sorted_rows, segment_count):
    gate_part = jnp.dot(tokens, gate_weight, preferred_element_type=jnp.float32)
    up_part = jnp.dot(tokens, up_weight, preferred_element_type=jnp.float32)
    seg_start = (jnp.cumsum(segment_count) - segment_count).astype(jnp.int32)
    slot_ids = jnp.arange(ROWS_PER_LIMIT, dtype=jnp.int32)

    def one_adapter(current_adapter):
        positions = jnp.clip(seg_start[current_adapter] + slot_ids, 0, ROWS - 1)
        selected_rows = tokens[sorted_rows[positions]]
        reduced_rows = jnp.dot(selected_rows, adapter_down_weight[current_adapter].T, preferred_element_type=jnp.float32).astype(jnp.bfloat16)
        expanded_rows = jnp.dot(reduced_rows, adapter_up_weight[current_adapter], preferred_element_type=jnp.float32)
        return (ADAPTER_SCALE * expanded_rows).astype(jnp.bfloat16)

    buckets = lax.map(one_adapter, jnp.arange(ADAPTER_TOTAL, dtype=jnp.int32))
    buckets = buckets.reshape(ADAPTER_TOTAL * ROWS_PER_LIMIT, HIDDEN_UNITS)
    inverse = jnp.zeros((ROWS,), jnp.int32).at[sorted_rows].set(jnp.arange(ROWS, dtype=jnp.int32))
    slot_row = jnp.clip(inverse - seg_start[row_adapter], 0, ROWS_PER_LIMIT - 1)
    delta_rows = buckets[row_adapter * ROWS_PER_LIMIT + slot_row]
    return (jax.nn.silu(gate_part) * (up_part + delta_rows.astype(jnp.float32))).astype(jnp.bfloat16)
```

```python
import jax
import jax.numpy as jnp
from jax import lax
from jax.sharding import PartitionSpec as P

ADAPTER_SCALE = 0.5


def per_device(
    tokens,
    gate_weight,
    up_weight,
    adapter_down_weight,
    adapter_up_weight,
    row_adapter,
    sorted_rows,
    segment_count,
):
    own_index = lax.axis_index("tensor")
    resident, rank, width = adapter_down_weight.shape
    rows_all = row_adapter.shape[0]
    up_maps = lax.all_to_all(
        adapter_up_weight.reshape(resident * rank, -1), "tensor", split_axis=1, concat_axis=0, tiled=True
    )
    gathered = lax.all_gather(tokens, "tensor", axis=0, tiled=True)
    shrunk = lax.dot_general(
        adapter_down_weight.reshape(resident * rank, width),
        gathered,
        (((1,), (1,)), ((), ())),
        preferred_element_type=jnp.float32,
    ).astype(jnp.bfloat16)
    own_adapters = own_index * resident + jnp.arange(resident, dtype=jnp.int32)
    uses = jnp.repeat(own_adapters, rank)[:, None] == row_adapter[None, :]
    shrunk = jnp.where(uses, shrunk, jnp.zeros_like(shrunk))
    shrunk_all = lax.all_gather(shrunk, "tensor", axis=0, tiled=True)
    gate_part = jnp.dot(gathered, gate_weight, preferred_element_type=jnp.float32)
    up_part = jnp.dot(gathered, up_weight, preferred_element_type=jnp.float32)
    delta = lax.dot_general(
        shrunk_all, up_maps, (((0,), (0,)), ((), ())), preferred_element_type=jnp.float32
    )
    delta = (ADAPTER_SCALE * delta).astype(jnp.bfloat16)
    return (jax.nn.silu(gate_part) * (up_part + delta.astype(jnp.float32))).astype(jnp.bfloat16)


def solution(mesh):
    placed = (
        P(("groups", "tensor"), None),
        P(None, "tensor"),
        P(None, "tensor"),
        P(("groups", "tensor"), None, None),
        P(("groups", "tensor"), None, None),
        P("groups"),
        P("groups"),
        P("groups"),
    )
    return jax.shard_map(
        per_device, mesh=mesh, in_specs=placed, out_specs=P("groups", "tensor"), check_vma=False
    )
```

```python
import functools

import jax
import jax.numpy as jnp
from jax import lax
from jax.experimental import pallas as pl
from jax.experimental.pallas import tpu as pltpu
from jax.sharding import PartitionSpec as P

ADAPTER_SCALE = 0.5
CORES = 2
MIB = 1024 * 1024


def chip_ring(chips):
    return list(range(0, chips, 2)) + list(range(chips - 1, 0, -2))


def ring_gather(block, axis):
    size = lax.axis_size(axis)
    me = lax.axis_index(axis)
    chips = size // CORES
    ring = chip_ring(chips)
    place = [ring.index(c) for c in range(chips)]
    ring_table = jnp.array(ring, jnp.int32)
    my_place = jnp.array(place, jnp.int32)[me // CORES]
    core = me % CORES

    def moved(value, shift):
        pairs = [
            (ring[p] * CORES + k, ring[(p + shift) % chips] * CORES + k)
            for p in range(chips)
            for k in range(CORES)
        ]
        return lax.ppermute(value, axis, pairs)

    def other_core(value):
        return lax.ppermute(value, axis, [(d, d ^ 1) for d in range(size)])

    pieces = []

    def arrived(value, column, distance):
        chip = ring_table[(my_place + distance) % chips]
        pieces.append((value, column, chip * CORES + core))
        pieces.append((other_core(value), column, chip * CORES + 1 - core))

    arrived(block, 0, 0)
    right = left = block
    for step in range(1, chips // 2):
        right = moved(right, 1)
        left = moved(left, -1)
        arrived(right, 0, -step)
        arrived(left, 0, step)
    half = block.shape[1] // 2
    far = chips // 2
    arrived(moved(right[:, :half], 1), 0, far)
    arrived(moved(left[:, half:], -1), half, far)
    return pieces


def assemble(spots, columns, piece_refs, tokens_vmem, sems):
    copies = []
    for i, ref in enumerate(piece_refs):
        rows, width = ref.shape
        start = pl.multiple_of(spots[i] * rows, rows)
        copies.append(
            pltpu.make_async_copy(
                ref, tokens_vmem.at[pl.ds(start, rows), pl.ds(columns[i], width)], sems.at[i]
            )
        )
    for copy in copies:
        copy.start()
    for copy in copies:
        copy.wait()


def split_kernel(in_ref, out_ref):
    out_ref[0] = in_ref[...]


def split_columns(weights, parts):
    rows, columns = weights.shape
    width = columns // parts
    return pl.pallas_call(
        split_kernel,
        grid=(parts,),
        in_specs=[pl.BlockSpec((rows, width), lambda i: (0, i))],
        out_specs=pl.BlockSpec((1, rows, width), lambda i: (i, 0, 0)),
        out_shape=jax.ShapeDtypeStruct((parts, rows, width), weights.dtype),
        name="split_columns",
    )(weights)


def shrink_kernel(columns, pieces, spots, users_ref, down_ref, *refs):
    piece_refs = refs[:pieces]
    out_ref, tokens_vmem, sems = refs[pieces:]
    assemble(spots, columns, piece_refs, tokens_vmem, sems)
    shrunk = lax.dot_general(
        tokens_vmem[...], down_ref[...], (((1,), (1,)), ((), ())), preferred_element_type=jnp.float32
    )
    turned = jnp.transpose(shrunk)
    out_ref[...] = jnp.where(users_ref[...] != 0, turned, 0.0).astype(out_ref.dtype)


def shrink(spots, columns, pieces, users, down):
    ranks, width = down.shape
    rows = users.shape[1]
    any_spec = pl.BlockSpec(memory_space=pl.ANY)
    return pl.pallas_call(
        functools.partial(shrink_kernel, columns, len(pieces)),
        grid_spec=pltpu.PrefetchScalarGridSpec(
            num_scalar_prefetch=1,
            grid=(1,),
            in_specs=[
                pl.BlockSpec((ranks, rows), lambda i, s: (0, 0)),
                pl.BlockSpec((ranks, width), lambda i, s: (0, 0)),
            ]
            + [any_spec] * len(pieces),
            out_specs=pl.BlockSpec((ranks, rows), lambda i, s: (0, 0)),
            scratch_shapes=[
                pltpu.VMEM((rows, width), jnp.bfloat16),
                pltpu.SemaphoreType.DMA((len(pieces),)),
            ],
        ),
        out_shape=jax.ShapeDtypeStruct((ranks, rows), jnp.bfloat16),
        compiler_params=pltpu.CompilerParams(vmem_limit_bytes=40 * MIB),
        cost_estimate=pl.CostEstimate(
            flops=2 * rows * width * ranks, bytes_accessed=2 * (rows + ranks) * width, transcendentals=0
        ),
        name="shrink",
    )(spots, users, down, *pieces)


def project_kernel(columns, pieces, spots, weight_ref, *refs):
    piece_refs = refs[:pieces]
    out_ref, tokens_vmem, sems = refs[pieces:]
    depth = weight_ref.shape[0]
    k = pl.program_id(1)

    @pl.when((pl.program_id(0) == 0) & (k == 0))
    def _():
        assemble(spots, columns, piece_refs, tokens_vmem, sems)

    part = jnp.dot(
        tokens_vmem[:, pl.ds(pl.multiple_of(k * depth, depth), depth)],
        weight_ref[...],
        preferred_element_type=jnp.float32,
    )

    @pl.when(k == 0)
    def _():
        out_ref[...] = part

    @pl.when(k > 0)
    def _():
        out_ref[...] += part


def project(spots, columns, pieces, weight, rows):
    width, units = weight.shape
    tile = min(256, units)
    depth = min(4096, width)
    any_spec = pl.BlockSpec(memory_space=pl.ANY)
    return pl.pallas_call(
        functools.partial(project_kernel, columns, len(pieces)),
        grid_spec=pltpu.PrefetchScalarGridSpec(
            num_scalar_prefetch=1,
            grid=(units // tile, width // depth),
            in_specs=[pl.BlockSpec((depth, tile), lambda n, k, s: (k, n))] + [any_spec] * len(pieces),
            out_specs=pl.BlockSpec((rows, tile), lambda n, k, s: (0, n)),
            scratch_shapes=[
                pltpu.VMEM((rows, width), jnp.bfloat16),
                pltpu.SemaphoreType.DMA((len(pieces),)),
            ],
        ),
        out_shape=jax.ShapeDtypeStruct((rows, units), jnp.float32),
        compiler_params=pltpu.CompilerParams(vmem_limit_bytes=40 * MIB),
        cost_estimate=pl.CostEstimate(
            flops=2 * rows * width * units, bytes_accessed=2 * (rows + units) * width, transcendentals=0
        ),
        name="project",
    )(spots, weight, *pieces)


def combine_kernel(pieces, ranks, holders, gate_ref, up_ref, maps_ref, *refs):
    piece_refs = refs[:pieces]
    out_ref, shrunk_vmem, sems = refs[pieces:]

    @pl.when(pl.program_id(0) == 0)
    def _():
        copies = []
        for ref in piece_refs:
            for part in range(ref.shape[0] // ranks):
                i = len(copies)
                start = pl.multiple_of(holders[i] * ranks, ranks)
                copies.append(
                    pltpu.make_async_copy(
                        ref.at[pl.ds(part * ranks, ranks)],
                        shrunk_vmem.at[pl.ds(start, ranks)],
                        sems.at[i],
                    )
                )
        for copy in copies:
            copy.start()
        for copy in copies:
            copy.wait()

    delta = lax.dot_general(
        shrunk_vmem[...], maps_ref[...], (((0,), (0,)), ((), ())), preferred_element_type=jnp.float32
    )
    delta = (ADAPTER_SCALE * delta).astype(jnp.bfloat16).astype(jnp.float32)
    gate = gate_ref[...]
    out_ref[...] = (gate / (1.0 + jnp.exp(-gate)) * (up_ref[...] + delta)).astype(out_ref.dtype)


def combine(holders, pieces, gate, up, maps, ranks):
    rows, units = gate.shape
    ranks_all = maps.shape[0]
    tile = min(256, units)
    any_spec = pl.BlockSpec(memory_space=pl.ANY)
    return pl.pallas_call(
        functools.partial(combine_kernel, len(pieces), ranks),
        grid_spec=pltpu.PrefetchScalarGridSpec(
            num_scalar_prefetch=1,
            grid=(units // tile,),
            in_specs=[
                pl.BlockSpec((rows, tile), lambda n, s: (0, n)),
                pl.BlockSpec((rows, tile), lambda n, s: (0, n)),
                pl.BlockSpec((ranks_all, tile), lambda n, s: (0, n)),
            ]
            + [any_spec] * len(pieces),
            out_specs=pl.BlockSpec((rows, tile), lambda n, s: (0, n)),
            scratch_shapes=[
                pltpu.VMEM((ranks_all, rows), jnp.bfloat16),
                pltpu.SemaphoreType.DMA((ranks_all // ranks,)),
            ],
        ),
        out_shape=jax.ShapeDtypeStruct((rows, units), jnp.bfloat16),
        compiler_params=pltpu.CompilerParams(vmem_limit_bytes=48 * MIB),
        cost_estimate=pl.CostEstimate(
            flops=2 * rows * ranks_all * units, bytes_accessed=10 * rows * units, transcendentals=rows * units
        ),
        name="combine",
    )(holders, gate, up, maps, *pieces)


def per_device(
    tokens,
    gate_weight,
    up_weight,
    adapter_down_weight,
    adapter_up_weight,
    row_adapter,
    sorted_rows,
    segment_count,
):
    axis = "tensor"
    size = lax.axis_size(axis)
    me = lax.axis_index(axis)
    resident, rank, width = adapter_down_weight.shape
    ranks = resident * rank
    rows = row_adapter.shape[0]

    own_maps = split_columns(adapter_up_weight.reshape(ranks, -1), size)
    maps = lax.all_to_all(own_maps, axis, split_axis=0, concat_axis=0, tiled=True)
    maps = maps.reshape(size * ranks, -1)

    found = ring_gather(tokens, axis)
    pieces = [piece for piece, _, _ in found]
    columns = [column for _, column, _ in found]
    spots = jnp.stack([spot for _, _, spot in found]).astype(jnp.int32)

    own_adapters = me * resident + jnp.arange(resident, dtype=jnp.int32)
    users = (jnp.repeat(own_adapters, rank)[:, None] == row_adapter[None, :]).astype(jnp.int32)
    shrunk = shrink(spots, columns, pieces, users, adapter_down_weight.reshape(ranks, width))

    near = min(4, size)
    plane = [shrunk]
    for flip in range(1, near):
        plane.append(lax.ppermute(shrunk, axis, [(d, d ^ flip) for d in range(size)]))
    plane_all = jnp.concatenate(plane, axis=0)
    plane_spots = [me ^ flip for flip in range(near)]
    shrunk_pieces = [plane_all]
    for shift in range(1, size // near):
        shrunk_pieces.append(
            lax.ppermute(plane_all, axis, [(d, (d + shift * near) % size) for d in range(size)])
        )
    gate = project(spots, columns, pieces, gate_weight, rows)
    up = project(spots, columns, pieces, up_weight, rows)
    holders = jnp.stack(
        [
            (me // near - shift) % (size // near) * near + ((me % near) ^ flip)
            for shift in range(size // near)
            for flip in range(near)
        ]
    ).astype(jnp.int32)
    return combine(holders, shrunk_pieces, gate, up, maps, ranks)


def solution(mesh):
    placed = (
        P(("groups", "tensor"), None),
        P(None, "tensor"),
        P(None, "tensor"),
        P(("groups", "tensor"), None, None),
        P(("groups", "tensor"), None, None),
        P("groups"),
        P("groups"),
        P("groups"),
    )
    return jax.shard_map(
        per_device, mesh=mesh, in_specs=placed, out_specs=P("groups", "tensor"), check_vma=False
    )
```

```python
import functools

import jax
import jax.numpy as jnp
from jax import lax
from jax.experimental import pallas as pl
from jax.experimental.pallas import tpu as pltpu
from jax.sharding import PartitionSpec as P

ADAPTER_SCALE = 0.5
CORES = 2
MIB = 1024 * 1024


def chip_ring(chips):
    return list(range(0, chips, 2)) + list(range(chips - 1, 0, -2))


def ring_gather(block, axis, extra, prepare):
    size = lax.axis_size(axis)
    chips = size // CORES
    ring = chip_ring(chips)

    def moved(value, shift):
        pairs = [
            (ring[p] * CORES + k, ring[(p + shift) % chips] * CORES + k)
            for p in range(chips)
            for k in range(CORES)
        ]
        return lax.ppermute(value, axis, pairs)

    def other_core(value):
        return lax.ppermute(value, axis, [(d, d ^ 1) for d in range(size)])

    pieces = []
    where = [[] for _ in range(size)]

    def arrived(value, column, distance):
        pieces.append((value, column))
        pieces.append((other_core(value), column))
        for device in range(size):
            chip = ring[(ring.index(device // CORES) + distance) % chips]
            core = device % CORES
            where[device] += [chip * CORES + core, chip * CORES + 1 - core]

    arrived(block, 0, 0)
    right = left = block
    for step in range(1, chips // 2):
        if step == 2:
            extra, right, left = lax.optimization_barrier((extra, right, left))
            extra = prepare(extra)
        if step == 3:
            extra, right, left = lax.optimization_barrier((extra, right, left))
        right = moved(right, 1)
        left = moved(left, -1)
        arrived(right, 0, -step)
        arrived(left, 0, step)
    half = block.shape[1] // 2
    far = chips // 2
    arrived(moved(right[:, :half], 1), 0, far)
    arrived(moved(left[:, half:], -1), half, far)
    return pieces, where, extra


def assemble(spots, columns, piece_refs, tokens_vmem, sems):
    copies = []
    for i, ref in enumerate(piece_refs):
        rows, width = ref.shape
        start = pl.multiple_of(spots[i] * rows, rows)
        copies.append(
            pltpu.make_async_copy(
                ref, tokens_vmem.at[pl.ds(start, rows), pl.ds(columns[i], width)], sems.at[i]
            )
        )
    for copy in copies:
        copy.start()
    for copy in copies:
        copy.wait()


def split_kernel(in_ref, out_ref):
    width = out_ref.shape[2]
    for part in range(out_ref.shape[0]):
        out_ref[part] = in_ref[:, part * width : (part + 1) * width]


def split_columns(weights, parts):
    rows, columns = weights.shape
    width = columns // parts
    group = min(4, parts)
    return pl.pallas_call(
        split_kernel,
        grid=(parts // group,),
        in_specs=[pl.BlockSpec((rows, group * width), lambda i: (0, i))],
        out_specs=pl.BlockSpec((group, rows, width), lambda i: (i, 0, 0)),
        out_shape=jax.ShapeDtypeStruct((parts, rows, width), weights.dtype),
        name="split_columns",
    )(weights)


HBM_SPEC = pl.BlockSpec(memory_space=pltpu.HBM)


def shrink_kernel(columns, pieces, rank, place, users_ref, down_ref, *refs):
    piece_refs = refs[:pieces]
    out_ref, tokens_vmem, sems = refs[pieces:]
    assemble(place, columns, piece_refs, tokens_vmem, sems)
    ranks = down_ref.shape[0]
    resident = ranks // rank
    shrunk = lax.dot_general(
        tokens_vmem[...], down_ref[...], (((1,), (1,)), ((), ())), preferred_element_type=jnp.float32
    )
    turned = jnp.transpose(shrunk)
    total = jnp.zeros(out_ref.shape, jnp.float32)
    for r in range(resident):
        mine = users_ref[...] == place[pieces] * resident + r
        total += jnp.where(mine, turned[r * rank : (r + 1) * rank], 0.0)
    out_ref[...] = total.astype(out_ref.dtype)


def shrink(place, columns, pieces, row_adapter, down, rank):
    ranks, width = down.shape
    rows = row_adapter.shape[0]
    return pl.pallas_call(
        functools.partial(shrink_kernel, columns, len(pieces), rank),
        grid_spec=pltpu.PrefetchScalarGridSpec(
            num_scalar_prefetch=1,
            grid=(1,),
            in_specs=[
                pl.BlockSpec((1, rows), lambda i, s: (0, 0)),
                pl.BlockSpec((ranks, width), lambda i, s: (0, 0)),
            ]
            + [HBM_SPEC] * len(pieces),
            out_specs=pl.BlockSpec((rank, rows), lambda i, s: (0, 0)),
            scratch_shapes=[
                pltpu.VMEM((rows, width), jnp.bfloat16),
                pltpu.SemaphoreType.DMA((len(pieces),)),
            ],
        ),
        out_shape=jax.ShapeDtypeStruct((rank, rows), jnp.bfloat16),
        compiler_params=pltpu.CompilerParams(vmem_limit_bytes=40 * MIB),
        cost_estimate=pl.CostEstimate(
            flops=2 * rows * width * ranks, bytes_accessed=2 * (rows + ranks) * width, transcendentals=0
        ),
        name="shrink",
    )(place, row_adapter.reshape(1, rows), down, *pieces)


def project_kernel(columns, pieces, place, gate_weight_ref, up_weight_ref, *refs):
    piece_refs = refs[:pieces]
    gate_ref, up_ref, tokens_vmem, sems = refs[pieces:]
    depth = gate_weight_ref.shape[0]
    k = pl.program_id(0)

    @pl.when(k == 0)
    def _():
        assemble(place, columns, piece_refs, tokens_vmem, sems)
        gate_ref[...] = jnp.zeros_like(gate_ref)
        up_ref[...] = jnp.zeros_like(up_ref)

    tokens = tokens_vmem[:, pl.ds(pl.multiple_of(k * depth, depth), depth)]
    gate_ref[...] += jnp.dot(tokens, gate_weight_ref[...], preferred_element_type=jnp.float32)
    up_ref[...] += jnp.dot(tokens, up_weight_ref[...], preferred_element_type=jnp.float32)

    @pl.when(k == pl.num_programs(0) - 1)
    def _():
        gate = gate_ref[...]
        gate_ref[...] = gate / (1.0 + jnp.exp(-gate))


def project(place, columns, pieces, gate_weight, up_weight, rows):
    width, units = gate_weight.shape
    depth = min(1024, width)
    weight_spec = pl.BlockSpec((depth, units), lambda k, s: (k, 0))
    out_spec = pl.BlockSpec((rows, units), lambda k, s: (0, 0))
    out = jax.ShapeDtypeStruct((rows, units), jnp.float32)
    return pl.pallas_call(
        functools.partial(project_kernel, columns, len(pieces)),
        grid_spec=pltpu.PrefetchScalarGridSpec(
            num_scalar_prefetch=1,
            grid=(width // depth,),
            in_specs=[weight_spec, weight_spec] + [HBM_SPEC] * len(pieces),
            out_specs=[out_spec, out_spec],
            scratch_shapes=[
                pltpu.VMEM((rows, width), jnp.bfloat16),
                pltpu.SemaphoreType.DMA((len(pieces),)),
            ],
        ),
        out_shape=[out, out],
        compiler_params=pltpu.CompilerParams(vmem_limit_bytes=48 * MIB),
        cost_estimate=pl.CostEstimate(
            flops=4 * rows * width * units,
            bytes_accessed=2 * (rows + 2 * units) * width,
            transcendentals=rows * units,
        ),
        name="project",
    )(place, gate_weight, up_weight, *pieces)


def combine_kernel(pieces, users_ref, gate_ref, up_ref, maps_ref, *refs):
    piece_refs = refs[:pieces]
    out_ref, shrunk_vmem = refs[pieces:]
    rank, rows = piece_refs[0].shape

    @pl.when(pl.program_id(0) == 0)
    def _():
        total = piece_refs[0][...].astype(jnp.float32)
        for ref in piece_refs[1:]:
            total += ref[...].astype(jnp.float32)
        pair = jnp.transpose(jnp.concatenate([total, total], axis=0))
        users = users_ref[...]
        column = lax.broadcasted_iota(jnp.int32, pair.shape, 1)
        for start in range(0, shrunk_vmem.shape[1], 2 * rank):
            mine = users == (start + column) // rank
            shrunk_vmem[:, start : start + 2 * rank] = jnp.where(mine, pair, 0.0).astype(jnp.bfloat16)

    delta = jnp.dot(shrunk_vmem[...], maps_ref[...], preferred_element_type=jnp.float32)
    delta = (ADAPTER_SCALE * delta).astype(jnp.bfloat16).astype(jnp.float32)
    out_ref[...] = (gate_ref[...] * (up_ref[...] + delta)).astype(out_ref.dtype)


def combine(row_adapter, pieces, gate, up, maps):
    rows, units = gate.shape
    ranks_all = maps.shape[0]
    rank = pieces[0].shape[0]
    tile = min(512, units)
    users = jnp.broadcast_to(row_adapter[:, None], (rows, 2 * rank))
    column_spec = pl.BlockSpec((rows, tile), lambda n: (0, n))
    return pl.pallas_call(
        functools.partial(combine_kernel, len(pieces)),
        grid=(units // tile,),
        in_specs=[
            pl.BlockSpec((rows, 2 * rank), lambda n: (0, 0)),
            column_spec,
            column_spec,
            pl.BlockSpec((ranks_all, tile), lambda n: (0, n)),
        ]
        + [pl.BlockSpec((rank, rows), lambda n: (0, 0))] * len(pieces),
        out_specs=column_spec,
        scratch_shapes=[pltpu.VMEM((rows, ranks_all), jnp.bfloat16)],
        out_shape=jax.ShapeDtypeStruct((rows, units), jnp.bfloat16),
        compiler_params=pltpu.CompilerParams(vmem_limit_bytes=48 * MIB),
        cost_estimate=pl.CostEstimate(
            flops=2 * rows * ranks_all * units, bytes_accessed=10 * rows * units, transcendentals=0
        ),
        name="combine",
    )(users, gate, up, maps, *pieces)


def per_device(
    tokens,
    gate_weight,
    up_weight,
    adapter_down_weight,
    adapter_up_weight,
    row_adapter,
    sorted_rows,
    segment_count,
):
    axis = "tensor"
    size = lax.axis_size(axis)
    me = lax.axis_index(axis)
    resident, rank, width = adapter_down_weight.shape
    ranks = resident * rank
    rows = row_adapter.shape[0]

    found, where, own_maps = ring_gather(
        tokens, axis, adapter_up_weight.reshape(ranks, -1), lambda weights: split_columns(weights, size)
    )
    pieces = [piece for piece, _ in found]
    columns = [column for _, column in found]
    table = jnp.array([row + [device] for device, row in enumerate(where)], jnp.int32)
    place = lax.dynamic_index_in_dim(table, me, 0, keepdims=False)

    own_maps, pieces[-2], pieces[-4] = lax.optimization_barrier((own_maps, pieces[-2], pieces[-4]))
    maps = lax.all_to_all(own_maps, axis, split_axis=0, concat_axis=0, tiled=True)
    maps = maps.reshape(size * ranks, -1)

    shrunk = shrink(place, columns, pieces, row_adapter, adapter_down_weight.reshape(ranks, width), rank)
    near = min(4, size)
    plane = shrunk
    for flip in range(1, near):
        plane = plane + lax.ppermute(shrunk, axis, [(d, d ^ flip) for d in range(size)])
    shrunk_pieces = [plane]
    for shift in range(1, size // near):
        shrunk_pieces.append(
            lax.ppermute(plane, axis, [(d, (d + shift * near) % size) for d in range(size)])
        )
    gate, up = project(place, columns, pieces, gate_weight, up_weight, rows)
    return combine(row_adapter, shrunk_pieces, gate, up, maps)


def solution(mesh):
    placed = (
        P(("groups", "tensor"), None),
        P(None, "tensor"),
        P(None, "tensor"),
        P(("groups", "tensor"), None, None),
        P(("groups", "tensor"), None, None),
        P("groups"),
        P("groups"),
        P("groups"),
    )
    return jax.shard_map(
        per_device, mesh=mesh, in_specs=placed, out_specs=P("groups", "tensor"), check_vma=False
    )
```

```python
import functools

import jax
import jax.numpy as jnp
from jax import lax
from jax.experimental import pallas as pl
from jax.experimental.pallas import tpu as pltpu
from jax.sharding import PartitionSpec as P

ADAPTER_SCALE = 0.5
CORES = 2
MIB = 1024 * 1024


def chip_ring(chips):
    return list(range(0, chips, 2)) + list(range(chips - 1, 0, -2))


def ring_gather(block, axis, beside):
    size = lax.axis_size(axis)
    chips = size // CORES
    ring = chip_ring(chips)

    def moved(value, shift):
        pairs = [
            (ring[p] * CORES + k, ring[(p + shift) % chips] * CORES + k)
            for p in range(chips)
            for k in range(CORES)
        ]
        return lax.ppermute(value, axis, pairs)

    def other_core(value):
        return lax.ppermute(value, axis, [(d, d ^ 1) for d in range(size)])

    pieces = []
    where = [[] for _ in range(size)]

    def arrived(value, column, distance):
        pieces.append((value, column))
        pieces.append((other_core(value), column))
        for device in range(size):
            chip = ring[(ring.index(device // CORES) + distance) % chips]
            core = device % CORES
            where[device] += [chip * CORES + core, chip * CORES + 1 - core]

    arrived(block, 0, 0)
    right = left = block
    for step in range(1, chips // 2):
        right = moved(right, 1)
        left = moved(left, -1)
        right, left = beside(step, (right, left))
        arrived(right, 0, -step)
        arrived(left, 0, step)
    half = block.shape[1] // 2
    far = chips // 2
    ends = beside(far, (moved(right[:, :half], 1), moved(left[:, half:], -1)))
    arrived(ends[0], 0, far)
    arrived(ends[1], half, far)
    return pieces, where


def assemble(spots, columns, piece_refs, tokens_vmem, sems):
    copies = []
    for i, ref in enumerate(piece_refs):
        rows, width = ref.shape
        start = pl.multiple_of(spots[i] * rows, rows)
        copies.append(
            pltpu.make_async_copy(
                ref, tokens_vmem.at[pl.ds(start, rows), pl.ds(columns[i], width)], sems.at[i]
            )
        )
    for copy in copies:
        copy.start()
    for copy in copies:
        copy.wait()


ANY_SPEC = pl.BlockSpec(memory_space=pl.ANY)


def cut_kernel(parts, units, me, maps_ref, *refs):
    outs, sems = refs[:-1], refs[-1]
    copies = []
    for i, part in enumerate(parts):
        start = pl.multiple_of((me[0] ^ part) * units, units)
        copies.append(pltpu.make_async_copy(maps_ref.at[:, pl.ds(start, units)], outs[i], sems.at[i]))
    for copy in copies:
        copy.start()
    for copy in copies:
        copy.wait()


def cut_columns(me, maps, parts, size):
    ranks, columns = maps.shape
    units = columns // size
    return pl.pallas_call(
        functools.partial(cut_kernel, parts, units),
        grid_spec=pltpu.PrefetchScalarGridSpec(
            num_scalar_prefetch=1,
            grid=(1,),
            in_specs=[ANY_SPEC],
            out_specs=[ANY_SPEC] * len(parts),
            scratch_shapes=[pltpu.SemaphoreType.DMA((len(parts),))],
        ),
        out_shape=[jax.ShapeDtypeStruct((ranks, units), maps.dtype)] * len(parts),
        cost_estimate=pl.CostEstimate(flops=0, bytes_accessed=4 * ranks * columns, transcendentals=0),
        name="cut_columns",
    )(me, maps)


def shrink_kernel(columns, pieces, rank, place, users_ref, down_ref, *refs):
    piece_refs = refs[:pieces]
    out_ref, tokens_vmem, sems = refs[pieces:]
    assemble(place, columns, piece_refs, tokens_vmem, sems)
    ranks = down_ref.shape[0]
    resident = ranks // rank
    shrunk = lax.dot_general(
        tokens_vmem[...], down_ref[...], (((1,), (1,)), ((), ())), preferred_element_type=jnp.float32
    )
    turned = jnp.transpose(shrunk)
    total = jnp.zeros(out_ref.shape, jnp.float32)
    for r in range(resident):
        mine = users_ref[...] == place[pieces] * resident + r
        total += jnp.where(mine, turned[r * rank : (r + 1) * rank], 0.0)
    out_ref[...] = total.astype(out_ref.dtype)


def shrink(place, columns, pieces, row_adapter, down, rank):
    ranks, width = down.shape
    rows = row_adapter.shape[0]
    return pl.pallas_call(
        functools.partial(shrink_kernel, columns, len(pieces), rank),
        grid_spec=pltpu.PrefetchScalarGridSpec(
            num_scalar_prefetch=1,
            grid=(1,),
            in_specs=[
                pl.BlockSpec((1, rows), lambda i, s: (0, 0)),
                pl.BlockSpec((ranks, width), lambda i, s: (0, 0)),
            ]
            + [ANY_SPEC] * len(pieces),
            out_specs=pl.BlockSpec((rank, rows), lambda i, s: (0, 0)),
            scratch_shapes=[
                pltpu.VMEM((rows, width), jnp.bfloat16),
                pltpu.SemaphoreType.DMA((len(pieces),)),
            ],
        ),
        out_shape=jax.ShapeDtypeStruct((rank, rows), jnp.bfloat16),
        compiler_params=pltpu.CompilerParams(vmem_limit_bytes=rows * width * 2 + 8 * MIB),
        cost_estimate=pl.CostEstimate(
            flops=2 * rows * width * ranks, bytes_accessed=2 * (rows + ranks) * width, transcendentals=0
        ),
        name="shrink",
    )(place, row_adapter.reshape(1, rows), down, *pieces)


def project_kernel(columns, pieces, place, gate_weight_ref, up_weight_ref, *refs):
    piece_refs = refs[:pieces]
    gate_ref, up_ref, tokens_vmem, sems = refs[pieces:]
    depth = gate_weight_ref.shape[0]
    k = pl.program_id(0)

    @pl.when(k == 0)
    def _():
        assemble(place, columns, piece_refs, tokens_vmem, sems)
        gate_ref[...] = jnp.zeros_like(gate_ref)
        up_ref[...] = jnp.zeros_like(up_ref)

    tokens = tokens_vmem[:, pl.ds(pl.multiple_of(k * depth, depth), depth)]
    gate_ref[...] += jnp.dot(tokens, gate_weight_ref[...], preferred_element_type=jnp.float32)
    up_ref[...] += jnp.dot(tokens, up_weight_ref[...], preferred_element_type=jnp.float32)

    @pl.when(k == pl.num_programs(0) - 1)
    def _():
        gate = gate_ref[...]
        gate_ref[...] = gate / (1.0 + jnp.exp(-gate))


def project(place, columns, pieces, gate_weight, up_weight, rows):
    width, units = gate_weight.shape
    depth = min(1024, width)
    weight_spec = pl.BlockSpec((depth, units), lambda k, s: (k, 0))
    out_spec = pl.BlockSpec((rows, units), lambda k, s: (0, 0))
    out = jax.ShapeDtypeStruct((rows, units), jnp.float32)
    return pl.pallas_call(
        functools.partial(project_kernel, columns, len(pieces)),
        grid_spec=pltpu.PrefetchScalarGridSpec(
            num_scalar_prefetch=1,
            grid=(width // depth,),
            in_specs=[weight_spec, weight_spec] + [ANY_SPEC] * len(pieces),
            out_specs=[out_spec, out_spec],
            scratch_shapes=[
                pltpu.VMEM((rows, width), jnp.bfloat16),
                pltpu.SemaphoreType.DMA((len(pieces),)),
            ],
        ),
        out_shape=[out, out],
        compiler_params=pltpu.CompilerParams(vmem_limit_bytes=rows * width * 2 + 20 * MIB),
        cost_estimate=pl.CostEstimate(
            flops=4 * rows * width * units,
            bytes_accessed=2 * (rows + 2 * units) * width,
            transcendentals=rows * units,
        ),
        name="project",
    )(place, gate_weight, up_weight, *pieces)


def combine_kernel(parts, shrunk_pieces, me, users_ref, gate_ref, up_ref, own_ref, *refs):
    part_refs = refs[: len(parts)]
    piece_refs = refs[len(parts) : len(parts) + shrunk_pieces]
    out_ref, shrunk_vmem, maps_vmem, sems = refs[len(parts) + shrunk_pieces :]
    rank, rows = piece_refs[0].shape
    ranks, units = part_refs[0].shape
    resident = ranks // rank
    tile = out_ref.shape[1]
    n = pl.program_id(0)

    @pl.when(n == 0)
    def _():
        start = pl.multiple_of(me[0] * units, units)
        copies = [pltpu.make_async_copy(own_ref.at[:, pl.ds(start, units)], maps_vmem.at[pl.ds(0, ranks)], sems.at[0])]
        for i, ref in enumerate(part_refs):
            copies.append(
                pltpu.make_async_copy(ref, maps_vmem.at[pl.ds((i + 1) * ranks, ranks)], sems.at[i + 1])
            )
        for copy in copies:
            copy.start()
        total = piece_refs[0][...].astype(jnp.float32)
        for ref in piece_refs[1:]:
            total += ref[...].astype(jnp.float32)
        pair = jnp.transpose(jnp.concatenate([total, total], axis=0))
        users = users_ref[...]
        first = lax.broadcasted_iota(jnp.int32, pair.shape, 1) < rank
        adapters = [(me[0] ^ part) * resident + r for part in (0,) + parts for r in range(resident)]
        for i in range(0, len(adapters), 2):
            mine = users == jnp.where(first, adapters[i], adapters[i + 1])
            shrunk_vmem[:, i * rank : (i + 2) * rank] = jnp.where(mine, pair, 0.0).astype(jnp.bfloat16)
        for copy in copies:
            copy.wait()

    maps = maps_vmem[:, pl.ds(pl.multiple_of(n * tile, tile), tile)]
    delta = jnp.dot(shrunk_vmem[...], maps, preferred_element_type=jnp.float32)
    delta = (ADAPTER_SCALE * delta).astype(jnp.bfloat16).astype(jnp.float32)
    out_ref[...] = (gate_ref[...] * (up_ref[...] + delta)).astype(out_ref.dtype)


def combine(me, row_adapter, gate, up, own_maps, parts, map_parts, pieces):
    rows, units = gate.shape
    ranks = own_maps.shape[0]
    ranks_all = ranks * (1 + len(parts))
    rank = pieces[0].shape[0]
    tile = min(512, units)
    users = jnp.broadcast_to(row_adapter[:, None], (rows, 2 * rank))
    column_spec = pl.BlockSpec((rows, tile), lambda n, s: (0, n))
    return pl.pallas_call(
        functools.partial(combine_kernel, parts, len(pieces)),
        grid_spec=pltpu.PrefetchScalarGridSpec(
            num_scalar_prefetch=1,
            grid=(units // tile,),
            in_specs=[pl.BlockSpec((rows, 2 * rank), lambda n, s: (0, 0)), column_spec, column_spec, ANY_SPEC]
            + [ANY_SPEC] * len(parts)
            + [pl.BlockSpec((rank, rows), lambda n, s: (0, 0))] * len(pieces),
            out_specs=column_spec,
            scratch_shapes=[
                pltpu.VMEM((rows, ranks_all), jnp.bfloat16),
                pltpu.VMEM((ranks_all, units), jnp.bfloat16),
                pltpu.SemaphoreType.DMA((1 + len(parts),)),
            ],
        ),
        out_shape=jax.ShapeDtypeStruct((rows, units), jnp.bfloat16),
        compiler_params=pltpu.CompilerParams(vmem_limit_bytes=rows * ranks_all * 2 + 16 * MIB),
        cost_estimate=pl.CostEstimate(
            flops=2 * rows * ranks_all * units, bytes_accessed=10 * rows * units, transcendentals=0
        ),
        name="combine",
    )(me, users, gate, up, own_maps, *map_parts, *pieces)


def exchange_order(size):
    return tuple(sorted(range(1, size), key=lambda part: -(part // 4)))


def per_device(
    tokens,
    gate_weight,
    up_weight,
    adapter_down_weight,
    adapter_up_weight,
    row_adapter,
    sorted_rows,
    segment_count,
):
    axis = "tensor"
    size = lax.axis_size(axis)
    me = lax.axis_index(axis)
    resident, rank, width = adapter_down_weight.shape
    ranks = resident * rank
    rows = row_adapter.shape[0]
    me_array = me.astype(jnp.int32).reshape(1)

    own_maps = adapter_up_weight.reshape(ranks, -1)
    parts = exchange_order(size)
    released = {2: 4, 3: 4}
    last_step = size // CORES // 2
    cut = []
    map_parts = []

    def beside(step, values):
        nonlocal cut
        if step == 1:
            maps, *values = lax.optimization_barrier((own_maps, *values))
            cut = cut_columns(me_array, maps, parts, size)
            return values
        count = released.get(step, 0) if step < last_step else len(parts)
        done = len(map_parts)
        chosen, values = lax.optimization_barrier((cut[done : done + count], values))
        for part, value in zip(parts[done:], chosen):
            map_parts.append(lax.ppermute(value, axis, [(d, d ^ part) for d in range(size)]))
        return values

    found, where = ring_gather(tokens, axis, beside)
    pieces = [piece for piece, _ in found]
    columns = [column for _, column in found]
    table = jnp.array([row + [device] for device, row in enumerate(where)], jnp.int32)
    place = lax.dynamic_index_in_dim(table, me, 0, keepdims=False)

    shrunk = shrink(place, columns, pieces, row_adapter, adapter_down_weight.reshape(ranks, width), rank)
    near = min(4, size)
    plane = shrunk
    for flip in range(1, near):
        plane = plane + lax.ppermute(shrunk, axis, [(d, d ^ flip) for d in range(size)])
    shrunk_pieces = [plane]
    for shift in range(1, size // near):
        shrunk_pieces.append(
            lax.ppermute(plane, axis, [(d, (d + shift * near) % size) for d in range(size)])
        )
    gate, up = project(place, columns, pieces, gate_weight, up_weight, rows)
    return combine(me_array, row_adapter, gate, up, own_maps, parts, map_parts, shrunk_pieces)


def solution(mesh):
    placed = (
        P(("groups", "tensor"), None),
        P(None, "tensor"),
        P(None, "tensor"),
        P(("groups", "tensor"), None, None),
        P(("groups", "tensor"), None, None),
        P("groups"),
        P("groups"),
        P("groups"),
    )
    return jax.shard_map(
        per_device, mesh=mesh, in_specs=placed, out_specs=P("groups", "tensor"), check_vma=False
    )
```

```python
import functools

import jax
import jax.numpy as jnp
from jax import lax
from jax.experimental import pallas as pl
from jax.experimental.pallas import tpu as pltpu
from jax.sharding import PartitionSpec as P

ADAPTER_SCALE = 0.5
CORES = 2
MIB = 1024 * 1024


def chip_ring(chips):
    return list(range(0, chips, 2)) + list(range(chips - 1, 0, -2))


def ring_gather(block, axis, beside):
    size = lax.axis_size(axis)
    chips = size // CORES
    ring = chip_ring(chips)

    def moved(value, shift):
        pairs = [
            (ring[p] * CORES + k, ring[(p + shift) % chips] * CORES + k)
            for p in range(chips)
            for k in range(CORES)
        ]
        return lax.ppermute(value, axis, pairs)

    def other_core(value):
        return lax.ppermute(value, axis, [(d, d ^ 1) for d in range(size)])

    pieces = [(block, 0)]
    where = [[device] for device in range(size)]

    def arrived(values, columns, distances):
        for value, column, distance in zip(values, columns, distances):
            pieces.append((value, column))
            for device in range(size):
                chip = ring[(ring.index(device // CORES) + distance) % chips]
                where[device].append(chip * CORES + device % CORES)

    def crossed(values, columns, distances):
        for value, column, distance in zip(values, columns, distances):
            pieces.append((value, column))
            for device in range(size):
                chip = ring[(ring.index(device // CORES) + distance) % chips]
                where[device].append(chip * CORES + 1 - device % CORES)

    waiting = ((block,), (0,), (0,))
    right = left = block
    for step in range(1, chips // 2):
        over = [other_core(value) for value in waiting[0]]
        right, left = moved(right, 1), moved(left, -1)
        right, left, *over = lax.optimization_barrier((right, left, *over))
        right, left = beside(step, (right, left))
        crossed(over, *waiting[1:])
        waiting = ((right, left), (0, 0), (-step, step))
        arrived(*waiting)
    half = block.shape[1] // 2
    far = chips // 2
    over = [other_core(value) for value in waiting[0]]
    ends = moved(right[:, :half], 1), moved(left[:, half:], -1)
    ends = beside(far, lax.optimization_barrier((*ends, *over)))
    ends, over = ends[:2], ends[2:]
    crossed(over, *waiting[1:])
    waiting = (ends, (0, half), (far, far))
    arrived(*waiting)
    crossed([other_core(value) for value in ends], *waiting[1:])
    return pieces, where


def assemble(spots, columns, piece_refs, tokens_vmem, sems):
    copies = []
    for i, ref in enumerate(piece_refs):
        rows, width = ref.shape
        start = pl.multiple_of(spots[i] * rows, rows)
        copies.append(
            pltpu.make_async_copy(
                ref, tokens_vmem.at[pl.ds(start, rows), pl.ds(columns[i], width)], sems.at[i]
            )
        )
    for copy in copies:
        copy.start()
    for copy in copies:
        copy.wait()


def split_kernel(in_ref, out_ref):
    width = out_ref.shape[2]
    for part in range(out_ref.shape[0]):
        out_ref[part] = in_ref[:, part * width : (part + 1) * width]


def split_columns(weights, parts):
    rows, columns = weights.shape
    width = columns // parts
    group = min(4, parts)
    return pl.pallas_call(
        split_kernel,
        grid=(parts // group,),
        in_specs=[pl.BlockSpec((rows, group * width), lambda i: (0, i))],
        out_specs=pl.BlockSpec((group, rows, width), lambda i: (i, 0, 0)),
        out_shape=jax.ShapeDtypeStruct((parts, rows, width), weights.dtype),
        name="split_columns",
    )(weights)


def in_hbm(values):
    return [pltpu.with_memory_space_constraint(value, pltpu.HBM) for value in values]


ANY_SPEC = pl.BlockSpec(memory_space=pl.ANY)


def shrink_kernel(columns, pieces, rank, place, users_ref, down_ref, *refs):
    piece_refs = refs[:pieces]
    out_ref, tokens_vmem, sems = refs[pieces:]
    assemble(place, columns, piece_refs, tokens_vmem, sems)
    ranks = down_ref.shape[0]
    resident = ranks // rank
    shrunk = lax.dot_general(
        tokens_vmem[...], down_ref[...], (((1,), (1,)), ((), ())), preferred_element_type=jnp.float32
    )
    turned = jnp.transpose(shrunk)
    total = jnp.zeros(out_ref.shape, jnp.float32)
    for r in range(resident):
        mine = users_ref[...] == place[pieces] * resident + r
        total += jnp.where(mine, turned[r * rank : (r + 1) * rank], 0.0)
    out_ref[...] = total.astype(out_ref.dtype)


def shrink(place, columns, pieces, row_adapter, down, rank):
    ranks, width = down.shape
    rows = row_adapter.shape[0]
    return pl.pallas_call(
        functools.partial(shrink_kernel, columns, len(pieces), rank),
        grid_spec=pltpu.PrefetchScalarGridSpec(
            num_scalar_prefetch=1,
            grid=(1,),
            in_specs=[
                pl.BlockSpec((1, rows), lambda i, s: (0, 0)),
                pl.BlockSpec((ranks, width), lambda i, s: (0, 0)),
            ]
            + [ANY_SPEC] * len(pieces),
            out_specs=pl.BlockSpec((rank, rows), lambda i, s: (0, 0)),
            scratch_shapes=[
                pltpu.VMEM((rows, width), jnp.bfloat16),
                pltpu.SemaphoreType.DMA((len(pieces),)),
            ],
        ),
        out_shape=jax.ShapeDtypeStruct((rank, rows), jnp.bfloat16),
        compiler_params=pltpu.CompilerParams(vmem_limit_bytes=rows * width * 2 + 8 * MIB),
        cost_estimate=pl.CostEstimate(
            flops=2 * rows * width * ranks, bytes_accessed=2 * (rows + ranks) * width, transcendentals=0
        ),
        name="shrink",
    )(place, row_adapter.reshape(1, rows), *in_hbm([down, *pieces]))


def project_kernel(columns, pieces, place, gate_weight_ref, up_weight_ref, *refs):
    piece_refs = refs[:pieces]
    gate_ref, up_ref, tokens_vmem, sems = refs[pieces:]
    depth = gate_weight_ref.shape[0]
    k = pl.program_id(0)

    @pl.when(k == 0)
    def _():
        assemble(place, columns, piece_refs, tokens_vmem, sems)
        gate_ref[...] = jnp.zeros_like(gate_ref)
        up_ref[...] = jnp.zeros_like(up_ref)

    tokens = tokens_vmem[:, pl.ds(pl.multiple_of(k * depth, depth), depth)]
    gate_ref[...] += jnp.dot(tokens, gate_weight_ref[...], preferred_element_type=jnp.float32)
    up_ref[...] += jnp.dot(tokens, up_weight_ref[...], preferred_element_type=jnp.float32)

    @pl.when(k == pl.num_programs(0) - 1)
    def _():
        gate = gate_ref[...]
        gate_ref[...] = gate / (1.0 + jnp.exp(-gate))


def project(place, columns, pieces, gate_weight, up_weight, rows):
    width, units = gate_weight.shape
    depth = min(1024, width)
    weight_spec = pl.BlockSpec((depth, units), lambda k, s: (k, 0))
    out_spec = pl.BlockSpec((rows, units), lambda k, s: (0, 0))
    out = pltpu.HBM((rows, units), jnp.float32)
    return pl.pallas_call(
        functools.partial(project_kernel, columns, len(pieces)),
        grid_spec=pltpu.PrefetchScalarGridSpec(
            num_scalar_prefetch=1,
            grid=(width // depth,),
            in_specs=[weight_spec, weight_spec] + [ANY_SPEC] * len(pieces),
            out_specs=[out_spec, out_spec],
            scratch_shapes=[
                pltpu.VMEM((rows, width), jnp.bfloat16),
                pltpu.SemaphoreType.DMA((len(pieces),)),
            ],
        ),
        out_shape=[out, out],
        compiler_params=pltpu.CompilerParams(vmem_limit_bytes=rows * width * 2 + 20 * MIB),
        cost_estimate=pl.CostEstimate(
            flops=4 * rows * width * units,
            bytes_accessed=2 * (rows + 2 * units) * width,
            transcendentals=rows * units,
        ),
        name="project",
    )(place, *in_hbm([gate_weight, up_weight, *pieces]))


def spread_kernel(pieces, users_ref, *refs):
    piece_refs = refs[:pieces]
    out_ref = refs[pieces]
    rank = piece_refs[0].shape[0]
    total = piece_refs[0][...].astype(jnp.float32)
    for ref in piece_refs[1:]:
        total += ref[...].astype(jnp.float32)
    pair = jnp.transpose(jnp.concatenate([total, total], axis=0))
    users = users_ref[...]
    column = lax.broadcasted_iota(jnp.int32, pair.shape, 1)
    for start in range(0, out_ref.shape[1], 2 * rank):
        mine = users == (start + column) // rank
        out_ref[:, start : start + 2 * rank] = jnp.where(mine, pair, 0.0).astype(out_ref.dtype)


def spread(row_adapter, pieces, ranks_all):
    rank, rows = pieces[0].shape
    users = jnp.broadcast_to(row_adapter[:, None], (rows, 2 * rank))
    return pl.pallas_call(
        functools.partial(spread_kernel, len(pieces)),
        out_shape=pltpu.HBM((rows, ranks_all), jnp.bfloat16),
        compiler_params=pltpu.CompilerParams(vmem_limit_bytes=rows * ranks_all * 2 + 12 * MIB),
        cost_estimate=pl.CostEstimate(
            flops=rows * ranks_all, bytes_accessed=2 * rows * ranks_all, transcendentals=0
        ),
        name="spread",
    )(users, *pieces)


def combine_kernel(shrunk_ref, gate_ref, up_ref, maps_ref, out_ref):
    delta = jnp.dot(shrunk_ref[...], maps_ref[...], preferred_element_type=jnp.float32)
    delta = (ADAPTER_SCALE * delta).astype(jnp.bfloat16).astype(jnp.float32)
    out_ref[...] = (gate_ref[...] * (up_ref[...] + delta)).astype(out_ref.dtype)


def combine(shrunk, gate, up, maps):
    rows, units = gate.shape
    ranks_all = maps.shape[0]
    tile = min(256, units)
    column_spec = pl.BlockSpec((rows, tile), lambda n: (0, n))
    return pl.pallas_call(
        combine_kernel,
        grid=(units // tile,),
        in_specs=[
            pl.BlockSpec((rows, ranks_all), lambda n: (0, 0)),
            column_spec,
            column_spec,
            pl.BlockSpec((ranks_all, tile), lambda n: (0, n)),
        ],
        out_specs=column_spec,
        out_shape=jax.ShapeDtypeStruct((rows, units), jnp.bfloat16),
        compiler_params=pltpu.CompilerParams(vmem_limit_bytes=rows * ranks_all * 4 + 16 * MIB),
        cost_estimate=pl.CostEstimate(
            flops=2 * rows * ranks_all * units, bytes_accessed=10 * rows * units, transcendentals=0
        ),
        name="combine",
    )(*in_hbm([shrunk, gate, up]), maps)


def per_device(
    tokens,
    gate_weight,
    up_weight,
    adapter_down_weight,
    adapter_up_weight,
    row_adapter,
    sorted_rows,
    segment_count,
):
    axis = "tensor"
    size = lax.axis_size(axis)
    me = lax.axis_index(axis)
    resident, rank, width = adapter_down_weight.shape
    ranks = resident * rank
    rows = row_adapter.shape[0]

    own_maps = adapter_up_weight.reshape(ranks, -1)
    steps = size // CORES // 2
    maps = None

    def beside(step, values):
        nonlocal own_maps, maps
        if step not in (1, 2, steps):
            return values
        own_maps, *values = lax.optimization_barrier((own_maps, *values))
        if step == 1:
            own_maps = split_columns(own_maps, size)
        if step == steps:
            maps = lax.all_to_all(own_maps, axis, split_axis=0, concat_axis=0, tiled=True)
        return values

    found, where = ring_gather(tokens, axis, beside)
    pieces = [piece for piece, _ in found]
    columns = [column for _, column in found]
    table = jnp.array([row + [device] for device, row in enumerate(where)], jnp.int32)
    place = lax.dynamic_index_in_dim(table, me, 0, keepdims=False)

    shrunk = shrink(place, columns, pieces, row_adapter, adapter_down_weight.reshape(ranks, width), rank)
    near = min(4, size)
    plane = shrunk
    for flip in range(1, near):
        plane = plane + lax.ppermute(shrunk, axis, [(d, d ^ flip) for d in range(size)])
    shrunk_pieces = [plane]
    for shift in range(1, size // near):
        shrunk_pieces.append(
            lax.ppermute(plane, axis, [(d, (d + shift * near) % size) for d in range(size)])
        )
    gate, up = project(place, columns, pieces, gate_weight, up_weight, rows)
    spread_shrunk = spread(row_adapter, shrunk_pieces, size * ranks)
    return combine(spread_shrunk, gate, up, maps.reshape(size * ranks, -1))


def solution(mesh):
    placed = (
        P(("groups", "tensor"), None),
        P(None, "tensor"),
        P(None, "tensor"),
        P(("groups", "tensor"), None, None),
        P(("groups", "tensor"), None, None),
        P("groups"),
        P("groups"),
        P("groups"),
    )
    return jax.shard_map(
        per_device, mesh=mesh, in_specs=placed, out_specs=P("groups", "tensor"), check_vma=False
    )
```

```python
import functools

import jax
import jax.numpy as jnp
from jax import lax
from jax.experimental import pallas as pl
from jax.experimental.pallas import tpu as pltpu
from jax.sharding import PartitionSpec as P

ADAPTER_SCALE = 0.5
CORES = 2
MIB = 1024 * 1024


def chip_ring(chips):
    return list(range(0, chips, 2)) + list(range(chips - 1, 0, -2))


def ring_gather(block, axis, beside):
    size = lax.axis_size(axis)
    chips = size // CORES
    ring = chip_ring(chips)

    def moved(value, shift):
        pairs = [
            (ring[p] * CORES + k, ring[(p + shift) % chips] * CORES + k)
            for p in range(chips)
            for k in range(CORES)
        ]
        return lax.ppermute(value, axis, pairs)

    pieces = [(block, 0, 0)]
    right = left = block
    for step in range(1, chips // 2):
        right, left = beside(step, (moved(right, 1), moved(left, -1)))
        pieces += [(right, 0, -step), (left, 0, step)]
    half = block.shape[1] // 2
    far = chips // 2
    right, left = beside(far, (moved(right[:, :half], 1), moved(left[:, half:], -1)))
    pieces += [(right, 0, far), (left, half, far)]

    flips = [(d, d ^ 1) for d in range(size)]
    found = [(value, column) for value, column, _ in pieces]
    found += [(lax.ppermute(value, axis, flips), column) for value, column, _ in pieces]
    where = [
        [
            ring[(ring.index(device // CORES) + distance) % chips] * CORES + core
            for core in (device % CORES, 1 - device % CORES)
            for _, _, distance in pieces
        ]
        for device in range(size)
    ]
    return found, where


def assemble(spots, columns, piece_refs, tokens_vmem, sems):
    copies = []
    for i, ref in enumerate(piece_refs):
        rows, width = ref.shape
        start = pl.multiple_of(spots[i] * rows, rows)
        copies.append(
            pltpu.make_async_copy(
                ref, tokens_vmem.at[pl.ds(start, rows), pl.ds(columns[i], width)], sems.at[i]
            )
        )
    for copy in copies:
        copy.start()
    for copy in copies:
        copy.wait()


def split_kernel(in_ref, out_ref):
    width = out_ref.shape[2]
    for part in range(out_ref.shape[0]):
        out_ref[part] = in_ref[:, part * width : (part + 1) * width]


def split_columns(weights, parts):
    rows, columns = weights.shape
    width = columns // parts
    group = min(4, parts)
    return pl.pallas_call(
        split_kernel,
        grid=(parts // group,),
        in_specs=[pl.BlockSpec((rows, group * width), lambda i: (0, i))],
        out_specs=pl.BlockSpec((group, rows, width), lambda i: (i, 0, 0)),
        out_shape=jax.ShapeDtypeStruct((parts, rows, width), weights.dtype),
        name="split_columns",
    )(weights)


def in_hbm(values):
    return [pltpu.with_memory_space_constraint(value, pltpu.HBM) for value in values]


ANY_SPEC = pl.BlockSpec(memory_space=pl.ANY)


def shrink_kernel(columns, pieces, rank, place, users_ref, down_ref, *refs):
    piece_refs = refs[:pieces]
    out_ref, tokens_vmem, sems = refs[pieces:]
    assemble(place, columns, piece_refs, tokens_vmem, sems)
    ranks = down_ref.shape[0]
    resident = ranks // rank
    shrunk = lax.dot_general(
        tokens_vmem[...], down_ref[...], (((1,), (1,)), ((), ())), preferred_element_type=jnp.float32
    )
    turned = jnp.transpose(shrunk)
    total = jnp.zeros(out_ref.shape, jnp.float32)
    for r in range(resident):
        mine = users_ref[...] == place[pieces] * resident + r
        total += jnp.where(mine, turned[r * rank : (r + 1) * rank], 0.0)
    out_ref[...] = total.astype(out_ref.dtype)


def shrink(place, columns, pieces, row_adapter, down, rank):
    ranks, width = down.shape
    rows = row_adapter.shape[0]
    return pl.pallas_call(
        functools.partial(shrink_kernel, columns, len(pieces), rank),
        grid_spec=pltpu.PrefetchScalarGridSpec(
            num_scalar_prefetch=1,
            grid=(1,),
            in_specs=[
                pl.BlockSpec((1, rows), lambda i, s: (0, 0)),
                pl.BlockSpec((ranks, width), lambda i, s: (0, 0)),
            ]
            + [ANY_SPEC] * len(pieces),
            out_specs=pl.BlockSpec((rank, rows), lambda i, s: (0, 0)),
            scratch_shapes=[
                pltpu.VMEM((rows, width), jnp.bfloat16),
                pltpu.SemaphoreType.DMA((len(pieces),)),
            ],
        ),
        out_shape=jax.ShapeDtypeStruct((rank, rows), jnp.bfloat16),
        compiler_params=pltpu.CompilerParams(vmem_limit_bytes=rows * width * 2 + 8 * MIB),
        cost_estimate=pl.CostEstimate(
            flops=2 * rows * width * ranks, bytes_accessed=2 * (rows + ranks) * width, transcendentals=0
        ),
        name="shrink",
    )(place, row_adapter.reshape(1, rows), *in_hbm([down, *pieces]))


def project_kernel(columns, pieces, place, gate_weight_ref, up_weight_ref, *refs):
    piece_refs = refs[:pieces]
    gate_ref, up_ref, tokens_vmem, sems = refs[pieces:]
    depth = gate_weight_ref.shape[0]
    k = pl.program_id(0)

    @pl.when(k == 0)
    def _():
        assemble(place, columns, piece_refs, tokens_vmem, sems)
        gate_ref[...] = jnp.zeros_like(gate_ref)
        up_ref[...] = jnp.zeros_like(up_ref)

    tokens = tokens_vmem[:, pl.ds(pl.multiple_of(k * depth, depth), depth)]
    gate_ref[...] += jnp.dot(tokens, gate_weight_ref[...], preferred_element_type=jnp.float32)
    up_ref[...] += jnp.dot(tokens, up_weight_ref[...], preferred_element_type=jnp.float32)

    @pl.when(k == pl.num_programs(0) - 1)
    def _():
        gate = gate_ref[...]
        gate_ref[...] = gate / (1.0 + jnp.exp(-gate))


def project(place, columns, pieces, gate_weight, up_weight, rows):
    width, units = gate_weight.shape
    depth = min(1024, width)
    weight_spec = pl.BlockSpec((depth, units), lambda k, s: (k, 0))
    out_spec = pl.BlockSpec((rows, units), lambda k, s: (0, 0))
    out = pltpu.HBM((rows, units), jnp.float32)
    return pl.pallas_call(
        functools.partial(project_kernel, columns, len(pieces)),
        grid_spec=pltpu.PrefetchScalarGridSpec(
            num_scalar_prefetch=1,
            grid=(width // depth,),
            in_specs=[weight_spec, weight_spec] + [ANY_SPEC] * len(pieces),
            out_specs=[out_spec, out_spec],
            scratch_shapes=[
                pltpu.VMEM((rows, width), jnp.bfloat16),
                pltpu.SemaphoreType.DMA((len(pieces),)),
            ],
        ),
        out_shape=[out, out],
        compiler_params=pltpu.CompilerParams(vmem_limit_bytes=rows * width * 2 + 20 * MIB),
        cost_estimate=pl.CostEstimate(
            flops=4 * rows * width * units,
            bytes_accessed=2 * (rows + 2 * units) * width,
            transcendentals=rows * units,
        ),
        name="project",
    )(place, *in_hbm([gate_weight, up_weight, *pieces]))


def combine_kernel(pieces, users_ref, gate_ref, up_ref, maps_ref, *refs):
    piece_refs = refs[:pieces]
    out_ref, shrunk_vmem = refs[pieces:]
    rank = piece_refs[0].shape[0]

    @pl.when(pl.program_id(0) == 0)
    def _():
        total = piece_refs[0][...].astype(jnp.float32)
        for ref in piece_refs[1:]:
            total += ref[...].astype(jnp.float32)
        pair = jnp.transpose(jnp.concatenate([total, total], axis=0))
        users = users_ref[...]
        column = lax.broadcasted_iota(jnp.int32, pair.shape, 1)
        for start in range(0, shrunk_vmem.shape[1], 2 * rank):
            mine = users == (start + column) // rank
            shrunk_vmem[:, start : start + 2 * rank] = jnp.where(mine, pair, 0.0).astype(jnp.bfloat16)

    delta = jnp.dot(shrunk_vmem[...], maps_ref[...], preferred_element_type=jnp.float32)
    delta = (ADAPTER_SCALE * delta).astype(jnp.bfloat16).astype(jnp.float32)
    out_ref[...] = (gate_ref[...] * (up_ref[...] + delta)).astype(out_ref.dtype)


def combine(row_adapter, pieces, gate, up, maps):
    rows, units = gate.shape
    ranks_all = maps.shape[0]
    rank = pieces[0].shape[0]
    tile = min(512, units)
    users = jnp.broadcast_to(row_adapter[:, None], (rows, 2 * rank))
    column_spec = pl.BlockSpec((rows, tile), lambda n: (0, n))
    return pl.pallas_call(
        functools.partial(combine_kernel, len(pieces)),
        grid=(units // tile,),
        in_specs=[
            pl.BlockSpec((rows, 2 * rank), lambda n: (0, 0)),
            column_spec,
            column_spec,
            pl.BlockSpec((ranks_all, tile), lambda n: (0, n)),
        ]
        + [pl.BlockSpec((rank, rows), lambda n: (0, 0))] * len(pieces),
        out_specs=column_spec,
        scratch_shapes=[pltpu.VMEM((rows, ranks_all), jnp.bfloat16)],
        out_shape=jax.ShapeDtypeStruct((rows, units), jnp.bfloat16),
        compiler_params=pltpu.CompilerParams(vmem_limit_bytes=rows * ranks_all * 4 + 16 * MIB),
        cost_estimate=pl.CostEstimate(
            flops=2 * rows * ranks_all * units, bytes_accessed=10 * rows * units, transcendentals=0
        ),
        name="combine",
    )(*in_hbm([users, gate, up]), maps, *in_hbm(pieces))


def per_device(
    tokens,
    gate_weight,
    up_weight,
    adapter_down_weight,
    adapter_up_weight,
    row_adapter,
    sorted_rows,
    segment_count,
):
    axis = "tensor"
    size = lax.axis_size(axis)
    me = lax.axis_index(axis)
    resident, rank, width = adapter_down_weight.shape
    ranks = resident * rank
    rows = row_adapter.shape[0]

    own_maps = adapter_up_weight.reshape(ranks, -1)
    steps = size // CORES // 2
    maps = None

    def beside(step, values):
        nonlocal own_maps, maps
        if step not in (1, 2, steps):
            return values
        own_maps, *values = lax.optimization_barrier((own_maps, *values))
        if step == 1:
            own_maps = split_columns(own_maps, size)
        if step == steps:
            maps = lax.all_to_all(own_maps, axis, split_axis=0, concat_axis=0, tiled=True)
        return values

    found, where = ring_gather(tokens, axis, beside)
    pieces = [piece for piece, _ in found]
    columns = [column for _, column in found]
    table = jnp.array([row + [device] for device, row in enumerate(where)], jnp.int32)
    place = lax.dynamic_index_in_dim(table, me, 0, keepdims=False)

    shrunk = shrink(place, columns, pieces, row_adapter, adapter_down_weight.reshape(ranks, width), rank)
    near = min(4, size)
    plane = shrunk
    for flip in range(1, near):
        plane = plane + lax.ppermute(shrunk, axis, [(d, d ^ flip) for d in range(size)])
    shrunk_pieces = [plane]
    for shift in range(1, size // near):
        shrunk_pieces.append(
            lax.ppermute(plane, axis, [(d, (d + shift * near) % size) for d in range(size)])
        )
    gate, up = project(place, columns, pieces, gate_weight, up_weight, rows)
    return combine(row_adapter, shrunk_pieces, gate, up, maps.reshape(size * ranks, -1))


def solution(mesh):
    placed = (
        P(("groups", "tensor"), None),
        P(None, "tensor"),
        P(None, "tensor"),
        P(("groups", "tensor"), None, None),
        P(("groups", "tensor"), None, None),
        P("groups"),
        P("groups"),
        P("groups"),
    )
    return jax.shard_map(
        per_device, mesh=mesh, in_specs=placed, out_specs=P("groups", "tensor"), check_vma=False
    )
```

```python
import functools

import jax
import jax.numpy as jnp
from jax import lax
from jax.experimental import pallas as pl
from jax.experimental.pallas import tpu as pltpu
from jax.sharding import PartitionSpec as P

ADAPTER_SCALE = 0.5
CORES = 2
MIB = 1024 * 1024


def chip_ring(chips):
    return list(range(0, chips, 2)) + list(range(chips - 1, 0, -2))


def ring_gather(block, axis, beside):
    size = lax.axis_size(axis)
    chips = size // CORES
    ring = chip_ring(chips)

    def moved(value, shift):
        pairs = [
            (ring[p] * CORES + k, ring[(p + shift) % chips] * CORES + k)
            for p in range(chips)
            for k in range(CORES)
        ]
        return lax.ppermute(value, axis, pairs)

    half = block.shape[1] // 2
    far = chips // 2
    halves = block[:, :half], block[:, half:]
    columns = (0, half), (half, 0)
    held = [halves, halves[::-1]]
    pieces = [(block, 0, 0)]
    for step in range(1, far + 1):
        for chain in range(1 if step == far else 2):
            right, left = held[chain]
            held[chain] = beside(chain, step, (moved(right, 1), moved(left, -1)))
            for value, column, distance in zip(held[chain], columns[chain], (-step, step)):
                pieces.append((value, column, distance))

    flips = [(d, d ^ 1) for d in range(size)]
    found = [(value, column) for value, column, _ in pieces]
    found += [(lax.ppermute(value, axis, flips), column) for value, column, _ in pieces]
    where = [
        [
            ring[(ring.index(device // CORES) + distance) % chips] * CORES + core
            for core in (device % CORES, 1 - device % CORES)
            for _, _, distance in pieces
        ]
        for device in range(size)
    ]
    return found, where


def assemble(spots, columns, piece_refs, tokens_vmem, sems):
    copies = []
    for i, ref in enumerate(piece_refs):
        rows, width = ref.shape
        start = pl.multiple_of(spots[i] * rows, rows)
        copies.append(
            pltpu.make_async_copy(
                ref, tokens_vmem.at[pl.ds(start, rows), pl.ds(columns[i], width)], sems.at[i]
            )
        )
    for copy in copies:
        copy.start()
    for copy in copies:
        copy.wait()


def split_kernel(in_ref, out_ref):
    width = out_ref.shape[2]
    for part in range(out_ref.shape[0]):
        out_ref[part] = in_ref[:, part * width : (part + 1) * width]


def split_columns(weights, parts):
    rows, columns = weights.shape
    width = columns // parts
    group = min(4, parts)
    return pl.pallas_call(
        split_kernel,
        grid=(parts // group,),
        in_specs=[pl.BlockSpec((rows, group * width), lambda i: (0, i))],
        out_specs=pl.BlockSpec((group, rows, width), lambda i: (i, 0, 0)),
        out_shape=jax.ShapeDtypeStruct((parts, rows, width), weights.dtype),
        name="split_columns",
    )(weights)


def in_hbm(values):
    return [pltpu.with_memory_space_constraint(value, pltpu.HBM) for value in values]


ANY_SPEC = pl.BlockSpec(memory_space=pl.ANY)


def shrink_kernel(columns, pieces, rank, place, users_ref, down_ref, *refs):
    piece_refs = refs[:pieces]
    out_ref, tokens_vmem, sems = refs[pieces:]
    assemble(place, columns, piece_refs, tokens_vmem, sems)
    ranks = down_ref.shape[0]
    resident = ranks // rank
    shrunk = lax.dot_general(
        tokens_vmem[...], down_ref[...], (((1,), (1,)), ((), ())), preferred_element_type=jnp.float32
    )
    turned = jnp.transpose(shrunk)
    total = jnp.zeros(out_ref.shape, jnp.float32)
    for r in range(resident):
        mine = users_ref[...] == place[pieces] * resident + r
        total += jnp.where(mine, turned[r * rank : (r + 1) * rank], 0.0)
    out_ref[...] = total.astype(out_ref.dtype)


def shrink(place, columns, pieces, row_adapter, down, rank):
    ranks, width = down.shape
    rows = row_adapter.shape[0]
    return pl.pallas_call(
        functools.partial(shrink_kernel, columns, len(pieces), rank),
        grid_spec=pltpu.PrefetchScalarGridSpec(
            num_scalar_prefetch=1,
            grid=(1,),
            in_specs=[
                pl.BlockSpec((1, rows), lambda i, s: (0, 0)),
                pl.BlockSpec((ranks, width), lambda i, s: (0, 0)),
            ]
            + [ANY_SPEC] * len(pieces),
            out_specs=pl.BlockSpec((rank, rows), lambda i, s: (0, 0)),
            scratch_shapes=[
                pltpu.VMEM((rows, width), jnp.bfloat16),
                pltpu.SemaphoreType.DMA((len(pieces),)),
            ],
        ),
        out_shape=jax.ShapeDtypeStruct((rank, rows), jnp.bfloat16),
        compiler_params=pltpu.CompilerParams(vmem_limit_bytes=rows * width * 2 + 8 * MIB),
        cost_estimate=pl.CostEstimate(
            flops=2 * rows * width * ranks, bytes_accessed=2 * (rows + ranks) * width, transcendentals=0
        ),
        name="shrink",
    )(place, row_adapter.reshape(1, rows), *in_hbm([down, *pieces]))


def project_kernel(columns, pieces, place, gate_weight_ref, up_weight_ref, *refs):
    piece_refs = refs[:pieces]
    gate_ref, up_ref, tokens_vmem, sems = refs[pieces:]
    depth = gate_weight_ref.shape[0]
    k = pl.program_id(0)

    @pl.when(k == 0)
    def _():
        assemble(place, columns, piece_refs, tokens_vmem, sems)
        gate_ref[...] = jnp.zeros_like(gate_ref)
        up_ref[...] = jnp.zeros_like(up_ref)

    tokens = tokens_vmem[:, pl.ds(pl.multiple_of(k * depth, depth), depth)]
    gate_ref[...] += jnp.dot(tokens, gate_weight_ref[...], preferred_element_type=jnp.float32)
    up_ref[...] += jnp.dot(tokens, up_weight_ref[...], preferred_element_type=jnp.float32)

    @pl.when(k == pl.num_programs(0) - 1)
    def _():
        gate = gate_ref[...]
        gate_ref[...] = gate / (1.0 + jnp.exp(-gate))


def project(place, columns, pieces, gate_weight, up_weight, rows):
    width, units = gate_weight.shape
    depth = min(1024, width)
    weight_spec = pl.BlockSpec((depth, units), lambda k, s: (k, 0))
    out_spec = pl.BlockSpec((rows, units), lambda k, s: (0, 0))
    out = pltpu.HBM((rows, units), jnp.float32)
    return pl.pallas_call(
        functools.partial(project_kernel, columns, len(pieces)),
        grid_spec=pltpu.PrefetchScalarGridSpec(
            num_scalar_prefetch=1,
            grid=(width // depth,),
            in_specs=[weight_spec, weight_spec] + [ANY_SPEC] * len(pieces),
            out_specs=[out_spec, out_spec],
            scratch_shapes=[
                pltpu.VMEM((rows, width), jnp.bfloat16),
                pltpu.SemaphoreType.DMA((len(pieces),)),
            ],
        ),
        out_shape=[out, out],
        compiler_params=pltpu.CompilerParams(vmem_limit_bytes=rows * width * 2 + 20 * MIB),
        cost_estimate=pl.CostEstimate(
            flops=4 * rows * width * units,
            bytes_accessed=2 * (rows + 2 * units) * width,
            transcendentals=rows * units,
        ),
        name="project",
    )(place, *in_hbm([gate_weight, up_weight, *pieces]))


def combine_kernel(pieces, users_ref, gate_ref, up_ref, maps_ref, *refs):
    piece_refs = refs[:pieces]
    out_ref, shrunk_vmem = refs[pieces:]
    rank = piece_refs[0].shape[0]

    @pl.when(pl.program_id(0) == 0)
    def _():
        total = piece_refs[0][...].astype(jnp.float32)
        for ref in piece_refs[1:]:
            total += ref[...].astype(jnp.float32)
        pair = jnp.transpose(jnp.concatenate([total, total], axis=0))
        users = users_ref[...]
        column = lax.broadcasted_iota(jnp.int32, pair.shape, 1)
        for start in range(0, shrunk_vmem.shape[1], 2 * rank):
            mine = users == (start + column) // rank
            shrunk_vmem[:, start : start + 2 * rank] = jnp.where(mine, pair, 0.0).astype(jnp.bfloat16)

    delta = jnp.dot(shrunk_vmem[...], maps_ref[...], preferred_element_type=jnp.float32)
    delta = (ADAPTER_SCALE * delta).astype(jnp.bfloat16).astype(jnp.float32)
    out_ref[...] = (gate_ref[...] * (up_ref[...] + delta)).astype(out_ref.dtype)


def combine(row_adapter, pieces, gate, up, maps):
    rows, units = gate.shape
    ranks_all = maps.shape[0]
    rank = pieces[0].shape[0]
    tile = min(512, units)
    users = jnp.broadcast_to(row_adapter[:, None], (rows, 2 * rank))
    column_spec = pl.BlockSpec((rows, tile), lambda n: (0, n))
    return pl.pallas_call(
        functools.partial(combine_kernel, len(pieces)),
        grid=(units // tile,),
        in_specs=[
            pl.BlockSpec((rows, 2 * rank), lambda n: (0, 0)),
            column_spec,
            column_spec,
            pl.BlockSpec((ranks_all, tile), lambda n: (0, n)),
        ]
        + [pl.BlockSpec((rank, rows), lambda n: (0, 0))] * len(pieces),
        out_specs=column_spec,
        scratch_shapes=[pltpu.VMEM((rows, ranks_all), jnp.bfloat16)],
        out_shape=jax.ShapeDtypeStruct((rows, units), jnp.bfloat16),
        compiler_params=pltpu.CompilerParams(vmem_limit_bytes=rows * ranks_all * 4 + 16 * MIB),
        cost_estimate=pl.CostEstimate(
            flops=2 * rows * ranks_all * units, bytes_accessed=10 * rows * units, transcendentals=0
        ),
        name="combine",
    )(*in_hbm([users, gate, up]), maps, *in_hbm(pieces))


def per_device(
    tokens,
    gate_weight,
    up_weight,
    adapter_down_weight,
    adapter_up_weight,
    row_adapter,
    sorted_rows,
    segment_count,
):
    axis = "tensor"
    size = lax.axis_size(axis)
    me = lax.axis_index(axis)
    resident, rank, width = adapter_down_weight.shape
    ranks = resident * rank
    rows = row_adapter.shape[0]

    own_maps = adapter_up_weight.reshape(ranks, -1)
    steps = size // CORES // 2
    maps = None

    def beside(chain, step, values):
        nonlocal own_maps, maps
        if (chain, step) not in ((0, 1), (0, 2), (1, steps - 1)):
            return values
        own_maps, *values = lax.optimization_barrier((own_maps, *values))
        if (chain, step) == (0, 1):
            own_maps = split_columns(own_maps, size)
        if chain == 1:
            maps = lax.all_to_all(own_maps, axis, split_axis=0, concat_axis=0, tiled=True)
        return values

    found, where = ring_gather(tokens, axis, beside)
    pieces = [piece for piece, _ in found]
    columns = [column for _, column in found]
    table = jnp.array([row + [device] for device, row in enumerate(where)], jnp.int32)
    place = lax.dynamic_index_in_dim(table, me, 0, keepdims=False)

    shrunk = shrink(place, columns, pieces, row_adapter, adapter_down_weight.reshape(ranks, width), rank)
    near = min(4, size)
    plane = shrunk
    for flip in range(1, near):
        plane = plane + lax.ppermute(shrunk, axis, [(d, d ^ flip) for d in range(size)])
    shrunk_pieces = [plane]
    for shift in range(1, size // near):
        shrunk_pieces.append(
            lax.ppermute(plane, axis, [(d, (d + shift * near) % size) for d in range(size)])
        )
    gate, up = project(place, columns, pieces, gate_weight, up_weight, rows)
    return combine(row_adapter, shrunk_pieces, gate, up, maps.reshape(size * ranks, -1))


def solution(mesh):
    placed = (
        P(("groups", "tensor"), None),
        P(None, "tensor"),
        P(None, "tensor"),
        P(("groups", "tensor"), None, None),
        P(("groups", "tensor"), None, None),
        P("groups"),
        P("groups"),
        P("groups"),
    )
    return jax.shard_map(
        per_device, mesh=mesh, in_specs=placed, out_specs=P("groups", "tensor"), check_vma=False
    )
```

```python
import functools

import jax
import jax.numpy as jnp
from jax import lax
from jax.experimental import pallas as pl
from jax.experimental.pallas import tpu as pltpu
from jax.sharding import PartitionSpec as P

ADAPTER_SCALE = 0.5
CORES = 2
MIB = 1024 * 1024


def chip_ring(chips):
    return list(range(0, chips, 2)) + list(range(chips - 1, 0, -2))


def ring_gather(block, axis, beside):
    size = lax.axis_size(axis)
    chips = size // CORES
    ring = chip_ring(chips)

    def moved(value, shift):
        pairs = [
            (ring[p] * CORES + k, ring[(p + shift) % chips] * CORES + k)
            for p in range(chips)
            for k in range(CORES)
        ]
        return lax.ppermute(value, axis, pairs)

    half = block.shape[1] // 2
    far = chips // 2
    halves = block[:, :half], block[:, half:]
    columns = (0, half), (half, 0)
    held = [halves, halves[::-1]]
    pieces = [(block, 0, 0)]
    for step in range(1, far + 1):
        for chain in range(1 if step == far else 2):
            right, left = held[chain]
            held[chain] = beside(chain, step, (moved(right, 1), moved(left, -1)))
            for value, column, distance in zip(held[chain], columns[chain], (-step, step)):
                pieces.append((value, column, distance))

    flips = [(d, d ^ 1) for d in range(size)]
    found = [(value, column) for value, column, _ in pieces]
    ready = lax.optimization_barrier([value for value, _, _ in pieces])
    found += [(lax.ppermute(value, axis, flips), column) for value, (_, column, _) in zip(ready, pieces)]
    where = [
        [
            ring[(ring.index(device // CORES) + distance) % chips] * CORES + core
            for core in (device % CORES, 1 - device % CORES)
            for _, _, distance in pieces
        ]
        for device in range(size)
    ]
    return found, where


def assemble(spots, columns, piece_refs, tokens_vmem, sems):
    copies = []
    for i, ref in enumerate(piece_refs):
        rows, width = ref.shape
        start = pl.multiple_of(spots[i] * rows, rows)
        copies.append(
            pltpu.make_async_copy(
                ref, tokens_vmem.at[pl.ds(start, rows), pl.ds(columns[i], width)], sems.at[i]
            )
        )
    for copy in copies:
        copy.start()
    for copy in copies:
        copy.wait()


def split_kernel(in_ref, out_ref):
    width = out_ref.shape[2]
    for part in range(out_ref.shape[0]):
        out_ref[part] = in_ref[:, part * width : (part + 1) * width]


def split_columns(weights, parts):
    rows, columns = weights.shape
    width = columns // parts
    group = min(4, parts)
    return pl.pallas_call(
        split_kernel,
        grid=(parts // group,),
        in_specs=[pl.BlockSpec((rows, group * width), lambda i: (0, i))],
        out_specs=pl.BlockSpec((group, rows, width), lambda i: (i, 0, 0)),
        out_shape=jax.ShapeDtypeStruct((parts, rows, width), weights.dtype),
        name="split_columns",
    )(weights)


def in_hbm(values):
    return [pltpu.with_memory_space_constraint(value, pltpu.HBM) for value in values]


ANY_SPEC = pl.BlockSpec(memory_space=pl.ANY)


def shrink_kernel(columns, pieces, rank, place, users_ref, down_ref, *refs):
    piece_refs = refs[:pieces]
    out_ref, tokens_vmem, sems = refs[pieces:]
    assemble(place, columns, piece_refs, tokens_vmem, sems)
    ranks = down_ref.shape[0]
    resident = ranks // rank
    shrunk = lax.dot_general(
        tokens_vmem[...], down_ref[...], (((1,), (1,)), ((), ())), preferred_element_type=jnp.float32
    )
    turned = jnp.transpose(shrunk)
    total = jnp.zeros(out_ref.shape, jnp.float32)
    for r in range(resident):
        mine = users_ref[...] == place[pieces] * resident + r
        total += jnp.where(mine, turned[r * rank : (r + 1) * rank], 0.0)
    out_ref[...] = total.astype(out_ref.dtype)


def shrink(place, columns, pieces, row_adapter, down, rank):
    ranks, width = down.shape
    rows = row_adapter.shape[0]
    return pl.pallas_call(
        functools.partial(shrink_kernel, columns, len(pieces), rank),
        grid_spec=pltpu.PrefetchScalarGridSpec(
            num_scalar_prefetch=1,
            grid=(1,),
            in_specs=[
                pl.BlockSpec((1, rows), lambda i, s: (0, 0)),
                pl.BlockSpec((ranks, width), lambda i, s: (0, 0)),
            ]
            + [ANY_SPEC] * len(pieces),
            out_specs=pl.BlockSpec((rank, rows), lambda i, s: (0, 0)),
            scratch_shapes=[
                pltpu.VMEM((rows, width), jnp.bfloat16),
                pltpu.SemaphoreType.DMA((len(pieces),)),
            ],
        ),
        out_shape=jax.ShapeDtypeStruct((rank, rows), jnp.bfloat16),
        compiler_params=pltpu.CompilerParams(vmem_limit_bytes=rows * width * 2 + 8 * MIB),
        cost_estimate=pl.CostEstimate(
            flops=2 * rows * width * ranks, bytes_accessed=2 * (rows + ranks) * width, transcendentals=0
        ),
        name="shrink",
    )(place, row_adapter.reshape(1, rows), *in_hbm([down, *pieces]))


def project_kernel(columns, pieces, place, gate_weight_ref, up_weight_ref, *refs):
    piece_refs = refs[:pieces]
    gate_ref, up_ref, tokens_vmem, sems = refs[pieces:]
    depth = gate_weight_ref.shape[0]
    k = pl.program_id(0)

    @pl.when(k == 0)
    def _():
        assemble(place, columns, piece_refs, tokens_vmem, sems)
        gate_ref[...] = jnp.zeros_like(gate_ref)
        up_ref[...] = jnp.zeros_like(up_ref)

    tokens = tokens_vmem[:, pl.ds(pl.multiple_of(k * depth, depth), depth)]
    gate_ref[...] += jnp.dot(tokens, gate_weight_ref[...], preferred_element_type=jnp.float32)
    up_ref[...] += jnp.dot(tokens, up_weight_ref[...], preferred_element_type=jnp.float32)

    @pl.when(k == pl.num_programs(0) - 1)
    def _():
        gate = gate_ref[...]
        gate_ref[...] = gate / (1.0 + jnp.exp(-gate))


def project(place, columns, pieces, gate_weight, up_weight, rows):
    width, units = gate_weight.shape
    depth = min(1024, width)
    weight_spec = pl.BlockSpec((depth, units), lambda k, s: (k, 0))
    out_spec = pl.BlockSpec((rows, units), lambda k, s: (0, 0))
    out = pltpu.HBM((rows, units), jnp.float32)
    return pl.pallas_call(
        functools.partial(project_kernel, columns, len(pieces)),
        grid_spec=pltpu.PrefetchScalarGridSpec(
            num_scalar_prefetch=1,
            grid=(width // depth,),
            in_specs=[weight_spec, weight_spec] + [ANY_SPEC] * len(pieces),
            out_specs=[out_spec, out_spec],
            scratch_shapes=[
                pltpu.VMEM((rows, width), jnp.bfloat16),
                pltpu.SemaphoreType.DMA((len(pieces),)),
            ],
        ),
        out_shape=[out, out],
        compiler_params=pltpu.CompilerParams(vmem_limit_bytes=rows * width * 2 + 20 * MIB),
        cost_estimate=pl.CostEstimate(
            flops=4 * rows * width * units,
            bytes_accessed=2 * (rows + 2 * units) * width,
            transcendentals=rows * units,
        ),
        name="project",
    )(place, *in_hbm([gate_weight, up_weight, *pieces]))


def combine_kernel(pieces, users_ref, gate_ref, up_ref, maps_ref, *refs):
    piece_refs = refs[:pieces]
    out_ref, shrunk_vmem = refs[pieces:]
    rank = piece_refs[0].shape[0]

    @pl.when(pl.program_id(0) == 0)
    def _():
        total = piece_refs[0][...].astype(jnp.float32)
        for ref in piece_refs[1:]:
            total += ref[...].astype(jnp.float32)
        pair = jnp.transpose(jnp.concatenate([total, total], axis=0))
        users = users_ref[...]
        column = lax.broadcasted_iota(jnp.int32, pair.shape, 1)
        for start in range(0, shrunk_vmem.shape[1], 2 * rank):
            mine = users == (start + column) // rank
            shrunk_vmem[:, start : start + 2 * rank] = jnp.where(mine, pair, 0.0).astype(jnp.bfloat16)

    delta = jnp.dot(shrunk_vmem[...], maps_ref[...], preferred_element_type=jnp.float32)
    delta = (ADAPTER_SCALE * delta).astype(jnp.bfloat16).astype(jnp.float32)
    out_ref[...] = (gate_ref[...] * (up_ref[...] + delta)).astype(out_ref.dtype)


def combine(row_adapter, pieces, gate, up, maps):
    rows, units = gate.shape
    ranks_all = maps.shape[0]
    rank = pieces[0].shape[0]
    tile = min(512, units)
    users = jnp.broadcast_to(row_adapter[:, None], (rows, 2 * rank))
    column_spec = pl.BlockSpec((rows, tile), lambda n: (0, n))
    return pl.pallas_call(
        functools.partial(combine_kernel, len(pieces)),
        grid=(units // tile,),
        in_specs=[
            pl.BlockSpec((rows, 2 * rank), lambda n: (0, 0)),
            column_spec,
            column_spec,
            pl.BlockSpec((ranks_all, tile), lambda n: (0, n)),
        ]
        + [pl.BlockSpec((rank, rows), lambda n: (0, 0))] * len(pieces),
        out_specs=column_spec,
        scratch_shapes=[pltpu.VMEM((rows, ranks_all), jnp.bfloat16)],
        out_shape=jax.ShapeDtypeStruct((rows, units), jnp.bfloat16),
        compiler_params=pltpu.CompilerParams(vmem_limit_bytes=rows * ranks_all * 4 + 16 * MIB),
        cost_estimate=pl.CostEstimate(
            flops=2 * rows * ranks_all * units, bytes_accessed=10 * rows * units, transcendentals=0
        ),
        name="combine",
    )(*in_hbm([users, gate, up]), maps, *in_hbm(pieces))


def per_device(
    tokens,
    gate_weight,
    up_weight,
    adapter_down_weight,
    adapter_up_weight,
    row_adapter,
    sorted_rows,
    segment_count,
):
    axis = "tensor"
    size = lax.axis_size(axis)
    me = lax.axis_index(axis)
    resident, rank, width = adapter_down_weight.shape
    ranks = resident * rank
    rows = row_adapter.shape[0]

    own_maps = adapter_up_weight.reshape(ranks, -1)
    steps = size // CORES // 2
    maps = None

    def beside(chain, step, values):
        nonlocal own_maps, maps
        if step == steps - 1:
            own_maps, *values = lax.optimization_barrier((own_maps, *values))
            if chain == 1:
                own_maps = split_columns(own_maps, size)
        if step == steps:
            own_maps, *values = lax.optimization_barrier((own_maps, *values))
            maps = lax.all_to_all(own_maps, axis, split_axis=0, concat_axis=0, tiled=True)
        return values

    found, where = ring_gather(tokens, axis, beside)
    pieces = [piece for piece, _ in found]
    columns = [column for _, column in found]
    table = jnp.array([row + [device] for device, row in enumerate(where)], jnp.int32)
    place = lax.dynamic_index_in_dim(table, me, 0, keepdims=False)

    shrunk = shrink(place, columns, pieces, row_adapter, adapter_down_weight.reshape(ranks, width), rank)
    near = min(4, size)
    plane = shrunk
    for flip in range(1, near):
        plane = plane + lax.ppermute(shrunk, axis, [(d, d ^ flip) for d in range(size)])
    shrunk_pieces = [plane]
    for shift in range(1, size // near):
        shrunk_pieces.append(
            lax.ppermute(plane, axis, [(d, (d + shift * near) % size) for d in range(size)])
        )
    gate, up = project(place, columns, pieces, gate_weight, up_weight, rows)
    return combine(row_adapter, shrunk_pieces, gate, up, maps.reshape(size * ranks, -1))


def solution(mesh):
    placed = (
        P(("groups", "tensor"), None),
        P(None, "tensor"),
        P(None, "tensor"),
        P(("groups", "tensor"), None, None),
        P(("groups", "tensor"), None, None),
        P("groups"),
        P("groups"),
        P("groups"),
    )
    return jax.shard_map(
        per_device, mesh=mesh, in_specs=placed, out_specs=P("groups", "tensor"), check_vma=False
    )
```

```python
import functools

import jax
import jax.numpy as jnp
from jax import lax
from jax.experimental import pallas as pl
from jax.experimental.pallas import tpu as pltpu
from jax.sharding import PartitionSpec as P

ADAPTER_SCALE = 0.5
ROWS_PER_LIMIT = 64
SLOT_SIZES = (80, 96)
CORES = 2
MIB = 1024 * 1024


def chip_ring(chips):
    return list(range(0, chips, 2)) + list(range(chips - 1, 0, -2))


def ring_gather(block, axis, beside):
    size = lax.axis_size(axis)
    chips = size // CORES
    ring = chip_ring(chips)

    def moved(value, shift):
        pairs = [
            (ring[p] * CORES + k, ring[(p + shift) % chips] * CORES + k)
            for p in range(chips)
            for k in range(CORES)
        ]
        return lax.ppermute(value, axis, pairs)

    half = block.shape[1] // 2
    far = chips // 2
    halves = block[:, :half], block[:, half:]
    columns = (0, half), (half, 0)
    held = [halves, halves[::-1]]
    pieces = [(block, 0, 0)]
    for step in range(1, far + 1):
        for chain in range(1 if step == far else 2):
            right, left = held[chain]
            held[chain] = beside(chain, step, (moved(right, 1), moved(left, -1)))
            for value, column, distance in zip(held[chain], columns[chain], (-step, step)):
                pieces.append((value, column, distance))

    found = [(value, column) for value, column, _ in pieces]
    where = [
        [ring[(ring.index(device // CORES) + distance) % chips] for _, _, distance in pieces]
        for device in range(size)
    ]
    return found, where


ANY_SPEC = pl.BlockSpec(memory_space=pl.ANY)


def in_hbm(values):
    return [pltpu.with_memory_space_constraint(value, pltpu.HBM) for value in values]


def run_copies(copies):
    for copy in copies:
        copy.start()
    for copy in copies:
        copy.wait()


def split_kernel(me, in_ref, keep_ref, send_ref):
    width = keep_ref.shape[2]
    core = me[0] % CORES
    for pair in range(keep_ref.shape[0]):
        even = in_ref[:, 2 * pair * width : (2 * pair + 1) * width]
        odd = in_ref[:, (2 * pair + 1) * width : (2 * pair + 2) * width]
        keep_ref[pair] = jnp.where(core == 0, even, odd)
        send_ref[pair] = jnp.where(core == 0, odd, even)


def split_columns(me, maps, chips):
    ranks, columns = maps.shape
    units = columns // chips // CORES
    group = min(2, chips)
    out_spec = pl.BlockSpec((group, ranks, units), lambda i, s: (i, 0, 0))
    out = jax.ShapeDtypeStruct((chips, ranks, units), maps.dtype)
    return pl.pallas_call(
        split_kernel,
        grid_spec=pltpu.PrefetchScalarGridSpec(
            num_scalar_prefetch=1,
            grid=(chips // group,),
            in_specs=[pl.BlockSpec((ranks, group * CORES * units), lambda i, s: (0, i))],
            out_specs=[out_spec, out_spec],
        ),
        out_shape=[out, out],
        cost_estimate=pl.CostEstimate(flops=0, bytes_accessed=4 * ranks * columns, transcendentals=0),
        name="split_columns",
    )(me, maps)


def shrink_kernel(columns, pieces, place, own_down_ref, other_down_ref, *refs):
    piece_refs = refs[:pieces]
    tokens_ref, shrunk_ref, tokens_vmem, down_vmem, sems = refs[pieces:]
    core = place[pieces] % CORES
    ranks = own_down_ref.shape[0]
    copies = [
        pltpu.make_async_copy(own_down_ref, down_vmem.at[pl.ds(pl.multiple_of(core * ranks, ranks), ranks)], sems.at[0]),
        pltpu.make_async_copy(
            other_down_ref, down_vmem.at[pl.ds(pl.multiple_of((1 - core) * ranks, ranks), ranks)], sems.at[1]
        ),
    ]
    for i, ref in enumerate(piece_refs):
        rows, width = ref.shape
        start = pl.multiple_of(place[i] * rows, rows)
        copies.append(
            pltpu.make_async_copy(
                ref, tokens_vmem.at[pl.ds(start, rows), pl.ds(columns[i], width)], sems.at[2 + i]
            )
        )
    run_copies(copies)
    out_copy = pltpu.make_async_copy(tokens_vmem, tokens_ref, sems.at[2 + pieces])
    out_copy.start()
    shrunk_ref[...] = lax.dot_general(
        tokens_vmem[...], down_vmem[...], (((1,), (1,)), ((), ())), preferred_element_type=jnp.float32
    ).astype(shrunk_ref.dtype)
    out_copy.wait()


def shrink(place, columns, pieces, rows, own_down, other_down):
    ranks, width = own_down.shape
    return pl.pallas_call(
        functools.partial(shrink_kernel, columns, len(pieces)),
        grid_spec=pltpu.PrefetchScalarGridSpec(
            num_scalar_prefetch=1,
            grid=(1,),
            in_specs=[ANY_SPEC] * (2 + len(pieces)),
            out_specs=[ANY_SPEC, pl.BlockSpec((rows, CORES * ranks), lambda i, s: (0, 0))],
            scratch_shapes=[
                pltpu.VMEM((rows, width), jnp.bfloat16),
                pltpu.VMEM((CORES * ranks, width), jnp.bfloat16),
                pltpu.SemaphoreType.DMA((3 + len(pieces),)),
            ],
        ),
        out_shape=[
            pltpu.HBM((rows, width), jnp.bfloat16),
            jax.ShapeDtypeStruct((rows, CORES * ranks), jnp.bfloat16),
        ],
        compiler_params=pltpu.CompilerParams(vmem_limit_bytes=rows * width * 2 + 16 * MIB),
        cost_estimate=pl.CostEstimate(
            flops=4 * rows * width * ranks, bytes_accessed=4 * (rows + ranks) * width, transcendentals=0
        ),
        name="shrink",
    )(place, own_down, other_down, *pieces)


def expand_kernel(block, bounds, rows_ref, own_ref, other_ref, keep_ref, got_ref, out_ref, shrunk_vmem, maps_vmem):
    adapters = bounds.shape[0] - 2
    core = bounds[adapters + 1] % CORES
    ranks = keep_ref.shape[1]

    @pl.when(pl.program_id(0) == 0)
    def _():
        wanted = rows_ref[:, 0:1]
        slots = wanted.shape[0]
        held = lax.broadcasted_iota(jnp.int32, (slots, own_ref.shape[0]), 1)
        row = held // block * (CORES * block) + held % block
        picked = jnp.zeros(shrunk_vmem.shape, jnp.float32)
        for ref, where in ((own_ref, core), (other_ref, 1 - core)):
            hit = (wanted == row + where * block).astype(jnp.float32).astype(jnp.bfloat16)
            picked += jnp.dot(hit, ref[...], preferred_element_type=jnp.float32)
        slot = lax.broadcasted_iota(jnp.int32, picked.shape, 0)
        adapter = lax.broadcasted_iota(jnp.int32, picked.shape, 1) // (picked.shape[1] // adapters)
        mine = jnp.zeros(picked.shape, jnp.int32)
        for a in range(adapters):
            inside = (adapter == a) & (slot >= bounds[a]) & (slot < bounds[a + 1])
            mine += inside.astype(jnp.int32)
        shrunk_vmem[...] = jnp.where(mine > 0, picked, 0.0).astype(jnp.bfloat16)

    for chip in range(keep_ref.shape[0]):
        maps_vmem[pl.ds(pl.multiple_of(core * ranks, ranks), ranks), :] = keep_ref[chip]
        maps_vmem[pl.ds(pl.multiple_of((1 - core) * ranks, ranks), ranks), :] = got_ref[chip]
        product = jnp.dot(shrunk_vmem[...], maps_vmem[...], preferred_element_type=jnp.float32)
        out_ref[chip] = (ADAPTER_SCALE * product).astype(out_ref.dtype)


def expand(bounds, rows_wanted, own_shrunk, other_shrunk, keep, got, slots, block):
    chips, ranks, units = keep.shape
    rows, ranks_all = own_shrunk.shape
    group = min(4, chips)
    maps_spec = pl.BlockSpec((group, ranks, units), lambda i, s: (i, 0, 0))
    shrunk_spec = pl.BlockSpec((rows, ranks_all), lambda i, s: (0, 0))
    return pl.pallas_call(
        functools.partial(expand_kernel, block),
        grid_spec=pltpu.PrefetchScalarGridSpec(
            num_scalar_prefetch=1,
            grid=(chips // group,),
            in_specs=[
                pl.BlockSpec((slots, 128), lambda i, s: (0, 0)),
                shrunk_spec,
                shrunk_spec,
                maps_spec,
                maps_spec,
            ],
            out_specs=pl.BlockSpec((group, slots, units), lambda i, s: (i, 0, 0)),
            scratch_shapes=[
                pltpu.VMEM((slots, ranks_all), jnp.bfloat16),
                pltpu.VMEM((ranks_all, units), jnp.bfloat16),
            ],
        ),
        out_shape=jax.ShapeDtypeStruct((chips, slots, units), jnp.bfloat16),
        compiler_params=pltpu.CompilerParams(vmem_limit_bytes=20 * MIB),
        cost_estimate=pl.CostEstimate(
            flops=2 * slots * ranks_all * chips * units,
            bytes_accessed=2 * (slots + ranks_all) * chips * units,
            transcendentals=0,
        ),
        name="expand",
    )(bounds, rows_wanted, own_shrunk, other_shrunk, keep, got)


def project_kernel(block, me, gate_weight_ref, up_weight_ref, own_ref, other_ref, gate_ref, up_ref, tokens_vmem, sems):
    depth = gate_weight_ref.shape[0]
    core = me[0] % CORES
    k = pl.program_id(0)

    @pl.when(k == 0)
    def _():
        copies = []
        for ref, where in ((own_ref, core), (other_ref, 1 - core)):
            for chip in range(ref.shape[0] // block):
                start = pl.multiple_of((chip * CORES + where) * block, block)
                copies.append(
                    pltpu.make_async_copy(
                        ref.at[pl.ds(chip * block, block)], tokens_vmem.at[pl.ds(start, block)], sems.at[len(copies)]
                    )
                )
        run_copies(copies)
        gate_ref[...] = jnp.zeros_like(gate_ref)
        up_ref[...] = jnp.zeros_like(up_ref)

    tokens = tokens_vmem[:, pl.ds(pl.multiple_of(k * depth, depth), depth)]
    gate_ref[...] += jnp.dot(tokens, gate_weight_ref[...], preferred_element_type=jnp.float32)
    up_ref[...] += jnp.dot(tokens, up_weight_ref[...], preferred_element_type=jnp.float32)

    @pl.when(k == pl.num_programs(0) - 1)
    def _():
        gate = gate_ref[...]
        gate_ref[...] = gate / (1.0 + jnp.exp(-gate))


def project(me, own, other, gate_weight, up_weight, block):
    width, units = gate_weight.shape
    rows = CORES * own.shape[0]
    depth = min(1024, width)
    weight_spec = pl.BlockSpec((depth, units), lambda k, s: (k, 0))
    out_spec = pl.BlockSpec((rows, units), lambda k, s: (0, 0))
    out = pltpu.HBM((rows, units), jnp.float32)
    return pl.pallas_call(
        functools.partial(project_kernel, block),
        grid_spec=pltpu.PrefetchScalarGridSpec(
            num_scalar_prefetch=1,
            grid=(width // depth,),
            in_specs=[weight_spec, weight_spec, ANY_SPEC, ANY_SPEC],
            out_specs=[out_spec, out_spec],
            scratch_shapes=[
                pltpu.VMEM((rows, width), jnp.bfloat16),
                pltpu.SemaphoreType.DMA((rows // block,)),
            ],
        ),
        out_shape=[out, out],
        compiler_params=pltpu.CompilerParams(vmem_limit_bytes=rows * width * 2 + 20 * MIB),
        cost_estimate=pl.CostEstimate(
            flops=4 * rows * width * units,
            bytes_accessed=2 * (rows + 2 * units) * width,
            transcendentals=rows * units,
        ),
        name="project",
    )(me, *in_hbm([gate_weight, up_weight, own, other]))


def combine_kernel(held_ref, gate_ref, up_ref, products_ref, out_ref, pick_vmem):
    @pl.when(pl.program_id(0) == 0)
    def _():
        row = lax.broadcasted_iota(jnp.int32, pick_vmem.shape, 0)
        pick_vmem[...] = (row == held_ref[0:1, :]).astype(jnp.float32).astype(jnp.bfloat16)

    delta = jnp.dot(pick_vmem[...], products_ref[...], preferred_element_type=jnp.float32)
    out_ref[...] = (gate_ref[...] * (up_ref[...] + delta)).astype(out_ref.dtype)


def combine(held, gate, up, products):
    rows, units = gate.shape
    slots_all = products.shape[0]
    tile = min(512, units)
    column_spec = pl.BlockSpec((rows, tile), lambda n: (0, n))
    return pl.pallas_call(
        combine_kernel,
        grid=(units // tile,),
        in_specs=[
            pl.BlockSpec((8, slots_all), lambda n: (0, 0)),
            column_spec,
            column_spec,
            pl.BlockSpec((slots_all, tile), lambda n: (0, n)),
        ],
        out_specs=column_spec,
        scratch_shapes=[pltpu.VMEM((rows, slots_all), jnp.bfloat16)],
        out_shape=jax.ShapeDtypeStruct((rows, units), jnp.bfloat16),
        compiler_params=pltpu.CompilerParams(vmem_limit_bytes=rows * slots_all * 2 + 20 * MIB),
        cost_estimate=pl.CostEstimate(
            flops=2 * rows * slots_all * units, bytes_accessed=10 * rows * units, transcendentals=0
        ),
        name="combine",
    )(*in_hbm([held, gate, up]), products)


def per_device(
    tokens,
    gate_weight,
    up_weight,
    adapter_down_weight,
    adapter_up_weight,
    row_adapter,
    sorted_rows,
    segment_count,
):
    axis = "tensor"
    size = lax.axis_size(axis)
    me = lax.axis_index(axis).astype(jnp.int32)
    chips = size // CORES
    chip = me // CORES
    resident, rank, width = adapter_down_weight.shape
    ranks = resident * rank
    rows = row_adapter.shape[0]
    block = tokens.shape[0]
    me_array = me.reshape(1)
    flips = [(d, d ^ 1) for d in range(size)]

    def other_core(value):
        return lax.ppermute(value, axis, flips)

    most = CORES * resident * ROWS_PER_LIMIT
    adapters = CORES * resident
    ends = jnp.cumsum(segment_count.reshape(chips, adapters), axis=1)
    totals = ends[:, -1]
    starts = jnp.cumsum(totals) - totals
    slot = jnp.arange(most, dtype=jnp.int32)
    position = starts[:, None] + slot[None, :]
    listed = position[:, :, None] == jnp.arange(rows, dtype=jnp.int32)[None, None, :]
    held = jnp.sum(jnp.where(listed, sorted_rows[None, None, :] + 1, 0), axis=2) - 1
    held = jnp.where(slot[None, :] < totals[:, None], held, -1).astype(jnp.int32)
    wanted = lax.dynamic_index_in_dim(held, chip, 0, keepdims=False)
    wanted = jnp.broadcast_to(wanted[:, None], (most, 128))
    own_ends = lax.dynamic_index_in_dim(ends, chip, 0, keepdims=False)
    bounds = jnp.concatenate([jnp.zeros((1,), jnp.int32), own_ends, me_array]).astype(jnp.int32)
    needed = jnp.full((8, 128), jnp.max(totals), jnp.int32)
    groups = lax.axis_size("groups")
    for shift in range(1, groups):
        needed = jnp.maximum(
            needed, lax.ppermute(needed, "groups", [(g, (g + shift) % groups) for g in range(groups)])
        )
    sizes = [slots for slots in SLOT_SIZES if slots < most] + [most]
    choice = jnp.sum((needed[0, 0] > jnp.array(sizes[:-1], jnp.int32)).astype(jnp.int32))

    own_down = adapter_down_weight.reshape(ranks, width)
    other_down = other_core(own_down)
    own_maps = adapter_up_weight.reshape(ranks, -1)
    steps = chips // 2
    keep = got = None

    def beside(chain, step, values):
        nonlocal own_maps, keep, got
        if step == steps - 1:
            own_maps, *values = lax.optimization_barrier((own_maps, *values))
            if chain == 1:
                keep, send = split_columns(me_array, own_maps, chips)
                got = other_core(send)
        return values

    found, where = ring_gather(tokens, axis, beside)
    pieces = [piece for piece, _ in found]
    columns = [column for _, column in found]
    table = jnp.array([row + [device] for device, row in enumerate(where)], jnp.int32)
    place = lax.dynamic_index_in_dim(table, me, 0, keepdims=False)
    own_tokens, own_shrunk = shrink(place, columns, pieces, rows // CORES, own_down, other_down)
    other_shrunk = other_core(own_shrunk)

    same_core = [[c * CORES + k for c in range(chips)] for k in range(CORES)]

    def finish(slots):
        def branch(own_tokens, own_shrunk, other_shrunk, keep, got, wanted, held, bounds, gate_weight, up_weight):
            products = expand(bounds, wanted[:slots], own_shrunk, other_shrunk, keep, got, slots, block)
            products = lax.all_to_all(
                products, axis, split_axis=0, concat_axis=0, axis_index_groups=same_core, tiled=True
            )
            other_tokens = other_core(own_tokens)
            gate, up = project(me_array, own_tokens, other_tokens, gate_weight, up_weight, block)
            held_rows = jnp.broadcast_to(held[:, :slots].reshape(1, chips * slots), (8, chips * slots))
            return combine(held_rows, gate, up, products.reshape(chips * slots, -1))

        return branch

    return lax.switch(
        choice,
        [finish(slots) for slots in sizes],
        own_tokens,
        own_shrunk,
        other_shrunk,
        keep,
        got,
        wanted,
        held,
        bounds,
        gate_weight,
        up_weight,
    )


def solution(mesh):
    placed = (
        P(("groups", "tensor"), None),
        P(None, "tensor"),
        P(None, "tensor"),
        P(("groups", "tensor"), None, None),
        P(("groups", "tensor"), None, None),
        P("groups"),
        P("groups"),
        P("groups"),
    )
    return jax.shard_map(
        per_device, mesh=mesh, in_specs=placed, out_specs=P("groups", "tensor"), check_vma=False
    )
```

```python
import functools

import jax
import jax.numpy as jnp
from jax import lax
from jax.experimental import pallas as pl
from jax.experimental.pallas import tpu as pltpu
from jax.sharding import PartitionSpec as P

ADAPTER_SCALE = 0.5
ROWS_PER_LIMIT = 64
SLOT_SIZES = (80, 96)
CORES = 2
MIB = 1024 * 1024


def chip_ring(chips):
    return list(range(0, chips, 2)) + list(range(chips - 1, 0, -2))


def ring_gather(block, axis, beside):
    size = lax.axis_size(axis)
    chips = size // CORES
    ring = chip_ring(chips)

    def moved(value, shift):
        pairs = [
            (ring[p] * CORES + k, ring[(p + shift) % chips] * CORES + k)
            for p in range(chips)
            for k in range(CORES)
        ]
        return lax.ppermute(value, axis, pairs)

    half = block.shape[1] // 2
    far = chips // 2
    halves = block[:, :half], block[:, half:]
    columns = (0, half), (half, 0)
    held = [halves, halves[::-1]]
    pieces = [(block, 0, 0)]
    for step in range(1, far + 1):
        for chain in range(1 if step == far else 2):
            right, left = held[chain]
            held[chain] = beside(chain, step, (moved(right, 1), moved(left, -1)))
            for value, column, distance in zip(held[chain], columns[chain], (-step, step)):
                pieces.append((value, column, distance))

    found = [(value, column) for value, column, _ in pieces]
    where = [
        [ring[(ring.index(device // CORES) + distance) % chips] for _, _, distance in pieces]
        for device in range(size)
    ]
    return found, where


ANY_SPEC = pl.BlockSpec(memory_space=pl.ANY)


def in_hbm(values):
    return [pltpu.with_memory_space_constraint(value, pltpu.HBM) for value in values]


def run_copies(copies):
    for copy in copies:
        copy.start()
    for copy in copies:
        copy.wait()


def plan_kernel(sizes, counts, sorted_ref, held_ref, choice_ref):
    chips, most = held_ref.shape
    rows = sorted_ref.shape[1]
    adapters = counts.shape[0] // chips
    listed = jnp.broadcast_to(sorted_ref[...], (8, rows))
    slot = lax.broadcasted_iota(jnp.int32, (8, most), 1)
    start = jnp.int32(0)
    largest = jnp.int32(0)
    for chip in range(chips):
        total = jnp.int32(0)
        for a in range(adapters):
            total += counts[chip * adapters + a]
        turned = pltpu.roll(listed, (rows - start) % rows, 1)
        held_ref[chip : chip + 1, :] = jnp.where(slot < total, turned[:, :most], -1)[0:1]
        start += total
        largest = jnp.maximum(largest, total)
    choice = jnp.int32(0)
    for size in sizes[:-1]:
        choice += (largest > size).astype(jnp.int32)
    choice_ref[0] = choice


def plan(counts, sorted_rows, chips, sizes):
    rows = sorted_rows.shape[0]
    most = sizes[-1]
    return pl.pallas_call(
        functools.partial(plan_kernel, sizes),
        grid_spec=pltpu.PrefetchScalarGridSpec(
            num_scalar_prefetch=1,
            grid=(1,),
            in_specs=[pl.BlockSpec((1, rows), lambda i, s: (0, 0))],
            out_specs=[pl.BlockSpec((chips, most), lambda i, s: (0, 0)), pl.BlockSpec(memory_space=pltpu.SMEM)],
        ),
        out_shape=[jax.ShapeDtypeStruct((chips, most), jnp.int32), jax.ShapeDtypeStruct((1,), jnp.int32)],
        name="plan",
    )(counts, sorted_rows.reshape(1, rows))


def down_copies(core, own_down_ref, other_down_ref, down_vmem, sems):
    ranks = own_down_ref.shape[0]
    return [
        pltpu.make_async_copy(ref, down_vmem.at[pl.ds(pl.multiple_of(where * ranks, ranks), ranks)], sems.at[i])
        for i, (ref, where) in enumerate(((own_down_ref, core), (other_down_ref, 1 - core)))
    ]


def shrink_near_kernel(columns, pieces, table, me, own_down_ref, other_down_ref, *refs):
    piece_refs = refs[:pieces]
    tokens_ref, shrunk_ref, tokens_vmem, down_vmem, sems = refs[pieces:]
    copies = down_copies(me[0] % CORES, own_down_ref, other_down_ref, down_vmem, sems)
    for i, ref in enumerate(piece_refs):
        rows, width = ref.shape
        start = pl.multiple_of(table[me[0] * (pieces + 1) + i] * rows, rows)
        copies.append(
            pltpu.make_async_copy(
                ref, tokens_vmem.at[pl.ds(start, rows), pl.ds(columns[i], width)], sems.at[2 + i]
            )
        )
    run_copies(copies)
    out_copy = pltpu.make_async_copy(tokens_vmem, tokens_ref, sems.at[2 + pieces])
    out_copy.start()
    shrunk_ref[...] = lax.dot_general(
        tokens_vmem[...], down_vmem[...], (((1,), (1,)), ((), ())), preferred_element_type=jnp.float32
    ).astype(shrunk_ref.dtype)
    out_copy.wait()


def shrink_far_kernel(table, me, tokens_in, shrunk_in, own_down_ref, other_down_ref, *refs):
    piece_refs = refs[:2]
    tokens_ref, shrunk_ref, far_vmem, down_vmem, sems = refs[2:]
    rows, width = far_vmem.shape
    entries = table.shape[0] // (CORES * tokens_in.shape[0] // rows)
    start = pl.multiple_of(table[me[0] * entries + entries - 1] * rows, rows)
    copies = down_copies(me[0] % CORES, own_down_ref, other_down_ref, down_vmem, sems)
    half = width // 2
    for i, ref in enumerate(piece_refs):
        copies.append(pltpu.make_async_copy(ref, far_vmem.at[:, pl.ds(i * half, half)], sems.at[2 + i]))
    run_copies(copies)
    out_copy = pltpu.make_async_copy(far_vmem, tokens_ref.at[pl.ds(start, rows)], sems.at[4])
    out_copy.start()
    shrunk_ref[...] = shrunk_in[...]
    shrunk_ref[pl.ds(start, rows), :] = lax.dot_general(
        far_vmem[...], down_vmem[...], (((1,), (1,)), ((), ())), preferred_element_type=jnp.float32
    ).astype(shrunk_ref.dtype)
    out_copy.wait()


def shrink(table, me, columns, pieces, rows, own_down, other_down):
    ranks, width = own_down.shape
    near = pieces[:-2]
    block = pieces[-1].shape[0]
    tokens_shape = pltpu.HBM((rows, width), jnp.bfloat16)
    shrunk_shape = jax.ShapeDtypeStruct((rows, CORES * ranks), jnp.bfloat16)
    shrunk_spec = pl.BlockSpec((rows, CORES * ranks), lambda i, s, t: (0, 0))
    down_vmem = pltpu.VMEM((CORES * ranks, width), jnp.bfloat16)
    tokens, shrunk = pl.pallas_call(
        functools.partial(shrink_near_kernel, columns, len(near)),
        grid_spec=pltpu.PrefetchScalarGridSpec(
            num_scalar_prefetch=2,
            grid=(1,),
            in_specs=[ANY_SPEC] * (2 + len(near)),
            out_specs=[ANY_SPEC, shrunk_spec],
            scratch_shapes=[
                pltpu.VMEM((rows, width), jnp.bfloat16),
                down_vmem,
                pltpu.SemaphoreType.DMA((3 + len(near),)),
            ],
        ),
        out_shape=[tokens_shape, shrunk_shape],
        compiler_params=pltpu.CompilerParams(vmem_limit_bytes=rows * width * 2 + 16 * MIB),
        name="shrink_near",
    )(table, me, own_down, other_down, *near)
    return pl.pallas_call(
        shrink_far_kernel,
        grid_spec=pltpu.PrefetchScalarGridSpec(
            num_scalar_prefetch=2,
            grid=(1,),
            in_specs=[ANY_SPEC, shrunk_spec] + [ANY_SPEC] * 4,
            out_specs=[ANY_SPEC, shrunk_spec],
            scratch_shapes=[
                pltpu.VMEM((block, width), jnp.bfloat16),
                down_vmem,
                pltpu.SemaphoreType.DMA((5,)),
            ],
        ),
        out_shape=[tokens_shape, shrunk_shape],
        input_output_aliases={2: 0},
        compiler_params=pltpu.CompilerParams(vmem_limit_bytes=16 * MIB),
        name="shrink_far",
    )(table, me, *in_hbm([tokens]), shrunk, own_down, other_down, *pieces[-2:])


def expand_kernel(block, counts, me, held_ref, own_ref, other_ref, keep_ref, got_ref, out_ref, maps_vmem, out_vmem, sems):
    chips, slots, units = out_vmem.shape
    most = held_ref.shape[1]
    ranks = keep_ref.shape[0]
    adapters = counts.shape[0] // chips
    chip = me[0] // CORES
    core = me[0] % CORES
    copies = []
    for c in range(chips):
        start = pl.multiple_of((c * CORES + core) * units, units)
        for ref, where in ((keep_ref, core), (got_ref, 1 - core)):
            copies.append(
                pltpu.make_async_copy(
                    ref.at[:, pl.ds(start, units)],
                    maps_vmem.at[c, pl.ds(pl.multiple_of(where * ranks, ranks), ranks)],
                    sems.at[len(copies)],
                )
            )
    for copy in copies:
        copy.start()

    wanted = held_ref[pl.ds(chip, 1), :]
    index = lax.broadcasted_iota(jnp.int32, (own_ref.shape[0], most), 0)
    row = index // block * (CORES * block) + index % block
    picked = jnp.zeros((most, own_ref.shape[1]), jnp.float32)
    for ref, where in ((own_ref, core), (other_ref, 1 - core)):
        hit = (row + where * block == wanted).astype(jnp.float32).astype(jnp.bfloat16)
        picked += lax.dot_general(hit, ref[...], (((0,), (0,)), ((), ())), preferred_element_type=jnp.float32)
    slot = lax.broadcasted_iota(jnp.int32, picked.shape, 0)
    adapter = lax.broadcasted_iota(jnp.int32, picked.shape, 1) // (picked.shape[1] // adapters)
    mine = jnp.zeros(picked.shape, jnp.int32)
    first = jnp.int32(0)
    for a in range(adapters):
        end = first + counts[chip * adapters + a]
        mine += ((adapter == a) & (slot >= first) & (slot < end)).astype(jnp.int32)
        first = end
    shrunk = jnp.where(mine > 0, picked, 0.0).astype(jnp.bfloat16)[:slots]

    out_copies = []
    for c in range(chips):
        copies[2 * c].wait()
        copies[2 * c + 1].wait()
        product = jnp.dot(shrunk, maps_vmem[c], preferred_element_type=jnp.float32)
        out_vmem[c] = (ADAPTER_SCALE * product).astype(out_vmem.dtype)
        out_copies.append(pltpu.make_async_copy(out_vmem.at[c], out_ref.at[c], sems.at[2 * chips + c]))
        out_copies[-1].start()
    for copy in out_copies:
        copy.wait()


def expand(counts, me, held, own_shrunk, other_shrunk, keep, got, slots, block):
    ranks, columns = keep.shape
    chips, most = held.shape
    units = columns // chips // CORES
    rows, ranks_all = own_shrunk.shape
    shrunk_spec = pl.BlockSpec((rows, ranks_all), lambda i, s, t: (0, 0))
    return pl.pallas_call(
        functools.partial(expand_kernel, block),
        grid_spec=pltpu.PrefetchScalarGridSpec(
            num_scalar_prefetch=2,
            grid=(1,),
            in_specs=[
                pl.BlockSpec((chips, most), lambda i, s, t: (0, 0)),
                shrunk_spec,
                shrunk_spec,
                ANY_SPEC,
                ANY_SPEC,
            ],
            out_specs=ANY_SPEC,
            scratch_shapes=[
                pltpu.VMEM((chips, ranks_all, units), jnp.bfloat16),
                pltpu.VMEM((chips, slots, units), jnp.bfloat16),
                pltpu.SemaphoreType.DMA((3 * chips,)),
            ],
        ),
        out_shape=pltpu.HBM((chips, slots, units), jnp.bfloat16),
        compiler_params=pltpu.CompilerParams(vmem_limit_bytes=16 * MIB),
        cost_estimate=pl.CostEstimate(
            flops=2 * slots * ranks_all * chips * units,
            bytes_accessed=2 * (slots + ranks_all) * chips * units,
            transcendentals=0,
        ),
        name="expand",
    )(counts, me, held, own_shrunk, other_shrunk, *in_hbm([keep, got]))


def project_kernel(block, me, gate_weight_ref, up_weight_ref, own_ref, other_ref, gate_ref, up_ref, tokens_vmem, sems):
    depth = gate_weight_ref.shape[0]
    core = me[0] % CORES
    k = pl.program_id(0)

    @pl.when(k == 0)
    def _():
        copies = []
        for ref, where in ((own_ref, core), (other_ref, 1 - core)):
            for chip in range(ref.shape[0] // block):
                start = pl.multiple_of((chip * CORES + where) * block, block)
                copies.append(
                    pltpu.make_async_copy(
                        ref.at[pl.ds(chip * block, block)], tokens_vmem.at[pl.ds(start, block)], sems.at[len(copies)]
                    )
                )
        run_copies(copies)
        gate_ref[...] = jnp.zeros_like(gate_ref)
        up_ref[...] = jnp.zeros_like(up_ref)

    tokens = tokens_vmem[:, pl.ds(pl.multiple_of(k * depth, depth), depth)]
    gate_ref[...] += jnp.dot(tokens, gate_weight_ref[...], preferred_element_type=jnp.float32)
    up_ref[...] += jnp.dot(tokens, up_weight_ref[...], preferred_element_type=jnp.float32)

    @pl.when(k == pl.num_programs(0) - 1)
    def _():
        gate = gate_ref[...]
        gate_ref[...] = gate / (1.0 + jnp.exp(-gate))


def project(me, own, other, gate_weight, up_weight, block):
    width, units = gate_weight.shape
    rows = CORES * own.shape[0]
    depth = min(1024, width)
    weight_spec = pl.BlockSpec((depth, units), lambda k, s: (k, 0))
    out_spec = pl.BlockSpec((rows, units), lambda k, s: (0, 0))
    out = pltpu.HBM((rows, units), jnp.float32)
    return pl.pallas_call(
        functools.partial(project_kernel, block),
        grid_spec=pltpu.PrefetchScalarGridSpec(
            num_scalar_prefetch=1,
            grid=(width // depth,),
            in_specs=[weight_spec, weight_spec, ANY_SPEC, ANY_SPEC],
            out_specs=[out_spec, out_spec],
            scratch_shapes=[
                pltpu.VMEM((rows, width), jnp.bfloat16),
                pltpu.SemaphoreType.DMA((rows // block,)),
            ],
        ),
        out_shape=[out, out],
        compiler_params=pltpu.CompilerParams(vmem_limit_bytes=rows * width * 2 + 20 * MIB),
        cost_estimate=pl.CostEstimate(
            flops=4 * rows * width * units,
            bytes_accessed=2 * (rows + 2 * units) * width,
            transcendentals=rows * units,
        ),
        name="project",
    )(me, *in_hbm([gate_weight, up_weight, own, other]))


def combine_kernel(pick_ref, gate_ref, up_ref, products_ref, out_ref):
    delta = jnp.dot(pick_ref[...], products_ref[...], preferred_element_type=jnp.float32)
    out_ref[...] = (gate_ref[...] * (up_ref[...] + delta)).astype(out_ref.dtype)


def combine(pick, gate, up, products):
    rows, units = gate.shape
    slots_all = products.shape[0]
    tile = min(512, units)
    column_spec = pl.BlockSpec((rows, tile), lambda n: (0, n))
    return pl.pallas_call(
        combine_kernel,
        grid=(units // tile,),
        in_specs=[
            pl.BlockSpec((rows, slots_all), lambda n: (0, 0)),
            column_spec,
            column_spec,
            pl.BlockSpec((slots_all, tile), lambda n: (0, n)),
        ],
        out_specs=column_spec,
        out_shape=pltpu.HBM((rows, units), jnp.bfloat16),
        compiler_params=pltpu.CompilerParams(vmem_limit_bytes=rows * slots_all * 4 + 20 * MIB),
        cost_estimate=pl.CostEstimate(
            flops=2 * rows * slots_all * units, bytes_accessed=10 * rows * units, transcendentals=0
        ),
        name="combine",
    )(*in_hbm([pick, gate, up]), products)


def per_device(
    tokens,
    gate_weight,
    up_weight,
    adapter_down_weight,
    adapter_up_weight,
    row_adapter,
    sorted_rows,
    segment_count,
):
    axis = "tensor"
    size = lax.axis_size(axis)
    me = lax.axis_index(axis).astype(jnp.int32)
    chips = size // CORES
    resident, rank, width = adapter_down_weight.shape
    ranks = resident * rank
    rows = row_adapter.shape[0]
    block = tokens.shape[0]
    me_array = me.reshape(1)
    flips = [(d, d ^ 1) for d in range(size)]

    def other_core(value):
        return lax.ppermute(value, axis, flips)

    most = CORES * resident * ROWS_PER_LIMIT
    sizes = [slots for slots in SLOT_SIZES if slots < most] + [most]
    held, choice = plan(segment_count, sorted_rows, chips, sizes)

    own_down = adapter_down_weight.reshape(ranks, width)
    other_down = other_core(own_down)
    own_maps = adapter_up_weight.reshape(ranks, -1)
    other_maps = other_core(own_maps)

    found, where = ring_gather(tokens, axis, lambda chain, step, values: values)
    pieces = [piece for piece, _ in found]
    columns = [column for _, column in found]
    table = jnp.array([row[:-1] for row in where], jnp.int32).reshape(-1)
    own_tokens, own_shrunk = shrink(table, me_array, columns, pieces, rows // CORES, own_down, other_down)
    choice, own_shrunk = lax.optimization_barrier((choice, own_shrunk))
    other_shrunk = other_core(own_shrunk)
    groups = lax.axis_size("groups")
    choices = [choice] + [
        lax.ppermute(choice, "groups", [(g, (g + shift) % groups) for g in range(groups)])
        for shift in range(1, groups)
    ]
    choice = functools.reduce(jnp.maximum, choices)[0]

    same_core = [[c * CORES + k for c in range(chips)] for k in range(CORES)]

    def finish(slots):
        def branch(own_tokens, own_shrunk, other_shrunk, own_maps, other_maps, held, gate_weight, up_weight):
            products = expand(
                segment_count, me_array, held, own_shrunk, other_shrunk, own_maps, other_maps, slots, block
            )
            products = lax.all_to_all(
                products, axis, split_axis=0, concat_axis=0, axis_index_groups=same_core, tiled=True
            )
            held_rows = held[:, :slots].reshape(1, chips * slots)
            pick = (jnp.arange(rows, dtype=jnp.int32)[:, None] == held_rows).astype(jnp.bfloat16)
            pick, own_tokens = lax.optimization_barrier((pick, own_tokens))
            other_tokens = other_core(own_tokens)
            gate, up = project(me_array, own_tokens, other_tokens, gate_weight, up_weight, block)
            return combine(pick, gate, up, products.reshape(chips * slots, -1))

        return branch

    return lax.switch(
        choice,
        [finish(slots) for slots in sizes],
        own_tokens,
        own_shrunk,
        other_shrunk,
        own_maps,
        other_maps,
        held,
        gate_weight,
        up_weight,
    )


def solution(mesh):
    placed = (
        P(("groups", "tensor"), None),
        P(None, "tensor"),
        P(None, "tensor"),
        P(("groups", "tensor"), None, None),
        P(("groups", "tensor"), None, None),
        P("groups"),
        P("groups"),
        P("groups"),
    )
    return jax.shard_map(
        per_device, mesh=mesh, in_specs=placed, out_specs=P("groups", "tensor"), check_vma=False
    )
```

```python
import functools

import jax
import jax.numpy as jnp
from jax import lax
from jax.experimental import pallas as pl
from jax.experimental.pallas import tpu as pltpu
from jax.sharding import PartitionSpec as P

ADAPTER_SCALE = 0.5
ROWS_PER_LIMIT = 64
SLOT_SIZES = (80, 96)
CORES = 2
MIB = 1024 * 1024


def chip_ring(chips):
    return list(range(0, chips, 2)) + list(range(chips - 1, 0, -2))


def ring_gather(block, axis, beside):
    size = lax.axis_size(axis)
    chips = size // CORES
    ring = chip_ring(chips)

    def moved(value, shift):
        pairs = [
            (ring[p] * CORES + k, ring[(p + shift) % chips] * CORES + k)
            for p in range(chips)
            for k in range(CORES)
        ]
        return lax.ppermute(value, axis, pairs)

    half = block.shape[1] // 2
    far = chips // 2
    halves = block[:, :half], block[:, half:]
    columns = (0, half), (half, 0)
    held = [halves, halves[::-1]]
    pieces = [(block, 0, 0)]
    for step in range(1, far + 1):
        for chain in range(1 if step == far else 2):
            right, left = held[chain]
            held[chain] = moved(right, 1), moved(left, -1)
            for value, column, distance in zip(held[chain], columns[chain], (-step, step)):
                pieces.append((value, column, distance))
        beside(step, held)

    found = [(value, column) for value, column, _ in pieces]
    where = [
        [ring[(ring.index(device // CORES) + distance) % chips] for _, _, distance in pieces]
        for device in range(size)
    ]
    return found, where


ANY_SPEC = pl.BlockSpec(memory_space=pl.ANY)


def in_hbm(values):
    return [pltpu.with_memory_space_constraint(value, pltpu.HBM) for value in values]


def run_copies(copies):
    for copy in copies:
        copy.start()
    for copy in copies:
        copy.wait()


def plan_kernel(sizes, counts, sorted_ref, held_ref, choice_ref):
    chips, most = held_ref.shape
    rows = sorted_ref.shape[1]
    adapters = counts.shape[0] // chips
    listed = jnp.broadcast_to(sorted_ref[...], (8, rows))
    slot = lax.broadcasted_iota(jnp.int32, (8, most), 1)
    start = jnp.int32(0)
    largest = jnp.int32(0)
    for chip in range(chips):
        total = jnp.int32(0)
        for a in range(adapters):
            total += counts[chip * adapters + a]
        turned = pltpu.roll(listed, (rows - start) % rows, 1)
        held_ref[chip : chip + 1, :] = jnp.where(slot < total, turned[:, :most], -1)[0:1]
        start += total
        largest = jnp.maximum(largest, total)
    choice = jnp.int32(0)
    for size in sizes[:-1]:
        choice += (largest > size).astype(jnp.int32)
    choice_ref[0] = choice


def plan(counts, sorted_rows, chips, sizes):
    rows = sorted_rows.shape[0]
    most = sizes[-1]
    return pl.pallas_call(
        functools.partial(plan_kernel, sizes),
        grid_spec=pltpu.PrefetchScalarGridSpec(
            num_scalar_prefetch=1,
            grid=(1,),
            in_specs=[pl.BlockSpec((1, rows), lambda i, s: (0, 0))],
            out_specs=[pl.BlockSpec((chips, most), lambda i, s: (0, 0)), pl.BlockSpec(memory_space=pltpu.SMEM)],
        ),
        out_shape=[jax.ShapeDtypeStruct((chips, most), jnp.int32), jax.ShapeDtypeStruct((1,), jnp.int32)],
        name="plan",
    )(counts, sorted_rows.reshape(1, rows))


def down_copies(core, own_down_ref, other_down_ref, down_vmem, sems):
    ranks = own_down_ref.shape[0]
    return [
        pltpu.make_async_copy(ref, down_vmem.at[pl.ds(pl.multiple_of(where * ranks, ranks), ranks)], sems.at[i])
        for i, (ref, where) in enumerate(((own_down_ref, core), (other_down_ref, 1 - core)))
    ]


def shrink_near_kernel(columns, pieces, table, me, own_down_ref, other_down_ref, *refs):
    piece_refs = refs[:pieces]
    tokens_ref, shrunk_ref, tokens_vmem, down_vmem, sems = refs[pieces:]
    copies = down_copies(me[0] % CORES, own_down_ref, other_down_ref, down_vmem, sems)
    for i, ref in enumerate(piece_refs):
        rows, width = ref.shape
        start = pl.multiple_of(table[me[0] * (pieces + 1) + i] * rows, rows)
        copies.append(
            pltpu.make_async_copy(
                ref, tokens_vmem.at[pl.ds(start, rows), pl.ds(columns[i], width)], sems.at[2 + i]
            )
        )
    run_copies(copies)
    out_copy = pltpu.make_async_copy(tokens_vmem, tokens_ref, sems.at[2 + pieces])
    out_copy.start()
    shrunk_ref[...] = lax.dot_general(
        tokens_vmem[...], down_vmem[...], (((1,), (1,)), ((), ())), preferred_element_type=jnp.float32
    ).astype(shrunk_ref.dtype)
    out_copy.wait()


def shrink_far_kernel(table, me, tokens_in, shrunk_in, own_down_ref, other_down_ref, *refs):
    piece_refs = refs[:2]
    tokens_ref, shrunk_ref, far_vmem, down_vmem, sems = refs[2:]
    rows, width = far_vmem.shape
    entries = table.shape[0] // (CORES * tokens_in.shape[0] // rows)
    start = pl.multiple_of(table[me[0] * entries + entries - 1] * rows, rows)
    copies = down_copies(me[0] % CORES, own_down_ref, other_down_ref, down_vmem, sems)
    half = width // 2
    for i, ref in enumerate(piece_refs):
        copies.append(pltpu.make_async_copy(ref, far_vmem.at[:, pl.ds(i * half, half)], sems.at[2 + i]))
    run_copies(copies)
    out_copy = pltpu.make_async_copy(far_vmem, tokens_ref.at[pl.ds(start, rows)], sems.at[4])
    out_copy.start()
    shrunk_ref[...] = shrunk_in[...]
    shrunk_ref[pl.ds(start, rows), :] = lax.dot_general(
        far_vmem[...], down_vmem[...], (((1,), (1,)), ((), ())), preferred_element_type=jnp.float32
    ).astype(shrunk_ref.dtype)
    out_copy.wait()


def shrink(table, me, columns, pieces, rows, own_down, other_down):
    ranks, width = own_down.shape
    near = pieces[:-2]
    block = pieces[-1].shape[0]
    tokens_shape = pltpu.HBM((rows, width), jnp.bfloat16)
    shrunk_shape = jax.ShapeDtypeStruct((rows, CORES * ranks), jnp.bfloat16)
    shrunk_spec = pl.BlockSpec((rows, CORES * ranks), lambda i, s, t: (0, 0))
    down_vmem = pltpu.VMEM((CORES * ranks, width), jnp.bfloat16)
    tokens, shrunk = pl.pallas_call(
        functools.partial(shrink_near_kernel, columns, len(near)),
        grid_spec=pltpu.PrefetchScalarGridSpec(
            num_scalar_prefetch=2,
            grid=(1,),
            in_specs=[ANY_SPEC] * (2 + len(near)),
            out_specs=[ANY_SPEC, shrunk_spec],
            scratch_shapes=[
                pltpu.VMEM((rows, width), jnp.bfloat16),
                down_vmem,
                pltpu.SemaphoreType.DMA((3 + len(near),)),
            ],
        ),
        out_shape=[tokens_shape, shrunk_shape],
        compiler_params=pltpu.CompilerParams(vmem_limit_bytes=rows * width * 2 + 16 * MIB),
        name="shrink_near",
    )(table, me, *in_hbm([own_down, other_down, *near]))
    return pl.pallas_call(
        shrink_far_kernel,
        grid_spec=pltpu.PrefetchScalarGridSpec(
            num_scalar_prefetch=2,
            grid=(1,),
            in_specs=[ANY_SPEC, shrunk_spec] + [ANY_SPEC] * 4,
            out_specs=[ANY_SPEC, shrunk_spec],
            scratch_shapes=[
                pltpu.VMEM((block, width), jnp.bfloat16),
                down_vmem,
                pltpu.SemaphoreType.DMA((5,)),
            ],
        ),
        out_shape=[tokens_shape, shrunk_shape],
        input_output_aliases={2: 0},
        compiler_params=pltpu.CompilerParams(vmem_limit_bytes=16 * MIB),
        name="shrink_far",
    )(table, me, *in_hbm([tokens]), shrunk, *in_hbm([own_down, other_down, *pieces[-2:]]))


def expand_kernel(block, counts, me, held_ref, own_ref, other_ref, keep_ref, got_ref, out_ref, maps_vmem, out_vmem, sems):
    chips, slots, units = out_vmem.shape
    most = held_ref.shape[1]
    ranks = keep_ref.shape[0]
    adapters = counts.shape[0] // chips
    chip = me[0] // CORES
    core = me[0] % CORES
    copies = []
    for c in range(chips):
        start = pl.multiple_of((c * CORES + core) * units, units)
        for ref, where in ((keep_ref, core), (got_ref, 1 - core)):
            copies.append(
                pltpu.make_async_copy(
                    ref.at[:, pl.ds(start, units)],
                    maps_vmem.at[c, pl.ds(pl.multiple_of(where * ranks, ranks), ranks)],
                    sems.at[len(copies)],
                )
            )
    for copy in copies:
        copy.start()

    wanted = held_ref[pl.ds(chip, 1), :]
    index = lax.broadcasted_iota(jnp.int32, (own_ref.shape[0], most), 0)
    row = index // block * (CORES * block) + index % block
    picked = jnp.zeros((most, own_ref.shape[1]), jnp.float32)
    for ref, where in ((own_ref, core), (other_ref, 1 - core)):
        hit = (row + where * block == wanted).astype(jnp.float32).astype(jnp.bfloat16)
        picked += lax.dot_general(hit, ref[...], (((0,), (0,)), ((), ())), preferred_element_type=jnp.float32)
    slot = lax.broadcasted_iota(jnp.int32, picked.shape, 0)
    adapter = lax.broadcasted_iota(jnp.int32, picked.shape, 1) // (picked.shape[1] // adapters)
    mine = jnp.zeros(picked.shape, jnp.int32)
    first = jnp.int32(0)
    for a in range(adapters):
        end = first + counts[chip * adapters + a]
        mine += ((adapter == a) & (slot >= first) & (slot < end)).astype(jnp.int32)
        first = end
    shrunk = jnp.where(mine > 0, picked, 0.0).astype(jnp.bfloat16)[:slots]

    out_copies = []
    for c in range(chips):
        copies[2 * c].wait()
        copies[2 * c + 1].wait()
        product = jnp.dot(shrunk, maps_vmem[c], preferred_element_type=jnp.float32)
        out_vmem[c] = (ADAPTER_SCALE * product).astype(out_vmem.dtype)
        out_copies.append(pltpu.make_async_copy(out_vmem.at[c], out_ref.at[c], sems.at[2 * chips + c]))
        out_copies[-1].start()
    for copy in out_copies:
        copy.wait()


def expand(counts, me, held, own_shrunk, other_shrunk, keep, got, slots, block):
    ranks, columns = keep.shape
    chips, most = held.shape
    units = columns // chips // CORES
    rows, ranks_all = own_shrunk.shape
    shrunk_spec = pl.BlockSpec((rows, ranks_all), lambda i, s, t: (0, 0))
    return pl.pallas_call(
        functools.partial(expand_kernel, block),
        grid_spec=pltpu.PrefetchScalarGridSpec(
            num_scalar_prefetch=2,
            grid=(1,),
            in_specs=[
                pl.BlockSpec((chips, most), lambda i, s, t: (0, 0)),
                shrunk_spec,
                shrunk_spec,
                ANY_SPEC,
                ANY_SPEC,
            ],
            out_specs=ANY_SPEC,
            scratch_shapes=[
                pltpu.VMEM((chips, ranks_all, units), jnp.bfloat16),
                pltpu.VMEM((chips, slots, units), jnp.bfloat16),
                pltpu.SemaphoreType.DMA((3 * chips,)),
            ],
        ),
        out_shape=pltpu.HBM((chips, slots, units), jnp.bfloat16),
        compiler_params=pltpu.CompilerParams(vmem_limit_bytes=16 * MIB),
        cost_estimate=pl.CostEstimate(
            flops=2 * slots * ranks_all * chips * units,
            bytes_accessed=2 * (slots + ranks_all) * chips * units,
            transcendentals=0,
        ),
        name="expand",
    )(counts, me, held, own_shrunk, other_shrunk, *in_hbm([keep, got]))


def project_kernel(block, me, gate_weight_ref, up_weight_ref, own_ref, other_ref, gate_ref, up_ref, tokens_vmem, sems):
    depth = gate_weight_ref.shape[0]
    core = me[0] % CORES
    k = pl.program_id(0)

    @pl.when(k == 0)
    def _():
        copies = []
        for ref, where in ((own_ref, core), (other_ref, 1 - core)):
            for chip in range(ref.shape[0] // block):
                start = pl.multiple_of((chip * CORES + where) * block, block)
                copies.append(
                    pltpu.make_async_copy(
                        ref.at[pl.ds(chip * block, block)], tokens_vmem.at[pl.ds(start, block)], sems.at[len(copies)]
                    )
                )
        run_copies(copies)
        gate_ref[...] = jnp.zeros_like(gate_ref)
        up_ref[...] = jnp.zeros_like(up_ref)

    tokens = tokens_vmem[:, pl.ds(pl.multiple_of(k * depth, depth), depth)]
    gate_ref[...] += jnp.dot(tokens, gate_weight_ref[...], preferred_element_type=jnp.float32)
    up_ref[...] += jnp.dot(tokens, up_weight_ref[...], preferred_element_type=jnp.float32)

    @pl.when(k == pl.num_programs(0) - 1)
    def _():
        gate = gate_ref[...]
        gate_ref[...] = gate / (1.0 + jnp.exp(-gate))


def project(me, own, other, gate_weight, up_weight, block):
    width, units = gate_weight.shape
    rows = CORES * own.shape[0]
    depth = min(1024, width)
    weight_spec = pl.BlockSpec((depth, units), lambda k, s: (k, 0))
    out_spec = pl.BlockSpec((rows, units), lambda k, s: (0, 0))
    out = pltpu.HBM((rows, units), jnp.float32)
    return pl.pallas_call(
        functools.partial(project_kernel, block),
        grid_spec=pltpu.PrefetchScalarGridSpec(
            num_scalar_prefetch=1,
            grid=(width // depth,),
            in_specs=[weight_spec, weight_spec, ANY_SPEC, ANY_SPEC],
            out_specs=[out_spec, out_spec],
            scratch_shapes=[
                pltpu.VMEM((rows, width), jnp.bfloat16),
                pltpu.SemaphoreType.DMA((rows // block,)),
            ],
        ),
        out_shape=[out, out],
        compiler_params=pltpu.CompilerParams(vmem_limit_bytes=rows * width * 2 + 20 * MIB),
        cost_estimate=pl.CostEstimate(
            flops=4 * rows * width * units,
            bytes_accessed=2 * (rows + 2 * units) * width,
            transcendentals=rows * units,
        ),
        name="project",
    )(me, *in_hbm([gate_weight, up_weight, own, other]))


def combine_kernel(pick_ref, gate_ref, up_ref, products_ref, out_ref):
    delta = jnp.dot(pick_ref[...], products_ref[...], preferred_element_type=jnp.float32)
    out_ref[...] = (gate_ref[...] * (up_ref[...] + delta)).astype(out_ref.dtype)


def combine(pick, gate, up, products):
    rows, units = gate.shape
    slots_all = products.shape[0]
    tile = min(512, units)
    column_spec = pl.BlockSpec((rows, tile), lambda n: (0, n))
    return pl.pallas_call(
        combine_kernel,
        grid=(units // tile,),
        in_specs=[
            pl.BlockSpec((rows, slots_all), lambda n: (0, 0)),
            column_spec,
            column_spec,
            pl.BlockSpec((slots_all, tile), lambda n: (0, n)),
        ],
        out_specs=column_spec,
        out_shape=pltpu.HBM((rows, units), jnp.bfloat16),
        compiler_params=pltpu.CompilerParams(vmem_limit_bytes=rows * slots_all * 4 + 20 * MIB),
        cost_estimate=pl.CostEstimate(
            flops=2 * rows * slots_all * units, bytes_accessed=10 * rows * units, transcendentals=0
        ),
        name="combine",
    )(*in_hbm([pick, gate, up]), products)


def per_device(
    tokens,
    gate_weight,
    up_weight,
    adapter_down_weight,
    adapter_up_weight,
    row_adapter,
    sorted_rows,
    segment_count,
):
    axis = "tensor"
    size = lax.axis_size(axis)
    me = lax.axis_index(axis).astype(jnp.int32)
    chips = size // CORES
    resident, rank, width = adapter_down_weight.shape
    ranks = resident * rank
    rows = row_adapter.shape[0]
    block = tokens.shape[0]
    me_array = me.reshape(1)
    flips = [(d, d ^ 1) for d in range(size)]

    def other_core(value):
        return lax.ppermute(value, axis, flips)

    most = CORES * resident * ROWS_PER_LIMIT
    sizes = [slots for slots in SLOT_SIZES if slots < most] + [most]
    groups = lax.axis_size("groups")
    own_down = adapter_down_weight.reshape(ranks, width)
    own_maps = adapter_up_weight.reshape(ranks, -1)
    other_down = other_core(own_down)
    held = choice = other_maps = None

    def beside(step, values):
        nonlocal other_down, held, choice, other_maps
        if step == 1:
            counts, other_down, _ = lax.optimization_barrier((segment_count, other_down, values))
            held, choice = plan(counts, sorted_rows, chips, sizes)
            choices = [choice] + [
                lax.ppermute(choice, "groups", [(g, (g + shift) % groups) for g in range(groups)])
                for shift in range(1, groups)
            ]
            choice = functools.reduce(jnp.maximum, choices)
        if step == 2:
            choice, maps, _ = lax.optimization_barrier((choice, own_maps, values))
            other_maps = other_core(maps)

    found, where = ring_gather(tokens, axis, beside)
    pieces = [piece for piece, _ in found]
    columns = [column for _, column in found]
    table = jnp.array([row[:-1] for row in where], jnp.int32).reshape(-1)
    own_tokens, own_shrunk = shrink(table, me_array, columns, pieces, rows // CORES, own_down, other_down)
    other_shrunk = other_core(own_shrunk)

    same_core = [[c * CORES + k for c in range(chips)] for k in range(CORES)]

    def finish(slots):
        def branch(own_tokens, own_shrunk, other_shrunk, own_maps, other_maps, held, gate_weight, up_weight):
            products = expand(
                segment_count, me_array, held, own_shrunk, other_shrunk, own_maps, other_maps, slots, block
            )
            products = lax.all_to_all(
                products, axis, split_axis=0, concat_axis=0, axis_index_groups=same_core, tiled=True
            )
            held, other_tokens = lax.optimization_barrier((held, other_core(own_tokens)))
            held_rows = held[:, :slots].reshape(1, chips * slots)
            pick = (jnp.arange(rows, dtype=jnp.int32)[:, None] == held_rows).astype(jnp.bfloat16)
            pick, other_tokens = lax.optimization_barrier((pick, other_tokens))
            gate, up = project(me_array, own_tokens, other_tokens, gate_weight, up_weight, block)
            return combine(pick, gate, up, products.reshape(chips * slots, -1))

        return branch

    return lax.switch(
        choice[0],
        [finish(slots) for slots in sizes],
        own_tokens,
        own_shrunk,
        other_shrunk,
        own_maps,
        other_maps,
        held,
        gate_weight,
        up_weight,
    )


def solution(mesh):
    placed = (
        P(("groups", "tensor"), None),
        P(None, "tensor"),
        P(None, "tensor"),
        P(("groups", "tensor"), None, None),
        P(("groups", "tensor"), None, None),
        P("groups"),
        P("groups"),
        P("groups"),
    )
    return jax.shard_map(
        per_device, mesh=mesh, in_specs=placed, out_specs=P("groups", "tensor"), check_vma=False
    )
```

```python
import functools

import jax
import jax.numpy as jnp
from jax import lax
from jax.experimental import pallas as pl
from jax.experimental.pallas import tpu as pltpu
from jax.sharding import PartitionSpec as P

ADAPTER_SCALE = 0.5
ROWS_PER_LIMIT = 64
SLOT_SIZES = (80, 96)
CORES = 2
MIB = 1024 * 1024


def chip_ring(chips):
    return list(range(0, chips, 2)) + list(range(chips - 1, 0, -2))


def ring_gather(block, axis, beside):
    size = lax.axis_size(axis)
    chips = size // CORES
    ring = chip_ring(chips)

    def moved(value, shift):
        pairs = [
            (ring[p] * CORES + k, ring[(p + shift) % chips] * CORES + k)
            for p in range(chips)
            for k in range(CORES)
        ]
        return lax.ppermute(value, axis, pairs)

    half = block.shape[1] // 2
    far = chips // 2
    halves = block[:, :half], block[:, half:]
    columns = (0, half), (half, 0)
    held = [halves, halves[::-1]]
    pieces = [(block, 0, 0)]
    for step in range(1, far + 1):
        for chain in range(1 if step == far else 2):
            right, left = held[chain]
            held[chain] = moved(right, 1), moved(left, -1)
            for value, column, distance in zip(held[chain], columns[chain], (-step, step)):
                pieces.append((value, column, distance))
        beside(step, held)

    found = [(value, column) for value, column, _ in pieces]
    where = [
        [ring[(ring.index(device // CORES) + distance) % chips] for _, _, distance in pieces]
        for device in range(size)
    ]
    return found, where


ANY_SPEC = pl.BlockSpec(memory_space=pl.ANY)


def in_hbm(values):
    return [pltpu.with_memory_space_constraint(value, pltpu.HBM) for value in values]


def run_copies(copies):
    for copy in copies:
        copy.start()
    for copy in copies:
        copy.wait()


def plan_kernel(sizes, counts, sorted_ref, held_ref, choice_ref):
    chips, most = held_ref.shape
    rows = sorted_ref.shape[1]
    adapters = counts.shape[0] // chips
    listed = jnp.broadcast_to(sorted_ref[...], (8, rows))
    slot = lax.broadcasted_iota(jnp.int32, (8, most), 1)
    start = jnp.int32(0)
    largest = jnp.int32(0)
    for chip in range(chips):
        total = jnp.int32(0)
        for a in range(adapters):
            total += counts[chip * adapters + a]
        turned = pltpu.roll(listed, (rows - start) % rows, 1)
        held_ref[chip : chip + 1, :] = jnp.where(slot < total, turned[:, :most], -1)[0:1]
        start += total
        largest = jnp.maximum(largest, total)
    choice = jnp.int32(0)
    for size in sizes[:-1]:
        choice += (largest > size).astype(jnp.int32)
    choice_ref[0] = choice


def plan(counts, sorted_rows, chips, sizes):
    rows = sorted_rows.shape[0]
    most = sizes[-1]
    return pl.pallas_call(
        functools.partial(plan_kernel, sizes),
        grid_spec=pltpu.PrefetchScalarGridSpec(
            num_scalar_prefetch=1,
            grid=(1,),
            in_specs=[pl.BlockSpec((1, rows), lambda i, s: (0, 0))],
            out_specs=[pl.BlockSpec((chips, most), lambda i, s: (0, 0)), pl.BlockSpec(memory_space=pltpu.SMEM)],
        ),
        out_shape=[jax.ShapeDtypeStruct((chips, most), jnp.int32), jax.ShapeDtypeStruct((1,), jnp.int32)],
        name="plan",
    )(counts, sorted_rows.reshape(1, rows))


def down_copies(core, own_down_ref, other_down_ref, down_vmem, sems):
    ranks = own_down_ref.shape[0]
    return [
        pltpu.make_async_copy(ref, down_vmem.at[pl.ds(pl.multiple_of(where * ranks, ranks), ranks)], sems.at[i])
        for i, (ref, where) in enumerate(((own_down_ref, core), (other_down_ref, 1 - core)))
    ]


def shrink_near_kernel(columns, pieces, table, me, own_down_ref, other_down_ref, *refs):
    piece_refs = refs[:pieces]
    tokens_ref, shrunk_ref, tokens_vmem, down_vmem, sems = refs[pieces:]
    copies = down_copies(me[0] % CORES, own_down_ref, other_down_ref, down_vmem, sems)
    for i, ref in enumerate(piece_refs):
        rows, width = ref.shape
        start = pl.multiple_of(table[me[0] * (pieces + 1) + i] * rows, rows)
        copies.append(
            pltpu.make_async_copy(
                ref, tokens_vmem.at[pl.ds(start, rows), pl.ds(columns[i], width)], sems.at[2 + i]
            )
        )
    run_copies(copies)
    out_copy = pltpu.make_async_copy(tokens_vmem, tokens_ref, sems.at[2 + pieces])
    out_copy.start()
    shrunk_ref[...] = lax.dot_general(
        tokens_vmem[...], down_vmem[...], (((1,), (1,)), ((), ())), preferred_element_type=jnp.float32
    ).astype(shrunk_ref.dtype)
    out_copy.wait()


def shrink_far_kernel(table, me, tokens_in, shrunk_in, own_down_ref, other_down_ref, *refs):
    piece_refs = refs[:2]
    tokens_ref, shrunk_ref, far_vmem, down_vmem, sems = refs[2:]
    rows, width = far_vmem.shape
    entries = table.shape[0] // (CORES * tokens_in.shape[0] // rows)
    start = pl.multiple_of(table[me[0] * entries + entries - 1] * rows, rows)
    copies = down_copies(me[0] % CORES, own_down_ref, other_down_ref, down_vmem, sems)
    half = width // 2
    for i, ref in enumerate(piece_refs):
        copies.append(pltpu.make_async_copy(ref, far_vmem.at[:, pl.ds(i * half, half)], sems.at[2 + i]))
    run_copies(copies)
    out_copy = pltpu.make_async_copy(far_vmem, tokens_ref.at[pl.ds(start, rows)], sems.at[4])
    out_copy.start()
    shrunk_ref[...] = shrunk_in[...]
    shrunk_ref[pl.ds(start, rows), :] = lax.dot_general(
        far_vmem[...], down_vmem[...], (((1,), (1,)), ((), ())), preferred_element_type=jnp.float32
    ).astype(shrunk_ref.dtype)
    out_copy.wait()


def shrink(table, me, columns, pieces, rows, own_down, other_down):
    ranks, width = own_down.shape
    near = pieces[:-2]
    block = pieces[-1].shape[0]
    tokens_shape = pltpu.HBM((rows, width), jnp.bfloat16)
    shrunk_shape = jax.ShapeDtypeStruct((rows, CORES * ranks), jnp.bfloat16)
    shrunk_spec = pl.BlockSpec((rows, CORES * ranks), lambda i, s, t: (0, 0))
    down_vmem = pltpu.VMEM((CORES * ranks, width), jnp.bfloat16)
    tokens, shrunk = pl.pallas_call(
        functools.partial(shrink_near_kernel, columns, len(near)),
        grid_spec=pltpu.PrefetchScalarGridSpec(
            num_scalar_prefetch=2,
            grid=(1,),
            in_specs=[ANY_SPEC] * (2 + len(near)),
            out_specs=[ANY_SPEC, shrunk_spec],
            scratch_shapes=[
                pltpu.VMEM((rows, width), jnp.bfloat16),
                down_vmem,
                pltpu.SemaphoreType.DMA((3 + len(near),)),
            ],
        ),
        out_shape=[tokens_shape, shrunk_shape],
        compiler_params=pltpu.CompilerParams(vmem_limit_bytes=rows * width * 2 + 16 * MIB),
        name="shrink_near",
    )(table, me, *in_hbm([own_down, other_down, near[0]]), *near[1:])
    return pl.pallas_call(
        shrink_far_kernel,
        grid_spec=pltpu.PrefetchScalarGridSpec(
            num_scalar_prefetch=2,
            grid=(1,),
            in_specs=[ANY_SPEC, shrunk_spec] + [ANY_SPEC] * 4,
            out_specs=[ANY_SPEC, shrunk_spec],
            scratch_shapes=[
                pltpu.VMEM((block, width), jnp.bfloat16),
                down_vmem,
                pltpu.SemaphoreType.DMA((5,)),
            ],
        ),
        out_shape=[tokens_shape, shrunk_shape],
        input_output_aliases={2: 0},
        compiler_params=pltpu.CompilerParams(vmem_limit_bytes=16 * MIB),
        name="shrink_far",
    )(table, me, *in_hbm([tokens]), shrunk, *in_hbm([own_down, other_down]), *pieces[-2:])


def expand_kernel(block, counts, me, held_ref, own_ref, other_ref, keep_ref, got_ref, out_ref, maps_vmem, out_vmem, sems):
    chips, slots, units = out_vmem.shape
    most = held_ref.shape[1]
    ranks = keep_ref.shape[0]
    adapters = counts.shape[0] // chips
    chip = me[0] // CORES
    core = me[0] % CORES
    copies = []
    for c in range(chips):
        start = pl.multiple_of((c * CORES + core) * units, units)
        for ref, where in ((keep_ref, core), (got_ref, 1 - core)):
            copies.append(
                pltpu.make_async_copy(
                    ref.at[:, pl.ds(start, units)],
                    maps_vmem.at[c, pl.ds(pl.multiple_of(where * ranks, ranks), ranks)],
                    sems.at[len(copies)],
                )
            )
    for copy in copies:
        copy.start()

    wanted = held_ref[pl.ds(chip, 1), :]
    index = lax.broadcasted_iota(jnp.int32, (own_ref.shape[0], most), 0)
    row = index // block * (CORES * block) + index % block
    picked = jnp.zeros((most, own_ref.shape[1]), jnp.float32)
    for ref, where in ((own_ref, core), (other_ref, 1 - core)):
        hit = (row + where * block == wanted).astype(jnp.float32).astype(jnp.bfloat16)
        picked += lax.dot_general(hit, ref[...], (((0,), (0,)), ((), ())), preferred_element_type=jnp.float32)
    slot = lax.broadcasted_iota(jnp.int32, picked.shape, 0)
    adapter = lax.broadcasted_iota(jnp.int32, picked.shape, 1) // (picked.shape[1] // adapters)
    mine = jnp.zeros(picked.shape, jnp.int32)
    first = jnp.int32(0)
    for a in range(adapters):
        end = first + counts[chip * adapters + a]
        mine += ((adapter == a) & (slot >= first) & (slot < end)).astype(jnp.int32)
        first = end
    shrunk = jnp.where(mine > 0, picked, 0.0).astype(jnp.bfloat16)[:slots]

    out_copies = []
    for c in range(chips):
        copies[2 * c].wait()
        copies[2 * c + 1].wait()
        product = jnp.dot(shrunk, maps_vmem[c], preferred_element_type=jnp.float32)
        out_vmem[c] = (ADAPTER_SCALE * product).astype(out_vmem.dtype)
        out_copies.append(pltpu.make_async_copy(out_vmem.at[c], out_ref.at[c], sems.at[2 * chips + c]))
        out_copies[-1].start()
    for copy in out_copies:
        copy.wait()


def expand(counts, me, held, own_shrunk, other_shrunk, keep, got, slots, block):
    ranks, columns = keep.shape
    chips, most = held.shape
    units = columns // chips // CORES
    rows, ranks_all = own_shrunk.shape
    shrunk_spec = pl.BlockSpec((rows, ranks_all), lambda i, s, t: (0, 0))
    return pl.pallas_call(
        functools.partial(expand_kernel, block),
        grid_spec=pltpu.PrefetchScalarGridSpec(
            num_scalar_prefetch=2,
            grid=(1,),
            in_specs=[
                pl.BlockSpec((chips, most), lambda i, s, t: (0, 0)),
                shrunk_spec,
                shrunk_spec,
                ANY_SPEC,
                ANY_SPEC,
            ],
            out_specs=ANY_SPEC,
            scratch_shapes=[
                pltpu.VMEM((chips, ranks_all, units), jnp.bfloat16),
                pltpu.VMEM((chips, slots, units), jnp.bfloat16),
                pltpu.SemaphoreType.DMA((3 * chips,)),
            ],
        ),
        out_shape=pltpu.HBM((chips, slots, units), jnp.bfloat16),
        compiler_params=pltpu.CompilerParams(vmem_limit_bytes=16 * MIB),
        cost_estimate=pl.CostEstimate(
            flops=2 * slots * ranks_all * chips * units,
            bytes_accessed=2 * (slots + ranks_all) * chips * units,
            transcendentals=0,
        ),
        name="expand",
    )(counts, me, held, own_shrunk, other_shrunk, *in_hbm([keep, got]))


def project_kernel(block, me, gate_weight_ref, up_weight_ref, own_ref, other_ref, gate_ref, up_ref, tokens_vmem, sems):
    depth = gate_weight_ref.shape[0]
    core = me[0] % CORES
    k = pl.program_id(0)

    @pl.when(k == 0)
    def _():
        copies = []
        for ref, where in ((own_ref, core), (other_ref, 1 - core)):
            for chip in range(ref.shape[0] // block):
                start = pl.multiple_of((chip * CORES + where) * block, block)
                copies.append(
                    pltpu.make_async_copy(
                        ref.at[pl.ds(chip * block, block)], tokens_vmem.at[pl.ds(start, block)], sems.at[len(copies)]
                    )
                )
        run_copies(copies)
        gate_ref[...] = jnp.zeros_like(gate_ref)
        up_ref[...] = jnp.zeros_like(up_ref)

    tokens = tokens_vmem[:, pl.ds(pl.multiple_of(k * depth, depth), depth)]
    gate_ref[...] += jnp.dot(tokens, gate_weight_ref[...], preferred_element_type=jnp.float32)
    up_ref[...] += jnp.dot(tokens, up_weight_ref[...], preferred_element_type=jnp.float32)

    @pl.when(k == pl.num_programs(0) - 1)
    def _():
        gate = gate_ref[...]
        gate_ref[...] = gate / (1.0 + jnp.exp(-gate))


def project(me, own, other, gate_weight, up_weight, block):
    width, units = gate_weight.shape
    rows = CORES * own.shape[0]
    depth = min(1024, width)
    weight_spec = pl.BlockSpec((depth, units), lambda k, s: (k, 0))
    out_spec = pl.BlockSpec((rows, units), lambda k, s: (0, 0))
    out = pltpu.HBM((rows, units), jnp.float32)
    return pl.pallas_call(
        functools.partial(project_kernel, block),
        grid_spec=pltpu.PrefetchScalarGridSpec(
            num_scalar_prefetch=1,
            grid=(width // depth,),
            in_specs=[weight_spec, weight_spec, ANY_SPEC, ANY_SPEC],
            out_specs=[out_spec, out_spec],
            scratch_shapes=[
                pltpu.VMEM((rows, width), jnp.bfloat16),
                pltpu.SemaphoreType.DMA((rows // block,)),
            ],
        ),
        out_shape=[out, out],
        compiler_params=pltpu.CompilerParams(vmem_limit_bytes=rows * width * 2 + 20 * MIB),
        cost_estimate=pl.CostEstimate(
            flops=4 * rows * width * units,
            bytes_accessed=2 * (rows + 2 * units) * width,
            transcendentals=rows * units,
        ),
        name="project",
    )(me, *in_hbm([gate_weight, up_weight, own, other]))


def combine_kernel(pick_ref, gate_ref, up_ref, products_ref, out_ref):
    delta = jnp.dot(pick_ref[...], products_ref[...], preferred_element_type=jnp.float32)
    out_ref[...] = (gate_ref[...] * (up_ref[...] + delta)).astype(out_ref.dtype)


def combine(pick, gate, up, products):
    rows, units = gate.shape
    slots_all = products.shape[0]
    tile = min(512, units)
    column_spec = pl.BlockSpec((rows, tile), lambda n: (0, n))
    return pl.pallas_call(
        combine_kernel,
        grid=(units // tile,),
        in_specs=[
            pl.BlockSpec((rows, slots_all), lambda n: (0, 0)),
            column_spec,
            column_spec,
            pl.BlockSpec((slots_all, tile), lambda n: (0, n)),
        ],
        out_specs=column_spec,
        out_shape=pltpu.HBM((rows, units), jnp.bfloat16),
        compiler_params=pltpu.CompilerParams(vmem_limit_bytes=rows * slots_all * 4 + 20 * MIB),
        cost_estimate=pl.CostEstimate(
            flops=2 * rows * slots_all * units, bytes_accessed=10 * rows * units, transcendentals=0
        ),
        name="combine",
    )(*in_hbm([pick, gate, up]), products)


def per_device(
    tokens,
    gate_weight,
    up_weight,
    adapter_down_weight,
    adapter_up_weight,
    row_adapter,
    sorted_rows,
    segment_count,
):
    axis = "tensor"
    size = lax.axis_size(axis)
    me = lax.axis_index(axis).astype(jnp.int32)
    chips = size // CORES
    resident, rank, width = adapter_down_weight.shape
    ranks = resident * rank
    rows = row_adapter.shape[0]
    block = tokens.shape[0]
    me_array = me.reshape(1)
    flips = [(d, d ^ 1) for d in range(size)]

    def other_core(value):
        return lax.ppermute(value, axis, flips)

    most = CORES * resident * ROWS_PER_LIMIT
    sizes = [slots for slots in SLOT_SIZES if slots < most] + [most]
    groups = lax.axis_size("groups")
    own_down = adapter_down_weight.reshape(ranks, width)
    own_maps = adapter_up_weight.reshape(ranks, -1)
    other_down = other_core(own_down)
    held = choice = other_maps = None

    def beside(step, values):
        nonlocal other_down, held, choice, other_maps
        if step == 1:
            counts, other_down, _ = lax.optimization_barrier((segment_count, other_down, values))
            held, choice = plan(counts, sorted_rows, chips, sizes)
            choices = [choice] + [
                lax.ppermute(choice, "groups", [(g, (g + shift) % groups) for g in range(groups)])
                for shift in range(1, groups)
            ]
            choice = functools.reduce(jnp.maximum, choices)
        if step == 2:
            maps, _ = lax.optimization_barrier((own_maps, values))
            other_maps = other_core(maps)

    found, where = ring_gather(tokens, axis, beside)
    pieces = [piece for piece, _ in found]
    columns = [column for _, column in found]
    choice, pieces[-2], pieces[-1] = lax.optimization_barrier((choice, pieces[-2], pieces[-1]))
    table = jnp.array([row[:-1] for row in where], jnp.int32).reshape(-1)
    own_tokens, own_shrunk = shrink(table, me_array, columns, pieces, rows // CORES, own_down, other_down)
    other_shrunk = other_core(own_shrunk)

    same_core = [[c * CORES + k for c in range(chips)] for k in range(CORES)]

    def finish(slots):
        def branch(own_tokens, own_shrunk, other_shrunk, own_maps, other_maps, held, gate_weight, up_weight):
            products = expand(
                segment_count, me_array, held, own_shrunk, other_shrunk, own_maps, other_maps, slots, block
            )
            products = lax.all_to_all(
                products, axis, split_axis=0, concat_axis=0, axis_index_groups=same_core, tiled=True
            )
            held, other_tokens = lax.optimization_barrier((held, other_core(own_tokens)))
            held_rows = held[:, :slots].reshape(1, chips * slots)
            pick = (jnp.arange(rows, dtype=jnp.int32)[:, None] == held_rows).astype(jnp.bfloat16)
            pick, other_tokens = lax.optimization_barrier((pick, other_tokens))
            gate, up = project(me_array, own_tokens, other_tokens, gate_weight, up_weight, block)
            return combine(pick, gate, up, products.reshape(chips * slots, -1))

        return branch

    return lax.switch(
        choice[0],
        [finish(slots) for slots in sizes],
        own_tokens,
        own_shrunk,
        other_shrunk,
        own_maps,
        other_maps,
        held,
        gate_weight,
        up_weight,
    )


def solution(mesh):
    placed = (
        P(("groups", "tensor"), None),
        P(None, "tensor"),
        P(None, "tensor"),
        P(("groups", "tensor"), None, None),
        P(("groups", "tensor"), None, None),
        P("groups"),
        P("groups"),
        P("groups"),
    )
    return jax.shard_map(
        per_device, mesh=mesh, in_specs=placed, out_specs=P("groups", "tensor"), check_vma=False
    )
```

```python
import functools

import jax
import jax.numpy as jnp
from jax import lax
from jax.experimental import pallas as pl
from jax.experimental.pallas import tpu as pltpu
from jax.sharding import PartitionSpec as P

ADAPTER_SCALE = 0.5
ROWS_PER_LIMIT = 64
SLOT_SIZES = (80, 96)
CORES = 2
MIB = 1024 * 1024


def chip_ring(chips):
    return list(range(0, chips, 2)) + list(range(chips - 1, 0, -2))


def ring_gather(block, axis, beside):
    size = lax.axis_size(axis)
    chips = size // CORES
    ring = chip_ring(chips)

    def moved(value, shift):
        pairs = [
            (ring[p] * CORES + k, ring[(p + shift) % chips] * CORES + k)
            for p in range(chips)
            for k in range(CORES)
        ]
        return lax.ppermute(value, axis, pairs)

    half = block.shape[1] // 2
    far = chips // 2
    halves = block[:, :half], block[:, half:]
    columns = (0, half), (half, 0)
    held = [halves, halves[::-1]]
    pieces = [(block, 0, 0)]
    for step in range(1, far + 1):
        for chain in range(1 if step == far else 2):
            right, left = held[chain]
            held[chain] = moved(right, 1), moved(left, -1)
            for value, column, distance in zip(held[chain], columns[chain], (-step, step)):
                pieces.append((value, column, distance))
        beside(step, held)

    found = [(value, column) for value, column, _ in pieces]
    where = [
        [ring[(ring.index(device // CORES) + distance) % chips] for _, _, distance in pieces]
        for device in range(size)
    ]
    return found, where


ANY_SPEC = pl.BlockSpec(memory_space=pl.ANY)


def in_hbm(values):
    return [pltpu.with_memory_space_constraint(value, pltpu.HBM) for value in values]


def run_copies(copies):
    for copy in copies:
        copy.start()
    for copy in copies:
        copy.wait()


def plan_kernel(sizes, counts, sorted_ref, held_ref, choice_ref):
    chips, most = held_ref.shape
    rows = sorted_ref.shape[1]
    adapters = counts.shape[0] // chips
    listed = jnp.broadcast_to(sorted_ref[...], (8, rows))
    slot = lax.broadcasted_iota(jnp.int32, (8, most), 1)
    start = jnp.int32(0)
    largest = jnp.int32(0)
    for chip in range(chips):
        total = jnp.int32(0)
        for a in range(adapters):
            total += counts[chip * adapters + a]
        turned = pltpu.roll(listed, (rows - start) % rows, 1)
        held_ref[chip : chip + 1, :] = jnp.where(slot < total, turned[:, :most], -1)[0:1]
        start += total
        largest = jnp.maximum(largest, total)
    choice = jnp.int32(0)
    for size in sizes[:-1]:
        choice += (largest > size).astype(jnp.int32)
    choice_ref[0] = choice


def plan(counts, sorted_rows, chips, sizes):
    rows = sorted_rows.shape[0]
    most = sizes[-1]
    return pl.pallas_call(
        functools.partial(plan_kernel, sizes),
        grid_spec=pltpu.PrefetchScalarGridSpec(
            num_scalar_prefetch=1,
            grid=(1,),
            in_specs=[pl.BlockSpec((1, rows), lambda i, s: (0, 0))],
            out_specs=[pl.BlockSpec((chips, most), lambda i, s: (0, 0)), pl.BlockSpec(memory_space=pltpu.SMEM)],
        ),
        out_shape=[jax.ShapeDtypeStruct((chips, most), jnp.int32), jax.ShapeDtypeStruct((1,), jnp.int32)],
        name="plan",
    )(counts, sorted_rows.reshape(1, rows))


def down_copies(core, own_down_ref, other_down_ref, down_vmem, sems):
    ranks = own_down_ref.shape[0]
    return [
        pltpu.make_async_copy(ref, down_vmem.at[pl.ds(pl.multiple_of(where * ranks, ranks), ranks)], sems.at[i])
        for i, (ref, where) in enumerate(((own_down_ref, core), (other_down_ref, 1 - core)))
    ]


def shrink_near_kernel(columns, pieces, table, me, own_down_ref, other_down_ref, *refs):
    piece_refs = refs[:pieces]
    tokens_ref, shrunk_ref, tokens_vmem, down_vmem, sems = refs[pieces:]
    copies = down_copies(me[0] % CORES, own_down_ref, other_down_ref, down_vmem, sems)
    for i, ref in enumerate(piece_refs):
        rows, width = ref.shape
        start = pl.multiple_of(table[me[0] * (pieces + 1) + i] * rows, rows)
        copies.append(
            pltpu.make_async_copy(
                ref, tokens_vmem.at[pl.ds(start, rows), pl.ds(columns[i], width)], sems.at[2 + i]
            )
        )
    run_copies(copies)
    out_copy = pltpu.make_async_copy(tokens_vmem, tokens_ref, sems.at[2 + pieces])
    out_copy.start()
    shrunk_ref[...] = lax.dot_general(
        tokens_vmem[...], down_vmem[...], (((1,), (1,)), ((), ())), preferred_element_type=jnp.float32
    ).astype(shrunk_ref.dtype)
    out_copy.wait()


def shrink_far_kernel(table, me, tokens_in, shrunk_in, own_down_ref, other_down_ref, *refs):
    piece_refs = refs[:2]
    tokens_ref, shrunk_ref, far_vmem, down_vmem, sems = refs[2:]
    rows, width = far_vmem.shape
    entries = table.shape[0] // (CORES * tokens_in.shape[0] // rows)
    start = pl.multiple_of(table[me[0] * entries + entries - 1] * rows, rows)
    copies = down_copies(me[0] % CORES, own_down_ref, other_down_ref, down_vmem, sems)
    half = width // 2
    for i, ref in enumerate(piece_refs):
        copies.append(pltpu.make_async_copy(ref, far_vmem.at[:, pl.ds(i * half, half)], sems.at[2 + i]))
    run_copies(copies)
    out_copy = pltpu.make_async_copy(far_vmem, tokens_ref.at[pl.ds(start, rows)], sems.at[4])
    out_copy.start()
    shrunk_ref[...] = shrunk_in[...]
    shrunk_ref[pl.ds(start, rows), :] = lax.dot_general(
        far_vmem[...], down_vmem[...], (((1,), (1,)), ((), ())), preferred_element_type=jnp.float32
    ).astype(shrunk_ref.dtype)
    out_copy.wait()


def shrink(table, me, columns, pieces, rows, own_down, other_down):
    ranks, width = own_down.shape
    near = pieces[:-2]
    block = pieces[-1].shape[0]
    tokens_shape = pltpu.HBM((rows, width), jnp.bfloat16)
    shrunk_shape = jax.ShapeDtypeStruct((rows, CORES * ranks), jnp.bfloat16)
    shrunk_spec = pl.BlockSpec((rows, CORES * ranks), lambda i, s, t: (0, 0))
    down_vmem = pltpu.VMEM((CORES * ranks, width), jnp.bfloat16)
    tokens, shrunk = pl.pallas_call(
        functools.partial(shrink_near_kernel, columns, len(near)),
        grid_spec=pltpu.PrefetchScalarGridSpec(
            num_scalar_prefetch=2,
            grid=(1,),
            in_specs=[ANY_SPEC] * (2 + len(near)),
            out_specs=[ANY_SPEC, shrunk_spec],
            scratch_shapes=[
                pltpu.VMEM((rows, width), jnp.bfloat16),
                down_vmem,
                pltpu.SemaphoreType.DMA((3 + len(near),)),
            ],
        ),
        out_shape=[tokens_shape, shrunk_shape],
        compiler_params=pltpu.CompilerParams(vmem_limit_bytes=rows * width * 2 + 16 * MIB),
        name="shrink_near",
    )(table, me, *in_hbm([own_down, other_down, near[0]]), *near[1:])
    return pl.pallas_call(
        shrink_far_kernel,
        grid_spec=pltpu.PrefetchScalarGridSpec(
            num_scalar_prefetch=2,
            grid=(1,),
            in_specs=[ANY_SPEC, shrunk_spec] + [ANY_SPEC] * 4,
            out_specs=[ANY_SPEC, shrunk_spec],
            scratch_shapes=[
                pltpu.VMEM((block, width), jnp.bfloat16),
                down_vmem,
                pltpu.SemaphoreType.DMA((5,)),
            ],
        ),
        out_shape=[tokens_shape, shrunk_shape],
        input_output_aliases={2: 0},
        compiler_params=pltpu.CompilerParams(vmem_limit_bytes=16 * MIB),
        name="shrink_far",
    )(table, me, *in_hbm([tokens]), shrunk, *in_hbm([own_down, other_down]), *pieces[-2:])


def expand_kernel(block, counts, me, held_ref, own_ref, other_ref, keep_ref, got_ref, out_ref, maps_vmem, out_vmem, sems):
    chips, slots, units = out_vmem.shape
    most = held_ref.shape[1]
    ranks = keep_ref.shape[0]
    adapters = counts.shape[0] // chips
    chip = me[0] // CORES
    core = me[0] % CORES
    copies = []
    for c in range(chips):
        start = pl.multiple_of((c * CORES + core) * units, units)
        for ref, where in ((keep_ref, core), (got_ref, 1 - core)):
            copies.append(
                pltpu.make_async_copy(
                    ref.at[:, pl.ds(start, units)],
                    maps_vmem.at[c, pl.ds(pl.multiple_of(where * ranks, ranks), ranks)],
                    sems.at[len(copies)],
                )
            )
    for copy in copies:
        copy.start()

    wanted = held_ref[pl.ds(chip, 1), :]
    index = lax.broadcasted_iota(jnp.int32, (own_ref.shape[0], most), 0)
    row = index // block * (CORES * block) + index % block
    picked = jnp.zeros((most, own_ref.shape[1]), jnp.float32)
    for ref, where in ((own_ref, core), (other_ref, 1 - core)):
        hit = (row + where * block == wanted).astype(jnp.float32).astype(jnp.bfloat16)
        picked += lax.dot_general(hit, ref[...], (((0,), (0,)), ((), ())), preferred_element_type=jnp.float32)
    slot = lax.broadcasted_iota(jnp.int32, picked.shape, 0)
    adapter = lax.broadcasted_iota(jnp.int32, picked.shape, 1) // (picked.shape[1] // adapters)
    mine = jnp.zeros(picked.shape, jnp.int32)
    first = jnp.int32(0)
    for a in range(adapters):
        end = first + counts[chip * adapters + a]
        mine += ((adapter == a) & (slot >= first) & (slot < end)).astype(jnp.int32)
        first = end
    shrunk = jnp.where(mine > 0, picked, 0.0).astype(jnp.bfloat16)[:slots]

    out_copies = []
    for c in range(chips):
        copies[2 * c].wait()
        copies[2 * c + 1].wait()
        product = jnp.dot(shrunk, maps_vmem[c], preferred_element_type=jnp.float32)
        out_vmem[c] = (ADAPTER_SCALE * product).astype(out_vmem.dtype)
        out_copies.append(pltpu.make_async_copy(out_vmem.at[c], out_ref.at[c], sems.at[2 * chips + c]))
        out_copies[-1].start()
    for copy in out_copies:
        copy.wait()


def expand(counts, me, held, own_shrunk, other_shrunk, keep, got, slots, block):
    ranks, columns = keep.shape
    chips, most = held.shape
    units = columns // chips // CORES
    rows, ranks_all = own_shrunk.shape
    shrunk_spec = pl.BlockSpec((rows, ranks_all), lambda i, s, t: (0, 0))
    return pl.pallas_call(
        functools.partial(expand_kernel, block),
        grid_spec=pltpu.PrefetchScalarGridSpec(
            num_scalar_prefetch=2,
            grid=(1,),
            in_specs=[
                pl.BlockSpec((chips, most), lambda i, s, t: (0, 0)),
                shrunk_spec,
                shrunk_spec,
                ANY_SPEC,
                ANY_SPEC,
            ],
            out_specs=ANY_SPEC,
            scratch_shapes=[
                pltpu.VMEM((chips, ranks_all, units), jnp.bfloat16),
                pltpu.VMEM((chips, slots, units), jnp.bfloat16),
                pltpu.SemaphoreType.DMA((3 * chips,)),
            ],
        ),
        out_shape=pltpu.HBM((chips, slots, units), jnp.bfloat16),
        compiler_params=pltpu.CompilerParams(vmem_limit_bytes=16 * MIB),
        cost_estimate=pl.CostEstimate(
            flops=2 * slots * ranks_all * chips * units,
            bytes_accessed=2 * (slots + ranks_all) * chips * units,
            transcendentals=0,
        ),
        name="expand",
    )(counts, me, held, own_shrunk, other_shrunk, *in_hbm([keep, got]))


def project_kernel(block, me, gate_weight_ref, up_weight_ref, own_ref, other_ref, gate_ref, up_ref, tokens_vmem, sems):
    depth = gate_weight_ref.shape[0]
    core = me[0] % CORES
    k = pl.program_id(0)

    @pl.when(k == 0)
    def _():
        copies = []
        for ref, where in ((own_ref, core), (other_ref, 1 - core)):
            for chip in range(ref.shape[0] // block):
                start = pl.multiple_of((chip * CORES + where) * block, block)
                copies.append(
                    pltpu.make_async_copy(
                        ref.at[pl.ds(chip * block, block)], tokens_vmem.at[pl.ds(start, block)], sems.at[len(copies)]
                    )
                )
        run_copies(copies)
        gate_ref[...] = jnp.zeros_like(gate_ref)
        up_ref[...] = jnp.zeros_like(up_ref)

    tokens = tokens_vmem[:, pl.ds(pl.multiple_of(k * depth, depth), depth)]
    gate_ref[...] += jnp.dot(tokens, gate_weight_ref[...], preferred_element_type=jnp.float32)
    up_ref[...] += jnp.dot(tokens, up_weight_ref[...], preferred_element_type=jnp.float32)

    @pl.when(k == pl.num_programs(0) - 1)
    def _():
        gate = gate_ref[...]
        gate_ref[...] = gate / (1.0 + jnp.exp(-gate))


def project(me, own, other, gate_weight, up_weight, block):
    width, units = gate_weight.shape
    rows = CORES * own.shape[0]
    depth = min(1024, width)
    weight_spec = pl.BlockSpec((depth, units), lambda k, s: (k, 0))
    out_spec = pl.BlockSpec((rows, units), lambda k, s: (0, 0))
    out = pltpu.HBM((rows, units), jnp.float32)
    return pl.pallas_call(
        functools.partial(project_kernel, block),
        grid_spec=pltpu.PrefetchScalarGridSpec(
            num_scalar_prefetch=1,
            grid=(width // depth,),
            in_specs=[weight_spec, weight_spec, ANY_SPEC, ANY_SPEC],
            out_specs=[out_spec, out_spec],
            scratch_shapes=[
                pltpu.VMEM((rows, width), jnp.bfloat16),
                pltpu.SemaphoreType.DMA((rows // block,)),
            ],
        ),
        out_shape=[out, out],
        compiler_params=pltpu.CompilerParams(vmem_limit_bytes=rows * width * 2 + 20 * MIB),
        cost_estimate=pl.CostEstimate(
            flops=4 * rows * width * units,
            bytes_accessed=2 * (rows + 2 * units) * width,
            transcendentals=rows * units,
        ),
        name="project",
    )(me, *in_hbm([gate_weight, up_weight, own, other]))


def combine_kernel(pick_ref, gate_ref, up_ref, products_ref, out_ref):
    delta = jnp.dot(pick_ref[...], products_ref[...], preferred_element_type=jnp.float32)
    out_ref[...] = (gate_ref[...] * (up_ref[...] + delta)).astype(out_ref.dtype)


def combine(pick, gate, up, products):
    rows, units = gate.shape
    slots_all = products.shape[0]
    tile = min(512, units)
    column_spec = pl.BlockSpec((rows, tile), lambda n: (0, n))
    return pl.pallas_call(
        combine_kernel,
        grid=(units // tile,),
        in_specs=[
            pl.BlockSpec((rows, slots_all), lambda n: (0, 0)),
            column_spec,
            column_spec,
            pl.BlockSpec((slots_all, tile), lambda n: (0, n)),
        ],
        out_specs=column_spec,
        out_shape=pltpu.HBM((rows, units), jnp.bfloat16),
        compiler_params=pltpu.CompilerParams(vmem_limit_bytes=rows * slots_all * 4 + 20 * MIB),
        cost_estimate=pl.CostEstimate(
            flops=2 * rows * slots_all * units, bytes_accessed=10 * rows * units, transcendentals=0
        ),
        name="combine",
    )(*in_hbm([pick, gate, up]), products)


def per_device(
    tokens,
    gate_weight,
    up_weight,
    adapter_down_weight,
    adapter_up_weight,
    row_adapter,
    sorted_rows,
    segment_count,
):
    axis = "tensor"
    size = lax.axis_size(axis)
    me = lax.axis_index(axis).astype(jnp.int32)
    chips = size // CORES
    resident, rank, width = adapter_down_weight.shape
    ranks = resident * rank
    rows = row_adapter.shape[0]
    block = tokens.shape[0]
    me_array = me.reshape(1)
    flips = [(d, d ^ 1) for d in range(size)]

    def other_core(value):
        return lax.ppermute(value, axis, flips)

    most = CORES * resident * ROWS_PER_LIMIT
    sizes = [slots for slots in SLOT_SIZES if slots < most] + [most]
    groups = lax.axis_size("groups")
    own_down = adapter_down_weight.reshape(ranks, width)
    own_maps = adapter_up_weight.reshape(ranks, -1)
    other_down = other_core(own_down)
    held = choice = other_maps = None

    def beside(step, values):
        nonlocal other_down, held, choice, other_maps
        if step == 1:
            counts, other_down, _ = lax.optimization_barrier((segment_count, other_down, values))
            held, choice = plan(counts, sorted_rows, chips, sizes)
            choice = [choice] + [
                lax.ppermute(choice, "groups", [(g, (g + shift) % groups) for g in range(groups)])
                for shift in range(1, groups)
            ]
        if step == chips // 2 - 1:
            maps, _ = lax.optimization_barrier((own_maps, values))
            other_maps = other_core(maps)

    found, where = ring_gather(tokens, axis, beside)
    pieces = [piece for piece, _ in found]
    columns = [column for _, column in found]
    choice, pieces[0] = lax.optimization_barrier((choice, pieces[0]))
    table = jnp.array([row[:-1] for row in where], jnp.int32).reshape(-1)
    own_tokens, own_shrunk = shrink(table, me_array, columns, pieces, rows // CORES, own_down, other_down)
    choice, own_shrunk = lax.optimization_barrier((choice, own_shrunk))
    other_shrunk = other_core(own_shrunk)
    choice = functools.reduce(jnp.maximum, choice)

    same_core = [[c * CORES + k for c in range(chips)] for k in range(CORES)]

    def finish(slots):
        def branch(own_tokens, own_shrunk, other_shrunk, own_maps, other_maps, held, gate_weight, up_weight):
            products = expand(
                segment_count, me_array, held, own_shrunk, other_shrunk, own_maps, other_maps, slots, block
            )
            products = lax.all_to_all(
                products, axis, split_axis=0, concat_axis=0, axis_index_groups=same_core, tiled=True
            )
            held, other_tokens = lax.optimization_barrier((held, other_core(own_tokens)))
            held_rows = held[:, :slots].reshape(1, chips * slots)
            pick = (jnp.arange(rows, dtype=jnp.int32)[:, None] == held_rows).astype(jnp.bfloat16)
            pick, other_tokens = lax.optimization_barrier((pick, other_tokens))
            gate, up = project(me_array, own_tokens, other_tokens, gate_weight, up_weight, block)
            return combine(pick, gate, up, products.reshape(chips * slots, -1))

        return branch

    return lax.switch(
        choice[0],
        [finish(slots) for slots in sizes],
        own_tokens,
        own_shrunk,
        other_shrunk,
        own_maps,
        other_maps,
        held,
        gate_weight,
        up_weight,
    )


def solution(mesh):
    placed = (
        P(("groups", "tensor"), None),
        P(None, "tensor"),
        P(None, "tensor"),
        P(("groups", "tensor"), None, None),
        P(("groups", "tensor"), None, None),
        P("groups"),
        P("groups"),
        P("groups"),
    )
    return jax.shard_map(
        per_device, mesh=mesh, in_specs=placed, out_specs=P("groups", "tensor"), check_vma=False
    )
```

```python
import functools

import jax
import jax.numpy as jnp
from jax import lax
from jax.experimental import pallas as pl
from jax.experimental.pallas import tpu as pltpu
from jax.sharding import PartitionSpec as P

ADAPTER_SCALE = 0.5
ROWS_PER_LIMIT = 64
SLOT_SIZES = (80, 96)
CORES = 2
MIB = 1024 * 1024


def chip_ring(chips):
    return list(range(0, chips, 2)) + list(range(chips - 1, 0, -2))


def ring_chip(me, chips, distance):
    chip = me // CORES
    place = jnp.where(chip % 2 == 0, chip // 2, chips // 2 + (chips - 1 - chip) // 2)
    place = (place + distance + chips) % chips
    return jnp.where(place < chips // 2, 2 * place, chips - 1 - 2 * (place - chips // 2))


def ring_gather(block, axis, beside):
    size = lax.axis_size(axis)
    chips = size // CORES
    ring = chip_ring(chips)

    def moved(value, shift):
        pairs = [
            (ring[p] * CORES + k, ring[(p + shift) % chips] * CORES + k)
            for p in range(chips)
            for k in range(CORES)
        ]
        return lax.ppermute(value, axis, pairs)

    half = block.shape[1] // 2
    far = chips // 2
    halves = block[:, :half], block[:, half:]
    columns = (0, half), (half, 0)
    held = [halves, halves[::-1]]
    pieces = [(block, 0, 0)]
    for step in range(1, far + 1):
        for chain in range(1 if step == far else 2):
            right, left = held[chain]
            held[chain] = moved(right, 1), moved(left, -1)
            for value, column, distance in zip(held[chain], columns[chain], (-step, step)):
                pieces.append((value, column, distance))
        held = beside(step, held)
    return pieces


ANY_SPEC = pl.BlockSpec(memory_space=pl.ANY)


def in_hbm(values):
    return [pltpu.with_memory_space_constraint(value, pltpu.HBM) for value in values]


def run_copies(copies):
    for copy in copies:
        copy.start()
    for copy in copies:
        copy.wait()


def make_plan(sizes, counts, sorted_ref, held_ref, choice_ref):
    chips, most = held_ref.shape
    rows = sorted_ref.shape[1]
    adapters = counts[0].shape[0] // chips

    def total(group, chip):
        return functools.reduce(jnp.add, [counts[group][chip * adapters + a] for a in range(adapters)])

    listed = jnp.broadcast_to(sorted_ref[...], (8, rows))
    slot = lax.broadcasted_iota(jnp.int32, (8, most), 1)
    start = jnp.int32(0)
    for chip in range(chips):
        turned = pltpu.roll(listed, (rows - start) % rows, 1)
        held_ref[chip : chip + 1, :] = jnp.where(slot < total(0, chip), turned[:, :most], -1)[0:1]
        start += total(0, chip)
    largest = functools.reduce(
        jnp.maximum, [total(group, chip) for group in range(len(counts)) for chip in range(chips)]
    )
    choice_ref[0] = functools.reduce(jnp.add, [(largest > size).astype(jnp.int32) for size in sizes[:-1]])


def down_copies(core, own_down_ref, other_down_ref, down_vmem, sems):
    ranks = own_down_ref.shape[0]
    return [
        pltpu.make_async_copy(ref, down_vmem.at[pl.ds(pl.multiple_of(where * ranks, ranks), ranks)], sems.at[i])
        for i, (ref, where) in enumerate(((own_down_ref, core), (other_down_ref, 1 - core)))
    ]


def shrink_near_kernel(sizes, places, groups, me, *refs):
    counts, refs = refs[:groups], refs[groups:]
    sorted_ref, own_down_ref, other_down_ref = refs[:3]
    refs = refs[3:]
    piece_refs = refs[: len(places)]
    tokens_ref, shrunk_ref, held_ref, choice_ref, tokens_vmem, down_vmem, sems = refs[len(places) :]
    chips = held_ref.shape[0]
    copies = down_copies(me[0] % CORES, own_down_ref, other_down_ref, down_vmem, sems)
    for ref, (column, distance) in zip(piece_refs, places):
        rows, width = ref.shape
        start = pl.multiple_of(ring_chip(me[0], chips, distance) * rows, rows)
        copies.append(
            pltpu.make_async_copy(
                ref, tokens_vmem.at[pl.ds(start, rows), pl.ds(column, width)], sems.at[len(copies)]
            )
        )
    for copy in copies:
        copy.start()
    make_plan(sizes, counts, sorted_ref, held_ref, choice_ref)
    for copy in copies:
        copy.wait()
    out_copy = pltpu.make_async_copy(tokens_vmem, tokens_ref, sems.at[len(copies)])
    out_copy.start()
    shrunk_ref[...] = lax.dot_general(
        tokens_vmem[...], down_vmem[...], (((1,), (1,)), ((), ())), preferred_element_type=jnp.float32
    ).astype(shrunk_ref.dtype)
    out_copy.wait()


def shrink_far_kernel(me, tokens_in, shrunk_in, own_down_ref, other_down_ref, *refs):
    piece_refs = refs[:2]
    tokens_ref, shrunk_ref, far_vmem, down_vmem, sems = refs[2:]
    rows, width = far_vmem.shape
    chips = tokens_in.shape[0] // rows
    start = pl.multiple_of(ring_chip(me[0], chips, chips // 2) * rows, rows)
    copies = down_copies(me[0] % CORES, own_down_ref, other_down_ref, down_vmem, sems)
    half = width // 2
    for i, ref in enumerate(piece_refs):
        copies.append(pltpu.make_async_copy(ref, far_vmem.at[:, pl.ds(i * half, half)], sems.at[2 + i]))
    run_copies(copies)
    out_copy = pltpu.make_async_copy(far_vmem, tokens_ref.at[pl.ds(start, rows)], sems.at[4])
    out_copy.start()
    shrunk_ref[...] = shrunk_in[...]
    shrunk_ref[pl.ds(start, rows), :] = lax.dot_general(
        far_vmem[...], down_vmem[...], (((1,), (1,)), ((), ())), preferred_element_type=jnp.float32
    ).astype(shrunk_ref.dtype)
    out_copy.wait()


def shrink(me, counts, sorted_rows, pieces, own_down, other_down, sizes):
    ranks, width = own_down.shape
    rows_all = sorted_rows.shape[0]
    rows = rows_all // CORES
    values = [value for value, _, _ in pieces]
    near = values[:-2]
    block = values[0].shape[0]
    tokens_shape = pltpu.HBM((rows, width), jnp.bfloat16)
    shrunk_shape = jax.ShapeDtypeStruct((rows, CORES * ranks), jnp.bfloat16)
    held_shape = jax.ShapeDtypeStruct((rows // block, sizes[-1]), jnp.int32)

    def whole(shape):
        return pl.BlockSpec(shape, lambda i, *_: (0, 0))

    down_vmem = pltpu.VMEM((CORES * ranks, width), jnp.bfloat16)
    downs = in_hbm([own_down, other_down])
    tokens, shrunk, held, choice = pl.pallas_call(
        functools.partial(shrink_near_kernel, sizes, [place[1:] for place in pieces[:-2]], len(counts)),
        grid_spec=pltpu.PrefetchScalarGridSpec(
            num_scalar_prefetch=1 + len(counts),
            grid=(1,),
            in_specs=[whole((1, rows_all))] + [ANY_SPEC] * (2 + len(near)),
            out_specs=[
                ANY_SPEC,
                whole(shrunk_shape.shape),
                whole(held_shape.shape),
                pl.BlockSpec(memory_space=pltpu.SMEM),
            ],
            scratch_shapes=[
                pltpu.VMEM((rows, width), jnp.bfloat16),
                down_vmem,
                pltpu.SemaphoreType.DMA((3 + len(near),)),
            ],
        ),
        out_shape=[tokens_shape, shrunk_shape, held_shape, jax.ShapeDtypeStruct((1,), jnp.int32)],
        compiler_params=pltpu.CompilerParams(vmem_limit_bytes=rows * width * 2 + 16 * MIB),
        name="shrink_near",
    )(me, *counts, sorted_rows.reshape(1, rows_all), *downs, *in_hbm(near[:1]), *near[1:])
    tokens, shrunk = pl.pallas_call(
        shrink_far_kernel,
        grid_spec=pltpu.PrefetchScalarGridSpec(
            num_scalar_prefetch=1,
            grid=(1,),
            in_specs=[ANY_SPEC, whole(shrunk_shape.shape)] + [ANY_SPEC] * 4,
            out_specs=[ANY_SPEC, whole(shrunk_shape.shape)],
            scratch_shapes=[
                pltpu.VMEM((block, width), jnp.bfloat16),
                down_vmem,
                pltpu.SemaphoreType.DMA((5,)),
            ],
        ),
        out_shape=[tokens_shape, shrunk_shape],
        input_output_aliases={1: 0},
        compiler_params=pltpu.CompilerParams(vmem_limit_bytes=16 * MIB),
        name="shrink_far",
    )(me, *in_hbm([tokens]), shrunk, *downs, *values[-2:])
    return tokens, shrunk, held, choice


def expand_kernel(block, counts, me, held_ref, own_ref, other_ref, keep_ref, got_ref, out_ref, maps_vmem, out_vmem, sems):
    chips, slots, units = out_vmem.shape
    most = held_ref.shape[1]
    ranks = keep_ref.shape[0]
    adapters = counts.shape[0] // chips
    chip = me[0] // CORES
    core = me[0] % CORES
    copies = []
    for c in range(chips):
        start = pl.multiple_of((c * CORES + core) * units, units)
        for ref, where in ((keep_ref, core), (got_ref, 1 - core)):
            copies.append(
                pltpu.make_async_copy(
                    ref.at[:, pl.ds(start, units)],
                    maps_vmem.at[c, pl.ds(pl.multiple_of(where * ranks, ranks), ranks)],
                    sems.at[len(copies)],
                )
            )
    for copy in copies:
        copy.start()

    wanted = held_ref[pl.ds(chip, 1), :]
    index = lax.broadcasted_iota(jnp.int32, (own_ref.shape[0], most), 0)
    row = index // block * (CORES * block) + index % block
    picked = jnp.zeros((most, own_ref.shape[1]), jnp.float32)
    for ref, where in ((own_ref, core), (other_ref, 1 - core)):
        hit = (row + where * block == wanted).astype(jnp.float32).astype(jnp.bfloat16)
        picked += lax.dot_general(hit, ref[...], (((0,), (0,)), ((), ())), preferred_element_type=jnp.float32)
    slot = lax.broadcasted_iota(jnp.int32, picked.shape, 0)
    adapter = lax.broadcasted_iota(jnp.int32, picked.shape, 1) // (picked.shape[1] // adapters)
    mine = jnp.zeros(picked.shape, jnp.int32)
    first = jnp.int32(0)
    for a in range(adapters):
        end = first + counts[chip * adapters + a]
        mine += ((adapter == a) & (slot >= first) & (slot < end)).astype(jnp.int32)
        first = end
    shrunk = jnp.where(mine > 0, picked, 0.0).astype(jnp.bfloat16)[:slots]

    out_copies = []
    for c in range(chips):
        copies[2 * c].wait()
        copies[2 * c + 1].wait()
        product = jnp.dot(shrunk, maps_vmem[c], preferred_element_type=jnp.float32)
        out_vmem[c] = (ADAPTER_SCALE * product).astype(out_vmem.dtype)
        out_copies.append(pltpu.make_async_copy(out_vmem.at[c], out_ref.at[c], sems.at[2 * chips + c]))
        out_copies[-1].start()
    for copy in out_copies:
        copy.wait()


def expand(counts, me, held, own_shrunk, other_shrunk, keep, got, slots, block):
    ranks, columns = keep.shape
    chips, most = held.shape
    units = columns // chips // CORES
    rows, ranks_all = own_shrunk.shape
    shrunk_spec = pl.BlockSpec((rows, ranks_all), lambda i, s, t: (0, 0))
    return pl.pallas_call(
        functools.partial(expand_kernel, block),
        grid_spec=pltpu.PrefetchScalarGridSpec(
            num_scalar_prefetch=2,
            grid=(1,),
            in_specs=[
                pl.BlockSpec((chips, most), lambda i, s, t: (0, 0)),
                shrunk_spec,
                shrunk_spec,
                ANY_SPEC,
                ANY_SPEC,
            ],
            out_specs=ANY_SPEC,
            scratch_shapes=[
                pltpu.VMEM((chips, ranks_all, units), jnp.bfloat16),
                pltpu.VMEM((chips, slots, units), jnp.bfloat16),
                pltpu.SemaphoreType.DMA((3 * chips,)),
            ],
        ),
        out_shape=pltpu.HBM((chips, slots, units), jnp.bfloat16),
        compiler_params=pltpu.CompilerParams(vmem_limit_bytes=16 * MIB),
        cost_estimate=pl.CostEstimate(
            flops=2 * slots * ranks_all * chips * units,
            bytes_accessed=2 * (slots + ranks_all) * chips * units,
            transcendentals=0,
        ),
        name="expand",
    )(counts, me, held, own_shrunk, other_shrunk, *in_hbm([keep, got]))


def project_kernel(block, me, gate_weight_ref, up_weight_ref, own_ref, other_ref, gate_ref, up_ref, tokens_vmem, sems):
    depth = gate_weight_ref.shape[0]
    core = me[0] % CORES
    k = pl.program_id(0)

    @pl.when(k == 0)
    def _():
        copies = []
        for ref, where in ((own_ref, core), (other_ref, 1 - core)):
            for chip in range(ref.shape[0] // block):
                start = pl.multiple_of((chip * CORES + where) * block, block)
                copies.append(
                    pltpu.make_async_copy(
                        ref.at[pl.ds(chip * block, block)], tokens_vmem.at[pl.ds(start, block)], sems.at[len(copies)]
                    )
                )
        run_copies(copies)
        gate_ref[...] = jnp.zeros_like(gate_ref)
        up_ref[...] = jnp.zeros_like(up_ref)

    tokens = tokens_vmem[:, pl.ds(pl.multiple_of(k * depth, depth), depth)]
    gate_ref[...] += jnp.dot(tokens, gate_weight_ref[...], preferred_element_type=jnp.float32)
    up_ref[...] += jnp.dot(tokens, up_weight_ref[...], preferred_element_type=jnp.float32)

    @pl.when(k == pl.num_programs(0) - 1)
    def _():
        gate = gate_ref[...]
        gate_ref[...] = gate / (1.0 + jnp.exp(-gate))


def project(me, own, other, gate_weight, up_weight, block):
    width, units = gate_weight.shape
    rows = CORES * own.shape[0]
    depth = min(1024, width)
    weight_spec = pl.BlockSpec((depth, units), lambda k, s: (k, 0))
    out_spec = pl.BlockSpec((rows, units), lambda k, s: (0, 0))
    out = pltpu.HBM((rows, units), jnp.float32)
    return pl.pallas_call(
        functools.partial(project_kernel, block),
        grid_spec=pltpu.PrefetchScalarGridSpec(
            num_scalar_prefetch=1,
            grid=(width // depth,),
            in_specs=[weight_spec, weight_spec, ANY_SPEC, ANY_SPEC],
            out_specs=[out_spec, out_spec],
            scratch_shapes=[
                pltpu.VMEM((rows, width), jnp.bfloat16),
                pltpu.SemaphoreType.DMA((rows // block,)),
            ],
        ),
        out_shape=[out, out],
        compiler_params=pltpu.CompilerParams(vmem_limit_bytes=rows * width * 2 + 20 * MIB),
        cost_estimate=pl.CostEstimate(
            flops=4 * rows * width * units,
            bytes_accessed=2 * (rows + 2 * units) * width,
            transcendentals=rows * units,
        ),
        name="project",
    )(me, *in_hbm([gate_weight, up_weight, own, other]))


def combine_kernel(pick_ref, gate_ref, up_ref, products_ref, out_ref):
    delta = jnp.dot(pick_ref[...], products_ref[...], preferred_element_type=jnp.float32)
    out_ref[...] = (gate_ref[...] * (up_ref[...] + delta)).astype(out_ref.dtype)


def combine(pick, gate, up, products):
    rows, units = gate.shape
    slots_all = products.shape[0]
    tile = min(512, units)
    column_spec = pl.BlockSpec((rows, tile), lambda n: (0, n))
    return pl.pallas_call(
        combine_kernel,
        grid=(units // tile,),
        in_specs=[
            pl.BlockSpec((rows, slots_all), lambda n: (0, 0)),
            column_spec,
            column_spec,
            pl.BlockSpec((slots_all, tile), lambda n: (0, n)),
        ],
        out_specs=column_spec,
        out_shape=pltpu.HBM((rows, units), jnp.bfloat16),
        compiler_params=pltpu.CompilerParams(vmem_limit_bytes=rows * slots_all * 4 + 20 * MIB),
        cost_estimate=pl.CostEstimate(
            flops=2 * rows * slots_all * units, bytes_accessed=10 * rows * units, transcendentals=0
        ),
        name="combine",
    )(*in_hbm([pick, gate, up]), products)


def per_device(
    tokens,
    gate_weight,
    up_weight,
    adapter_down_weight,
    adapter_up_weight,
    row_adapter,
    sorted_rows,
    segment_count,
):
    axis = "tensor"
    size = lax.axis_size(axis)
    me = lax.axis_index(axis).astype(jnp.int32)
    chips = size // CORES
    resident, rank, width = adapter_down_weight.shape
    ranks = resident * rank
    rows = row_adapter.shape[0]
    block = tokens.shape[0]
    me_array = me.reshape(1)
    flips = [(d, d ^ 1) for d in range(size)]

    def other_core(value):
        return lax.ppermute(value, axis, flips)

    most = CORES * resident * ROWS_PER_LIMIT
    sizes = [slots for slots in SLOT_SIZES if slots < most] + [most]
    groups = lax.axis_size("groups")
    own_down = adapter_down_weight.reshape(ranks, width)
    own_maps = adapter_up_weight.reshape(ranks, -1)
    other_down = other_core(own_down)
    counts = [segment_count] + [
        lax.ppermute(segment_count, "groups", [(g, (g + shift) % groups) for g in range(groups)])
        for shift in range(1, groups)
    ]
    other_maps = None

    def beside(step, values):
        nonlocal other_down, other_maps
        values = list(values)
        for chain in range(2):
            if step == 1:
                other_down, values[chain] = lax.optimization_barrier((other_down, values[chain]))
        if step == chips // 2 - 1:
            maps, _ = lax.optimization_barrier((own_maps, values))
            other_maps = other_core(maps)
        return values

    pieces = ring_gather(tokens, axis, beside)
    own_tokens, own_shrunk, held, choice = shrink(
        me_array, counts, sorted_rows, pieces, own_down, other_down, sizes
    )
    other_shrunk = other_core(own_shrunk)

    same_core = [[c * CORES + k for c in range(chips)] for k in range(CORES)]

    def finish(slots):
        def branch(own_tokens, own_shrunk, other_shrunk, own_maps, other_maps, held, gate_weight, up_weight):
            products = expand(
                segment_count, me_array, held, own_shrunk, other_shrunk, own_maps, other_maps, slots, block
            )
            products = lax.all_to_all(
                products, axis, split_axis=0, concat_axis=0, axis_index_groups=same_core, tiled=True
            )
            held, other_tokens = lax.optimization_barrier((held, other_core(own_tokens)))
            held_rows = held[:, :slots].reshape(1, chips * slots)
            pick = (jnp.arange(rows, dtype=jnp.int32)[:, None] == held_rows).astype(jnp.bfloat16)
            pick, other_tokens = lax.optimization_barrier((pick, other_tokens))
            gate, up = project(me_array, own_tokens, other_tokens, gate_weight, up_weight, block)
            return combine(pick, gate, up, products.reshape(chips * slots, -1))

        return branch

    return lax.switch(
        choice[0],
        [finish(slots) for slots in sizes],
        own_tokens,
        own_shrunk,
        other_shrunk,
        own_maps,
        other_maps,
        held,
        gate_weight,
        up_weight,
    )


def solution(mesh):
    placed = (
        P(("groups", "tensor"), None),
        P(None, "tensor"),
        P(None, "tensor"),
        P(("groups", "tensor"), None, None),
        P(("groups", "tensor"), None, None),
        P("groups"),
        P("groups"),
        P("groups"),
    )
    return jax.shard_map(
        per_device, mesh=mesh, in_specs=placed, out_specs=P("groups", "tensor"), check_vma=False
    )
```

```python
import functools

import jax
import jax.numpy as jnp
from jax import lax
from jax.experimental import pallas as pl
from jax.experimental.pallas import tpu as pltpu
from jax.sharding import PartitionSpec as P

ADAPTER_SCALE = 0.5
ROWS_PER_LIMIT = 64
SLOT_SIZES = (80, 96)
CORES = 2
MIB = 1024 * 1024


def chip_ring(chips):
    return list(range(0, chips, 2)) + list(range(chips - 1, 0, -2))


def ring_chip(me, chips, distance):
    chip = me // CORES
    place = jnp.where(chip % 2 == 0, chip // 2, chips // 2 + (chips - 1 - chip) // 2)
    place = (place + distance + chips) % chips
    return jnp.where(place < chips // 2, 2 * place, chips - 1 - 2 * (place - chips // 2))


def ring_gather(block, axis, beside):
    size = lax.axis_size(axis)
    chips = size // CORES
    ring = chip_ring(chips)

    def moved(value, shift):
        pairs = [
            (ring[p] * CORES + k, ring[(p + shift) % chips] * CORES + k)
            for p in range(chips)
            for k in range(CORES)
        ]
        return lax.ppermute(value, axis, pairs)

    half = block.shape[1] // 2
    far = chips // 2
    halves = block[:, :half], block[:, half:]
    columns = (0, half), (half, 0)
    held = [halves, halves[::-1]]
    pieces = [(block, 0, 0)]
    for step in range(1, far + 1):
        for chain in range(1 if step == far else 2):
            right, left = held[chain]
            held[chain] = moved(right, 1), moved(left, -1)
            for value, column, distance in zip(held[chain], columns[chain], (-step, step)):
                pieces.append((value, column, distance))
        held = beside(step, held)
    return pieces


ANY_SPEC = pl.BlockSpec(memory_space=pl.ANY)


def in_hbm(values):
    return [pltpu.with_memory_space_constraint(value, pltpu.HBM) for value in values]


def run_copies(copies):
    for copy in copies:
        copy.start()
    for copy in copies:
        copy.wait()


def make_plan(sizes, counts, sorted_ref, held_ref, choice_ref):
    chips, most = held_ref.shape
    rows = sorted_ref.shape[1]
    adapters = counts[0].shape[0] // chips

    def total(group, chip):
        return functools.reduce(jnp.add, [counts[group][chip * adapters + a] for a in range(adapters)])

    listed = jnp.broadcast_to(sorted_ref[...], (8, rows))
    slot = lax.broadcasted_iota(jnp.int32, (8, most), 1)
    start = jnp.int32(0)
    for chip in range(chips):
        turned = pltpu.roll(listed, (rows - start) % rows, 1)
        held_ref[chip : chip + 1, :] = jnp.where(slot < total(0, chip), turned[:, :most], -1)[0:1]
        start += total(0, chip)
    largest = functools.reduce(
        jnp.maximum, [total(group, chip) for group in range(len(counts)) for chip in range(chips)]
    )
    choice_ref[0] = functools.reduce(jnp.add, [(largest > size).astype(jnp.int32) for size in sizes[:-1]])


def down_copies(core, own_down_ref, other_down_ref, down_vmem, sems):
    ranks = own_down_ref.shape[0]
    return [
        pltpu.make_async_copy(ref, down_vmem.at[pl.ds(pl.multiple_of(where * ranks, ranks), ranks)], sems.at[i])
        for i, (ref, where) in enumerate(((own_down_ref, core), (other_down_ref, 1 - core)))
    ]


def shrink_near_kernel(sizes, places, groups, me, *refs):
    counts, refs = refs[:groups], refs[groups:]
    sorted_ref, own_down_ref, other_down_ref = refs[:3]
    refs = refs[3:]
    piece_refs = refs[: len(places)]
    tokens_ref, shrunk_ref, held_ref, choice_ref, tokens_vmem, down_vmem, sems = refs[len(places) :]
    chips = held_ref.shape[0]
    copies = down_copies(me[0] % CORES, own_down_ref, other_down_ref, down_vmem, sems)
    for ref, (column, distance) in zip(piece_refs, places):
        rows, width = ref.shape
        start = pl.multiple_of(ring_chip(me[0], chips, distance) * rows, rows)
        copies.append(
            pltpu.make_async_copy(
                ref, tokens_vmem.at[pl.ds(start, rows), pl.ds(column, width)], sems.at[len(copies)]
            )
        )
    for copy in copies:
        copy.start()
    make_plan(sizes, counts, sorted_ref, held_ref, choice_ref)
    for copy in copies:
        copy.wait()
    out_copy = pltpu.make_async_copy(tokens_vmem, tokens_ref, sems.at[len(copies)])
    out_copy.start()
    shrunk_ref[...] = lax.dot_general(
        tokens_vmem[...], down_vmem[...], (((1,), (1,)), ((), ())), preferred_element_type=jnp.float32
    ).astype(shrunk_ref.dtype)
    out_copy.wait()


def shrink_far_kernel(me, tokens_in, shrunk_in, own_down_ref, other_down_ref, *refs):
    piece_refs = refs[:2]
    tokens_ref, shrunk_ref, far_vmem, down_vmem, sems = refs[2:]
    rows, width = far_vmem.shape
    chips = tokens_in.shape[0] // rows
    start = pl.multiple_of(ring_chip(me[0], chips, chips // 2) * rows, rows)
    copies = down_copies(me[0] % CORES, own_down_ref, other_down_ref, down_vmem, sems)
    half = width // 2
    for i, ref in enumerate(piece_refs):
        copies.append(pltpu.make_async_copy(ref, far_vmem.at[:, pl.ds(i * half, half)], sems.at[2 + i]))
    run_copies(copies)
    out_copy = pltpu.make_async_copy(far_vmem, tokens_ref.at[pl.ds(start, rows)], sems.at[4])
    out_copy.start()
    shrunk_ref[...] = shrunk_in[...]
    shrunk_ref[pl.ds(start, rows), :] = lax.dot_general(
        far_vmem[...], down_vmem[...], (((1,), (1,)), ((), ())), preferred_element_type=jnp.float32
    ).astype(shrunk_ref.dtype)
    out_copy.wait()


def shrink(me, counts, sorted_rows, pieces, own_down, other_down, sizes):
    ranks, width = own_down.shape
    rows_all = sorted_rows.shape[0]
    rows = rows_all // CORES
    values = [value for value, _, _ in pieces]
    near = values[:-2]
    block = values[0].shape[0]
    tokens_shape = pltpu.HBM((rows, width), jnp.bfloat16)
    shrunk_shape = jax.ShapeDtypeStruct((rows, CORES * ranks), jnp.bfloat16)
    held_shape = jax.ShapeDtypeStruct((rows // block, sizes[-1]), jnp.int32)

    def whole(shape):
        return pl.BlockSpec(shape, lambda i, *_: (0, 0))

    down_vmem = pltpu.VMEM((CORES * ranks, width), jnp.bfloat16)
    downs = in_hbm([own_down, other_down])
    tokens, shrunk, held, choice = pl.pallas_call(
        functools.partial(shrink_near_kernel, sizes, [place[1:] for place in pieces[:-2]], len(counts)),
        grid_spec=pltpu.PrefetchScalarGridSpec(
            num_scalar_prefetch=1 + len(counts),
            grid=(1,),
            in_specs=[whole((1, rows_all))] + [ANY_SPEC] * (2 + len(near)),
            out_specs=[
                ANY_SPEC,
                whole(shrunk_shape.shape),
                whole(held_shape.shape),
                pl.BlockSpec(memory_space=pltpu.SMEM),
            ],
            scratch_shapes=[
                pltpu.VMEM((rows, width), jnp.bfloat16),
                down_vmem,
                pltpu.SemaphoreType.DMA((3 + len(near),)),
            ],
        ),
        out_shape=[tokens_shape, shrunk_shape, held_shape, jax.ShapeDtypeStruct((1,), jnp.int32)],
        compiler_params=pltpu.CompilerParams(vmem_limit_bytes=rows * width * 2 + 16 * MIB),
        name="shrink_near",
    )(me, *counts, sorted_rows.reshape(1, rows_all), *downs, *in_hbm(near[:1]), *near[1:])
    tokens, shrunk = pl.pallas_call(
        shrink_far_kernel,
        grid_spec=pltpu.PrefetchScalarGridSpec(
            num_scalar_prefetch=1,
            grid=(1,),
            in_specs=[ANY_SPEC, whole(shrunk_shape.shape)] + [ANY_SPEC] * 4,
            out_specs=[ANY_SPEC, whole(shrunk_shape.shape)],
            scratch_shapes=[
                pltpu.VMEM((block, width), jnp.bfloat16),
                down_vmem,
                pltpu.SemaphoreType.DMA((5,)),
            ],
        ),
        out_shape=[tokens_shape, shrunk_shape],
        input_output_aliases={1: 0},
        compiler_params=pltpu.CompilerParams(vmem_limit_bytes=16 * MIB),
        name="shrink_far",
    )(me, *in_hbm([tokens]), shrunk, *downs, *values[-2:])
    return tokens, shrunk, held, choice


def expand_kernel(block, counts, me, held_ref, own_ref, other_ref, keep_ref, got_ref, out_ref, maps_vmem, out_vmem, sems):
    chips, slots, units = out_vmem.shape
    most = held_ref.shape[1]
    ranks = keep_ref.shape[0]
    adapters = counts.shape[0] // chips
    chip = me[0] // CORES
    core = me[0] % CORES
    copies = []
    for c in range(chips):
        start = pl.multiple_of((c * CORES + core) * units, units)
        for ref, where in ((keep_ref, core), (got_ref, 1 - core)):
            copies.append(
                pltpu.make_async_copy(
                    ref.at[:, pl.ds(start, units)],
                    maps_vmem.at[c, pl.ds(pl.multiple_of(where * ranks, ranks), ranks)],
                    sems.at[len(copies)],
                )
            )
    for copy in copies:
        copy.start()

    wanted = held_ref[pl.ds(chip, 1), :]
    index = lax.broadcasted_iota(jnp.int32, (own_ref.shape[0], most), 0)
    row = index // block * (CORES * block) + index % block
    picked = jnp.zeros((most, own_ref.shape[1]), jnp.float32)
    for ref, where in ((own_ref, core), (other_ref, 1 - core)):
        hit = (row + where * block == wanted).astype(jnp.float32).astype(jnp.bfloat16)
        picked += lax.dot_general(hit, ref[...], (((0,), (0,)), ((), ())), preferred_element_type=jnp.float32)
    slot = lax.broadcasted_iota(jnp.int32, picked.shape, 0)
    adapter = lax.broadcasted_iota(jnp.int32, picked.shape, 1) // (picked.shape[1] // adapters)
    mine = jnp.zeros(picked.shape, jnp.int32)
    first = jnp.int32(0)
    for a in range(adapters):
        end = first + counts[chip * adapters + a]
        mine += ((adapter == a) & (slot >= first) & (slot < end)).astype(jnp.int32)
        first = end
    shrunk = jnp.where(mine > 0, picked, 0.0).astype(jnp.bfloat16)[:slots]

    out_copies = []
    for c in range(chips):
        copies[2 * c].wait()
        copies[2 * c + 1].wait()
        product = jnp.dot(shrunk, maps_vmem[c], preferred_element_type=jnp.float32)
        out_vmem[c] = (ADAPTER_SCALE * product).astype(out_vmem.dtype)
        out_copies.append(pltpu.make_async_copy(out_vmem.at[c], out_ref.at[c], sems.at[2 * chips + c]))
        out_copies[-1].start()
    for copy in out_copies:
        copy.wait()


def expand(counts, me, held, own_shrunk, other_shrunk, keep, got, slots, block):
    ranks, columns = keep.shape
    chips, most = held.shape
    units = columns // chips // CORES
    rows, ranks_all = own_shrunk.shape
    shrunk_spec = pl.BlockSpec((rows, ranks_all), lambda i, s, t: (0, 0))
    return pl.pallas_call(
        functools.partial(expand_kernel, block),
        grid_spec=pltpu.PrefetchScalarGridSpec(
            num_scalar_prefetch=2,
            grid=(1,),
            in_specs=[
                pl.BlockSpec((chips, most), lambda i, s, t: (0, 0)),
                shrunk_spec,
                shrunk_spec,
                ANY_SPEC,
                ANY_SPEC,
            ],
            out_specs=ANY_SPEC,
            scratch_shapes=[
                pltpu.VMEM((chips, ranks_all, units), jnp.bfloat16),
                pltpu.VMEM((chips, slots, units), jnp.bfloat16),
                pltpu.SemaphoreType.DMA((3 * chips,)),
            ],
        ),
        out_shape=pltpu.HBM((chips, slots, units), jnp.bfloat16),
        compiler_params=pltpu.CompilerParams(vmem_limit_bytes=16 * MIB),
        cost_estimate=pl.CostEstimate(
            flops=2 * slots * ranks_all * chips * units,
            bytes_accessed=2 * (slots + ranks_all) * chips * units,
            transcendentals=0,
        ),
        name="expand",
    )(counts, me, held, own_shrunk, other_shrunk, *in_hbm([keep, got]))


def project_kernel(block, me, gate_weight_ref, up_weight_ref, own_ref, other_ref, gate_ref, up_ref, tokens_vmem, sems):
    depth = gate_weight_ref.shape[0]
    core = me[0] % CORES
    k = pl.program_id(0)

    @pl.when(k == 0)
    def _():
        copies = []
        for ref, where in ((own_ref, core), (other_ref, 1 - core)):
            for chip in range(ref.shape[0] // block):
                start = pl.multiple_of((chip * CORES + where) * block, block)
                copies.append(
                    pltpu.make_async_copy(
                        ref.at[pl.ds(chip * block, block)], tokens_vmem.at[pl.ds(start, block)], sems.at[len(copies)]
                    )
                )
        run_copies(copies)
        gate_ref[...] = jnp.zeros_like(gate_ref)
        up_ref[...] = jnp.zeros_like(up_ref)

    tokens = tokens_vmem[:, pl.ds(pl.multiple_of(k * depth, depth), depth)]
    gate_ref[...] += jnp.dot(tokens, gate_weight_ref[...], preferred_element_type=jnp.float32)
    up_ref[...] += jnp.dot(tokens, up_weight_ref[...], preferred_element_type=jnp.float32)

    @pl.when(k == pl.num_programs(0) - 1)
    def _():
        gate = gate_ref[...]
        gate_ref[...] = gate / (1.0 + jnp.exp(-gate))


def project(me, own, other, gate_weight, up_weight, block):
    width, units = gate_weight.shape
    rows = CORES * own.shape[0]
    depth = min(1024, width)
    weight_spec = pl.BlockSpec((depth, units), lambda k, s: (k, 0))
    out_spec = pl.BlockSpec((rows, units), lambda k, s: (0, 0))
    out = pltpu.HBM((rows, units), jnp.float32)
    return pl.pallas_call(
        functools.partial(project_kernel, block),
        grid_spec=pltpu.PrefetchScalarGridSpec(
            num_scalar_prefetch=1,
            grid=(width // depth,),
            in_specs=[weight_spec, weight_spec, ANY_SPEC, ANY_SPEC],
            out_specs=[out_spec, out_spec],
            scratch_shapes=[
                pltpu.VMEM((rows, width), jnp.bfloat16),
                pltpu.SemaphoreType.DMA((rows // block,)),
            ],
        ),
        out_shape=[out, out],
        compiler_params=pltpu.CompilerParams(vmem_limit_bytes=rows * width * 2 + 20 * MIB),
        cost_estimate=pl.CostEstimate(
            flops=4 * rows * width * units,
            bytes_accessed=2 * (rows + 2 * units) * width,
            transcendentals=rows * units,
        ),
        name="project",
    )(me, *in_hbm([gate_weight, up_weight, own, other]))


def combine_kernel(pick_ref, gate_ref, up_ref, products_ref, out_ref):
    delta = jnp.dot(pick_ref[...], products_ref[...], preferred_element_type=jnp.float32)
    out_ref[...] = (gate_ref[...] * (up_ref[...] + delta)).astype(out_ref.dtype)


def combine(pick, gate, up, products):
    rows, units = gate.shape
    slots_all = products.shape[0]
    tile = min(512, units)
    column_spec = pl.BlockSpec((rows, tile), lambda n: (0, n))
    return pl.pallas_call(
        combine_kernel,
        grid=(units // tile,),
        in_specs=[
            pl.BlockSpec((rows, slots_all), lambda n: (0, 0)),
            column_spec,
            column_spec,
            pl.BlockSpec((slots_all, tile), lambda n: (0, n)),
        ],
        out_specs=column_spec,
        out_shape=pltpu.HBM((rows, units), jnp.bfloat16),
        compiler_params=pltpu.CompilerParams(vmem_limit_bytes=rows * slots_all * 4 + 20 * MIB),
        cost_estimate=pl.CostEstimate(
            flops=2 * rows * slots_all * units, bytes_accessed=10 * rows * units, transcendentals=0
        ),
        name="combine",
    )(*in_hbm([pick, gate, up]), products)


def per_device(
    tokens,
    gate_weight,
    up_weight,
    adapter_down_weight,
    adapter_up_weight,
    row_adapter,
    sorted_rows,
    segment_count,
):
    axis = "tensor"
    size = lax.axis_size(axis)
    me = lax.axis_index(axis).astype(jnp.int32)
    chips = size // CORES
    resident, rank, width = adapter_down_weight.shape
    ranks = resident * rank
    rows = row_adapter.shape[0]
    block = tokens.shape[0]
    me_array = me.reshape(1)
    flips = [(d, d ^ 1) for d in range(size)]

    def other_core(value):
        return lax.ppermute(value, axis, flips)

    most = CORES * resident * ROWS_PER_LIMIT
    sizes = [slots for slots in SLOT_SIZES if slots < most] + [most]
    groups = lax.axis_size("groups")
    own_down = adapter_down_weight.reshape(ranks, width)
    own_maps = adapter_up_weight.reshape(ranks, -1)
    other_down = other_core(own_down)
    counts = [segment_count] + [
        lax.ppermute(segment_count, "groups", [(g, (g + shift) % groups) for g in range(groups)])
        for shift in range(1, groups)
    ]
    other_maps = other_core(own_maps)

    def beside(step, values):
        nonlocal other_down, counts, other_maps
        if step == 1:
            other_down, counts, values[1] = lax.optimization_barrier((other_down, counts, values[1]))
        return values

    pieces = ring_gather(tokens, axis, beside)
    own_tokens, own_shrunk, held, choice = shrink(
        me_array, counts, sorted_rows, pieces, own_down, other_down, sizes
    )
    other_shrunk = other_core(own_shrunk)

    same_core = [[c * CORES + k for c in range(chips)] for k in range(CORES)]

    def finish(slots):
        def branch(own_tokens, own_shrunk, other_shrunk, own_maps, other_maps, held, gate_weight, up_weight):
            products = expand(
                segment_count, me_array, held, own_shrunk, other_shrunk, own_maps, other_maps, slots, block
            )
            products = lax.all_to_all(
                products, axis, split_axis=0, concat_axis=0, axis_index_groups=same_core, tiled=True
            )
            held, other_tokens = lax.optimization_barrier((held, other_core(own_tokens)))
            held_rows = held[:, :slots].reshape(1, chips * slots)
            pick = (jnp.arange(rows, dtype=jnp.int32)[:, None] == held_rows).astype(jnp.bfloat16)
            pick, other_tokens = lax.optimization_barrier((pick, other_tokens))
            gate, up = project(me_array, own_tokens, other_tokens, gate_weight, up_weight, block)
            return combine(pick, gate, up, products.reshape(chips * slots, -1))

        return branch

    return lax.switch(
        choice[0],
        [finish(slots) for slots in sizes],
        own_tokens,
        own_shrunk,
        other_shrunk,
        own_maps,
        other_maps,
        held,
        gate_weight,
        up_weight,
    )


def solution(mesh):
    placed = (
        P(("groups", "tensor"), None),
        P(None, "tensor"),
        P(None, "tensor"),
        P(("groups", "tensor"), None, None),
        P(("groups", "tensor"), None, None),
        P("groups"),
        P("groups"),
        P("groups"),
    )
    return jax.shard_map(
        per_device, mesh=mesh, in_specs=placed, out_specs=P("groups", "tensor"), check_vma=False
    )
```

```python
import functools

import jax
import jax.numpy as jnp
from jax import lax
from jax.experimental import pallas as pl
from jax.experimental.pallas import tpu as pltpu
from jax.sharding import PartitionSpec as P

ADAPTER_SCALE = 0.5
ROWS_PER_LIMIT = 64
SLOT_SIZES = (80, 96)
CORES = 2
MIB = 1024 * 1024


def chip_ring(chips):
    return list(range(0, chips, 2)) + list(range(chips - 1, 0, -2))


def ring_chip(me, chips, distance):
    chip = me // CORES
    place = jnp.where(chip % 2 == 0, chip // 2, chips // 2 + (chips - 1 - chip) // 2)
    place = (place + distance + chips) % chips
    return jnp.where(place < chips // 2, 2 * place, chips - 1 - 2 * (place - chips // 2))


def ring_gather(block, axis, beside):
    size = lax.axis_size(axis)
    chips = size // CORES
    ring = chip_ring(chips)

    def moved(value, shift):
        pairs = [
            (ring[p] * CORES + k, ring[(p + shift) % chips] * CORES + k)
            for p in range(chips)
            for k in range(CORES)
        ]
        return lax.ppermute(value, axis, pairs)

    half = block.shape[1] // 2
    far = chips // 2
    halves = block[:, :half], block[:, half:]
    columns = (0, half), (half, 0)
    held = [halves, halves[::-1]]
    pieces = [(block, 0, 0)]
    for step in range(1, far + 1):
        for chain in range(1 if step == far else 2):
            right, left = held[chain]
            held[chain] = moved(right, 1), moved(left, -1)
            for value, column, distance in zip(held[chain], columns[chain], (-step, step)):
                pieces.append((value, column, distance))
        held = beside(step, held)
    return pieces


ANY_SPEC = pl.BlockSpec(memory_space=pl.ANY)


def in_hbm(values):
    return [pltpu.with_memory_space_constraint(value, pltpu.HBM) for value in values]


def run_copies(copies):
    for copy in copies:
        copy.start()
    for copy in copies:
        copy.wait()


def make_plan(sizes, counts, sorted_ref, held_ref, choice_ref):
    chips, most = held_ref.shape
    rows = sorted_ref.shape[1]
    adapters = counts[0].shape[0] // chips

    def total(group, chip):
        return functools.reduce(jnp.add, [counts[group][chip * adapters + a] for a in range(adapters)])

    listed = jnp.broadcast_to(sorted_ref[...], (8, rows))
    slot = lax.broadcasted_iota(jnp.int32, (8, most), 1)
    start = jnp.int32(0)
    for chip in range(chips):
        turned = pltpu.roll(listed, (rows - start) % rows, 1)
        held_ref[chip : chip + 1, :] = jnp.where(slot < total(0, chip), turned[:, :most], -1)[0:1]
        start += total(0, chip)
    largest = functools.reduce(
        jnp.maximum, [total(group, chip) for group in range(len(counts)) for chip in range(chips)]
    )
    choice_ref[0] = functools.reduce(jnp.add, [(largest > size).astype(jnp.int32) for size in sizes[:-1]])


def down_copies(core, own_down_ref, other_down_ref, down_vmem, sems):
    ranks = own_down_ref.shape[0]
    return [
        pltpu.make_async_copy(ref, down_vmem.at[pl.ds(pl.multiple_of(where * ranks, ranks), ranks)], sems.at[i])
        for i, (ref, where) in enumerate(((own_down_ref, core), (other_down_ref, 1 - core)))
    ]


def shrink_near_kernel(sizes, places, groups, me, *refs):
    counts, refs = refs[:groups], refs[groups:]
    sorted_ref, own_down_ref, other_down_ref = refs[:3]
    refs = refs[3:]
    piece_refs = refs[: len(places)]
    tokens_ref, shrunk_ref, held_ref, choice_ref, tokens_vmem, down_vmem, sems = refs[len(places) :]
    chips = held_ref.shape[0]
    copies = down_copies(me[0] % CORES, own_down_ref, other_down_ref, down_vmem, sems)
    for ref, (column, distance) in zip(piece_refs, places):
        rows, width = ref.shape
        start = pl.multiple_of(ring_chip(me[0], chips, distance) * rows, rows)
        copies.append(
            pltpu.make_async_copy(
                ref, tokens_vmem.at[pl.ds(start, rows), pl.ds(column, width)], sems.at[len(copies)]
            )
        )
    for copy in copies:
        copy.start()
    make_plan(sizes, counts, sorted_ref, held_ref, choice_ref)
    for copy in copies:
        copy.wait()
    out_copy = pltpu.make_async_copy(tokens_vmem, tokens_ref, sems.at[len(copies)])
    out_copy.start()
    shrunk_ref[...] = lax.dot_general(
        tokens_vmem[...], down_vmem[...], (((1,), (1,)), ((), ())), preferred_element_type=jnp.float32
    ).astype(shrunk_ref.dtype)
    out_copy.wait()


def shrink_far_kernel(places, me, tokens_in, shrunk_in, own_down_ref, other_down_ref, *refs):
    piece_refs = refs[: len(places)]
    tokens_ref, shrunk_ref, far_vmem, down_vmem, sems = refs[len(places) :]
    rows, half = piece_refs[0].shape
    chips = tokens_in.shape[0] // rows
    slots = {distance % chips: i for i, distance in enumerate(range(chips // 2 - 1, chips // 2 + 2))}
    copies = down_copies(me[0] % CORES, own_down_ref, other_down_ref, down_vmem, sems)
    for ref, (column, distance) in zip(piece_refs, places):
        slot = slots[distance % chips]
        copies.append(
            pltpu.make_async_copy(
                ref, far_vmem.at[pl.ds(slot * rows, rows), pl.ds(column, half)], sems.at[len(copies)]
            )
        )
    run_copies(copies)
    starts = [pl.multiple_of(ring_chip(me[0], chips, distance) * rows, rows) for distance in slots]
    out_copies = [
        pltpu.make_async_copy(
            far_vmem.at[pl.ds(i * rows, rows)], tokens_ref.at[pl.ds(start, rows)], sems.at[len(copies) + i]
        )
        for i, start in enumerate(starts)
    ]
    for copy in out_copies:
        copy.start()
    shrunk = lax.dot_general(
        far_vmem[...], down_vmem[...], (((1,), (1,)), ((), ())), preferred_element_type=jnp.float32
    ).astype(shrunk_ref.dtype)
    shrunk_ref[...] = shrunk_in[...]
    for i, start in enumerate(starts):
        shrunk_ref[pl.ds(start, rows), :] = shrunk[i * rows : (i + 1) * rows]
    for copy in out_copies:
        copy.wait()


def shrink(me, counts, sorted_rows, pieces, own_down, other_down, sizes):
    ranks, width = own_down.shape
    rows_all = sorted_rows.shape[0]
    rows = rows_all // CORES
    values = [value for value, _, _ in pieces]
    near = values[:-6]
    block = values[0].shape[0]
    tokens_shape = pltpu.HBM((rows, width), jnp.bfloat16)
    shrunk_shape = jax.ShapeDtypeStruct((rows, CORES * ranks), jnp.bfloat16)
    held_shape = jax.ShapeDtypeStruct((rows // block, sizes[-1]), jnp.int32)

    def whole(shape):
        return pl.BlockSpec(shape, lambda i, *_: (0, 0))

    down_vmem = pltpu.VMEM((CORES * ranks, width), jnp.bfloat16)
    downs = in_hbm([own_down, other_down])
    tokens, shrunk, held, choice = pl.pallas_call(
        functools.partial(shrink_near_kernel, sizes, [place[1:] for place in pieces[:-6]], len(counts)),
        grid_spec=pltpu.PrefetchScalarGridSpec(
            num_scalar_prefetch=1 + len(counts),
            grid=(1,),
            in_specs=[whole((1, rows_all))] + [ANY_SPEC] * (2 + len(near)),
            out_specs=[
                ANY_SPEC,
                whole(shrunk_shape.shape),
                whole(held_shape.shape),
                pl.BlockSpec(memory_space=pltpu.SMEM),
            ],
            scratch_shapes=[
                pltpu.VMEM((rows, width), jnp.bfloat16),
                down_vmem,
                pltpu.SemaphoreType.DMA((3 + len(near),)),
            ],
        ),
        out_shape=[tokens_shape, shrunk_shape, held_shape, jax.ShapeDtypeStruct((1,), jnp.int32)],
        compiler_params=pltpu.CompilerParams(vmem_limit_bytes=rows * width * 2 + 16 * MIB),
        name="shrink_near",
    )(me, *counts, *in_hbm([sorted_rows.reshape(1, rows_all)]), *downs, *in_hbm(near[:1]), *near[1:])
    tokens, shrunk = pl.pallas_call(
        functools.partial(shrink_far_kernel, [place[1:] for place in pieces[-6:]]),
        grid_spec=pltpu.PrefetchScalarGridSpec(
            num_scalar_prefetch=1,
            grid=(1,),
            in_specs=[ANY_SPEC, whole(shrunk_shape.shape)] + [ANY_SPEC] * 8,
            out_specs=[ANY_SPEC, whole(shrunk_shape.shape)],
            scratch_shapes=[
                pltpu.VMEM((3 * block, width), jnp.bfloat16),
                down_vmem,
                pltpu.SemaphoreType.DMA((11,)),
            ],
        ),
        out_shape=[tokens_shape, shrunk_shape],
        input_output_aliases={1: 0},
        compiler_params=pltpu.CompilerParams(vmem_limit_bytes=16 * MIB),
        name="shrink_far",
    )(me, *in_hbm([tokens]), shrunk, *downs, *values[-6:])
    return tokens, shrunk, held, choice


def expand_kernel(block, counts, me, held_ref, own_ref, other_ref, keep_ref, got_ref, out_ref, maps_vmem, out_vmem, sems):
    chips, slots, units = out_vmem.shape
    most = held_ref.shape[1]
    ranks = keep_ref.shape[0]
    adapters = counts.shape[0] // chips
    chip = me[0] // CORES
    core = me[0] % CORES
    copies = []
    for c in range(chips):
        start = pl.multiple_of((c * CORES + core) * units, units)
        for ref, where in ((keep_ref, core), (got_ref, 1 - core)):
            copies.append(
                pltpu.make_async_copy(
                    ref.at[:, pl.ds(start, units)],
                    maps_vmem.at[c, pl.ds(pl.multiple_of(where * ranks, ranks), ranks)],
                    sems.at[len(copies)],
                )
            )
    for copy in copies:
        copy.start()

    wanted = held_ref[pl.ds(chip, 1), :]
    index = lax.broadcasted_iota(jnp.int32, (own_ref.shape[0], most), 0)
    row = index // block * (CORES * block) + index % block
    picked = jnp.zeros((most, own_ref.shape[1]), jnp.float32)
    for ref, where in ((own_ref, core), (other_ref, 1 - core)):
        hit = (row + where * block == wanted).astype(jnp.float32).astype(jnp.bfloat16)
        picked += lax.dot_general(hit, ref[...], (((0,), (0,)), ((), ())), preferred_element_type=jnp.float32)
    slot = lax.broadcasted_iota(jnp.int32, picked.shape, 0)
    adapter = lax.broadcasted_iota(jnp.int32, picked.shape, 1) // (picked.shape[1] // adapters)
    mine = jnp.zeros(picked.shape, jnp.int32)
    first = jnp.int32(0)
    for a in range(adapters):
        end = first + counts[chip * adapters + a]
        mine += ((adapter == a) & (slot >= first) & (slot < end)).astype(jnp.int32)
        first = end
    shrunk = jnp.where(mine > 0, picked, 0.0).astype(jnp.bfloat16)[:slots]

    out_copies = []
    for c in range(chips):
        copies[2 * c].wait()
        copies[2 * c + 1].wait()
        product = jnp.dot(shrunk, maps_vmem[c], preferred_element_type=jnp.float32)
        out_vmem[c] = (ADAPTER_SCALE * product).astype(out_vmem.dtype)
        out_copies.append(pltpu.make_async_copy(out_vmem.at[c], out_ref.at[c], sems.at[2 * chips + c]))
        out_copies[-1].start()
    for copy in out_copies:
        copy.wait()


def expand(counts, me, held, own_shrunk, other_shrunk, keep, got, slots, block):
    ranks, columns = keep.shape
    chips, most = held.shape
    units = columns // chips // CORES
    rows, ranks_all = own_shrunk.shape
    shrunk_spec = pl.BlockSpec((rows, ranks_all), lambda i, s, t: (0, 0))
    return pl.pallas_call(
        functools.partial(expand_kernel, block),
        grid_spec=pltpu.PrefetchScalarGridSpec(
            num_scalar_prefetch=2,
            grid=(1,),
            in_specs=[
                pl.BlockSpec((chips, most), lambda i, s, t: (0, 0)),
                shrunk_spec,
                shrunk_spec,
                ANY_SPEC,
                ANY_SPEC,
            ],
            out_specs=ANY_SPEC,
            scratch_shapes=[
                pltpu.VMEM((chips, ranks_all, units), jnp.bfloat16),
                pltpu.VMEM((chips, slots, units), jnp.bfloat16),
                pltpu.SemaphoreType.DMA((3 * chips,)),
            ],
        ),
        out_shape=pltpu.HBM((chips, slots, units), jnp.bfloat16),
        compiler_params=pltpu.CompilerParams(vmem_limit_bytes=16 * MIB),
        cost_estimate=pl.CostEstimate(
            flops=2 * slots * ranks_all * chips * units,
            bytes_accessed=2 * (slots + ranks_all) * chips * units,
            transcendentals=0,
        ),
        name="expand",
    )(counts, me, held, own_shrunk, other_shrunk, *in_hbm([keep, got]))


def project_kernel(block, me, gate_weight_ref, up_weight_ref, own_ref, other_ref, gate_ref, up_ref, tokens_vmem, sems):
    depth = gate_weight_ref.shape[0]
    core = me[0] % CORES
    k = pl.program_id(0)

    @pl.when(k == 0)
    def _():
        copies = []
        for ref, where in ((own_ref, core), (other_ref, 1 - core)):
            for chip in range(ref.shape[0] // block):
                start = pl.multiple_of((chip * CORES + where) * block, block)
                copies.append(
                    pltpu.make_async_copy(
                        ref.at[pl.ds(chip * block, block)], tokens_vmem.at[pl.ds(start, block)], sems.at[len(copies)]
                    )
                )
        run_copies(copies)
        gate_ref[...] = jnp.zeros_like(gate_ref)
        up_ref[...] = jnp.zeros_like(up_ref)

    tokens = tokens_vmem[:, pl.ds(pl.multiple_of(k * depth, depth), depth)]
    gate_ref[...] += jnp.dot(tokens, gate_weight_ref[...], preferred_element_type=jnp.float32)
    up_ref[...] += jnp.dot(tokens, up_weight_ref[...], preferred_element_type=jnp.float32)

    @pl.when(k == pl.num_programs(0) - 1)
    def _():
        gate = gate_ref[...]
        gate_ref[...] = gate / (1.0 + jnp.exp(-gate))


def project(me, own, other, gate_weight, up_weight, block):
    width, units = gate_weight.shape
    rows = CORES * own.shape[0]
    depth = min(1024, width)
    weight_spec = pl.BlockSpec((depth, units), lambda k, s: (k, 0))
    out_spec = pl.BlockSpec((rows, units), lambda k, s: (0, 0))
    out = pltpu.HBM((rows, units), jnp.float32)
    return pl.pallas_call(
        functools.partial(project_kernel, block),
        grid_spec=pltpu.PrefetchScalarGridSpec(
            num_scalar_prefetch=1,
            grid=(width // depth,),
            in_specs=[weight_spec, weight_spec, ANY_SPEC, ANY_SPEC],
            out_specs=[out_spec, out_spec],
            scratch_shapes=[
                pltpu.VMEM((rows, width), jnp.bfloat16),
                pltpu.SemaphoreType.DMA((rows // block,)),
            ],
        ),
        out_shape=[out, out],
        compiler_params=pltpu.CompilerParams(vmem_limit_bytes=rows * width * 2 + 20 * MIB),
        cost_estimate=pl.CostEstimate(
            flops=4 * rows * width * units,
            bytes_accessed=2 * (rows + 2 * units) * width,
            transcendentals=rows * units,
        ),
        name="project",
    )(me, *in_hbm([gate_weight, up_weight, own, other]))


def combine_kernel(pick_ref, gate_ref, up_ref, products_ref, out_ref):
    delta = jnp.dot(pick_ref[...], products_ref[...], preferred_element_type=jnp.float32)
    out_ref[...] = (gate_ref[...] * (up_ref[...] + delta)).astype(out_ref.dtype)


def combine(pick, gate, up, products):
    rows, units = gate.shape
    slots_all = products.shape[0]
    tile = min(512, units)
    column_spec = pl.BlockSpec((rows, tile), lambda n: (0, n))
    return pl.pallas_call(
        combine_kernel,
        grid=(units // tile,),
        in_specs=[
            pl.BlockSpec((rows, slots_all), lambda n: (0, 0)),
            column_spec,
            column_spec,
            pl.BlockSpec((slots_all, tile), lambda n: (0, n)),
        ],
        out_specs=column_spec,
        out_shape=pltpu.HBM((rows, units), jnp.bfloat16),
        compiler_params=pltpu.CompilerParams(vmem_limit_bytes=rows * slots_all * 4 + 20 * MIB),
        cost_estimate=pl.CostEstimate(
            flops=2 * rows * slots_all * units, bytes_accessed=10 * rows * units, transcendentals=0
        ),
        name="combine",
    )(*in_hbm([pick, gate, up]), products)


def per_device(
    tokens,
    gate_weight,
    up_weight,
    adapter_down_weight,
    adapter_up_weight,
    row_adapter,
    sorted_rows,
    segment_count,
):
    axis = "tensor"
    size = lax.axis_size(axis)
    me = lax.axis_index(axis).astype(jnp.int32)
    chips = size // CORES
    resident, rank, width = adapter_down_weight.shape
    ranks = resident * rank
    rows = row_adapter.shape[0]
    block = tokens.shape[0]
    me_array = me.reshape(1)
    flips = [(d, d ^ 1) for d in range(size)]

    def other_core(value):
        return lax.ppermute(value, axis, flips)

    most = CORES * resident * ROWS_PER_LIMIT
    sizes = [slots for slots in SLOT_SIZES if slots < most] + [most]
    groups = lax.axis_size("groups")
    own_down = adapter_down_weight.reshape(ranks, width)
    own_maps = adapter_up_weight.reshape(ranks, -1)
    other_down = other_core(own_down)
    counts = [segment_count] + [
        lax.ppermute(segment_count, "groups", [(g, (g + shift) % groups) for g in range(groups)])
        for shift in range(1, groups)
    ]
    other_maps = other_core(own_maps)

    def beside(step, values):
        nonlocal other_down, counts, other_maps
        if step == 1:
            other_down, counts, values[1] = lax.optimization_barrier((other_down, counts, values[1]))
        return values

    pieces = ring_gather(tokens, axis, beside)
    own_tokens, own_shrunk, held, choice = shrink(
        me_array, counts, sorted_rows, pieces, own_down, other_down, sizes
    )
    other_shrunk = other_core(own_shrunk)

    same_core = [[c * CORES + k for c in range(chips)] for k in range(CORES)]

    def finish(slots):
        def branch(own_tokens, own_shrunk, other_shrunk, own_maps, other_maps, held, gate_weight, up_weight):
            products = expand(
                segment_count, me_array, held, own_shrunk, other_shrunk, own_maps, other_maps, slots, block
            )
            products = lax.all_to_all(
                products, axis, split_axis=0, concat_axis=0, axis_index_groups=same_core, tiled=True
            )
            held, other_tokens = lax.optimization_barrier((held, other_core(own_tokens)))
            held_rows = held[:, :slots].reshape(1, chips * slots)
            pick = (jnp.arange(rows, dtype=jnp.int32)[:, None] == held_rows).astype(jnp.bfloat16)
            pick, other_tokens = lax.optimization_barrier((pick, other_tokens))
            gate, up = project(me_array, own_tokens, other_tokens, gate_weight, up_weight, block)
            return combine(pick, gate, up, products.reshape(chips * slots, -1))

        return branch

    return lax.switch(
        choice[0],
        [finish(slots) for slots in sizes],
        own_tokens,
        own_shrunk,
        other_shrunk,
        own_maps,
        other_maps,
        held,
        gate_weight,
        up_weight,
    )


def solution(mesh):
    placed = (
        P(("groups", "tensor"), None),
        P(None, "tensor"),
        P(None, "tensor"),
        P(("groups", "tensor"), None, None),
        P(("groups", "tensor"), None, None),
        P("groups"),
        P("groups"),
        P("groups"),
    )
    return jax.shard_map(
        per_device, mesh=mesh, in_specs=placed, out_specs=P("groups", "tensor"), check_vma=False
    )
```

```python
import functools

import jax
import jax.numpy as jnp
from jax import lax
from jax.experimental import pallas as pl
from jax.experimental.pallas import tpu as pltpu
from jax.sharding import PartitionSpec as P

ADAPTER_SCALE = 0.5
ROWS_PER_LIMIT = 64
SLOT_SIZES = (80, 96)
CORES = 2
MIB = 1024 * 1024


def chip_ring(chips):
    return list(range(0, chips, 2)) + list(range(chips - 1, 0, -2))


def ring_chip(me, chips, distance):
    chip = me // CORES
    place = jnp.where(chip % 2 == 0, chip // 2, chips // 2 + (chips - 1 - chip) // 2)
    place = (place + distance + chips) % chips
    return jnp.where(place < chips // 2, 2 * place, chips - 1 - 2 * (place - chips // 2))


def ring_gather(block, axis, beside):
    size = lax.axis_size(axis)
    chips = size // CORES
    ring = chip_ring(chips)

    def moved(value, shift):
        pairs = [
            (ring[p] * CORES + k, ring[(p + shift) % chips] * CORES + k)
            for p in range(chips)
            for k in range(CORES)
        ]
        return lax.ppermute(value, axis, pairs)

    right, left = moved(block, 1), moved(block, -1)
    pieces = [(block, 0, 0), (right, 0, -1), (left, 0, 1)]
    half = block.shape[1] // 2
    far = chips // 2
    columns = (0, half), (half, 0)
    held = [(right[:, a : a + half], left[:, b : b + half]) for a, b in columns]
    held = beside(1, held)
    for step in range(2, far + 1):
        for chain in range(1 if step == far else 2):
            right, left = held[chain]
            held[chain] = moved(right, 1), moved(left, -1)
            for value, column, distance in zip(held[chain], columns[chain], (-step, step)):
                pieces.append((value, column, distance))
        held = beside(step, held)
    return pieces


ANY_SPEC = pl.BlockSpec(memory_space=pl.ANY)


def in_hbm(values):
    return [pltpu.with_memory_space_constraint(value, pltpu.HBM) for value in values]


def run_copies(copies):
    for copy in copies:
        copy.start()
    for copy in copies:
        copy.wait()


def make_plan(sizes, counts, sorted_ref, held_ref, choice_ref):
    chips, most = held_ref.shape
    rows = sorted_ref.shape[1]
    adapters = counts[0].shape[0] // chips

    def total(group, chip):
        return functools.reduce(jnp.add, [counts[group][chip * adapters + a] for a in range(adapters)])

    listed = jnp.broadcast_to(sorted_ref[...], (8, rows))
    slot = lax.broadcasted_iota(jnp.int32, (8, most), 1)
    start = jnp.int32(0)
    for chip in range(chips):
        turned = pltpu.roll(listed, (rows - start) % rows, 1)
        held_ref[chip : chip + 1, :] = jnp.where(slot < total(0, chip), turned[:, :most], -1)[0:1]
        start += total(0, chip)
    largest = functools.reduce(
        jnp.maximum, [total(group, chip) for group in range(len(counts)) for chip in range(chips)]
    )
    choice_ref[0] = functools.reduce(jnp.add, [(largest > size).astype(jnp.int32) for size in sizes[:-1]])


def down_copies(core, own_down_ref, other_down_ref, down_vmem, sems):
    ranks = own_down_ref.shape[0]
    return [
        pltpu.make_async_copy(ref, down_vmem.at[pl.ds(pl.multiple_of(where * ranks, ranks), ranks)], sems.at[i])
        for i, (ref, where) in enumerate(((own_down_ref, core), (other_down_ref, 1 - core)))
    ]


def shrink_near_kernel(sizes, places, groups, me, *refs):
    counts, refs = refs[:groups], refs[groups:]
    sorted_ref, own_down_ref, other_down_ref = refs[:3]
    refs = refs[3:]
    piece_refs = refs[: len(places)]
    tokens_ref, shrunk_ref, held_ref, choice_ref, tokens_vmem, down_vmem, sems = refs[len(places) :]
    chips = held_ref.shape[0]
    copies = down_copies(me[0] % CORES, own_down_ref, other_down_ref, down_vmem, sems)
    for ref, (column, distance) in zip(piece_refs, places):
        rows, width = ref.shape
        start = pl.multiple_of(ring_chip(me[0], chips, distance) * rows, rows)
        copies.append(
            pltpu.make_async_copy(
                ref, tokens_vmem.at[pl.ds(start, rows), pl.ds(column, width)], sems.at[len(copies)]
            )
        )
    for copy in copies:
        copy.start()
    make_plan(sizes, counts, sorted_ref, held_ref, choice_ref)
    for copy in copies:
        copy.wait()
    out_copy = pltpu.make_async_copy(tokens_vmem, tokens_ref, sems.at[len(copies)])
    out_copy.start()
    shrunk_ref[...] = lax.dot_general(
        tokens_vmem[...], down_vmem[...], (((1,), (1,)), ((), ())), preferred_element_type=jnp.float32
    ).astype(shrunk_ref.dtype)
    out_copy.wait()


def shrink_far_kernel(places, me, tokens_in, shrunk_in, own_down_ref, other_down_ref, *refs):
    piece_refs = refs[: len(places)]
    tokens_ref, shrunk_ref, far_vmem, down_vmem, sems = refs[len(places) :]
    rows, half = piece_refs[0].shape
    chips = tokens_in.shape[0] // rows
    slots = {distance % chips: i for i, distance in enumerate(range(chips // 2 - 1, chips // 2 + 2))}
    copies = down_copies(me[0] % CORES, own_down_ref, other_down_ref, down_vmem, sems)
    for ref, (column, distance) in zip(piece_refs, places):
        slot = slots[distance % chips]
        copies.append(
            pltpu.make_async_copy(
                ref, far_vmem.at[pl.ds(slot * rows, rows), pl.ds(column, half)], sems.at[len(copies)]
            )
        )
    run_copies(copies)
    starts = [pl.multiple_of(ring_chip(me[0], chips, distance) * rows, rows) for distance in slots]
    out_copies = [
        pltpu.make_async_copy(
            far_vmem.at[pl.ds(i * rows, rows)], tokens_ref.at[pl.ds(start, rows)], sems.at[len(copies) + i]
        )
        for i, start in enumerate(starts)
    ]
    for copy in out_copies:
        copy.start()
    shrunk = lax.dot_general(
        far_vmem[...], down_vmem[...], (((1,), (1,)), ((), ())), preferred_element_type=jnp.float32
    ).astype(shrunk_ref.dtype)
    shrunk_ref[...] = shrunk_in[...]
    for i, start in enumerate(starts):
        shrunk_ref[pl.ds(start, rows), :] = shrunk[i * rows : (i + 1) * rows]
    for copy in out_copies:
        copy.wait()


def shrink(me, counts, sorted_rows, pieces, own_down, other_down, sizes):
    ranks, width = own_down.shape
    rows_all = sorted_rows.shape[0]
    rows = rows_all // CORES
    values = [value for value, _, _ in pieces]
    near = values[:-6]
    block = values[0].shape[0]
    tokens_shape = pltpu.HBM((rows, width), jnp.bfloat16)
    shrunk_shape = jax.ShapeDtypeStruct((rows, CORES * ranks), jnp.bfloat16)
    held_shape = jax.ShapeDtypeStruct((rows // block, sizes[-1]), jnp.int32)

    def whole(shape):
        return pl.BlockSpec(shape, lambda i, *_: (0, 0))

    down_vmem = pltpu.VMEM((CORES * ranks, width), jnp.bfloat16)
    downs = in_hbm([own_down, other_down])
    tokens, shrunk, held, choice = pl.pallas_call(
        functools.partial(shrink_near_kernel, sizes, [place[1:] for place in pieces[:-6]], len(counts)),
        grid_spec=pltpu.PrefetchScalarGridSpec(
            num_scalar_prefetch=1 + len(counts),
            grid=(1,),
            in_specs=[whole((1, rows_all))] + [ANY_SPEC] * (2 + len(near)),
            out_specs=[
                ANY_SPEC,
                whole(shrunk_shape.shape),
                whole(held_shape.shape),
                pl.BlockSpec(memory_space=pltpu.SMEM),
            ],
            scratch_shapes=[
                pltpu.VMEM((rows, width), jnp.bfloat16),
                down_vmem,
                pltpu.SemaphoreType.DMA((3 + len(near),)),
            ],
        ),
        out_shape=[tokens_shape, shrunk_shape, held_shape, jax.ShapeDtypeStruct((1,), jnp.int32)],
        compiler_params=pltpu.CompilerParams(vmem_limit_bytes=rows * width * 2 + 16 * MIB),
        name="shrink_near",
    )(me, *counts, *in_hbm([sorted_rows.reshape(1, rows_all)]), *downs, *in_hbm(near[:1]), *near[1:])
    tokens, shrunk = pl.pallas_call(
        functools.partial(shrink_far_kernel, [place[1:] for place in pieces[-6:]]),
        grid_spec=pltpu.PrefetchScalarGridSpec(
            num_scalar_prefetch=1,
            grid=(1,),
            in_specs=[ANY_SPEC, whole(shrunk_shape.shape)] + [ANY_SPEC] * 8,
            out_specs=[ANY_SPEC, whole(shrunk_shape.shape)],
            scratch_shapes=[
                pltpu.VMEM((3 * block, width), jnp.bfloat16),
                down_vmem,
                pltpu.SemaphoreType.DMA((11,)),
            ],
        ),
        out_shape=[tokens_shape, shrunk_shape],
        input_output_aliases={1: 0},
        compiler_params=pltpu.CompilerParams(vmem_limit_bytes=16 * MIB),
        name="shrink_far",
    )(me, *in_hbm([tokens]), shrunk, *downs, *values[-6:])
    return tokens, shrunk, held, choice


def expand_kernel(block, counts, me, held_ref, own_ref, other_ref, keep_ref, got_ref, out_ref, maps_vmem, out_vmem, sems):
    chips, slots, units = out_vmem.shape
    most = held_ref.shape[1]
    ranks = keep_ref.shape[0]
    adapters = counts.shape[0] // chips
    chip = me[0] // CORES
    core = me[0] % CORES
    copies = []
    for c in range(chips):
        start = pl.multiple_of((c * CORES + core) * units, units)
        for ref, where in ((keep_ref, core), (got_ref, 1 - core)):
            copies.append(
                pltpu.make_async_copy(
                    ref.at[:, pl.ds(start, units)],
                    maps_vmem.at[c, pl.ds(pl.multiple_of(where * ranks, ranks), ranks)],
                    sems.at[len(copies)],
                )
            )
    for copy in copies:
        copy.start()

    wanted = held_ref[pl.ds(chip, 1), :]
    index = lax.broadcasted_iota(jnp.int32, (own_ref.shape[0], most), 0)
    row = index // block * (CORES * block) + index % block
    picked = jnp.zeros((most, own_ref.shape[1]), jnp.float32)
    for ref, where in ((own_ref, core), (other_ref, 1 - core)):
        hit = (row + where * block == wanted).astype(jnp.float32).astype(jnp.bfloat16)
        picked += lax.dot_general(hit, ref[...], (((0,), (0,)), ((), ())), preferred_element_type=jnp.float32)
    slot = lax.broadcasted_iota(jnp.int32, picked.shape, 0)
    adapter = lax.broadcasted_iota(jnp.int32, picked.shape, 1) // (picked.shape[1] // adapters)
    mine = jnp.zeros(picked.shape, jnp.int32)
    first = jnp.int32(0)
    for a in range(adapters):
        end = first + counts[chip * adapters + a]
        mine += ((adapter == a) & (slot >= first) & (slot < end)).astype(jnp.int32)
        first = end
    shrunk = jnp.where(mine > 0, picked, 0.0).astype(jnp.bfloat16)[:slots]

    out_copies = []
    for c in range(chips):
        copies[2 * c].wait()
        copies[2 * c + 1].wait()
        product = jnp.dot(shrunk, maps_vmem[c], preferred_element_type=jnp.float32)
        out_vmem[c] = (ADAPTER_SCALE * product).astype(out_vmem.dtype)
        out_copies.append(pltpu.make_async_copy(out_vmem.at[c], out_ref.at[c], sems.at[2 * chips + c]))
        out_copies[-1].start()
    for copy in out_copies:
        copy.wait()


def expand(counts, me, held, own_shrunk, other_shrunk, keep, got, slots, block):
    ranks, columns = keep.shape
    chips, most = held.shape
    units = columns // chips // CORES
    rows, ranks_all = own_shrunk.shape
    shrunk_spec = pl.BlockSpec((rows, ranks_all), lambda i, s, t: (0, 0))
    return pl.pallas_call(
        functools.partial(expand_kernel, block),
        grid_spec=pltpu.PrefetchScalarGridSpec(
            num_scalar_prefetch=2,
            grid=(1,),
            in_specs=[
                pl.BlockSpec((chips, most), lambda i, s, t: (0, 0)),
                shrunk_spec,
                shrunk_spec,
                ANY_SPEC,
                ANY_SPEC,
            ],
            out_specs=ANY_SPEC,
            scratch_shapes=[
                pltpu.VMEM((chips, ranks_all, units), jnp.bfloat16),
                pltpu.VMEM((chips, slots, units), jnp.bfloat16),
                pltpu.SemaphoreType.DMA((3 * chips,)),
            ],
        ),
        out_shape=pltpu.HBM((chips, slots, units), jnp.bfloat16),
        compiler_params=pltpu.CompilerParams(vmem_limit_bytes=16 * MIB),
        cost_estimate=pl.CostEstimate(
            flops=2 * slots * ranks_all * chips * units,
            bytes_accessed=2 * (slots + ranks_all) * chips * units,
            transcendentals=0,
        ),
        name="expand",
    )(counts, me, held, own_shrunk, other_shrunk, *in_hbm([keep, got]))


def project_kernel(block, me, gate_weight_ref, up_weight_ref, own_ref, other_ref, gate_ref, up_ref, tokens_vmem, sems):
    depth = gate_weight_ref.shape[0]
    core = me[0] % CORES
    k = pl.program_id(0)

    @pl.when(k == 0)
    def _():
        copies = []
        for ref, where in ((own_ref, core), (other_ref, 1 - core)):
            for chip in range(ref.shape[0] // block):
                start = pl.multiple_of((chip * CORES + where) * block, block)
                copies.append(
                    pltpu.make_async_copy(
                        ref.at[pl.ds(chip * block, block)], tokens_vmem.at[pl.ds(start, block)], sems.at[len(copies)]
                    )
                )
        run_copies(copies)
        gate_ref[...] = jnp.zeros_like(gate_ref)
        up_ref[...] = jnp.zeros_like(up_ref)

    tokens = tokens_vmem[:, pl.ds(pl.multiple_of(k * depth, depth), depth)]
    gate_ref[...] += jnp.dot(tokens, gate_weight_ref[...], preferred_element_type=jnp.float32)
    up_ref[...] += jnp.dot(tokens, up_weight_ref[...], preferred_element_type=jnp.float32)

    @pl.when(k == pl.num_programs(0) - 1)
    def _():
        gate = gate_ref[...]
        gate_ref[...] = gate / (1.0 + jnp.exp(-gate))


def project(me, own, other, gate_weight, up_weight, block):
    width, units = gate_weight.shape
    rows = CORES * own.shape[0]
    depth = min(1024, width)
    weight_spec = pl.BlockSpec((depth, units), lambda k, s: (k, 0))
    out_spec = pl.BlockSpec((rows, units), lambda k, s: (0, 0))
    out = pltpu.HBM((rows, units), jnp.float32)
    return pl.pallas_call(
        functools.partial(project_kernel, block),
        grid_spec=pltpu.PrefetchScalarGridSpec(
            num_scalar_prefetch=1,
            grid=(width // depth,),
            in_specs=[weight_spec, weight_spec, ANY_SPEC, ANY_SPEC],
            out_specs=[out_spec, out_spec],
            scratch_shapes=[
                pltpu.VMEM((rows, width), jnp.bfloat16),
                pltpu.SemaphoreType.DMA((rows // block,)),
            ],
        ),
        out_shape=[out, out],
        compiler_params=pltpu.CompilerParams(vmem_limit_bytes=rows * width * 2 + 20 * MIB),
        cost_estimate=pl.CostEstimate(
            flops=4 * rows * width * units,
            bytes_accessed=2 * (rows + 2 * units) * width,
            transcendentals=rows * units,
        ),
        name="project",
    )(me, *in_hbm([gate_weight, up_weight, own, other]))


def combine_kernel(pick_ref, gate_ref, up_ref, products_ref, out_ref):
    delta = jnp.dot(pick_ref[...], products_ref[...], preferred_element_type=jnp.float32)
    out_ref[...] = (gate_ref[...] * (up_ref[...] + delta)).astype(out_ref.dtype)


def combine(pick, gate, up, products):
    rows, units = gate.shape
    slots_all = products.shape[0]
    tile = min(512, units)
    column_spec = pl.BlockSpec((rows, tile), lambda n: (0, n))
    return pl.pallas_call(
        combine_kernel,
        grid=(units // tile,),
        in_specs=[
            pl.BlockSpec((rows, slots_all), lambda n: (0, 0)),
            column_spec,
            column_spec,
            pl.BlockSpec((slots_all, tile), lambda n: (0, n)),
        ],
        out_specs=column_spec,
        out_shape=pltpu.HBM((rows, units), jnp.bfloat16),
        compiler_params=pltpu.CompilerParams(vmem_limit_bytes=rows * slots_all * 4 + 20 * MIB),
        cost_estimate=pl.CostEstimate(
            flops=2 * rows * slots_all * units, bytes_accessed=10 * rows * units, transcendentals=0
        ),
        name="combine",
    )(*in_hbm([pick, gate, up]), products)


def per_device(
    tokens,
    gate_weight,
    up_weight,
    adapter_down_weight,
    adapter_up_weight,
    row_adapter,
    sorted_rows,
    segment_count,
):
    axis = "tensor"
    size = lax.axis_size(axis)
    me = lax.axis_index(axis).astype(jnp.int32)
    chips = size // CORES
    resident, rank, width = adapter_down_weight.shape
    ranks = resident * rank
    rows = row_adapter.shape[0]
    block = tokens.shape[0]
    me_array = me.reshape(1)
    flips = [(d, d ^ 1) for d in range(size)]

    def other_core(value):
        return lax.ppermute(value, axis, flips)

    most = CORES * resident * ROWS_PER_LIMIT
    sizes = [slots for slots in SLOT_SIZES if slots < most] + [most]
    groups = lax.axis_size("groups")
    own_down = adapter_down_weight.reshape(ranks, width)
    own_maps = adapter_up_weight.reshape(ranks, -1)
    other_down = other_core(own_down)
    counts = [segment_count] + [
        lax.ppermute(segment_count, "groups", [(g, (g + shift) % groups) for g in range(groups)])
        for shift in range(1, groups)
    ]
    other_maps = other_core(own_maps)

    def beside(step, values):
        nonlocal other_down, counts, other_maps
        if step == 1:
            other_down, counts, values[0], values[1] = lax.optimization_barrier((other_down, counts, *values))
        return values

    pieces = ring_gather(tokens, axis, beside)
    own_tokens, own_shrunk, held, choice = shrink(
        me_array, counts, sorted_rows, pieces, own_down, other_down, sizes
    )
    other_shrunk = other_core(own_shrunk)

    same_core = [[c * CORES + k for c in range(chips)] for k in range(CORES)]

    def finish(slots):
        def branch(own_tokens, own_shrunk, other_shrunk, own_maps, other_maps, held, gate_weight, up_weight):
            products = expand(
                segment_count, me_array, held, own_shrunk, other_shrunk, own_maps, other_maps, slots, block
            )
            products = lax.all_to_all(
                products, axis, split_axis=0, concat_axis=0, axis_index_groups=same_core, tiled=True
            )
            held, other_tokens = lax.optimization_barrier((held, other_core(own_tokens)))
            held_rows = held[:, :slots].reshape(1, chips * slots)
            pick = (jnp.arange(rows, dtype=jnp.int32)[:, None] == held_rows).astype(jnp.bfloat16)
            pick, other_tokens = lax.optimization_barrier((pick, other_tokens))
            gate, up = project(me_array, own_tokens, other_tokens, gate_weight, up_weight, block)
            return combine(pick, gate, up, products.reshape(chips * slots, -1))

        return branch

    return lax.switch(
        choice[0],
        [finish(slots) for slots in sizes],
        own_tokens,
        own_shrunk,
        other_shrunk,
        own_maps,
        other_maps,
        held,
        gate_weight,
        up_weight,
    )


def solution(mesh):
    placed = (
        P(("groups", "tensor"), None),
        P(None, "tensor"),
        P(None, "tensor"),
        P(("groups", "tensor"), None, None),
        P(("groups", "tensor"), None, None),
        P("groups"),
        P("groups"),
        P("groups"),
    )
    return jax.shard_map(
        per_device, mesh=mesh, in_specs=placed, out_specs=P("groups", "tensor"), check_vma=False
    )
```

```python
import functools

import jax
import jax.numpy as jnp
from jax import lax
from jax.experimental import pallas as pl
from jax.experimental.pallas import tpu as pltpu
from jax.sharding import PartitionSpec as P

ADAPTER_SCALE = 0.5
ROWS_PER_LIMIT = 64
SLOT_SIZES = (80, 96)
CORES = 2
MIB = 1024 * 1024


def chip_ring(chips):
    return list(range(0, chips, 2)) + list(range(chips - 1, 0, -2))


def ring_chip(me, chips, distance):
    chip = me // CORES
    place = jnp.where(chip % 2 == 0, chip // 2, chips // 2 + (chips - 1 - chip) // 2)
    place = (place + distance + chips) % chips
    return jnp.where(place < chips // 2, 2 * place, chips - 1 - 2 * (place - chips // 2))


def ring_gather(block, axis, beside):
    size = lax.axis_size(axis)
    chips = size // CORES
    ring = chip_ring(chips)

    def moved(value, shift):
        pairs = [
            (ring[p] * CORES + k, ring[(p + shift) % chips] * CORES + k)
            for p in range(chips)
            for k in range(CORES)
        ]
        return lax.ppermute(value, axis, pairs)

    right, left = moved(block, 1), moved(block, -1)
    pieces = [(block, 0, 0), (right, 0, -1), (left, 0, 1)]
    half = block.shape[1] // 2
    far = chips // 2
    columns = (0, half), (half, 0)
    held = [(right[:, a : a + half], left[:, b : b + half]) for a, b in columns]
    held = beside(1, held)
    for step in range(2, far + 1):
        for chain in range(1 if step == far else 2):
            right, left = held[chain]
            held[chain] = moved(right, 1), moved(left, -1)
            for value, column, distance in zip(held[chain], columns[chain], (-step, step)):
                pieces.append((value, column, distance))
        held = beside(step, held)
    return pieces


ANY_SPEC = pl.BlockSpec(memory_space=pl.ANY)


def in_hbm(values):
    return [pltpu.with_memory_space_constraint(value, pltpu.HBM) for value in values]


def run_copies(copies):
    for copy in copies:
        copy.start()
    for copy in copies:
        copy.wait()


def make_plan(sizes, counts, sorted_ref, held_ref, choice_ref):
    chips, most = held_ref.shape
    rows = sorted_ref.shape[1]
    adapters = counts[0].shape[0] // chips

    def total(group, chip):
        return functools.reduce(jnp.add, [counts[group][chip * adapters + a] for a in range(adapters)])

    listed = jnp.broadcast_to(sorted_ref[...], (8, rows))
    slot = lax.broadcasted_iota(jnp.int32, (8, most), 1)
    start = jnp.int32(0)
    for chip in range(chips):
        turned = pltpu.roll(listed, (rows - start) % rows, 1)
        held_ref[chip : chip + 1, :] = jnp.where(slot < total(0, chip), turned[:, :most], -1)[0:1]
        start += total(0, chip)
    largest = functools.reduce(
        jnp.maximum, [total(group, chip) for group in range(len(counts)) for chip in range(chips)]
    )
    choice_ref[0] = functools.reduce(jnp.add, [(largest > size).astype(jnp.int32) for size in sizes[:-1]])


def down_copies(core, own_down_ref, other_down_ref, down_vmem, sems):
    ranks = own_down_ref.shape[0]
    return [
        pltpu.make_async_copy(ref, down_vmem.at[pl.ds(pl.multiple_of(where * ranks, ranks), ranks)], sems.at[i])
        for i, (ref, where) in enumerate(((own_down_ref, core), (other_down_ref, 1 - core)))
    ]


def shrink_near_kernel(sizes, places, groups, me, *refs):
    counts, refs = refs[:groups], refs[groups:]
    sorted_ref, own_down_ref, other_down_ref = refs[:3]
    refs = refs[3:]
    piece_refs = refs[: len(places)]
    tokens_ref, shrunk_ref, held_ref, choice_ref, tokens_vmem, down_vmem, sems = refs[len(places) :]
    chips = held_ref.shape[0]
    copies = down_copies(me[0] % CORES, own_down_ref, other_down_ref, down_vmem, sems)
    for ref, (column, distance) in zip(piece_refs, places):
        rows, width = ref.shape
        start = pl.multiple_of(ring_chip(me[0], chips, distance) * rows, rows)
        copies.append(
            pltpu.make_async_copy(
                ref, tokens_vmem.at[pl.ds(start, rows), pl.ds(column, width)], sems.at[len(copies)]
            )
        )
    for copy in copies:
        copy.start()
    make_plan(sizes, counts, sorted_ref, held_ref, choice_ref)
    for copy in copies:
        copy.wait()
    out_copy = pltpu.make_async_copy(tokens_vmem, tokens_ref, sems.at[len(copies)])
    out_copy.start()
    shrunk_ref[...] = lax.dot_general(
        tokens_vmem[...], down_vmem[...], (((1,), (1,)), ((), ())), preferred_element_type=jnp.float32
    ).astype(shrunk_ref.dtype)
    out_copy.wait()


def shrink_far_kernel(places, me, tokens_in, shrunk_in, own_down_ref, other_down_ref, *refs):
    piece_refs = refs[: len(places)]
    tokens_ref, shrunk_ref, far_vmem, down_vmem, sems = refs[len(places) :]
    rows, half = piece_refs[0].shape
    chips = tokens_in.shape[0] // rows
    slots = {distance % chips: i for i, distance in enumerate(range(chips // 2 - 1, chips // 2 + 2))}
    copies = down_copies(me[0] % CORES, own_down_ref, other_down_ref, down_vmem, sems)
    for ref, (column, distance) in zip(piece_refs, places):
        slot = slots[distance % chips]
        copies.append(
            pltpu.make_async_copy(
                ref, far_vmem.at[pl.ds(slot * rows, rows), pl.ds(column, half)], sems.at[len(copies)]
            )
        )
    run_copies(copies)
    starts = [pl.multiple_of(ring_chip(me[0], chips, distance) * rows, rows) for distance in slots]
    out_copies = [
        pltpu.make_async_copy(
            far_vmem.at[pl.ds(i * rows, rows)], tokens_ref.at[pl.ds(start, rows)], sems.at[len(copies) + i]
        )
        for i, start in enumerate(starts)
    ]
    for copy in out_copies:
        copy.start()
    shrunk = lax.dot_general(
        far_vmem[...], down_vmem[...], (((1,), (1,)), ((), ())), preferred_element_type=jnp.float32
    ).astype(shrunk_ref.dtype)
    shrunk_ref[...] = shrunk_in[...]
    for i, start in enumerate(starts):
        shrunk_ref[pl.ds(start, rows), :] = shrunk[i * rows : (i + 1) * rows]
    for copy in out_copies:
        copy.wait()


def shrink(me, counts, sorted_rows, pieces, own_down, other_down, sizes):
    ranks, width = own_down.shape
    rows_all = sorted_rows.shape[0]
    rows = rows_all // CORES
    values = [value for value, _, _ in pieces]
    near = values[:-6]
    block = values[0].shape[0]
    tokens_shape = pltpu.HBM((rows, width), jnp.bfloat16)
    shrunk_shape = jax.ShapeDtypeStruct((rows, CORES * ranks), jnp.bfloat16)
    held_shape = jax.ShapeDtypeStruct((rows // block, sizes[-1]), jnp.int32)

    def whole(shape):
        return pl.BlockSpec(shape, lambda i, *_: (0, 0))

    down_vmem = pltpu.VMEM((CORES * ranks, width), jnp.bfloat16)
    downs = in_hbm([own_down]) + [other_down]
    tokens, shrunk, held, choice = pl.pallas_call(
        functools.partial(shrink_near_kernel, sizes, [place[1:] for place in pieces[:-6]], len(counts)),
        grid_spec=pltpu.PrefetchScalarGridSpec(
            num_scalar_prefetch=1 + len(counts),
            grid=(1,),
            in_specs=[whole((1, rows_all))] + [ANY_SPEC] * (2 + len(near)),
            out_specs=[
                ANY_SPEC,
                whole(shrunk_shape.shape),
                whole(held_shape.shape),
                pl.BlockSpec(memory_space=pltpu.SMEM),
            ],
            scratch_shapes=[
                pltpu.VMEM((rows, width), jnp.bfloat16),
                down_vmem,
                pltpu.SemaphoreType.DMA((3 + len(near),)),
            ],
        ),
        out_shape=[tokens_shape, shrunk_shape, held_shape, jax.ShapeDtypeStruct((1,), jnp.int32)],
        compiler_params=pltpu.CompilerParams(vmem_limit_bytes=rows * width * 2 + 16 * MIB),
        name="shrink_near",
    )(me, *counts, *in_hbm([sorted_rows.reshape(1, rows_all)]), *downs, *in_hbm(near[:1]), *near[1:])
    tokens, shrunk = pl.pallas_call(
        functools.partial(shrink_far_kernel, [place[1:] for place in pieces[-6:]]),
        grid_spec=pltpu.PrefetchScalarGridSpec(
            num_scalar_prefetch=1,
            grid=(1,),
            in_specs=[ANY_SPEC, whole(shrunk_shape.shape)] + [ANY_SPEC] * 8,
            out_specs=[ANY_SPEC, whole(shrunk_shape.shape)],
            scratch_shapes=[
                pltpu.VMEM((3 * block, width), jnp.bfloat16),
                down_vmem,
                pltpu.SemaphoreType.DMA((11,)),
            ],
        ),
        out_shape=[tokens_shape, shrunk_shape],
        input_output_aliases={1: 0},
        compiler_params=pltpu.CompilerParams(vmem_limit_bytes=16 * MIB),
        name="shrink_far",
    )(me, *in_hbm([tokens]), shrunk, *downs, *values[-6:])
    return tokens, shrunk, held, choice


def expand_kernel(order, block, counts, me, held_ref, own_ref, other_ref, keep_ref, got_ref, out_ref, maps_vmem, out_vmem, sems):
    chips, slots, units = out_vmem.shape
    most = held_ref.shape[1]
    ranks = keep_ref.shape[0]
    adapters = counts.shape[0] // chips
    chip = me[0] // CORES
    core = me[0] % CORES
    copies = []
    for c in range(chips):
        start = pl.multiple_of((order[c] * CORES + core) * units, units)
        for ref, where in ((keep_ref, core), (got_ref, 1 - core)):
            copies.append(
                pltpu.make_async_copy(
                    ref.at[:, pl.ds(start, units)],
                    maps_vmem.at[c, pl.ds(pl.multiple_of(where * ranks, ranks), ranks)],
                    sems.at[len(copies)],
                )
            )
    for copy in copies:
        copy.start()

    wanted = held_ref[pl.ds(chip, 1), :]
    index = lax.broadcasted_iota(jnp.int32, (own_ref.shape[0], most), 0)
    row = index // block * (CORES * block) + index % block
    picked = jnp.zeros((most, own_ref.shape[1]), jnp.float32)
    for ref, where in ((own_ref, core), (other_ref, 1 - core)):
        hit = (row + where * block == wanted).astype(jnp.float32).astype(jnp.bfloat16)
        picked += lax.dot_general(hit, ref[...], (((0,), (0,)), ((), ())), preferred_element_type=jnp.float32)
    slot = lax.broadcasted_iota(jnp.int32, picked.shape, 0)
    adapter = lax.broadcasted_iota(jnp.int32, picked.shape, 1) // (picked.shape[1] // adapters)
    mine = jnp.zeros(picked.shape, jnp.int32)
    first = jnp.int32(0)
    for a in range(adapters):
        end = first + counts[chip * adapters + a]
        mine += ((adapter == a) & (slot >= first) & (slot < end)).astype(jnp.int32)
        first = end
    shrunk = jnp.where(mine > 0, picked, 0.0).astype(jnp.bfloat16)[:slots]

    out_copies = []
    for c in range(chips):
        copies[2 * c].wait()
        copies[2 * c + 1].wait()
        product = jnp.dot(shrunk, maps_vmem[c], preferred_element_type=jnp.float32)
        out_vmem[c] = (ADAPTER_SCALE * product).astype(out_vmem.dtype)
        out_copies.append(pltpu.make_async_copy(out_vmem.at[c], out_ref.at[c], sems.at[2 * chips + c]))
        out_copies[-1].start()
    for copy in out_copies:
        copy.wait()


def expand(counts, me, held, own_shrunk, other_shrunk, keep, got, order, slots, block):
    ranks, columns = keep.shape
    chips, most = held.shape
    units = columns // chips // CORES
    rows, ranks_all = own_shrunk.shape
    shrunk_spec = pl.BlockSpec((rows, ranks_all), lambda i, s, t: (0, 0))
    return pl.pallas_call(
        functools.partial(expand_kernel, order, block),
        grid_spec=pltpu.PrefetchScalarGridSpec(
            num_scalar_prefetch=2,
            grid=(1,),
            in_specs=[
                pl.BlockSpec((chips, most), lambda i, s, t: (0, 0)),
                shrunk_spec,
                shrunk_spec,
                ANY_SPEC,
                ANY_SPEC,
            ],
            out_specs=ANY_SPEC,
            scratch_shapes=[
                pltpu.VMEM((chips, ranks_all, units), jnp.bfloat16),
                pltpu.VMEM((chips, slots, units), jnp.bfloat16),
                pltpu.SemaphoreType.DMA((3 * chips,)),
            ],
        ),
        out_shape=pltpu.HBM((chips, slots, units), jnp.bfloat16),
        compiler_params=pltpu.CompilerParams(vmem_limit_bytes=16 * MIB),
        cost_estimate=pl.CostEstimate(
            flops=2 * slots * ranks_all * chips * units,
            bytes_accessed=2 * (slots + ranks_all) * chips * units,
            transcendentals=0,
        ),
        name="expand",
    )(counts, me, held, own_shrunk, other_shrunk, *in_hbm([keep, got]))


def project_kernel(block, me, gate_weight_ref, up_weight_ref, own_ref, other_ref, gate_ref, up_ref, tokens_vmem, sems):
    depth = gate_weight_ref.shape[0]
    core = me[0] % CORES
    k = pl.program_id(0)

    @pl.when(k == 0)
    def _():
        copies = []
        for ref, where in ((own_ref, core), (other_ref, 1 - core)):
            for chip in range(ref.shape[0] // block):
                start = pl.multiple_of((chip * CORES + where) * block, block)
                copies.append(
                    pltpu.make_async_copy(
                        ref.at[pl.ds(chip * block, block)], tokens_vmem.at[pl.ds(start, block)], sems.at[len(copies)]
                    )
                )
        run_copies(copies)
        gate_ref[...] = jnp.zeros_like(gate_ref)
        up_ref[...] = jnp.zeros_like(up_ref)

    tokens = tokens_vmem[:, pl.ds(pl.multiple_of(k * depth, depth), depth)]
    gate_ref[...] += jnp.dot(tokens, gate_weight_ref[...], preferred_element_type=jnp.float32)
    up_ref[...] += jnp.dot(tokens, up_weight_ref[...], preferred_element_type=jnp.float32)

    @pl.when(k == pl.num_programs(0) - 1)
    def _():
        gate = gate_ref[...]
        gate_ref[...] = gate / (1.0 + jnp.exp(-gate))


def project(me, own, other, gate_weight, up_weight, block):
    width, units = gate_weight.shape
    rows = CORES * own.shape[0]
    depth = min(1024, width)
    weight_spec = pl.BlockSpec((depth, units), lambda k, s: (k, 0))
    out_spec = pl.BlockSpec((rows, units), lambda k, s: (0, 0))
    out = pltpu.HBM((rows, units), jnp.float32)
    return pl.pallas_call(
        functools.partial(project_kernel, block),
        grid_spec=pltpu.PrefetchScalarGridSpec(
            num_scalar_prefetch=1,
            grid=(width // depth,),
            in_specs=[weight_spec, weight_spec, ANY_SPEC, ANY_SPEC],
            out_specs=[out_spec, out_spec],
            scratch_shapes=[
                pltpu.VMEM((rows, width), jnp.bfloat16),
                pltpu.SemaphoreType.DMA((rows // block,)),
            ],
        ),
        out_shape=[out, out],
        compiler_params=pltpu.CompilerParams(vmem_limit_bytes=rows * width * 2 + 20 * MIB),
        cost_estimate=pl.CostEstimate(
            flops=4 * rows * width * units,
            bytes_accessed=2 * (rows + 2 * units) * width,
            transcendentals=rows * units,
        ),
        name="project",
    )(me, *in_hbm([gate_weight, up_weight, own, other]))


def combine_kernel(pick_ref, gate_ref, up_ref, products_ref, out_ref):
    delta = jnp.dot(pick_ref[...], products_ref[...], preferred_element_type=jnp.float32)
    out_ref[...] = (gate_ref[...] * (up_ref[...] + delta)).astype(out_ref.dtype)


def combine(pick, gate, up, products):
    rows, units = gate.shape
    slots_all = products.shape[0]
    tile = min(512, units)
    column_spec = pl.BlockSpec((rows, tile), lambda n: (0, n))
    return pl.pallas_call(
        combine_kernel,
        grid=(units // tile,),
        in_specs=[
            pl.BlockSpec((rows, slots_all), lambda n: (0, 0)),
            column_spec,
            column_spec,
            pl.BlockSpec((slots_all, tile), lambda n: (0, n)),
        ],
        out_specs=column_spec,
        out_shape=pltpu.HBM((rows, units), jnp.bfloat16),
        compiler_params=pltpu.CompilerParams(vmem_limit_bytes=rows * slots_all * 4 + 20 * MIB),
        cost_estimate=pl.CostEstimate(
            flops=2 * rows * slots_all * units, bytes_accessed=10 * rows * units, transcendentals=0
        ),
        name="combine",
    )(*in_hbm([pick, gate, up]), products)


def per_device(
    tokens,
    gate_weight,
    up_weight,
    adapter_down_weight,
    adapter_up_weight,
    row_adapter,
    sorted_rows,
    segment_count,
):
    axis = "tensor"
    size = lax.axis_size(axis)
    me = lax.axis_index(axis).astype(jnp.int32)
    chips = size // CORES
    resident, rank, width = adapter_down_weight.shape
    ranks = resident * rank
    rows = row_adapter.shape[0]
    block = tokens.shape[0]
    me_array = me.reshape(1)
    flips = [(d, d ^ 1) for d in range(size)]

    def other_core(value):
        return lax.ppermute(value, axis, flips)

    most = CORES * resident * ROWS_PER_LIMIT
    sizes = [slots for slots in SLOT_SIZES if slots < most] + [most]
    groups = lax.axis_size("groups")
    own_down = adapter_down_weight.reshape(ranks, width)
    own_maps = adapter_up_weight.reshape(ranks, -1)
    other_down = other_core(own_down)
    counts = [segment_count] + [
        lax.ppermute(segment_count, "groups", [(g, (g + shift) % groups) for g in range(groups)])
        for shift in range(1, groups)
    ]
    other_maps = other_core(own_maps)

    def beside(step, values):
        nonlocal other_down, counts, other_maps
        if step == 1:
            other_down, counts, values[0], values[1] = lax.optimization_barrier((other_down, counts, *values))
        return values

    pieces = ring_gather(tokens, axis, beside)
    own_tokens, own_shrunk, held, choice = shrink(
        me_array, counts, sorted_rows, pieces, own_down, other_down, sizes
    )
    other_shrunk = other_core(own_shrunk)

    order = [half * (chips // 2) + c for c in range(chips // 2) for half in range(2)]
    same_core = [[c * CORES + k for c in order] for k in range(CORES)]

    def finish(slots):
        def branch(own_tokens, own_shrunk, other_shrunk, own_maps, other_maps, held, gate_weight, up_weight):
            products = expand(
                segment_count, me_array, held, own_shrunk, other_shrunk, own_maps, other_maps, order, slots, block
            )
            products = lax.all_to_all(
                products, axis, split_axis=0, concat_axis=0, axis_index_groups=same_core, tiled=True
            )
            held, other_tokens = lax.optimization_barrier((held, other_core(own_tokens)))
            held_rows = jnp.stack([held[c, :slots] for c in order]).reshape(1, chips * slots)
            pick = (jnp.arange(rows, dtype=jnp.int32)[:, None] == held_rows).astype(jnp.bfloat16)
            pick, other_tokens = lax.optimization_barrier((pick, other_tokens))
            gate, up = project(me_array, own_tokens, other_tokens, gate_weight, up_weight, block)
            return combine(pick, gate, up, products.reshape(chips * slots, -1))

        return branch

    return lax.switch(
        choice[0],
        [finish(slots) for slots in sizes],
        own_tokens,
        own_shrunk,
        other_shrunk,
        own_maps,
        other_maps,
        held,
        gate_weight,
        up_weight,
    )


def solution(mesh):
    placed = (
        P(("groups", "tensor"), None),
        P(None, "tensor"),
        P(None, "tensor"),
        P(("groups", "tensor"), None, None),
        P(("groups", "tensor"), None, None),
        P("groups"),
        P("groups"),
        P("groups"),
    )
    return jax.shard_map(
        per_device, mesh=mesh, in_specs=placed, out_specs=P("groups", "tensor"), check_vma=False
    )
```

```python
import functools

import jax
import jax.numpy as jnp
from jax import lax
from jax.experimental import pallas as pl
from jax.experimental.pallas import tpu as pltpu
from jax.sharding import PartitionSpec as P

ADAPTER_SCALE = 0.5
ROWS_PER_LIMIT = 64
SLOT_SIZES = (80, 96)
CORES = 2
MIB = 1024 * 1024


def chip_ring(chips):
    return list(range(0, chips, 2)) + list(range(chips - 1, 0, -2))


def ring_chip(me, chips, distance):
    chip = me // CORES
    place = jnp.where(chip % 2 == 0, chip // 2, chips // 2 + (chips - 1 - chip) // 2)
    place = (place + distance + chips) % chips
    return jnp.where(place < chips // 2, 2 * place, chips - 1 - 2 * (place - chips // 2))


def ring_gather(block, axis, beside):
    size = lax.axis_size(axis)
    chips = size // CORES
    ring = chip_ring(chips)

    def moved(value, shift):
        pairs = [
            (ring[p] * CORES + k, ring[(p + shift) % chips] * CORES + k)
            for p in range(chips)
            for k in range(CORES)
        ]
        return lax.ppermute(value, axis, pairs)

    right, left = moved(block, 1), moved(block, -1)
    pieces = [(block, 0, 0), (right, 0, -1), (left, 0, 1)]
    half = block.shape[1] // 2
    far = chips // 2
    columns = (0, half), (half, 0)
    held = [(right[:, a : a + half], left[:, b : b + half]) for a, b in columns]
    held = beside(1, held)
    for step in range(2, far + 1):
        for chain in range(1 if step == far else 2):
            right, left = held[chain]
            held[chain] = moved(right, 1), moved(left, -1)
            for value, column, distance in zip(held[chain], columns[chain], (-step, step)):
                pieces.append((value, column, distance))
        held = beside(step, held)
    return pieces


ANY_SPEC = pl.BlockSpec(memory_space=pl.ANY)


def in_hbm(values):
    return [pltpu.with_memory_space_constraint(value, pltpu.HBM) for value in values]


def run_copies(copies):
    for copy in copies:
        copy.start()
    for copy in copies:
        copy.wait()


def make_plan(sizes, counts, sorted_ref, held_ref, choice_ref):
    chips, most = held_ref.shape
    rows = sorted_ref.shape[1]
    adapters = counts[0].shape[0] // chips

    def total(group, chip):
        return functools.reduce(jnp.add, [counts[group][chip * adapters + a] for a in range(adapters)])

    listed = jnp.broadcast_to(sorted_ref[...], (8, rows))
    slot = lax.broadcasted_iota(jnp.int32, (8, most), 1)
    start = jnp.int32(0)
    for chip in range(chips):
        turned = pltpu.roll(listed, (rows - start) % rows, 1)
        held_ref[chip : chip + 1, :] = jnp.where(slot < total(0, chip), turned[:, :most], -1)[0:1]
        start += total(0, chip)
    largest = functools.reduce(
        jnp.maximum, [total(group, chip) for group in range(len(counts)) for chip in range(chips)]
    )
    choice_ref[0] = functools.reduce(jnp.add, [(largest > size).astype(jnp.int32) for size in sizes[:-1]])


def down_copies(core, own_down_ref, other_down_ref, down_vmem, sems):
    ranks = own_down_ref.shape[0]
    return [
        pltpu.make_async_copy(ref, down_vmem.at[pl.ds(pl.multiple_of(where * ranks, ranks), ranks)], sems.at[i])
        for i, (ref, where) in enumerate(((own_down_ref, core), (other_down_ref, 1 - core)))
    ]


def shrink_near_kernel(sizes, places, groups, me, *refs):
    counts, refs = refs[:groups], refs[groups:]
    sorted_ref, own_down_ref, other_down_ref = refs[:3]
    refs = refs[3:]
    piece_refs = refs[: len(places)]
    tokens_ref, shrunk_ref, held_ref, choice_ref, tokens_vmem, down_vmem, sems = refs[len(places) :]
    chips = held_ref.shape[0]
    copies = down_copies(me[0] % CORES, own_down_ref, other_down_ref, down_vmem, sems)
    for ref, (column, distance) in zip(piece_refs, places):
        rows, width = ref.shape
        start = pl.multiple_of(ring_chip(me[0], chips, distance) * rows, rows)
        copies.append(
            pltpu.make_async_copy(
                ref, tokens_vmem.at[pl.ds(start, rows), pl.ds(column, width)], sems.at[len(copies)]
            )
        )
    for copy in copies:
        copy.start()
    make_plan(sizes, counts, sorted_ref, held_ref, choice_ref)
    for copy in copies:
        copy.wait()
    out_copy = pltpu.make_async_copy(tokens_vmem, tokens_ref, sems.at[len(copies)])
    out_copy.start()
    shrunk_ref[...] = lax.dot_general(
        tokens_vmem[...], down_vmem[...], (((1,), (1,)), ((), ())), preferred_element_type=jnp.float32
    ).astype(shrunk_ref.dtype)
    out_copy.wait()


def shrink_far_kernel(places, me, tokens_in, shrunk_in, own_down_ref, other_down_ref, *refs):
    piece_refs = refs[: len(places)]
    tokens_ref, shrunk_ref, far_vmem, down_vmem, sems = refs[len(places) :]
    rows, half = piece_refs[0].shape
    chips = tokens_in.shape[0] // rows
    slots = {distance % chips: i for i, distance in enumerate(range(chips // 2 - 1, chips // 2 + 2))}
    copies = down_copies(me[0] % CORES, own_down_ref, other_down_ref, down_vmem, sems)
    copies.append(pltpu.make_async_copy(shrunk_in, shrunk_ref, sems.at[2]))
    for ref, (column, distance) in zip(piece_refs, places):
        slot = slots[distance % chips]
        copies.append(
            pltpu.make_async_copy(
                ref, far_vmem.at[pl.ds(slot * rows, rows), pl.ds(column, half)], sems.at[len(copies)]
            )
        )
    run_copies(copies)
    starts = [pl.multiple_of(ring_chip(me[0], chips, distance) * rows, rows) for distance in slots]
    out_copies = [
        pltpu.make_async_copy(
            far_vmem.at[pl.ds(i * rows, rows)], tokens_ref.at[pl.ds(start, rows)], sems.at[len(copies) + i]
        )
        for i, start in enumerate(starts)
    ]
    for copy in out_copies:
        copy.start()
    shrunk = lax.dot_general(
        far_vmem[...], down_vmem[...], (((1,), (1,)), ((), ())), preferred_element_type=jnp.float32
    ).astype(shrunk_ref.dtype)
    for i, start in enumerate(starts):
        shrunk_ref[pl.ds(start, rows), :] = shrunk[i * rows : (i + 1) * rows]
    for copy in out_copies:
        copy.wait()


def shrink(me, counts, sorted_rows, pieces, own_down, other_down, sizes):
    ranks, width = own_down.shape
    rows_all = sorted_rows.shape[0]
    rows = rows_all // CORES
    values = [value for value, _, _ in pieces]
    near = values[:-6]
    block = values[0].shape[0]
    tokens_shape = pltpu.HBM((rows, width), jnp.bfloat16)
    shrunk_shape = jax.ShapeDtypeStruct((rows, CORES * ranks), jnp.bfloat16)
    held_shape = jax.ShapeDtypeStruct((rows // block, sizes[-1]), jnp.int32)

    def whole(shape):
        return pl.BlockSpec(shape, lambda i, *_: (0, 0))

    down_vmem = pltpu.VMEM((CORES * ranks, width), jnp.bfloat16)
    downs = in_hbm([own_down]) + [other_down]
    tokens, shrunk, held, choice = pl.pallas_call(
        functools.partial(shrink_near_kernel, sizes, [place[1:] for place in pieces[:-6]], len(counts)),
        grid_spec=pltpu.PrefetchScalarGridSpec(
            num_scalar_prefetch=1 + len(counts),
            grid=(1,),
            in_specs=[whole((1, rows_all))] + [ANY_SPEC] * (2 + len(near)),
            out_specs=[
                ANY_SPEC,
                whole(shrunk_shape.shape),
                whole(held_shape.shape),
                pl.BlockSpec(memory_space=pltpu.SMEM),
            ],
            scratch_shapes=[
                pltpu.VMEM((rows, width), jnp.bfloat16),
                down_vmem,
                pltpu.SemaphoreType.DMA((3 + len(near),)),
            ],
        ),
        out_shape=[tokens_shape, shrunk_shape, held_shape, jax.ShapeDtypeStruct((1,), jnp.int32)],
        compiler_params=pltpu.CompilerParams(vmem_limit_bytes=rows * width * 2 + 16 * MIB),
        name="shrink_near",
    )(me, *counts, *in_hbm([sorted_rows.reshape(1, rows_all)]), *downs, *in_hbm(near[:1]), *near[1:])
    tokens, shrunk = pl.pallas_call(
        functools.partial(shrink_far_kernel, [place[1:] for place in pieces[-6:]]),
        grid_spec=pltpu.PrefetchScalarGridSpec(
            num_scalar_prefetch=1,
            grid=(1,),
            in_specs=[ANY_SPEC] * 10,
            out_specs=[ANY_SPEC, whole(shrunk_shape.shape)],
            scratch_shapes=[
                pltpu.VMEM((3 * block, width), jnp.bfloat16),
                down_vmem,
                pltpu.SemaphoreType.DMA((12,)),
            ],
        ),
        out_shape=[tokens_shape, shrunk_shape],
        input_output_aliases={1: 0},
        compiler_params=pltpu.CompilerParams(vmem_limit_bytes=16 * MIB),
        name="shrink_far",
    )(me, *in_hbm([tokens]), shrunk, *downs, *values[-6:])
    return tokens, shrunk, held, choice


def expand_kernel(order, block, counts, me, held_hbm, own_hbm, other_hbm, keep_ref, got_ref, out_ref, *scratch):
    held_ref, own_ref, other_ref, maps_vmem, out_vmem, sems = scratch
    chips, slots, units = out_vmem.shape
    most = held_ref.shape[1]
    ranks = keep_ref.shape[0]
    adapters = counts.shape[0] // chips
    chip = me[0] // CORES
    core = me[0] % CORES
    copies = []
    for c in range(chips):
        start = pl.multiple_of((order[c] * CORES + core) * units, units)
        for ref, where in ((keep_ref, core), (got_ref, 1 - core)):
            copies.append(
                pltpu.make_async_copy(
                    ref.at[:, pl.ds(start, units)],
                    maps_vmem.at[c, pl.ds(pl.multiple_of(where * ranks, ranks), ranks)],
                    sems.at[len(copies)],
                )
            )
    small = [
        pltpu.make_async_copy(ref, held, sems.at[3 * chips + i])
        for i, (ref, held) in enumerate(((held_hbm, held_ref), (own_hbm, own_ref), (other_hbm, other_ref)))
    ]
    for copy in small + copies:
        copy.start()
    for copy in small:
        copy.wait()

    wanted = held_ref[pl.ds(chip, 1), :]
    index = lax.broadcasted_iota(jnp.int32, (own_ref.shape[0], most), 0)
    row = index // block * (CORES * block) + index % block
    picked = jnp.zeros((most, own_ref.shape[1]), jnp.float32)
    for ref, where in ((own_ref, core), (other_ref, 1 - core)):
        hit = (row + where * block == wanted).astype(jnp.float32).astype(jnp.bfloat16)
        picked += lax.dot_general(hit, ref[...], (((0,), (0,)), ((), ())), preferred_element_type=jnp.float32)
    slot = lax.broadcasted_iota(jnp.int32, picked.shape, 0)
    adapter = lax.broadcasted_iota(jnp.int32, picked.shape, 1) // (picked.shape[1] // adapters)
    mine = jnp.zeros(picked.shape, jnp.int32)
    first = jnp.int32(0)
    for a in range(adapters):
        end = first + counts[chip * adapters + a]
        mine += ((adapter == a) & (slot >= first) & (slot < end)).astype(jnp.int32)
        first = end
    shrunk = jnp.where(mine > 0, picked, 0.0).astype(jnp.bfloat16)[:slots]

    out_copies = []
    for c in range(chips):
        copies[2 * c].wait()
        copies[2 * c + 1].wait()
        product = jnp.dot(shrunk, maps_vmem[c], preferred_element_type=jnp.float32)
        out_vmem[c] = (ADAPTER_SCALE * product).astype(out_vmem.dtype)
        out_copies.append(pltpu.make_async_copy(out_vmem.at[c], out_ref.at[c], sems.at[2 * chips + c]))
        out_copies[-1].start()
    for copy in out_copies:
        copy.wait()


def expand(counts, me, held, own_shrunk, other_shrunk, keep, got, order, slots, block):
    ranks, columns = keep.shape
    chips, most = held.shape
    units = columns // chips // CORES
    rows, ranks_all = own_shrunk.shape
    return pl.pallas_call(
        functools.partial(expand_kernel, order, block),
        grid_spec=pltpu.PrefetchScalarGridSpec(
            num_scalar_prefetch=2,
            grid=(1,),
            in_specs=[ANY_SPEC] * 5,
            out_specs=ANY_SPEC,
            scratch_shapes=[
                pltpu.VMEM((chips, most), jnp.int32),
                pltpu.VMEM((rows, ranks_all), jnp.bfloat16),
                pltpu.VMEM((rows, ranks_all), jnp.bfloat16),
                pltpu.VMEM((chips, ranks_all, units), jnp.bfloat16),
                pltpu.VMEM((chips, slots, units), jnp.bfloat16),
                pltpu.SemaphoreType.DMA((3 * chips + 3,)),
            ],
        ),
        out_shape=pltpu.HBM((chips, slots, units), jnp.bfloat16),
        compiler_params=pltpu.CompilerParams(vmem_limit_bytes=16 * MIB),
        cost_estimate=pl.CostEstimate(
            flops=2 * slots * ranks_all * chips * units,
            bytes_accessed=2 * (slots + ranks_all) * chips * units,
            transcendentals=0,
        ),
        name="expand",
    )(counts, me, held, own_shrunk, other_shrunk, *in_hbm([keep, got]))


def project_kernel(block, me, gate_weight_ref, up_weight_ref, own_ref, other_ref, gate_ref, up_ref, tokens_vmem, sems):
    depth = gate_weight_ref.shape[0]
    core = me[0] % CORES
    k = pl.program_id(0)

    @pl.when(k == 0)
    def _():
        copies = []
        for ref, where in ((own_ref, core), (other_ref, 1 - core)):
            for chip in range(ref.shape[0] // block):
                start = pl.multiple_of((chip * CORES + where) * block, block)
                copies.append(
                    pltpu.make_async_copy(
                        ref.at[pl.ds(chip * block, block)], tokens_vmem.at[pl.ds(start, block)], sems.at[len(copies)]
                    )
                )
        run_copies(copies)
        gate_ref[...] = jnp.zeros_like(gate_ref)
        up_ref[...] = jnp.zeros_like(up_ref)

    tokens = tokens_vmem[:, pl.ds(pl.multiple_of(k * depth, depth), depth)]
    gate_ref[...] += jnp.dot(tokens, gate_weight_ref[...], preferred_element_type=jnp.float32)
    up_ref[...] += jnp.dot(tokens, up_weight_ref[...], preferred_element_type=jnp.float32)

    @pl.when(k == pl.num_programs(0) - 1)
    def _():
        gate = gate_ref[...]
        gate_ref[...] = gate / (1.0 + jnp.exp(-gate))


def project(me, own, other, gate_weight, up_weight, block):
    width, units = gate_weight.shape
    rows = CORES * own.shape[0]
    depth = min(1024, width)
    weight_spec = pl.BlockSpec((depth, units), lambda k, s: (k, 0))
    out_spec = pl.BlockSpec((rows, units), lambda k, s: (0, 0))
    out = pltpu.HBM((rows, units), jnp.float32)
    return pl.pallas_call(
        functools.partial(project_kernel, block),
        grid_spec=pltpu.PrefetchScalarGridSpec(
            num_scalar_prefetch=1,
            grid=(width // depth,),
            in_specs=[weight_spec, weight_spec, ANY_SPEC, ANY_SPEC],
            out_specs=[out_spec, out_spec],
            scratch_shapes=[
                pltpu.VMEM((rows, width), jnp.bfloat16),
                pltpu.SemaphoreType.DMA((rows // block,)),
            ],
        ),
        out_shape=[out, out],
        compiler_params=pltpu.CompilerParams(vmem_limit_bytes=rows * width * 2 + 20 * MIB),
        cost_estimate=pl.CostEstimate(
            flops=4 * rows * width * units,
            bytes_accessed=2 * (rows + 2 * units) * width,
            transcendentals=rows * units,
        ),
        name="project",
    )(me, *in_hbm([gate_weight, up_weight, own, other]))


def combine_kernel(tile, pick_hbm, gate_hbm, up_hbm, products_hbm, out_hbm, *scratch):
    pick_ref, gate_ref, up_ref, products_ref, out_ref, sems = scratch
    tiles = gate_ref.shape[1] // tile
    pick_copy = pltpu.make_async_copy(pick_hbm, pick_ref, sems.at[4 * tiles])
    pick_copy.start()
    copies = []
    for t in range(tiles):
        part = pl.ds(t * tile, tile)
        copies.append(
            [
                pltpu.make_async_copy(source.at[:, part], target.at[:, part], sems.at[4 * t + i])
                for i, (source, target) in enumerate(
                    ((products_hbm, products_ref), (gate_hbm, gate_ref), (up_hbm, up_ref))
                )
            ]
        )
        for copy in copies[t]:
            copy.start()
    pick_copy.wait()
    out_copies = []
    for t in range(tiles):
        part = pl.ds(t * tile, tile)
        for copy in copies[t]:
            copy.wait()
        delta = jnp.dot(pick_ref[...], products_ref[:, part], preferred_element_type=jnp.float32)
        out_ref[:, part] = (gate_ref[:, part] * (up_ref[:, part] + delta)).astype(out_ref.dtype)
        out_copies.append(pltpu.make_async_copy(out_ref.at[:, part], out_hbm.at[:, part], sems.at[4 * t + 3]))
        out_copies[t].start()
    for copy in out_copies:
        copy.wait()


def combine(pick, gate, up, products):
    rows, units = gate.shape
    slots_all = products.shape[0]
    tile = min(256, units)
    return pl.pallas_call(
        functools.partial(combine_kernel, tile),
        grid=(1,),
        in_specs=[ANY_SPEC] * 4,
        out_specs=ANY_SPEC,
        scratch_shapes=[
            pltpu.VMEM((rows, slots_all), jnp.bfloat16),
            pltpu.VMEM((rows, units), jnp.float32),
            pltpu.VMEM((rows, units), jnp.float32),
            pltpu.VMEM((slots_all, units), jnp.bfloat16),
            pltpu.VMEM((rows, units), jnp.bfloat16),
            pltpu.SemaphoreType.DMA((4 * (units // tile) + 1,)),
        ],
        out_shape=pltpu.HBM((rows, units), jnp.bfloat16),
        compiler_params=pltpu.CompilerParams(vmem_limit_bytes=rows * slots_all * 2 + 20 * MIB),
        cost_estimate=pl.CostEstimate(
            flops=2 * rows * slots_all * units, bytes_accessed=10 * rows * units, transcendentals=0
        ),
        name="combine",
    )(*in_hbm([pick, gate, up]), products)


def per_device(
    tokens,
    gate_weight,
    up_weight,
    adapter_down_weight,
    adapter_up_weight,
    row_adapter,
    sorted_rows,
    segment_count,
):
    axis = "tensor"
    size = lax.axis_size(axis)
    me = lax.axis_index(axis).astype(jnp.int32)
    chips = size // CORES
    resident, rank, width = adapter_down_weight.shape
    ranks = resident * rank
    rows = row_adapter.shape[0]
    block = tokens.shape[0]
    me_array = me.reshape(1)
    flips = [(d, d ^ 1) for d in range(size)]

    def other_core(value):
        return lax.ppermute(value, axis, flips)

    most = CORES * resident * ROWS_PER_LIMIT
    sizes = [slots for slots in SLOT_SIZES if slots < most] + [most]
    groups = lax.axis_size("groups")
    own_down = adapter_down_weight.reshape(ranks, width)
    own_maps = adapter_up_weight.reshape(ranks, -1)
    other_down = other_core(own_down)
    counts = [segment_count] + [
        lax.ppermute(segment_count, "groups", [(g, (g + shift) % groups) for g in range(groups)])
        for shift in range(1, groups)
    ]
    other_maps = other_core(own_maps)

    def beside(step, values):
        nonlocal other_down, counts, other_maps
        if step == 1:
            other_down, counts, values[0], values[1] = lax.optimization_barrier((other_down, counts, *values))
        return values

    pieces = ring_gather(tokens, axis, beside)
    own_tokens, own_shrunk, held, choice = shrink(
        me_array, counts, sorted_rows, pieces, own_down, other_down, sizes
    )
    other_shrunk = other_core(own_shrunk)

    order = [half * (chips // 2) + c for c in range(chips // 2) for half in range(2)]
    same_core = [[c * CORES + k for c in order] for k in range(CORES)]

    def finish(slots):
        def branch(own_tokens, own_shrunk, other_shrunk, own_maps, other_maps, held, gate_weight, up_weight):
            products = expand(
                segment_count, me_array, held, own_shrunk, other_shrunk, own_maps, other_maps, order, slots, block
            )
            products = lax.all_to_all(
                products, axis, split_axis=0, concat_axis=0, axis_index_groups=same_core, tiled=True
            )
            held, other_tokens = lax.optimization_barrier((held, other_core(own_tokens)))
            held_rows = jnp.stack([held[c, :slots] for c in order]).reshape(1, chips * slots)
            pick = (jnp.arange(rows, dtype=jnp.int32)[:, None] == held_rows).astype(jnp.bfloat16)
            pick, other_tokens = lax.optimization_barrier((pick, other_tokens))
            gate, up = project(me_array, own_tokens, other_tokens, gate_weight, up_weight, block)
            return combine(pick, gate, up, products.reshape(chips * slots, -1))

        return branch

    return lax.switch(
        choice[0],
        [finish(slots) for slots in sizes],
        own_tokens,
        own_shrunk,
        other_shrunk,
        own_maps,
        other_maps,
        held,
        gate_weight,
        up_weight,
    )


def solution(mesh):
    placed = (
        P(("groups", "tensor"), None),
        P(None, "tensor"),
        P(None, "tensor"),
        P(("groups", "tensor"), None, None),
        P(("groups", "tensor"), None, None),
        P("groups"),
        P("groups"),
        P("groups"),
    )
    return jax.shard_map(
        per_device, mesh=mesh, in_specs=placed, out_specs=P("groups", "tensor"), check_vma=False
    )
```

```python
import functools

import jax
import jax.numpy as jnp
from jax import lax
from jax.experimental import pallas as pl
from jax.experimental.pallas import tpu as pltpu
from jax.sharding import PartitionSpec as P

ADAPTER_SCALE = 0.5
ROWS_PER_LIMIT = 64
SLOT_SIZES = (80, 96)
CORES = 2
MIB = 1024 * 1024


def chip_ring(chips):
    return list(range(0, chips, 2)) + list(range(chips - 1, 0, -2))


def ring_chip(me, chips, distance):
    chip = me // CORES
    place = jnp.where(chip % 2 == 0, chip // 2, chips // 2 + (chips - 1 - chip) // 2)
    place = (place + distance + chips) % chips
    return jnp.where(place < chips // 2, 2 * place, chips - 1 - 2 * (place - chips // 2))


def ring_gather(block, axis, beside):
    size = lax.axis_size(axis)
    chips = size // CORES
    ring = chip_ring(chips)

    def moved(value, shift):
        pairs = [
            (ring[p] * CORES + k, ring[(p + shift) % chips] * CORES + k)
            for p in range(chips)
            for k in range(CORES)
        ]
        return lax.ppermute(value, axis, pairs)

    right, left = moved(block, 1), moved(block, -1)
    pieces = [(block, 0, 0), (right, 0, -1), (left, 0, 1)]
    half = block.shape[1] // 2
    far = chips // 2
    columns = (0, half), (half, 0)
    held = [(right[:, a : a + half], left[:, b : b + half]) for a, b in columns]
    held = beside(1, held)
    for step in range(2, far + 1):
        for chain in range(1 if step == far else 2):
            right, left = held[chain]
            held[chain] = moved(right, 1), moved(left, -1)
            for value, column, distance in zip(held[chain], columns[chain], (-step, step)):
                pieces.append((value, column, distance))
        held = beside(step, held)
    return pieces


ANY_SPEC = pl.BlockSpec(memory_space=pl.ANY)


def in_hbm(values):
    return [pltpu.with_memory_space_constraint(value, pltpu.HBM) for value in values]


def run_copies(copies):
    for copy in copies:
        copy.start()
    for copy in copies:
        copy.wait()


def make_plan(sizes, counts, sorted_ref, held_ref, choice_ref):
    chips, most = held_ref.shape
    rows = sorted_ref.shape[1]
    adapters = counts[0].shape[0] // chips

    def total(group, chip):
        return functools.reduce(jnp.add, [counts[group][chip * adapters + a] for a in range(adapters)])

    listed = jnp.broadcast_to(sorted_ref[...], (8, rows))
    slot = lax.broadcasted_iota(jnp.int32, (8, most), 1)
    start = jnp.int32(0)
    for chip in range(chips):
        turned = pltpu.roll(listed, (rows - start) % rows, 1)
        held_ref[chip : chip + 1, :] = jnp.where(slot < total(0, chip), turned[:, :most], -1)[0:1]
        start += total(0, chip)
    largest = functools.reduce(
        jnp.maximum, [total(group, chip) for group in range(len(counts)) for chip in range(chips)]
    )
    choice_ref[0] = functools.reduce(jnp.add, [(largest > size).astype(jnp.int32) for size in sizes[:-1]])


def down_copies(core, own_down_ref, other_down_ref, down_vmem, sems):
    ranks = own_down_ref.shape[0]
    return [
        pltpu.make_async_copy(ref, down_vmem.at[pl.ds(pl.multiple_of(where * ranks, ranks), ranks)], sems.at[i])
        for i, (ref, where) in enumerate(((own_down_ref, core), (other_down_ref, 1 - core)))
    ]


def shrink_near_kernel(sizes, places, groups, me, *refs):
    counts, refs = refs[:groups], refs[groups:]
    sorted_ref, own_down_ref, other_down_ref = refs[:3]
    refs = refs[3:]
    piece_refs = refs[: len(places)]
    tokens_ref, shrunk_ref, held_ref, choice_ref, tokens_vmem, down_vmem, sems = refs[len(places) :]
    chips = held_ref.shape[0]
    copies = down_copies(me[0] % CORES, own_down_ref, other_down_ref, down_vmem, sems)
    for ref, (column, distance) in zip(piece_refs, places):
        rows, width = ref.shape
        start = pl.multiple_of(ring_chip(me[0], chips, distance) * rows, rows)
        copies.append(
            pltpu.make_async_copy(
                ref, tokens_vmem.at[pl.ds(start, rows), pl.ds(column, width)], sems.at[len(copies)]
            )
        )
    for copy in copies:
        copy.start()
    make_plan(sizes, counts, sorted_ref, held_ref, choice_ref)
    for copy in copies:
        copy.wait()
    out_copy = pltpu.make_async_copy(tokens_vmem, tokens_ref, sems.at[len(copies)])
    out_copy.start()
    shrunk_ref[...] = lax.dot_general(
        tokens_vmem[...], down_vmem[...], (((1,), (1,)), ((), ())), preferred_element_type=jnp.float32
    ).astype(shrunk_ref.dtype)
    out_copy.wait()


def shrink_far_kernel(places, me, tokens_in, shrunk_in, own_down_ref, other_down_ref, *refs):
    piece_refs = refs[: len(places)]
    tokens_ref, shrunk_ref, far_vmem, down_vmem, sems = refs[len(places) :]
    rows, half = piece_refs[0].shape
    chips = tokens_in.shape[0] // rows
    slots = {distance % chips: i for i, distance in enumerate(range(chips // 2 - 1, chips // 2 + 2))}
    copies = down_copies(me[0] % CORES, own_down_ref, other_down_ref, down_vmem, sems)
    copies.append(pltpu.make_async_copy(shrunk_in, shrunk_ref, sems.at[2]))
    for ref, (column, distance) in zip(piece_refs, places):
        slot = slots[distance % chips]
        copies.append(
            pltpu.make_async_copy(
                ref, far_vmem.at[pl.ds(slot * rows, rows), pl.ds(column, half)], sems.at[len(copies)]
            )
        )
    run_copies(copies)
    starts = [pl.multiple_of(ring_chip(me[0], chips, distance) * rows, rows) for distance in slots]
    out_copies = [
        pltpu.make_async_copy(
            far_vmem.at[pl.ds(i * rows, rows)], tokens_ref.at[pl.ds(start, rows)], sems.at[len(copies) + i]
        )
        for i, start in enumerate(starts)
    ]
    for copy in out_copies:
        copy.start()
    shrunk = lax.dot_general(
        far_vmem[...], down_vmem[...], (((1,), (1,)), ((), ())), preferred_element_type=jnp.float32
    ).astype(shrunk_ref.dtype)
    for i, start in enumerate(starts):
        shrunk_ref[pl.ds(start, rows), :] = shrunk[i * rows : (i + 1) * rows]
    for copy in out_copies:
        copy.wait()


def shrink(me, counts, sorted_rows, pieces, own_down, other_down, sizes):
    ranks, width = own_down.shape
    rows_all = sorted_rows.shape[0]
    rows = rows_all // CORES
    values = [value for value, _, _ in pieces]
    near = values[:-6]
    block = values[0].shape[0]
    tokens_shape = pltpu.HBM((rows, width), jnp.bfloat16)
    shrunk_shape = jax.ShapeDtypeStruct((rows, CORES * ranks), jnp.bfloat16)
    held_shape = jax.ShapeDtypeStruct((rows // block, sizes[-1]), jnp.int32)

    def whole(shape):
        return pl.BlockSpec(shape, lambda i, *_: (0, 0))

    down_vmem = pltpu.VMEM((CORES * ranks, width), jnp.bfloat16)
    downs = in_hbm([own_down]) + [other_down]
    tokens, shrunk, held, choice = pl.pallas_call(
        functools.partial(shrink_near_kernel, sizes, [place[1:] for place in pieces[:-6]], len(counts)),
        grid_spec=pltpu.PrefetchScalarGridSpec(
            num_scalar_prefetch=1 + len(counts),
            grid=(1,),
            in_specs=[whole((1, rows_all))] + [ANY_SPEC] * (2 + len(near)),
            out_specs=[
                ANY_SPEC,
                whole(shrunk_shape.shape),
                whole(held_shape.shape),
                pl.BlockSpec(memory_space=pltpu.SMEM),
            ],
            scratch_shapes=[
                pltpu.VMEM((rows, width), jnp.bfloat16),
                down_vmem,
                pltpu.SemaphoreType.DMA((3 + len(near),)),
            ],
        ),
        out_shape=[tokens_shape, shrunk_shape, held_shape, jax.ShapeDtypeStruct((1,), jnp.int32)],
        compiler_params=pltpu.CompilerParams(vmem_limit_bytes=rows * width * 2 + 16 * MIB),
        name="shrink_near",
    )(me, *counts, *in_hbm([sorted_rows.reshape(1, rows_all)]), *downs, *in_hbm(near[:1]), *near[1:])
    tokens, shrunk = pl.pallas_call(
        functools.partial(shrink_far_kernel, [place[1:] for place in pieces[-6:]]),
        grid_spec=pltpu.PrefetchScalarGridSpec(
            num_scalar_prefetch=1,
            grid=(1,),
            in_specs=[ANY_SPEC] * 10,
            out_specs=[ANY_SPEC, whole(shrunk_shape.shape)],
            scratch_shapes=[
                pltpu.VMEM((3 * block, width), jnp.bfloat16),
                down_vmem,
                pltpu.SemaphoreType.DMA((12,)),
            ],
        ),
        out_shape=[tokens_shape, shrunk_shape],
        input_output_aliases={1: 0},
        compiler_params=pltpu.CompilerParams(vmem_limit_bytes=16 * MIB),
        name="shrink_far",
    )(me, *in_hbm([tokens]), shrunk, *downs, *values[-6:])
    return tokens, shrunk, held, choice


def expand_kernel(order, block, counts, me, held_hbm, own_hbm, other_hbm, keep_ref, got_ref, out_ref, *scratch):
    held_ref, own_ref, other_ref, maps_vmem, out_vmem, sems = scratch
    chips, slots, units = out_vmem.shape
    most = held_ref.shape[1]
    ranks = keep_ref.shape[0]
    adapters = counts.shape[0] // chips
    chip = me[0] // CORES
    core = me[0] % CORES
    copies = []
    for c in range(chips):
        start = pl.multiple_of((order[c] * CORES + core) * units, units)
        for ref, where in ((keep_ref, core), (got_ref, 1 - core)):
            copies.append(
                pltpu.make_async_copy(
                    ref.at[:, pl.ds(start, units)],
                    maps_vmem.at[c, pl.ds(pl.multiple_of(where * ranks, ranks), ranks)],
                    sems.at[len(copies)],
                )
            )
    small = [
        pltpu.make_async_copy(ref, held, sems.at[3 * chips + i])
        for i, (ref, held) in enumerate(((held_hbm, held_ref), (own_hbm, own_ref), (other_hbm, other_ref)))
    ]
    for copy in small + copies:
        copy.start()
    for copy in small:
        copy.wait()

    wanted = held_ref[pl.ds(chip, 1), :]
    index = lax.broadcasted_iota(jnp.int32, (own_ref.shape[0], most), 0)
    row = index // block * (CORES * block) + index % block
    picked = jnp.zeros((most, own_ref.shape[1]), jnp.float32)
    for ref, where in ((own_ref, core), (other_ref, 1 - core)):
        hit = (row + where * block == wanted).astype(jnp.float32).astype(jnp.bfloat16)
        picked += lax.dot_general(hit, ref[...], (((0,), (0,)), ((), ())), preferred_element_type=jnp.float32)
    slot = lax.broadcasted_iota(jnp.int32, picked.shape, 0)
    adapter = lax.broadcasted_iota(jnp.int32, picked.shape, 1) // (picked.shape[1] // adapters)
    mine = jnp.zeros(picked.shape, jnp.int32)
    first = jnp.int32(0)
    for a in range(adapters):
        end = first + counts[chip * adapters + a]
        mine += ((adapter == a) & (slot >= first) & (slot < end)).astype(jnp.int32)
        first = end
    shrunk = jnp.where(mine > 0, ADAPTER_SCALE * picked, 0.0).astype(jnp.bfloat16)[:slots]

    out_copies = []
    for c in range(chips):
        copies[2 * c].wait()
        copies[2 * c + 1].wait()
        product = jnp.dot(shrunk, maps_vmem[c], preferred_element_type=jnp.float32)
        out_vmem[c] = product.astype(out_vmem.dtype)
        out_copies.append(pltpu.make_async_copy(out_vmem.at[c], out_ref.at[c], sems.at[2 * chips + c]))
        out_copies[-1].start()
    for copy in out_copies:
        copy.wait()


def expand(counts, me, held, own_shrunk, other_shrunk, keep, got, order, slots, block):
    ranks, columns = keep.shape
    chips, most = held.shape
    units = columns // chips // CORES
    rows, ranks_all = own_shrunk.shape
    return pl.pallas_call(
        functools.partial(expand_kernel, order, block),
        grid_spec=pltpu.PrefetchScalarGridSpec(
            num_scalar_prefetch=2,
            grid=(1,),
            in_specs=[ANY_SPEC] * 5,
            out_specs=ANY_SPEC,
            scratch_shapes=[
                pltpu.VMEM((chips, most), jnp.int32),
                pltpu.VMEM((rows, ranks_all), jnp.bfloat16),
                pltpu.VMEM((rows, ranks_all), jnp.bfloat16),
                pltpu.VMEM((chips, ranks_all, units), jnp.bfloat16),
                pltpu.VMEM((chips, slots, units), jnp.bfloat16),
                pltpu.SemaphoreType.DMA((3 * chips + 3,)),
            ],
        ),
        out_shape=pltpu.HBM((chips, slots, units), jnp.bfloat16),
        compiler_params=pltpu.CompilerParams(vmem_limit_bytes=16 * MIB),
        cost_estimate=pl.CostEstimate(
            flops=2 * slots * ranks_all * chips * units,
            bytes_accessed=2 * (slots + ranks_all) * chips * units,
            transcendentals=0,
        ),
        name="expand",
    )(counts, me, held, own_shrunk, other_shrunk, *in_hbm([keep, got]))


def project_kernel(block, me, gate_weight_ref, up_weight_ref, own_ref, other_ref, gate_ref, up_ref, tokens_vmem, sems):
    depth = gate_weight_ref.shape[0]
    core = me[0] % CORES
    k = pl.program_id(0)

    @pl.when(k == 0)
    def _():
        copies = []
        for ref, where in ((own_ref, core), (other_ref, 1 - core)):
            for chip in range(ref.shape[0] // block):
                start = pl.multiple_of((chip * CORES + where) * block, block)
                copies.append(
                    pltpu.make_async_copy(
                        ref.at[pl.ds(chip * block, block)], tokens_vmem.at[pl.ds(start, block)], sems.at[len(copies)]
                    )
                )
        run_copies(copies)
        gate_ref[...] = jnp.zeros_like(gate_ref)
        up_ref[...] = jnp.zeros_like(up_ref)

    tokens = tokens_vmem[:, pl.ds(pl.multiple_of(k * depth, depth), depth)]
    gate_ref[...] += jnp.dot(tokens, gate_weight_ref[...], preferred_element_type=jnp.float32)
    up_ref[...] += jnp.dot(tokens, up_weight_ref[...], preferred_element_type=jnp.float32)

    @pl.when(k == pl.num_programs(0) - 1)
    def _():
        gate = gate_ref[...]
        gate_ref[...] = gate / (1.0 + jnp.exp(-gate))


def project(me, own, other, gate_weight, up_weight, block):
    width, units = gate_weight.shape
    rows = CORES * own.shape[0]
    depth = min(1024, width)
    weight_spec = pl.BlockSpec((depth, units), lambda k, s: (k, 0))
    out_spec = pl.BlockSpec((rows, units), lambda k, s: (0, 0))
    out = pltpu.HBM((rows, units), jnp.float32)
    return pl.pallas_call(
        functools.partial(project_kernel, block),
        grid_spec=pltpu.PrefetchScalarGridSpec(
            num_scalar_prefetch=1,
            grid=(width // depth,),
            in_specs=[weight_spec, weight_spec, ANY_SPEC, ANY_SPEC],
            out_specs=[out_spec, out_spec],
            scratch_shapes=[
                pltpu.VMEM((rows, width), jnp.bfloat16),
                pltpu.SemaphoreType.DMA((rows // block,)),
            ],
        ),
        out_shape=[out, out],
        compiler_params=pltpu.CompilerParams(vmem_limit_bytes=rows * width * 2 + 20 * MIB),
        cost_estimate=pl.CostEstimate(
            flops=4 * rows * width * units,
            bytes_accessed=2 * (rows + 2 * units) * width,
            transcendentals=rows * units,
        ),
        name="project",
    )(me, *in_hbm([gate_weight, up_weight, own, other]))


def combine_kernel(pick_ref, gate_ref, up_ref, products_ref, out_ref):
    delta = jnp.dot(pick_ref[...], products_ref[...], preferred_element_type=jnp.float32)
    out_ref[...] = (gate_ref[...] * (up_ref[...] + delta)).astype(out_ref.dtype)


def combine(pick, gate, up, products):
    rows, units = gate.shape
    slots_all = products.shape[0]
    tile = min(512, units)
    column_spec = pl.BlockSpec((rows, tile), lambda n: (0, n))
    return pl.pallas_call(
        combine_kernel,
        grid=(units // tile,),
        in_specs=[
            pl.BlockSpec((rows, slots_all), lambda n: (0, 0)),
            column_spec,
            column_spec,
            pl.BlockSpec((slots_all, tile), lambda n: (0, n)),
        ],
        out_specs=column_spec,
        out_shape=pltpu.HBM((rows, units), jnp.bfloat16),
        compiler_params=pltpu.CompilerParams(vmem_limit_bytes=rows * slots_all * 4 + 20 * MIB),
        cost_estimate=pl.CostEstimate(
            flops=2 * rows * slots_all * units, bytes_accessed=10 * rows * units, transcendentals=0
        ),
        name="combine",
    )(*in_hbm([pick, gate, up]), products)


def per_device(
    tokens,
    gate_weight,
    up_weight,
    adapter_down_weight,
    adapter_up_weight,
    row_adapter,
    sorted_rows,
    segment_count,
):
    axis = "tensor"
    size = lax.axis_size(axis)
    me = lax.axis_index(axis).astype(jnp.int32)
    chips = size // CORES
    resident, rank, width = adapter_down_weight.shape
    ranks = resident * rank
    rows = row_adapter.shape[0]
    block = tokens.shape[0]
    me_array = me.reshape(1)
    flips = [(d, d ^ 1) for d in range(size)]

    def other_core(value):
        return lax.ppermute(value, axis, flips)

    most = CORES * resident * ROWS_PER_LIMIT
    sizes = [slots for slots in SLOT_SIZES if slots < most] + [most]
    groups = lax.axis_size("groups")
    own_down = adapter_down_weight.reshape(ranks, width)
    own_maps = adapter_up_weight.reshape(ranks, -1)
    other_down = other_core(own_down)
    counts = [segment_count] + [
        lax.ppermute(segment_count, "groups", [(g, (g + shift) % groups) for g in range(groups)])
        for shift in range(1, groups)
    ]
    other_maps = other_core(own_maps)

    def beside(step, values):
        nonlocal other_down, counts, other_maps
        if step == 1:
            other_down, counts, values[0], values[1] = lax.optimization_barrier((other_down, counts, *values))
        return values

    pieces = ring_gather(tokens, axis, beside)
    own_tokens, own_shrunk, held, choice = shrink(
        me_array, counts, sorted_rows, pieces, own_down, other_down, sizes
    )
    other_shrunk = other_core(own_shrunk)

    order = [half * (chips // 2) + c for c in range(chips // 2) for half in range(2)]
    same_core = [[c * CORES + k for c in order] for k in range(CORES)]

    def finish(slots):
        def branch(own_tokens, own_shrunk, other_shrunk, own_maps, other_maps, held, gate_weight, up_weight):
            products = expand(
                segment_count, me_array, held, own_shrunk, other_shrunk, own_maps, other_maps, order, slots, block
            )
            products = lax.all_to_all(
                products, axis, split_axis=0, concat_axis=0, axis_index_groups=same_core, tiled=True
            )
            held, other_tokens = lax.optimization_barrier((held, other_core(own_tokens)))
            held_rows = jnp.stack([held[c, :slots] for c in order]).reshape(1, chips * slots)
            pick = (jnp.arange(rows, dtype=jnp.int32)[:, None] == held_rows).astype(jnp.bfloat16)
            pick, other_tokens = lax.optimization_barrier((pick, other_tokens))
            gate, up = project(me_array, own_tokens, other_tokens, gate_weight, up_weight, block)
            return combine(pick, gate, up, products.reshape(chips * slots, -1))

        return branch

    return lax.switch(
        choice[0],
        [finish(slots) for slots in sizes],
        own_tokens,
        own_shrunk,
        other_shrunk,
        own_maps,
        other_maps,
        held,
        gate_weight,
        up_weight,
    )


def solution(mesh):
    placed = (
        P(("groups", "tensor"), None),
        P(None, "tensor"),
        P(None, "tensor"),
        P(("groups", "tensor"), None, None),
        P(("groups", "tensor"), None, None),
        P("groups"),
        P("groups"),
        P("groups"),
    )
    return jax.shard_map(
        per_device, mesh=mesh, in_specs=placed, out_specs=P("groups", "tensor"), check_vma=False
    )
```

```python
import functools

import jax
import jax.numpy as jnp
from jax import lax
from jax.experimental import pallas as pl
from jax.experimental.pallas import tpu as pltpu
from jax.sharding import PartitionSpec as P

ADAPTER_SCALE = 0.5
ROWS_PER_LIMIT = 64
SLOT_SIZES = (72, 80, 88, 104)
CORES = 2
MIB = 1024 * 1024


def chip_ring(chips):
    return list(range(0, chips, 2)) + list(range(chips - 1, 0, -2))


def ring_chip(me, chips, distance):
    chip = me // CORES
    place = jnp.where(chip % 2 == 0, chip // 2, chips // 2 + (chips - 1 - chip) // 2)
    place = (place + distance + chips) % chips
    return jnp.where(place < chips // 2, 2 * place, chips - 1 - 2 * (place - chips // 2))


def ring_gather(block, axis, beside):
    size = lax.axis_size(axis)
    chips = size // CORES
    ring = chip_ring(chips)

    def moved(value, shift):
        pairs = [
            (ring[p] * CORES + k, ring[(p + shift) % chips] * CORES + k)
            for p in range(chips)
            for k in range(CORES)
        ]
        return lax.ppermute(value, axis, pairs)

    right, left = moved(block, 1), moved(block, -1)
    pieces = [(block, 0, 0), (right, 0, -1), (left, 0, 1)]
    half = block.shape[1] // 2
    far = chips // 2
    columns = (0, half), (half, 0)
    held = [(right[:, a : a + half], left[:, b : b + half]) for a, b in columns]
    held = beside(1, held)
    for step in range(2, far + 1):
        for chain in range(1 if step == far else 2):
            right, left = held[chain]
            held[chain] = moved(right, 1), moved(left, -1)
            for value, column, distance in zip(held[chain], columns[chain], (-step, step)):
                pieces.append((value, column, distance))
        held = beside(step, held)
    return pieces


ANY_SPEC = pl.BlockSpec(memory_space=pl.ANY)


def in_hbm(values):
    return [pltpu.with_memory_space_constraint(value, pltpu.HBM) for value in values]


def run_copies(copies):
    for copy in copies:
        copy.start()
    for copy in copies:
        copy.wait()


def make_plan(sizes, counts, sorted_ref, held_ref, choice_ref):
    chips, most = held_ref.shape
    rows = sorted_ref.shape[1]
    adapters = counts[0].shape[0] // chips

    def total(group, chip):
        return functools.reduce(jnp.add, [counts[group][chip * adapters + a] for a in range(adapters)])

    listed = jnp.broadcast_to(sorted_ref[...], (8, rows))
    slot = lax.broadcasted_iota(jnp.int32, (8, most), 1)
    start = jnp.int32(0)
    for chip in range(chips):
        turned = pltpu.roll(listed, (rows - start) % rows, 1)
        held_ref[chip : chip + 1, :] = jnp.where(slot < total(0, chip), turned[:, :most], -1)[0:1]
        start += total(0, chip)
    largest = functools.reduce(
        jnp.maximum, [total(group, chip) for group in range(len(counts)) for chip in range(chips)]
    )
    choice_ref[0] = functools.reduce(jnp.add, [(largest > size).astype(jnp.int32) for size in sizes[:-1]])


def down_copies(core, own_down_ref, other_down_ref, down_vmem, sems):
    ranks = own_down_ref.shape[0]
    return [
        pltpu.make_async_copy(ref, down_vmem.at[pl.ds(pl.multiple_of(where * ranks, ranks), ranks)], sems.at[i])
        for i, (ref, where) in enumerate(((own_down_ref, core), (other_down_ref, 1 - core)))
    ]


def shrink_near_kernel(sizes, places, groups, me, *refs):
    counts, refs = refs[:groups], refs[groups:]
    sorted_ref, own_down_ref, other_down_ref = refs[:3]
    refs = refs[3:]
    piece_refs = refs[: len(places)]
    tokens_ref, shrunk_ref, held_ref, choice_ref, tokens_vmem, down_vmem, sems = refs[len(places) :]
    chips = held_ref.shape[0]
    copies = down_copies(me[0] % CORES, own_down_ref, other_down_ref, down_vmem, sems)
    for ref, (column, distance) in zip(piece_refs, places):
        rows, width = ref.shape
        start = pl.multiple_of(ring_chip(me[0], chips, distance) * rows, rows)
        copies.append(
            pltpu.make_async_copy(
                ref, tokens_vmem.at[pl.ds(start, rows), pl.ds(column, width)], sems.at[len(copies)]
            )
        )
    for copy in copies:
        copy.start()
    make_plan(sizes, counts, sorted_ref, held_ref, choice_ref)
    for copy in copies:
        copy.wait()
    out_copy = pltpu.make_async_copy(tokens_vmem, tokens_ref, sems.at[len(copies)])
    out_copy.start()
    shrunk_ref[...] = lax.dot_general(
        tokens_vmem[...], down_vmem[...], (((1,), (1,)), ((), ())), preferred_element_type=jnp.float32
    ).astype(shrunk_ref.dtype)
    out_copy.wait()


def shrink_far_kernel(places, me, tokens_in, shrunk_in, own_down_ref, other_down_ref, *refs):
    piece_refs = refs[: len(places)]
    tokens_ref, shrunk_ref, far_vmem, down_vmem, sems = refs[len(places) :]
    rows, half = piece_refs[0].shape
    chips = tokens_in.shape[0] // rows
    slots = {distance % chips: i for i, distance in enumerate(range(chips // 2 - 1, chips // 2 + 2))}
    copies = down_copies(me[0] % CORES, own_down_ref, other_down_ref, down_vmem, sems)
    copies.append(pltpu.make_async_copy(shrunk_in, shrunk_ref, sems.at[2]))
    for ref, (column, distance) in zip(piece_refs, places):
        slot = slots[distance % chips]
        copies.append(
            pltpu.make_async_copy(
                ref, far_vmem.at[pl.ds(slot * rows, rows), pl.ds(column, half)], sems.at[len(copies)]
            )
        )
    run_copies(copies)
    starts = [pl.multiple_of(ring_chip(me[0], chips, distance) * rows, rows) for distance in slots]
    out_copies = [
        pltpu.make_async_copy(
            far_vmem.at[pl.ds(i * rows, rows)], tokens_ref.at[pl.ds(start, rows)], sems.at[len(copies) + i]
        )
        for i, start in enumerate(starts)
    ]
    for copy in out_copies:
        copy.start()
    shrunk = lax.dot_general(
        far_vmem[...], down_vmem[...], (((1,), (1,)), ((), ())), preferred_element_type=jnp.float32
    ).astype(shrunk_ref.dtype)
    for i, start in enumerate(starts):
        shrunk_ref[pl.ds(start, rows), :] = shrunk[i * rows : (i + 1) * rows]
    for copy in out_copies:
        copy.wait()


def shrink(me, counts, sorted_rows, pieces, own_down, other_down, sizes):
    ranks, width = own_down.shape
    rows_all = sorted_rows.shape[0]
    rows = rows_all // CORES
    values = [value for value, _, _ in pieces]
    near = values[:-6]
    block = values[0].shape[0]
    tokens_shape = pltpu.HBM((rows, width), jnp.bfloat16)
    shrunk_shape = jax.ShapeDtypeStruct((rows, CORES * ranks), jnp.bfloat16)
    held_shape = jax.ShapeDtypeStruct((rows // block, sizes[-1]), jnp.int32)

    def whole(shape):
        return pl.BlockSpec(shape, lambda i, *_: (0, 0))

    down_vmem = pltpu.VMEM((CORES * ranks, width), jnp.bfloat16)
    downs = in_hbm([own_down]) + [other_down]
    tokens, shrunk, held, choice = pl.pallas_call(
        functools.partial(shrink_near_kernel, sizes, [place[1:] for place in pieces[:-6]], len(counts)),
        grid_spec=pltpu.PrefetchScalarGridSpec(
            num_scalar_prefetch=1 + len(counts),
            grid=(1,),
            in_specs=[whole((1, rows_all))] + [ANY_SPEC] * (2 + len(near)),
            out_specs=[
                ANY_SPEC,
                whole(shrunk_shape.shape),
                whole(held_shape.shape),
                pl.BlockSpec(memory_space=pltpu.SMEM),
            ],
            scratch_shapes=[
                pltpu.VMEM((rows, width), jnp.bfloat16),
                down_vmem,
                pltpu.SemaphoreType.DMA((3 + len(near),)),
            ],
        ),
        out_shape=[tokens_shape, shrunk_shape, held_shape, jax.ShapeDtypeStruct((1,), jnp.int32)],
        compiler_params=pltpu.CompilerParams(vmem_limit_bytes=rows * width * 2 + 16 * MIB),
        name="shrink_near",
    )(me, *counts, *in_hbm([sorted_rows.reshape(1, rows_all)]), *downs, *in_hbm(near[:1]), *near[1:])
    tokens, shrunk = pl.pallas_call(
        functools.partial(shrink_far_kernel, [place[1:] for place in pieces[-6:]]),
        grid_spec=pltpu.PrefetchScalarGridSpec(
            num_scalar_prefetch=1,
            grid=(1,),
            in_specs=[ANY_SPEC] * 10,
            out_specs=[ANY_SPEC, whole(shrunk_shape.shape)],
            scratch_shapes=[
                pltpu.VMEM((3 * block, width), jnp.bfloat16),
                down_vmem,
                pltpu.SemaphoreType.DMA((12,)),
            ],
        ),
        out_shape=[tokens_shape, shrunk_shape],
        input_output_aliases={1: 0},
        compiler_params=pltpu.CompilerParams(vmem_limit_bytes=16 * MIB),
        name="shrink_far",
    )(me, *in_hbm([tokens]), shrunk, *downs, *values[-6:])
    return tokens, shrunk, held, choice


def expand_kernel(order, block, counts, me, held_hbm, own_hbm, other_hbm, keep_ref, got_ref, out_ref, *scratch):
    held_ref, own_ref, other_ref, maps_vmem, out_vmem, sems = scratch
    chips, most = held_ref.shape
    slots = out_vmem.shape[0] // chips
    units = out_vmem.shape[1]
    ranks = keep_ref.shape[0]
    adapters = counts.shape[0] // chips
    chip = me[0] // CORES
    core = me[0] % CORES
    copies = []
    for c in range(chips):
        start = pl.multiple_of((order[c] * CORES + core) * units, units)
        for ref, where in ((keep_ref, core), (got_ref, 1 - core)):
            copies.append(
                pltpu.make_async_copy(
                    ref.at[:, pl.ds(start, units)],
                    maps_vmem.at[c, pl.ds(pl.multiple_of(where * ranks, ranks), ranks)],
                    sems.at[len(copies)],
                )
            )
    small = [
        pltpu.make_async_copy(ref, held, sems.at[3 * chips + i])
        for i, (ref, held) in enumerate(((held_hbm, held_ref), (own_hbm, own_ref), (other_hbm, other_ref)))
    ]
    for copy in small + copies:
        copy.start()
    for copy in small:
        copy.wait()

    wanted = held_ref[pl.ds(chip, 1), :]
    index = lax.broadcasted_iota(jnp.int32, (own_ref.shape[0], most), 0)
    row = index // block * (CORES * block) + index % block
    picked = jnp.zeros((most, own_ref.shape[1]), jnp.float32)
    for ref, where in ((own_ref, core), (other_ref, 1 - core)):
        hit = (row + where * block == wanted).astype(jnp.float32).astype(jnp.bfloat16)
        picked += lax.dot_general(hit, ref[...], (((0,), (0,)), ((), ())), preferred_element_type=jnp.float32)
    slot = lax.broadcasted_iota(jnp.int32, picked.shape, 0)
    adapter = lax.broadcasted_iota(jnp.int32, picked.shape, 1) // (picked.shape[1] // adapters)
    mine = jnp.zeros(picked.shape, jnp.int32)
    first = jnp.int32(0)
    for a in range(adapters):
        end = first + counts[chip * adapters + a]
        mine += ((adapter == a) & (slot >= first) & (slot < end)).astype(jnp.int32)
        first = end
    shrunk = jnp.where(mine > 0, ADAPTER_SCALE * picked, 0.0)[:slots].astype(jnp.bfloat16)

    out_copies = []
    for c in range(0, chips, 2):
        products = []
        for i in (c, c + 1):
            copies[2 * i].wait()
            copies[2 * i + 1].wait()
            products.append(jnp.dot(shrunk, maps_vmem[i], preferred_element_type=jnp.float32))
        part = pl.ds(c * slots, 2 * slots)
        out_vmem[part, :] = jnp.concatenate(products, axis=0).astype(out_vmem.dtype)
        out_copies.append(pltpu.make_async_copy(out_vmem.at[part], out_ref.at[part], sems.at[2 * chips + c]))
        out_copies[-1].start()
    for copy in out_copies:
        copy.wait()


def expand(counts, me, held, own_shrunk, other_shrunk, keep, got, order, slots, block):
    ranks, columns = keep.shape
    chips, most = held.shape
    units = columns // chips // CORES
    rows, ranks_all = own_shrunk.shape
    return pl.pallas_call(
        functools.partial(expand_kernel, order, block),
        grid_spec=pltpu.PrefetchScalarGridSpec(
            num_scalar_prefetch=2,
            grid=(1,),
            in_specs=[ANY_SPEC] * 5,
            out_specs=ANY_SPEC,
            scratch_shapes=[
                pltpu.VMEM((chips, most), jnp.int32),
                pltpu.VMEM((rows, ranks_all), jnp.bfloat16),
                pltpu.VMEM((rows, ranks_all), jnp.bfloat16),
                pltpu.VMEM((chips, ranks_all, units), jnp.bfloat16),
                pltpu.VMEM((chips * slots, units), jnp.bfloat16),
                pltpu.SemaphoreType.DMA((3 * chips + 3,)),
            ],
        ),
        out_shape=pltpu.HBM((chips * slots, units), jnp.bfloat16),
        compiler_params=pltpu.CompilerParams(vmem_limit_bytes=16 * MIB),
        cost_estimate=pl.CostEstimate(
            flops=2 * slots * ranks_all * chips * units,
            bytes_accessed=2 * (slots + ranks_all) * chips * units,
            transcendentals=0,
        ),
        name="expand",
    )(counts, me, held, own_shrunk, other_shrunk, *in_hbm([keep, got]))


def project_kernel(block, me, gate_weight_ref, up_weight_ref, own_ref, other_ref, gate_ref, up_ref, tokens_vmem, sems):
    depth = gate_weight_ref.shape[0]
    core = me[0] % CORES
    k = pl.program_id(0)

    @pl.when(k == 0)
    def _():
        copies = []
        for ref, where in ((own_ref, core), (other_ref, 1 - core)):
            for chip in range(ref.shape[0] // block):
                start = pl.multiple_of((chip * CORES + where) * block, block)
                copies.append(
                    pltpu.make_async_copy(
                        ref.at[pl.ds(chip * block, block)], tokens_vmem.at[pl.ds(start, block)], sems.at[len(copies)]
                    )
                )
        run_copies(copies)
        gate_ref[...] = jnp.zeros_like(gate_ref)
        up_ref[...] = jnp.zeros_like(up_ref)

    tokens = tokens_vmem[:, pl.ds(pl.multiple_of(k * depth, depth), depth)]
    gate_ref[...] += jnp.dot(tokens, gate_weight_ref[...], preferred_element_type=jnp.float32)
    up_ref[...] += jnp.dot(tokens, up_weight_ref[...], preferred_element_type=jnp.float32)

    @pl.when(k == pl.num_programs(0) - 1)
    def _():
        gate = gate_ref[...]
        gate_ref[...] = gate / (1.0 + jnp.exp(-gate))


def project(me, own, other, gate_weight, up_weight, block):
    width, units = gate_weight.shape
    rows = CORES * own.shape[0]
    depth = min(1024, width)
    weight_spec = pl.BlockSpec((depth, units), lambda k, s: (k, 0))
    out_spec = pl.BlockSpec((rows, units), lambda k, s: (0, 0))
    out = pltpu.HBM((rows, units), jnp.float32)
    return pl.pallas_call(
        functools.partial(project_kernel, block),
        grid_spec=pltpu.PrefetchScalarGridSpec(
            num_scalar_prefetch=1,
            grid=(width // depth,),
            in_specs=[weight_spec, weight_spec, ANY_SPEC, ANY_SPEC],
            out_specs=[out_spec, out_spec],
            scratch_shapes=[
                pltpu.VMEM((rows, width), jnp.bfloat16),
                pltpu.SemaphoreType.DMA((rows // block,)),
            ],
        ),
        out_shape=[out, out],
        compiler_params=pltpu.CompilerParams(vmem_limit_bytes=rows * width * 2 + 20 * MIB),
        cost_estimate=pl.CostEstimate(
            flops=4 * rows * width * units,
            bytes_accessed=2 * (rows + 2 * units) * width,
            transcendentals=rows * units,
        ),
        name="project",
    )(me, *in_hbm([gate_weight, up_weight, own, other]))


def combine_kernel(pick_ref, gate_ref, up_ref, products_ref, out_ref):
    delta = jnp.dot(pick_ref[...], products_ref[...], preferred_element_type=jnp.float32)
    out_ref[...] = (gate_ref[...] * (up_ref[...] + delta)).astype(out_ref.dtype)


def combine(pick, gate, up, products):
    rows, units = gate.shape
    slots_all = products.shape[0]
    tile = min(512, units)
    column_spec = pl.BlockSpec((rows, tile), lambda n: (0, n))
    return pl.pallas_call(
        combine_kernel,
        grid=(units // tile,),
        in_specs=[
            pl.BlockSpec((rows, slots_all), lambda n: (0, 0)),
            column_spec,
            column_spec,
            pl.BlockSpec((slots_all, tile), lambda n: (0, n)),
        ],
        out_specs=column_spec,
        out_shape=pltpu.HBM((rows, units), jnp.bfloat16),
        compiler_params=pltpu.CompilerParams(vmem_limit_bytes=rows * slots_all * 4 + 20 * MIB),
        cost_estimate=pl.CostEstimate(
            flops=2 * rows * slots_all * units, bytes_accessed=10 * rows * units, transcendentals=0
        ),
        name="combine",
    )(*in_hbm([pick, gate, up]), products)


def per_device(
    tokens,
    gate_weight,
    up_weight,
    adapter_down_weight,
    adapter_up_weight,
    row_adapter,
    sorted_rows,
    segment_count,
):
    axis = "tensor"
    size = lax.axis_size(axis)
    me = lax.axis_index(axis).astype(jnp.int32)
    chips = size // CORES
    resident, rank, width = adapter_down_weight.shape
    ranks = resident * rank
    rows = row_adapter.shape[0]
    block = tokens.shape[0]
    me_array = me.reshape(1)
    flips = [(d, d ^ 1) for d in range(size)]

    def other_core(value):
        return lax.ppermute(value, axis, flips)

    most = CORES * resident * ROWS_PER_LIMIT
    sizes = [slots for slots in SLOT_SIZES if slots < most] + [most]
    groups = lax.axis_size("groups")
    own_down = adapter_down_weight.reshape(ranks, width)
    own_maps = adapter_up_weight.reshape(ranks, -1)
    other_down = other_core(own_down)
    counts = [segment_count] + [
        lax.ppermute(segment_count, "groups", [(g, (g + shift) % groups) for g in range(groups)])
        for shift in range(1, groups)
    ]
    other_maps = other_core(own_maps)

    def beside(step, values):
        nonlocal other_down, counts, other_maps
        if step == 1:
            other_down, counts, values[0], values[1] = lax.optimization_barrier((other_down, counts, *values))
        return values

    pieces = ring_gather(tokens, axis, beside)
    own_tokens, own_shrunk, held, choice = shrink(
        me_array, counts, sorted_rows, pieces, own_down, other_down, sizes
    )
    other_shrunk = other_core(own_shrunk)

    order = [half * (chips // 2) + c for c in range(chips // 2) for half in range(2)]
    same_core = [[c * CORES + k for c in order] for k in range(CORES)]

    def finish(slots):
        def branch(own_tokens, own_shrunk, other_shrunk, own_maps, other_maps, held, gate_weight, up_weight):
            products = expand(
                segment_count, me_array, held, own_shrunk, other_shrunk, own_maps, other_maps, order, slots, block
            )
            products = lax.all_to_all(
                products, axis, split_axis=0, concat_axis=0, axis_index_groups=same_core, tiled=True
            )
            held, other_tokens = lax.optimization_barrier((held, other_core(own_tokens)))
            held_rows = jnp.stack([held[c, :slots] for c in order]).reshape(1, chips * slots)
            pick = (jnp.arange(rows, dtype=jnp.int32)[:, None] == held_rows).astype(jnp.bfloat16)
            pick, other_tokens = lax.optimization_barrier((pick, other_tokens))
            gate, up = project(me_array, own_tokens, other_tokens, gate_weight, up_weight, block)
            return combine(pick, gate, up, products)

        return branch

    return lax.switch(
        choice[0],
        [finish(slots) for slots in sizes],
        own_tokens,
        own_shrunk,
        other_shrunk,
        own_maps,
        other_maps,
        held,
        gate_weight,
        up_weight,
    )


def solution(mesh):
    placed = (
        P(("groups", "tensor"), None),
        P(None, "tensor"),
        P(None, "tensor"),
        P(("groups", "tensor"), None, None),
        P(("groups", "tensor"), None, None),
        P("groups"),
        P("groups"),
        P("groups"),
    )
    return jax.shard_map(
        per_device, mesh=mesh, in_specs=placed, out_specs=P("groups", "tensor"), check_vma=False
    )
```

```python
import functools

import jax
import jax.numpy as jnp
from jax import lax
from jax.experimental import pallas as pl
from jax.experimental.pallas import tpu as pltpu
from jax.sharding import PartitionSpec as P

ADAPTER_SCALE = 0.5
ROWS_PER_LIMIT = 64
SLOT_SIZES = (72, 80, 88, 104)
CORES = 2
MIB = 1024 * 1024


def chip_ring(chips):
    return list(range(0, chips, 2)) + list(range(chips - 1, 0, -2))


def ring_chip(me, chips, distance):
    chip = me // CORES
    place = jnp.where(chip % 2 == 0, chip // 2, chips // 2 + (chips - 1 - chip) // 2)
    place = (place + distance * (1 - 2 * (me % CORES)) + chips) % chips
    return jnp.where(place < chips // 2, 2 * place, chips - 1 - 2 * (place - chips // 2))


def ring_gather(block, axis, beside):
    size = lax.axis_size(axis)
    chips = size // CORES
    ring = chip_ring(chips)

    def moved(value, shift):
        pairs = [
            (ring[p] * CORES + k, ring[(p + shift * (1 - 2 * k)) % chips] * CORES + k)
            for p in range(chips)
            for k in range(CORES)
        ]
        return lax.ppermute(value, axis, pairs)

    right, left = moved(block, 1), moved(block, -1)
    pieces = [(block, 0, 0), (right, 0, -1), (left, 0, 1)]
    half = block.shape[1] // 2
    far = chips // 2
    columns = (0, half), (half, 0)
    held = [(right[:, a : a + half], left[:, b : b + half]) for a, b in columns]
    held = beside(1, held)
    for step in range(2, far + 1):
        for chain in range(1 if step == far else 2):
            right, left = held[chain]
            held[chain] = moved(right, 1), moved(left, -1)
            for value, column, distance in zip(held[chain], columns[chain], (-step, step)):
                pieces.append((value, column, distance))
        held = beside(step, held)
    return pieces


ANY_SPEC = pl.BlockSpec(memory_space=pl.ANY)


def in_hbm(values):
    return [pltpu.with_memory_space_constraint(value, pltpu.HBM) for value in values]


def run_copies(copies):
    for copy in copies:
        copy.start()
    for copy in copies:
        copy.wait()


def make_plan(sizes, counts, sorted_ref, held_ref, choice_ref):
    chips, most = held_ref.shape
    rows = sorted_ref.shape[1]
    adapters = counts[0].shape[0] // chips

    def total(group, chip):
        return functools.reduce(jnp.add, [counts[group][chip * adapters + a] for a in range(adapters)])

    listed = jnp.broadcast_to(sorted_ref[...], (8, rows))
    slot = lax.broadcasted_iota(jnp.int32, (8, most), 1)
    start = jnp.int32(0)
    for chip in range(chips):
        turned = pltpu.roll(listed, (rows - start) % rows, 1)
        held_ref[chip : chip + 1, :] = jnp.where(slot < total(0, chip), turned[:, :most], -1)[0:1]
        start += total(0, chip)
    largest = functools.reduce(
        jnp.maximum, [total(group, chip) for group in range(len(counts)) for chip in range(chips)]
    )
    choice_ref[0] = functools.reduce(jnp.add, [(largest > size).astype(jnp.int32) for size in sizes[:-1]])


def down_copies(core, own_down_ref, other_down_ref, down_vmem, sems):
    ranks = own_down_ref.shape[0]
    return [
        pltpu.make_async_copy(ref, down_vmem.at[pl.ds(pl.multiple_of(where * ranks, ranks), ranks)], sems.at[i])
        for i, (ref, where) in enumerate(((own_down_ref, core), (other_down_ref, 1 - core)))
    ]


def shrink_near_kernel(sizes, places, groups, me, *refs):
    counts, refs = refs[:groups], refs[groups:]
    sorted_ref, own_down_ref, other_down_ref = refs[:3]
    refs = refs[3:]
    piece_refs = refs[: len(places)]
    tokens_ref, shrunk_ref, held_ref, choice_ref, tokens_vmem, down_vmem, sems = refs[len(places) :]
    chips = held_ref.shape[0]
    copies = down_copies(me[0] % CORES, own_down_ref, other_down_ref, down_vmem, sems)
    for ref, (column, distance) in zip(piece_refs, places):
        rows, width = ref.shape
        start = pl.multiple_of(ring_chip(me[0], chips, distance) * rows, rows)
        copies.append(
            pltpu.make_async_copy(
                ref, tokens_vmem.at[pl.ds(start, rows), pl.ds(column, width)], sems.at[len(copies)]
            )
        )
    for copy in copies:
        copy.start()
    make_plan(sizes, counts, sorted_ref, held_ref, choice_ref)
    for copy in copies:
        copy.wait()
    out_copy = pltpu.make_async_copy(tokens_vmem, tokens_ref, sems.at[len(copies)])
    out_copy.start()
    shrunk_ref[...] = lax.dot_general(
        tokens_vmem[...], down_vmem[...], (((1,), (1,)), ((), ())), preferred_element_type=jnp.float32
    ).astype(shrunk_ref.dtype)
    out_copy.wait()


def shrink_far_kernel(places, me, tokens_in, shrunk_in, own_down_ref, other_down_ref, *refs):
    piece_refs = refs[: len(places)]
    tokens_ref, shrunk_ref, far_vmem, down_vmem, sems = refs[len(places) :]
    rows, half = piece_refs[0].shape
    chips = tokens_in.shape[0] // rows
    slots = {distance % chips: i for i, distance in enumerate(range(chips // 2 - 1, chips // 2 + 2))}
    copies = down_copies(me[0] % CORES, own_down_ref, other_down_ref, down_vmem, sems)
    copies.append(pltpu.make_async_copy(shrunk_in, shrunk_ref, sems.at[2]))
    for ref, (column, distance) in zip(piece_refs, places):
        slot = slots[distance % chips]
        copies.append(
            pltpu.make_async_copy(
                ref, far_vmem.at[pl.ds(slot * rows, rows), pl.ds(column, half)], sems.at[len(copies)]
            )
        )
    run_copies(copies)
    starts = [pl.multiple_of(ring_chip(me[0], chips, distance) * rows, rows) for distance in slots]
    out_copies = [
        pltpu.make_async_copy(
            far_vmem.at[pl.ds(i * rows, rows)], tokens_ref.at[pl.ds(start, rows)], sems.at[len(copies) + i]
        )
        for i, start in enumerate(starts)
    ]
    for copy in out_copies:
        copy.start()
    shrunk = lax.dot_general(
        far_vmem[...], down_vmem[...], (((1,), (1,)), ((), ())), preferred_element_type=jnp.float32
    ).astype(shrunk_ref.dtype)
    for i, start in enumerate(starts):
        shrunk_ref[pl.ds(start, rows), :] = shrunk[i * rows : (i + 1) * rows]
    for copy in out_copies:
        copy.wait()


def shrink(me, counts, sorted_rows, pieces, own_down, other_down, sizes):
    ranks, width = own_down.shape
    rows_all = sorted_rows.shape[0]
    rows = rows_all // CORES
    values = [value for value, _, _ in pieces]
    near = values[:-6]
    block = values[0].shape[0]
    tokens_shape = pltpu.HBM((rows, width), jnp.bfloat16)
    shrunk_shape = jax.ShapeDtypeStruct((rows, CORES * ranks), jnp.bfloat16)
    held_shape = jax.ShapeDtypeStruct((rows // block, sizes[-1]), jnp.int32)

    def whole(shape):
        return pl.BlockSpec(shape, lambda i, *_: (0, 0))

    down_vmem = pltpu.VMEM((CORES * ranks, width), jnp.bfloat16)
    downs = in_hbm([own_down]) + [other_down]
    tokens, shrunk, held, choice = pl.pallas_call(
        functools.partial(shrink_near_kernel, sizes, [place[1:] for place in pieces[:-6]], len(counts)),
        grid_spec=pltpu.PrefetchScalarGridSpec(
            num_scalar_prefetch=1 + len(counts),
            grid=(1,),
            in_specs=[whole((1, rows_all))] + [ANY_SPEC] * (2 + len(near)),
            out_specs=[
                ANY_SPEC,
                whole(shrunk_shape.shape),
                whole(held_shape.shape),
                pl.BlockSpec(memory_space=pltpu.SMEM),
            ],
            scratch_shapes=[
                pltpu.VMEM((rows, width), jnp.bfloat16),
                down_vmem,
                pltpu.SemaphoreType.DMA((3 + len(near),)),
            ],
        ),
        out_shape=[tokens_shape, shrunk_shape, held_shape, jax.ShapeDtypeStruct((1,), jnp.int32)],
        compiler_params=pltpu.CompilerParams(vmem_limit_bytes=rows * width * 2 + 16 * MIB),
        name="shrink_near",
    )(me, *counts, *in_hbm([sorted_rows.reshape(1, rows_all)]), *downs, *in_hbm(near[:1]), *near[1:])
    tokens, shrunk = pl.pallas_call(
        functools.partial(shrink_far_kernel, [place[1:] for place in pieces[-6:]]),
        grid_spec=pltpu.PrefetchScalarGridSpec(
            num_scalar_prefetch=1,
            grid=(1,),
            in_specs=[ANY_SPEC] * 10,
            out_specs=[ANY_SPEC, whole(shrunk_shape.shape)],
            scratch_shapes=[
                pltpu.VMEM((3 * block, width), jnp.bfloat16),
                down_vmem,
                pltpu.SemaphoreType.DMA((12,)),
            ],
        ),
        out_shape=[tokens_shape, shrunk_shape],
        input_output_aliases={1: 0},
        compiler_params=pltpu.CompilerParams(vmem_limit_bytes=16 * MIB),
        name="shrink_far",
    )(me, *in_hbm([tokens]), shrunk, *downs, *values[-6:])
    return tokens, shrunk, held, choice


def expand_kernel(order, block, counts, me, held_hbm, own_hbm, other_hbm, keep_ref, got_ref, out_ref, *scratch):
    held_ref, own_ref, other_ref, maps_vmem, out_vmem, sems = scratch
    chips, most = held_ref.shape
    slots = out_vmem.shape[0] // chips
    units = out_vmem.shape[1]
    ranks = keep_ref.shape[0]
    adapters = counts.shape[0] // chips
    chip = me[0] // CORES
    core = me[0] % CORES
    copies = []
    for c in range(chips):
        start = pl.multiple_of((order[c] * CORES + core) * units, units)
        for ref, where in ((keep_ref, core), (got_ref, 1 - core)):
            copies.append(
                pltpu.make_async_copy(
                    ref.at[:, pl.ds(start, units)],
                    maps_vmem.at[c, pl.ds(pl.multiple_of(where * ranks, ranks), ranks)],
                    sems.at[len(copies)],
                )
            )
    small = [
        pltpu.make_async_copy(ref, held, sems.at[3 * chips + i])
        for i, (ref, held) in enumerate(((held_hbm, held_ref), (own_hbm, own_ref), (other_hbm, other_ref)))
    ]
    for copy in small + copies:
        copy.start()
    for copy in small:
        copy.wait()

    wanted = held_ref[pl.ds(chip, 1), :]
    index = lax.broadcasted_iota(jnp.int32, (own_ref.shape[0], most), 0)
    row = index // block * (CORES * block) + index % block
    picked = jnp.zeros((most, own_ref.shape[1]), jnp.float32)
    for ref, where in ((own_ref, core), (other_ref, 1 - core)):
        hit = (row + where * block == wanted).astype(jnp.float32).astype(jnp.bfloat16)
        picked += lax.dot_general(hit, ref[...], (((0,), (0,)), ((), ())), preferred_element_type=jnp.float32)
    slot = lax.broadcasted_iota(jnp.int32, picked.shape, 0)
    adapter = lax.broadcasted_iota(jnp.int32, picked.shape, 1) // (picked.shape[1] // adapters)
    mine = jnp.zeros(picked.shape, jnp.int32)
    first = jnp.int32(0)
    for a in range(adapters):
        end = first + counts[chip * adapters + a]
        mine += ((adapter == a) & (slot >= first) & (slot < end)).astype(jnp.int32)
        first = end
    shrunk = jnp.where(mine > 0, ADAPTER_SCALE * picked, 0.0)[:slots].astype(jnp.bfloat16)

    out_copies = []
    for c in range(0, chips, 2):
        products = []
        for i in (c, c + 1):
            copies[2 * i].wait()
            copies[2 * i + 1].wait()
            products.append(jnp.dot(shrunk, maps_vmem[i], preferred_element_type=jnp.float32))
        part = pl.ds(c * slots, 2 * slots)
        out_vmem[part, :] = jnp.concatenate(products, axis=0).astype(out_vmem.dtype)
        out_copies.append(pltpu.make_async_copy(out_vmem.at[part], out_ref.at[part], sems.at[2 * chips + c]))
        out_copies[-1].start()
    for copy in out_copies:
        copy.wait()


def expand(counts, me, held, own_shrunk, other_shrunk, keep, got, order, slots, block):
    ranks, columns = keep.shape
    chips, most = held.shape
    units = columns // chips // CORES
    rows, ranks_all = own_shrunk.shape
    return pl.pallas_call(
        functools.partial(expand_kernel, order, block),
        grid_spec=pltpu.PrefetchScalarGridSpec(
            num_scalar_prefetch=2,
            grid=(1,),
            in_specs=[ANY_SPEC] * 5,
            out_specs=ANY_SPEC,
            scratch_shapes=[
                pltpu.VMEM((chips, most), jnp.int32),
                pltpu.VMEM((rows, ranks_all), jnp.bfloat16),
                pltpu.VMEM((rows, ranks_all), jnp.bfloat16),
                pltpu.VMEM((chips, ranks_all, units), jnp.bfloat16),
                pltpu.VMEM((chips * slots, units), jnp.bfloat16),
                pltpu.SemaphoreType.DMA((3 * chips + 3,)),
            ],
        ),
        out_shape=pltpu.HBM((chips * slots, units), jnp.bfloat16),
        compiler_params=pltpu.CompilerParams(vmem_limit_bytes=16 * MIB),
        cost_estimate=pl.CostEstimate(
            flops=2 * slots * ranks_all * chips * units,
            bytes_accessed=2 * (slots + ranks_all) * chips * units,
            transcendentals=0,
        ),
        name="expand",
    )(counts, me, held, own_shrunk, other_shrunk, *in_hbm([keep, got]))


def project_kernel(block, me, gate_weight_ref, up_weight_ref, own_ref, other_ref, gate_ref, up_ref, tokens_vmem, sems):
    depth = gate_weight_ref.shape[0]
    core = me[0] % CORES
    k = pl.program_id(0)

    @pl.when(k == 0)
    def _():
        copies = []
        for ref, where in ((own_ref, core), (other_ref, 1 - core)):
            for chip in range(ref.shape[0] // block):
                start = pl.multiple_of((chip * CORES + where) * block, block)
                copies.append(
                    pltpu.make_async_copy(
                        ref.at[pl.ds(chip * block, block)], tokens_vmem.at[pl.ds(start, block)], sems.at[len(copies)]
                    )
                )
        run_copies(copies)
        gate_ref[...] = jnp.zeros_like(gate_ref)
        up_ref[...] = jnp.zeros_like(up_ref)

    tokens = tokens_vmem[:, pl.ds(pl.multiple_of(k * depth, depth), depth)]
    gate_ref[...] += jnp.dot(tokens, gate_weight_ref[...], preferred_element_type=jnp.float32)
    up_ref[...] += jnp.dot(tokens, up_weight_ref[...], preferred_element_type=jnp.float32)

    @pl.when(k == pl.num_programs(0) - 1)
    def _():
        gate = gate_ref[...]
        gate_ref[...] = gate / (1.0 + jnp.exp(-gate))


def project(me, own, other, gate_weight, up_weight, block):
    width, units = gate_weight.shape
    rows = CORES * own.shape[0]
    depth = min(1024, width)
    weight_spec = pl.BlockSpec((depth, units), lambda k, s: (k, 0))
    out_spec = pl.BlockSpec((rows, units), lambda k, s: (0, 0))
    out = pltpu.HBM((rows, units), jnp.float32)
    return pl.pallas_call(
        functools.partial(project_kernel, block),
        grid_spec=pltpu.PrefetchScalarGridSpec(
            num_scalar_prefetch=1,
            grid=(width // depth,),
            in_specs=[weight_spec, weight_spec, ANY_SPEC, ANY_SPEC],
            out_specs=[out_spec, out_spec],
            scratch_shapes=[
                pltpu.VMEM((rows, width), jnp.bfloat16),
                pltpu.SemaphoreType.DMA((rows // block,)),
            ],
        ),
        out_shape=[out, out],
        compiler_params=pltpu.CompilerParams(vmem_limit_bytes=rows * width * 2 + 20 * MIB),
        cost_estimate=pl.CostEstimate(
            flops=4 * rows * width * units,
            bytes_accessed=2 * (rows + 2 * units) * width,
            transcendentals=rows * units,
        ),
        name="project",
    )(me, *in_hbm([gate_weight, up_weight, own, other]))


def combine_kernel(pick_ref, gate_ref, up_ref, products_ref, out_ref):
    delta = jnp.dot(pick_ref[...], products_ref[...], preferred_element_type=jnp.float32)
    out_ref[...] = (gate_ref[...] * (up_ref[...] + delta)).astype(out_ref.dtype)


def combine(pick, gate, up, products):
    rows, units = gate.shape
    slots_all = products.shape[0]
    tile = min(512, units)
    column_spec = pl.BlockSpec((rows, tile), lambda n: (0, n))
    return pl.pallas_call(
        combine_kernel,
        grid=(units // tile,),
        in_specs=[
            pl.BlockSpec((rows, slots_all), lambda n: (0, 0)),
            column_spec,
            column_spec,
            pl.BlockSpec((slots_all, tile), lambda n: (0, n)),
        ],
        out_specs=column_spec,
        out_shape=pltpu.HBM((rows, units), jnp.bfloat16),
        compiler_params=pltpu.CompilerParams(vmem_limit_bytes=rows * slots_all * 4 + 20 * MIB),
        cost_estimate=pl.CostEstimate(
            flops=2 * rows * slots_all * units, bytes_accessed=10 * rows * units, transcendentals=0
        ),
        name="combine",
    )(*in_hbm([pick, gate, up]), products)


def per_device(
    tokens,
    gate_weight,
    up_weight,
    adapter_down_weight,
    adapter_up_weight,
    row_adapter,
    sorted_rows,
    segment_count,
):
    axis = "tensor"
    size = lax.axis_size(axis)
    me = lax.axis_index(axis).astype(jnp.int32)
    chips = size // CORES
    resident, rank, width = adapter_down_weight.shape
    ranks = resident * rank
    rows = row_adapter.shape[0]
    block = tokens.shape[0]
    me_array = me.reshape(1)
    flips = [(d, d ^ 1) for d in range(size)]

    def other_core(value):
        return lax.ppermute(value, axis, flips)

    most = CORES * resident * ROWS_PER_LIMIT
    sizes = [slots for slots in SLOT_SIZES if slots < most] + [most]
    groups = lax.axis_size("groups")
    own_down = adapter_down_weight.reshape(ranks, width)
    own_maps = adapter_up_weight.reshape(ranks, -1)
    other_down = other_core(own_down)
    counts = [segment_count] + [
        lax.ppermute(segment_count, "groups", [(g, (g + shift) % groups) for g in range(groups)])
        for shift in range(1, groups)
    ]
    other_maps = other_core(own_maps)

    def beside(step, values):
        nonlocal other_down, counts, other_maps
        if step == 1:
            other_down, counts, values[0], values[1] = lax.optimization_barrier((other_down, counts, *values))
        return values

    pieces = ring_gather(tokens, axis, beside)
    own_tokens, own_shrunk, held, choice = shrink(
        me_array, counts, sorted_rows, pieces, own_down, other_down, sizes
    )
    other_shrunk = other_core(own_shrunk)

    order = [half * (chips // 2) + c for c in range(chips // 2) for half in range(2)]
    same_core = [[c * CORES + k for c in order] for k in range(CORES)]

    def finish(slots):
        def branch(own_tokens, own_shrunk, other_shrunk, own_maps, other_maps, held, gate_weight, up_weight):
            products = expand(
                segment_count, me_array, held, own_shrunk, other_shrunk, own_maps, other_maps, order, slots, block
            )
            products = lax.all_to_all(
                products, axis, split_axis=0, concat_axis=0, axis_index_groups=same_core, tiled=True
            )
            held, other_tokens = lax.optimization_barrier((held, other_core(own_tokens)))
            held_rows = jnp.stack([held[c, :slots] for c in order]).reshape(1, chips * slots)
            pick = (jnp.arange(rows, dtype=jnp.int32)[:, None] == held_rows).astype(jnp.bfloat16)
            pick, other_tokens = lax.optimization_barrier((pick, other_tokens))
            gate, up = project(me_array, own_tokens, other_tokens, gate_weight, up_weight, block)
            return combine(pick, gate, up, products)

        return branch

    return lax.switch(
        choice[0],
        [finish(slots) for slots in sizes],
        own_tokens,
        own_shrunk,
        other_shrunk,
        own_maps,
        other_maps,
        held,
        gate_weight,
        up_weight,
    )


def solution(mesh):
    placed = (
        P(("groups", "tensor"), None),
        P(None, "tensor"),
        P(None, "tensor"),
        P(("groups", "tensor"), None, None),
        P(("groups", "tensor"), None, None),
        P("groups"),
        P("groups"),
        P("groups"),
    )
    return jax.shard_map(
        per_device, mesh=mesh, in_specs=placed, out_specs=P("groups", "tensor"), check_vma=False
    )
```

```python
import functools

import jax
import jax.numpy as jnp
from jax import lax
from jax.experimental import pallas as pl
from jax.experimental.pallas import tpu as pltpu
from jax.sharding import PartitionSpec as P

ADAPTER_SCALE = 0.5
ROWS_PER_LIMIT = 64
SLOT_SIZES = (72, 80, 88, 104)
CORES = 2
MIB = 1024 * 1024


def chip_ring(chips):
    return list(range(0, chips, 2)) + list(range(chips - 1, 0, -2))


def ring_chip(me, chips, distance):
    chip = me // CORES
    place = jnp.where(chip % 2 == 0, chip // 2, chips // 2 + (chips - 1 - chip) // 2)
    place = (place + distance + chips) % chips
    return jnp.where(place < chips // 2, 2 * place, chips - 1 - 2 * (place - chips // 2))


def ring_gather(block, axis, beside):
    size = lax.axis_size(axis)
    chips = size // CORES
    ring = chip_ring(chips)

    def moved(value, shift):
        pairs = [
            (ring[p] * CORES + k, ring[(p + shift) % chips] * CORES + k)
            for p in range(chips)
            for k in range(CORES)
        ]
        return lax.ppermute(value, axis, pairs)

    right, left = moved(block, 1), moved(block, -1)
    pieces = [(block, 0, 0), (right, 0, -1), (left, 0, 1)]
    half = block.shape[1] // 2
    far = chips // 2
    columns = (0, half), (half, 0)
    held = [(right[:, a : a + half], left[:, b : b + half]) for a, b in columns]
    held = beside(1, held)
    for step in range(2, far + 1):
        for chain in range(1 if step == far else 2):
            right, left = held[chain]
            held[chain] = moved(right, 1), moved(left, -1)
            for value, column, distance in zip(held[chain], columns[chain], (-step, step)):
                pieces.append((value, column, distance))
        held = beside(step, held)
    return pieces


ANY_SPEC = pl.BlockSpec(memory_space=pl.ANY)


def in_hbm(values):
    return [pltpu.with_memory_space_constraint(value, pltpu.HBM) for value in values]


def run_copies(copies):
    for copy in copies:
        copy.start()
    for copy in copies:
        copy.wait()


def make_plan(sizes, counts, sorted_ref, held_ref, choice_ref):
    chips, most = held_ref.shape
    rows = sorted_ref.shape[1]
    adapters = counts[0].shape[0] // chips

    def total(group, chip):
        return functools.reduce(jnp.add, [counts[group][chip * adapters + a] for a in range(adapters)])

    listed = jnp.broadcast_to(sorted_ref[...], (8, rows))
    slot = lax.broadcasted_iota(jnp.int32, (8, most), 1)
    start = jnp.int32(0)
    for chip in range(chips):
        turned = pltpu.roll(listed, (rows - start) % rows, 1)
        held_ref[chip : chip + 1, :] = jnp.where(slot < total(0, chip), turned[:, :most], -1)[0:1]
        start += total(0, chip)
    largest = functools.reduce(
        jnp.maximum, [total(group, chip) for group in range(len(counts)) for chip in range(chips)]
    )
    choice_ref[0] = functools.reduce(jnp.add, [(largest > size).astype(jnp.int32) for size in sizes[:-1]])


def down_copies(core, own_down_ref, other_down_ref, down_vmem, sems):
    ranks = own_down_ref.shape[0]
    return [
        pltpu.make_async_copy(ref, down_vmem.at[pl.ds(pl.multiple_of(where * ranks, ranks), ranks)], sems.at[i])
        for i, (ref, where) in enumerate(((own_down_ref, core), (other_down_ref, 1 - core)))
    ]


def shrink_near_kernel(sizes, places, groups, me, *refs):
    counts, refs = refs[:groups], refs[groups:]
    sorted_hbm, own_down_ref, other_down_ref = refs[:3]
    refs = refs[3:]
    piece_refs = refs[: len(places)]
    tokens_ref, shrunk_ref, held_ref, choice_ref, sorted_ref, tokens_vmem, down_vmem, sems = refs[len(places) :]
    chips = held_ref.shape[0]
    sorted_copy = pltpu.make_async_copy(sorted_hbm, sorted_ref, sems.at[3 + len(places)])
    sorted_copy.start()
    copies = down_copies(me[0] % CORES, own_down_ref, other_down_ref, down_vmem, sems)
    for ref, (column, distance) in zip(piece_refs, places):
        rows, width = ref.shape
        start = pl.multiple_of(ring_chip(me[0], chips, distance) * rows, rows)
        copies.append(
            pltpu.make_async_copy(
                ref, tokens_vmem.at[pl.ds(start, rows), pl.ds(column, width)], sems.at[len(copies)]
            )
        )
    for copy in copies:
        copy.start()
    sorted_copy.wait()
    make_plan(sizes, counts, sorted_ref, held_ref, choice_ref)
    for copy in copies:
        copy.wait()
    out_copy = pltpu.make_async_copy(tokens_vmem, tokens_ref, sems.at[len(copies)])
    out_copy.start()
    shrunk_ref[...] = lax.dot_general(
        tokens_vmem[...], down_vmem[...], (((1,), (1,)), ((), ())), preferred_element_type=jnp.float32
    ).astype(shrunk_ref.dtype)
    out_copy.wait()


def shrink_far_kernel(places, me, tokens_in, shrunk_in, own_down_ref, other_down_ref, *refs):
    piece_refs = refs[: len(places)]
    tokens_ref, shrunk_ref, far_vmem, down_vmem, sems = refs[len(places) :]
    rows, half = piece_refs[0].shape
    chips = tokens_in.shape[0] // rows
    slots = {distance % chips: i for i, distance in enumerate(range(chips // 2 - 1, chips // 2 + 2))}
    copies = down_copies(me[0] % CORES, own_down_ref, other_down_ref, down_vmem, sems)
    copies.append(pltpu.make_async_copy(shrunk_in, shrunk_ref, sems.at[2]))
    for ref, (column, distance) in zip(piece_refs, places):
        slot = slots[distance % chips]
        copies.append(
            pltpu.make_async_copy(
                ref, far_vmem.at[pl.ds(slot * rows, rows), pl.ds(column, half)], sems.at[len(copies)]
            )
        )
    run_copies(copies)
    starts = [pl.multiple_of(ring_chip(me[0], chips, distance) * rows, rows) for distance in slots]
    out_copies = [
        pltpu.make_async_copy(
            far_vmem.at[pl.ds(i * rows, rows)], tokens_ref.at[pl.ds(start, rows)], sems.at[len(copies) + i]
        )
        for i, start in enumerate(starts)
    ]
    for copy in out_copies:
        copy.start()
    shrunk = lax.dot_general(
        far_vmem[...], down_vmem[...], (((1,), (1,)), ((), ())), preferred_element_type=jnp.float32
    ).astype(shrunk_ref.dtype)
    for i, start in enumerate(starts):
        shrunk_ref[pl.ds(start, rows), :] = shrunk[i * rows : (i + 1) * rows]
    for copy in out_copies:
        copy.wait()


def shrink(me, counts, sorted_rows, pieces, own_down, other_down, sizes):
    ranks, width = own_down.shape
    rows_all = sorted_rows.shape[0]
    rows = rows_all // CORES
    values = [value for value, _, _ in pieces]
    near = values[:-6]
    block = values[0].shape[0]
    tokens_shape = pltpu.HBM((rows, width), jnp.bfloat16)
    shrunk_shape = jax.ShapeDtypeStruct((rows, CORES * ranks), jnp.bfloat16)
    held_shape = jax.ShapeDtypeStruct((rows // block, sizes[-1]), jnp.int32)

    def whole(shape):
        return pl.BlockSpec(shape, lambda i, *_: (0, 0))

    down_vmem = pltpu.VMEM((CORES * ranks, width), jnp.bfloat16)
    downs = in_hbm([own_down]) + [other_down]
    tokens, shrunk, held, choice = pl.pallas_call(
        functools.partial(shrink_near_kernel, sizes, [place[1:] for place in pieces[:-6]], len(counts)),
        grid_spec=pltpu.PrefetchScalarGridSpec(
            num_scalar_prefetch=1 + len(counts),
            grid=(1,),
            in_specs=[ANY_SPEC] * (3 + len(near)),
            out_specs=[
                ANY_SPEC,
                whole(shrunk_shape.shape),
                whole(held_shape.shape),
                pl.BlockSpec(memory_space=pltpu.SMEM),
            ],
            scratch_shapes=[
                pltpu.VMEM((1, rows_all), jnp.int32),
                pltpu.VMEM((rows, width), jnp.bfloat16),
                down_vmem,
                pltpu.SemaphoreType.DMA((4 + len(near),)),
            ],
        ),
        out_shape=[tokens_shape, shrunk_shape, held_shape, jax.ShapeDtypeStruct((1,), jnp.int32)],
        compiler_params=pltpu.CompilerParams(vmem_limit_bytes=rows * width * 2 + 16 * MIB),
        name="shrink_near",
    )(me, *counts, *in_hbm([sorted_rows.reshape(1, rows_all)]), *downs, *in_hbm(near[:1]), *near[1:])
    tokens, shrunk = pl.pallas_call(
        functools.partial(shrink_far_kernel, [place[1:] for place in pieces[-6:]]),
        grid_spec=pltpu.PrefetchScalarGridSpec(
            num_scalar_prefetch=1,
            grid=(1,),
            in_specs=[ANY_SPEC] * 10,
            out_specs=[ANY_SPEC, whole(shrunk_shape.shape)],
            scratch_shapes=[
                pltpu.VMEM((3 * block, width), jnp.bfloat16),
                down_vmem,
                pltpu.SemaphoreType.DMA((12,)),
            ],
        ),
        out_shape=[tokens_shape, shrunk_shape],
        input_output_aliases={1: 0},
        compiler_params=pltpu.CompilerParams(vmem_limit_bytes=16 * MIB),
        name="shrink_far",
    )(me, *in_hbm([tokens]), shrunk, *downs, *values[-6:])
    return tokens, shrunk, held, choice


def expand_kernel(order, block, counts, me, held_hbm, own_hbm, other_hbm, keep_ref, got_ref, out_ref, *scratch):
    held_ref, own_ref, other_ref, maps_vmem, out_vmem, sems = scratch
    chips, most = held_ref.shape
    slots = out_vmem.shape[0] // chips
    units = out_vmem.shape[1]
    ranks = keep_ref.shape[0]
    adapters = counts.shape[0] // chips
    chip = me[0] // CORES
    core = me[0] % CORES
    copies = []
    for c in range(chips):
        start = pl.multiple_of((order[c] * CORES + core) * units, units)
        for ref, where in ((keep_ref, core), (got_ref, 1 - core)):
            copies.append(
                pltpu.make_async_copy(
                    ref.at[:, pl.ds(start, units)],
                    maps_vmem.at[c, pl.ds(pl.multiple_of(where * ranks, ranks), ranks)],
                    sems.at[len(copies)],
                )
            )
    small = [
        pltpu.make_async_copy(ref, held, sems.at[3 * chips + i])
        for i, (ref, held) in enumerate(((held_hbm, held_ref), (own_hbm, own_ref), (other_hbm, other_ref)))
    ]
    for copy in small + copies:
        copy.start()
    for copy in small:
        copy.wait()

    wanted = held_ref[pl.ds(chip, 1), :]
    index = lax.broadcasted_iota(jnp.int32, (own_ref.shape[0], most), 0)
    row = index // block * (CORES * block) + index % block
    picked = jnp.zeros((most, own_ref.shape[1]), jnp.float32)
    for ref, where in ((own_ref, core), (other_ref, 1 - core)):
        hit = (row + where * block == wanted).astype(jnp.float32).astype(jnp.bfloat16)
        picked += lax.dot_general(hit, ref[...], (((0,), (0,)), ((), ())), preferred_element_type=jnp.float32)
    slot = lax.broadcasted_iota(jnp.int32, picked.shape, 0)
    adapter = lax.broadcasted_iota(jnp.int32, picked.shape, 1) // (picked.shape[1] // adapters)
    mine = jnp.zeros(picked.shape, jnp.int32)
    first = jnp.int32(0)
    for a in range(adapters):
        end = first + counts[chip * adapters + a]
        mine += ((adapter == a) & (slot >= first) & (slot < end)).astype(jnp.int32)
        first = end
    shrunk = jnp.where(mine > 0, ADAPTER_SCALE * picked, 0.0)[:slots].astype(jnp.bfloat16)

    out_copies = []
    for c in range(0, chips, 2):
        products = []
        for i in (c, c + 1):
            copies[2 * i].wait()
            copies[2 * i + 1].wait()
            products.append(jnp.dot(shrunk, maps_vmem[i], preferred_element_type=jnp.float32))
        part = pl.ds(c * slots, 2 * slots)
        out_vmem[part, :] = jnp.concatenate(products, axis=0).astype(out_vmem.dtype)
        out_copies.append(pltpu.make_async_copy(out_vmem.at[part], out_ref.at[part], sems.at[2 * chips + c]))
        out_copies[-1].start()
    for copy in out_copies:
        copy.wait()


def expand(counts, me, held, own_shrunk, other_shrunk, keep, got, order, slots, block):
    ranks, columns = keep.shape
    chips, most = held.shape
    units = columns // chips // CORES
    rows, ranks_all = own_shrunk.shape
    return pl.pallas_call(
        functools.partial(expand_kernel, order, block),
        grid_spec=pltpu.PrefetchScalarGridSpec(
            num_scalar_prefetch=2,
            grid=(1,),
            in_specs=[ANY_SPEC] * 5,
            out_specs=ANY_SPEC,
            scratch_shapes=[
                pltpu.VMEM((chips, most), jnp.int32),
                pltpu.VMEM((rows, ranks_all), jnp.bfloat16),
                pltpu.VMEM((rows, ranks_all), jnp.bfloat16),
                pltpu.VMEM((chips, ranks_all, units), jnp.bfloat16),
                pltpu.VMEM((chips * slots, units), jnp.bfloat16),
                pltpu.SemaphoreType.DMA((3 * chips + 3,)),
            ],
        ),
        out_shape=pltpu.HBM((chips * slots, units), jnp.bfloat16),
        compiler_params=pltpu.CompilerParams(vmem_limit_bytes=16 * MIB),
        cost_estimate=pl.CostEstimate(
            flops=2 * slots * ranks_all * chips * units,
            bytes_accessed=2 * (slots + ranks_all) * chips * units,
            transcendentals=0,
        ),
        name="expand",
    )(counts, me, held, own_shrunk, other_shrunk, *in_hbm([keep, got]))


def project_kernel(block, me, gate_weight_ref, up_weight_ref, own_ref, other_ref, gate_ref, up_ref, tokens_vmem, sems):
    depth = gate_weight_ref.shape[0]
    core = me[0] % CORES
    k = pl.program_id(0)

    @pl.when(k == 0)
    def _():
        copies = []
        for ref, where in ((own_ref, core), (other_ref, 1 - core)):
            for chip in range(ref.shape[0] // block):
                start = pl.multiple_of((chip * CORES + where) * block, block)
                copies.append(
                    pltpu.make_async_copy(
                        ref.at[pl.ds(chip * block, block)], tokens_vmem.at[pl.ds(start, block)], sems.at[len(copies)]
                    )
                )
        run_copies(copies)
        gate_ref[...] = jnp.zeros_like(gate_ref)
        up_ref[...] = jnp.zeros_like(up_ref)

    tokens = tokens_vmem[:, pl.ds(pl.multiple_of(k * depth, depth), depth)]
    gate_ref[...] += jnp.dot(tokens, gate_weight_ref[...], preferred_element_type=jnp.float32)
    up_ref[...] += jnp.dot(tokens, up_weight_ref[...], preferred_element_type=jnp.float32)

    @pl.when(k == pl.num_programs(0) - 1)
    def _():
        gate = gate_ref[...]
        gate_ref[...] = gate / (1.0 + jnp.exp(-gate))


def project(me, own, other, gate_weight, up_weight, block):
    width, units = gate_weight.shape
    rows = CORES * own.shape[0]
    depth = min(1024, width)
    weight_spec = pl.BlockSpec((depth, units), lambda k, s: (k, 0))
    out_spec = pl.BlockSpec((rows, units), lambda k, s: (0, 0))
    out = pltpu.HBM((rows, units), jnp.float32)
    return pl.pallas_call(
        functools.partial(project_kernel, block),
        grid_spec=pltpu.PrefetchScalarGridSpec(
            num_scalar_prefetch=1,
            grid=(width // depth,),
            in_specs=[weight_spec, weight_spec, ANY_SPEC, ANY_SPEC],
            out_specs=[out_spec, out_spec],
            scratch_shapes=[
                pltpu.VMEM((rows, width), jnp.bfloat16),
                pltpu.SemaphoreType.DMA((rows // block,)),
            ],
        ),
        out_shape=[out, out],
        compiler_params=pltpu.CompilerParams(vmem_limit_bytes=rows * width * 2 + 20 * MIB),
        cost_estimate=pl.CostEstimate(
            flops=4 * rows * width * units,
            bytes_accessed=2 * (rows + 2 * units) * width,
            transcendentals=rows * units,
        ),
        name="project",
    )(me, *in_hbm([gate_weight, up_weight, own, other]))


def combine_kernel(pick_ref, gate_ref, up_ref, products_ref, out_ref):
    delta = jnp.dot(pick_ref[...], products_ref[...], preferred_element_type=jnp.float32)
    out_ref[...] = (gate_ref[...] * (up_ref[...] + delta)).astype(out_ref.dtype)


def combine(pick, gate, up, products):
    rows, units = gate.shape
    slots_all = products.shape[0]
    tile = min(512, units)
    column_spec = pl.BlockSpec((rows, tile), lambda n: (0, n))
    return pl.pallas_call(
        combine_kernel,
        grid=(units // tile,),
        in_specs=[
            pl.BlockSpec((rows, slots_all), lambda n: (0, 0)),
            column_spec,
            column_spec,
            pl.BlockSpec((slots_all, tile), lambda n: (0, n)),
        ],
        out_specs=column_spec,
        out_shape=pltpu.HBM((rows, units), jnp.bfloat16),
        compiler_params=pltpu.CompilerParams(vmem_limit_bytes=rows * slots_all * 4 + 20 * MIB),
        cost_estimate=pl.CostEstimate(
            flops=2 * rows * slots_all * units, bytes_accessed=10 * rows * units, transcendentals=0
        ),
        name="combine",
    )(*in_hbm([pick, gate, up]), products)


def per_device(
    tokens,
    gate_weight,
    up_weight,
    adapter_down_weight,
    adapter_up_weight,
    row_adapter,
    sorted_rows,
    segment_count,
):
    axis = "tensor"
    size = lax.axis_size(axis)
    me = lax.axis_index(axis).astype(jnp.int32)
    chips = size // CORES
    resident, rank, width = adapter_down_weight.shape
    ranks = resident * rank
    rows = row_adapter.shape[0]
    block = tokens.shape[0]
    me_array = me.reshape(1)
    flips = [(d, d ^ 1) for d in range(size)]

    def other_core(value):
        return lax.ppermute(value, axis, flips)

    most = CORES * resident * ROWS_PER_LIMIT
    sizes = [slots for slots in SLOT_SIZES if slots < most] + [most]
    groups = lax.axis_size("groups")
    own_down = adapter_down_weight.reshape(ranks, width)
    own_maps = adapter_up_weight.reshape(ranks, -1)
    other_down = other_core(own_down)
    counts = [segment_count] + [
        lax.ppermute(segment_count, "groups", [(g, (g + shift) % groups) for g in range(groups)])
        for shift in range(1, groups)
    ]
    other_maps = other_core(own_maps)

    def beside(step, values):
        nonlocal other_down, counts, other_maps
        if step == 1:
            other_down, counts, values[0], values[1] = lax.optimization_barrier((other_down, counts, *values))
        return values

    pieces = ring_gather(tokens, axis, beside)
    own_tokens, own_shrunk, held, choice = shrink(
        me_array, counts, sorted_rows, pieces, own_down, other_down, sizes
    )
    other_shrunk = other_core(own_shrunk)

    order = [half * (chips // 2) + c for c in range(chips // 2) for half in range(2)]
    same_core = [[c * CORES + k for c in order] for k in range(CORES)]

    def finish(slots):
        def branch(own_tokens, own_shrunk, other_shrunk, own_maps, other_maps, held, gate_weight, up_weight):
            products = expand(
                segment_count, me_array, held, own_shrunk, other_shrunk, own_maps, other_maps, order, slots, block
            )
            products = lax.all_to_all(
                products, axis, split_axis=0, concat_axis=0, axis_index_groups=same_core, tiled=True
            )
            held, other_tokens = lax.optimization_barrier((held, other_core(own_tokens)))
            held_rows = jnp.stack([held[c, :slots] for c in order]).reshape(1, chips * slots)
            pick = (jnp.arange(rows, dtype=jnp.int32)[:, None] == held_rows).astype(jnp.bfloat16)
            pick, other_tokens = lax.optimization_barrier((pick, other_tokens))
            gate, up = project(me_array, own_tokens, other_tokens, gate_weight, up_weight, block)
            return combine(pick, gate, up, products)

        return branch

    return lax.switch(
        choice[0],
        [finish(slots) for slots in sizes],
        own_tokens,
        own_shrunk,
        other_shrunk,
        own_maps,
        other_maps,
        held,
        gate_weight,
        up_weight,
    )


def solution(mesh):
    placed = (
        P(("groups", "tensor"), None),
        P(None, "tensor"),
        P(None, "tensor"),
        P(("groups", "tensor"), None, None),
        P(("groups", "tensor"), None, None),
        P("groups"),
        P("groups"),
        P("groups"),
    )
    return jax.shard_map(
        per_device, mesh=mesh, in_specs=placed, out_specs=P("groups", "tensor"), check_vma=False
    )
```

```python
import functools

import jax
import jax.numpy as jnp
from jax import lax
from jax.experimental import pallas as pl
from jax.experimental.pallas import tpu as pltpu
from jax.sharding import PartitionSpec as P

ADAPTER_SCALE = 0.5
ROWS_PER_LIMIT = 64
SLOT_SIZES = (72, 80, 88, 104)
CORES = 2
MIB = 1024 * 1024


def chip_ring(chips):
    return list(range(0, chips, 2)) + list(range(chips - 1, 0, -2))


def ring_chip(me, chips, distance):
    chip = me // CORES
    place = jnp.where(chip % 2 == 0, chip // 2, chips // 2 + (chips - 1 - chip) // 2)
    place = (place + distance + chips) % chips
    return jnp.where(place < chips // 2, 2 * place, chips - 1 - 2 * (place - chips // 2))


def ring_gather(block, axis, beside):
    size = lax.axis_size(axis)
    chips = size // CORES
    ring = chip_ring(chips)

    def moved(value, shift):
        pairs = [
            (ring[p] * CORES + k, ring[(p + shift) % chips] * CORES + k)
            for p in range(chips)
            for k in range(CORES)
        ]
        return lax.ppermute(value, axis, pairs)

    right, left = moved(block, 1), moved(block, -1)
    pieces = [(block, 0, 0), (right, 0, -1), (left, 0, 1)]
    half = block.shape[1] // 2
    far = chips // 2
    columns = (0, half), (half, 0)
    held = [(right[:, a : a + half], left[:, b : b + half]) for a, b in columns]
    held = beside(1, held)
    for step in range(2, far + 1):
        for chain in range(1 if step == far else 2):
            right, left = held[chain]
            held[chain] = moved(right, 1), moved(left, -1)
            for value, column, distance in zip(held[chain], columns[chain], (-step, step)):
                pieces.append((value, column, distance))
        held = beside(step, held)
    return pieces


ANY_SPEC = pl.BlockSpec(memory_space=pl.ANY)


def in_hbm(values):
    return [pltpu.with_memory_space_constraint(value, pltpu.HBM) for value in values]


def run_copies(copies):
    for copy in copies:
        copy.start()
    for copy in copies:
        copy.wait()


def make_plan(sizes, counts, sorted_ref, held_ref, choice_ref):
    chips, most = held_ref.shape
    rows = sorted_ref.shape[1]
    adapters = counts[0].shape[0] // chips

    def total(group, chip):
        return functools.reduce(jnp.add, [counts[group][chip * adapters + a] for a in range(adapters)])

    listed = jnp.broadcast_to(sorted_ref[...], (8, rows))
    slot = lax.broadcasted_iota(jnp.int32, (8, most), 1)
    start = jnp.int32(0)
    for chip in range(chips):
        turned = pltpu.roll(listed, (rows - start) % rows, 1)
        held_ref[chip : chip + 1, :] = jnp.where(slot < total(0, chip), turned[:, :most], -1)[0:1]
        start += total(0, chip)
    largest = functools.reduce(
        jnp.maximum, [total(group, chip) for group in range(len(counts)) for chip in range(chips)]
    )
    choice_ref[0] = functools.reduce(jnp.add, [(largest > size).astype(jnp.int32) for size in sizes[:-1]])


def down_copies(core, own_down_ref, other_down_ref, down_vmem, sems):
    ranks = own_down_ref.shape[0]
    return [
        pltpu.make_async_copy(ref, down_vmem.at[pl.ds(pl.multiple_of(where * ranks, ranks), ranks)], sems.at[i])
        for i, (ref, where) in enumerate(((own_down_ref, core), (other_down_ref, 1 - core)))
    ]


def shrink_near_kernel(sizes, places, groups, me, *refs):
    counts, refs = refs[:groups], refs[groups:]
    sorted_hbm, own_down_ref, other_down_ref = refs[:3]
    refs = refs[3:]
    piece_refs = refs[: len(places)]
    tokens_ref, shrunk_ref, held_ref, choice_ref, sorted_ref, tokens_vmem, down_vmem, sems = refs[len(places) :]
    chips = held_ref.shape[0]
    sorted_copy = pltpu.make_async_copy(sorted_hbm, sorted_ref, sems.at[3 + len(places)])
    sorted_copy.start()
    copies = down_copies(me[0] % CORES, own_down_ref, other_down_ref, down_vmem, sems)
    for ref, (column, distance) in zip(piece_refs, places):
        rows, width = ref.shape
        start = pl.multiple_of(ring_chip(me[0], chips, distance) * rows, rows)
        copies.append(
            pltpu.make_async_copy(
                ref, tokens_vmem.at[pl.ds(start, rows), pl.ds(column, width)], sems.at[len(copies)]
            )
        )
    for copy in copies:
        copy.start()
    sorted_copy.wait()
    make_plan(sizes, counts, sorted_ref, held_ref, choice_ref)
    for copy in copies:
        copy.wait()
    out_copy = pltpu.make_async_copy(tokens_vmem, tokens_ref, sems.at[len(copies)])
    out_copy.start()
    shrunk_ref[...] = lax.dot_general(
        tokens_vmem[...], down_vmem[...], (((1,), (1,)), ((), ())), preferred_element_type=jnp.float32
    ).astype(shrunk_ref.dtype)
    out_copy.wait()


def shrink_far_kernel(places, me, tokens_in, shrunk_in, own_down_ref, other_down_ref, *refs):
    piece_refs = refs[: len(places)]
    tokens_ref, shrunk_ref, far_vmem, down_vmem, sems = refs[len(places) :]
    rows, half = piece_refs[0].shape
    chips = tokens_in.shape[0] // rows
    slots = {distance % chips: i for i, distance in enumerate(range(chips // 2 - 1, chips // 2 + 2))}
    copies = down_copies(me[0] % CORES, own_down_ref, other_down_ref, down_vmem, sems)
    copies.append(pltpu.make_async_copy(shrunk_in, shrunk_ref, sems.at[2]))
    for ref, (column, distance) in zip(piece_refs, places):
        slot = slots[distance % chips]
        copies.append(
            pltpu.make_async_copy(
                ref, far_vmem.at[pl.ds(slot * rows, rows), pl.ds(column, half)], sems.at[len(copies)]
            )
        )
    run_copies(copies)
    starts = [pl.multiple_of(ring_chip(me[0], chips, distance) * rows, rows) for distance in slots]
    out_copies = [
        pltpu.make_async_copy(
            far_vmem.at[pl.ds(i * rows, rows)], tokens_ref.at[pl.ds(start, rows)], sems.at[len(copies) + i]
        )
        for i, start in enumerate(starts)
    ]
    for copy in out_copies:
        copy.start()
    shrunk = jnp.transpose(
        lax.dot_general(
            down_vmem[...], far_vmem[...], (((1,), (1,)), ((), ())), preferred_element_type=jnp.float32
        )
    ).astype(shrunk_ref.dtype)
    for i, start in enumerate(starts):
        shrunk_ref[pl.ds(start, rows), :] = shrunk[i * rows : (i + 1) * rows]
    for copy in out_copies:
        copy.wait()


def shrink(me, counts, sorted_rows, pieces, own_down, other_down, sizes):
    ranks, width = own_down.shape
    rows_all = sorted_rows.shape[0]
    rows = rows_all // CORES
    values = [value for value, _, _ in pieces]
    near = values[:-6]
    block = values[0].shape[0]
    tokens_shape = pltpu.HBM((rows, width), jnp.bfloat16)
    shrunk_shape = jax.ShapeDtypeStruct((rows, CORES * ranks), jnp.bfloat16)
    held_shape = jax.ShapeDtypeStruct((rows // block, sizes[-1]), jnp.int32)

    def whole(shape):
        return pl.BlockSpec(shape, lambda i, *_: (0, 0))

    down_vmem = pltpu.VMEM((CORES * ranks, width), jnp.bfloat16)
    downs = in_hbm([own_down]) + [other_down]
    tokens, shrunk, held, choice = pl.pallas_call(
        functools.partial(shrink_near_kernel, sizes, [place[1:] for place in pieces[:-6]], len(counts)),
        grid_spec=pltpu.PrefetchScalarGridSpec(
            num_scalar_prefetch=1 + len(counts),
            grid=(1,),
            in_specs=[ANY_SPEC] * (3 + len(near)),
            out_specs=[
                ANY_SPEC,
                whole(shrunk_shape.shape),
                whole(held_shape.shape),
                pl.BlockSpec(memory_space=pltpu.SMEM),
            ],
            scratch_shapes=[
                pltpu.VMEM((1, rows_all), jnp.int32),
                pltpu.VMEM((rows, width), jnp.bfloat16),
                down_vmem,
                pltpu.SemaphoreType.DMA((4 + len(near),)),
            ],
        ),
        out_shape=[tokens_shape, shrunk_shape, held_shape, jax.ShapeDtypeStruct((1,), jnp.int32)],
        compiler_params=pltpu.CompilerParams(vmem_limit_bytes=rows * width * 2 + 16 * MIB),
        name="shrink_near",
    )(me, *counts, *in_hbm([sorted_rows.reshape(1, rows_all)]), *downs, *in_hbm(near[:1]), *near[1:])
    tokens, shrunk = pl.pallas_call(
        functools.partial(shrink_far_kernel, [place[1:] for place in pieces[-6:]]),
        grid_spec=pltpu.PrefetchScalarGridSpec(
            num_scalar_prefetch=1,
            grid=(1,),
            in_specs=[ANY_SPEC] * 10,
            out_specs=[ANY_SPEC, whole(shrunk_shape.shape)],
            scratch_shapes=[
                pltpu.VMEM((3 * block, width), jnp.bfloat16),
                down_vmem,
                pltpu.SemaphoreType.DMA((12,)),
            ],
        ),
        out_shape=[tokens_shape, shrunk_shape],
        input_output_aliases={1: 0},
        compiler_params=pltpu.CompilerParams(vmem_limit_bytes=16 * MIB),
        name="shrink_far",
    )(me, *in_hbm([tokens]), shrunk, *downs, *values[-6:])
    return tokens, shrunk, held, choice


def expand_kernel(order, block, counts, me, held_hbm, own_hbm, other_hbm, keep_ref, got_ref, out_ref, *scratch):
    held_ref, own_ref, other_ref, maps_vmem, out_vmem, sems = scratch
    chips, most = held_ref.shape
    slots = out_vmem.shape[0] // chips
    units = out_vmem.shape[1]
    ranks = keep_ref.shape[0]
    adapters = counts.shape[0] // chips
    chip = me[0] // CORES
    core = me[0] % CORES
    copies = []
    for c in range(chips):
        start = pl.multiple_of((order[c] * CORES + core) * units, units)
        for ref, where in ((keep_ref, core), (got_ref, 1 - core)):
            copies.append(
                pltpu.make_async_copy(
                    ref.at[:, pl.ds(start, units)],
                    maps_vmem.at[c, pl.ds(pl.multiple_of(where * ranks, ranks), ranks)],
                    sems.at[len(copies)],
                )
            )
    small = [
        pltpu.make_async_copy(ref, held, sems.at[3 * chips + i])
        for i, (ref, held) in enumerate(((held_hbm, held_ref), (own_hbm, own_ref), (other_hbm, other_ref)))
    ]
    for copy in small + copies:
        copy.start()
    for copy in small:
        copy.wait()

    wanted = held_ref[pl.ds(chip, 1), :]
    index = lax.broadcasted_iota(jnp.int32, (own_ref.shape[0], most), 0)
    row = index // block * (CORES * block) + index % block
    picked = jnp.zeros((most, own_ref.shape[1]), jnp.float32)
    for ref, where in ((own_ref, core), (other_ref, 1 - core)):
        hit = (row + where * block == wanted).astype(jnp.float32).astype(jnp.bfloat16)
        picked += lax.dot_general(hit, ref[...], (((0,), (0,)), ((), ())), preferred_element_type=jnp.float32)
    slot = lax.broadcasted_iota(jnp.int32, picked.shape, 0)
    adapter = lax.broadcasted_iota(jnp.int32, picked.shape, 1) // (picked.shape[1] // adapters)
    mine = jnp.zeros(picked.shape, jnp.int32)
    first = jnp.int32(0)
    for a in range(adapters):
        end = first + counts[chip * adapters + a]
        mine += ((adapter == a) & (slot >= first) & (slot < end)).astype(jnp.int32)
        first = end
    shrunk = jnp.where(mine > 0, ADAPTER_SCALE * picked, 0.0)[:slots].astype(jnp.bfloat16)

    out_copies = []
    for c in range(0, chips, 2):
        products = []
        for i in (c, c + 1):
            copies[2 * i].wait()
            copies[2 * i + 1].wait()
            products.append(jnp.dot(shrunk, maps_vmem[i], preferred_element_type=jnp.float32))
        part = pl.ds(c * slots, 2 * slots)
        out_vmem[part, :] = jnp.concatenate(products, axis=0).astype(out_vmem.dtype)
        out_copies.append(pltpu.make_async_copy(out_vmem.at[part], out_ref.at[part], sems.at[2 * chips + c]))
        out_copies[-1].start()
    for copy in out_copies:
        copy.wait()


def expand(counts, me, held, own_shrunk, other_shrunk, keep, got, order, slots, block):
    ranks, columns = keep.shape
    chips, most = held.shape
    units = columns // chips // CORES
    rows, ranks_all = own_shrunk.shape
    return pl.pallas_call(
        functools.partial(expand_kernel, order, block),
        grid_spec=pltpu.PrefetchScalarGridSpec(
            num_scalar_prefetch=2,
            grid=(1,),
            in_specs=[ANY_SPEC] * 5,
            out_specs=ANY_SPEC,
            scratch_shapes=[
                pltpu.VMEM((chips, most), jnp.int32),
                pltpu.VMEM((rows, ranks_all), jnp.bfloat16),
                pltpu.VMEM((rows, ranks_all), jnp.bfloat16),
                pltpu.VMEM((chips, ranks_all, units), jnp.bfloat16),
                pltpu.VMEM((chips * slots, units), jnp.bfloat16),
                pltpu.SemaphoreType.DMA((3 * chips + 3,)),
            ],
        ),
        out_shape=pltpu.HBM((chips * slots, units), jnp.bfloat16),
        compiler_params=pltpu.CompilerParams(vmem_limit_bytes=16 * MIB),
        cost_estimate=pl.CostEstimate(
            flops=2 * slots * ranks_all * chips * units,
            bytes_accessed=2 * (slots + ranks_all) * chips * units,
            transcendentals=0,
        ),
        name="expand",
    )(counts, me, held, own_shrunk, other_shrunk, *in_hbm([keep, got]))


def project_kernel(block, me, gate_weight_ref, up_weight_ref, own_ref, other_ref, gate_ref, up_ref, tokens_vmem, sems):
    depth = gate_weight_ref.shape[0]
    core = me[0] % CORES
    k = pl.program_id(0)

    @pl.when(k == 0)
    def _():
        copies = []
        for ref, where in ((own_ref, core), (other_ref, 1 - core)):
            for chip in range(ref.shape[0] // block):
                start = pl.multiple_of((chip * CORES + where) * block, block)
                copies.append(
                    pltpu.make_async_copy(
                        ref.at[pl.ds(chip * block, block)], tokens_vmem.at[pl.ds(start, block)], sems.at[len(copies)]
                    )
                )
        run_copies(copies)
        gate_ref[...] = jnp.zeros_like(gate_ref)
        up_ref[...] = jnp.zeros_like(up_ref)

    tokens = tokens_vmem[:, pl.ds(pl.multiple_of(k * depth, depth), depth)]
    gate_ref[...] += jnp.dot(tokens, gate_weight_ref[...], preferred_element_type=jnp.float32)
    up_ref[...] += jnp.dot(tokens, up_weight_ref[...], preferred_element_type=jnp.float32)

    @pl.when(k == pl.num_programs(0) - 1)
    def _():
        gate = gate_ref[...]
        gate_ref[...] = gate / (1.0 + jnp.exp(-gate))


def project(me, own, other, gate_weight, up_weight, block):
    width, units = gate_weight.shape
    rows = CORES * own.shape[0]
    depth = min(1024, width)
    weight_spec = pl.BlockSpec((depth, units), lambda k, s: (k, 0))
    out_spec = pl.BlockSpec((rows, units), lambda k, s: (0, 0))
    out = pltpu.HBM((rows, units), jnp.float32)
    return pl.pallas_call(
        functools.partial(project_kernel, block),
        grid_spec=pltpu.PrefetchScalarGridSpec(
            num_scalar_prefetch=1,
            grid=(width // depth,),
            in_specs=[weight_spec, weight_spec, ANY_SPEC, ANY_SPEC],
            out_specs=[out_spec, out_spec],
            scratch_shapes=[
                pltpu.VMEM((rows, width), jnp.bfloat16),
                pltpu.SemaphoreType.DMA((rows // block,)),
            ],
        ),
        out_shape=[out, out],
        compiler_params=pltpu.CompilerParams(vmem_limit_bytes=rows * width * 2 + 20 * MIB),
        cost_estimate=pl.CostEstimate(
            flops=4 * rows * width * units,
            bytes_accessed=2 * (rows + 2 * units) * width,
            transcendentals=rows * units,
        ),
        name="project",
    )(me, *in_hbm([gate_weight, up_weight, own, other]))


def combine_kernel(pick_ref, gate_ref, up_ref, products_ref, out_ref):
    delta = jnp.dot(pick_ref[...], products_ref[...], preferred_element_type=jnp.float32)
    out_ref[...] = (gate_ref[...] * (up_ref[...] + delta)).astype(out_ref.dtype)


def combine(pick, gate, up, products):
    rows, units = gate.shape
    slots_all = products.shape[0]
    tile = min(512, units)
    column_spec = pl.BlockSpec((rows, tile), lambda n: (0, n))
    return pl.pallas_call(
        combine_kernel,
        grid=(units // tile,),
        in_specs=[
            pl.BlockSpec((rows, slots_all), lambda n: (0, 0)),
            column_spec,
            column_spec,
            pl.BlockSpec((slots_all, tile), lambda n: (0, n)),
        ],
        out_specs=column_spec,
        out_shape=pltpu.HBM((rows, units), jnp.bfloat16),
        compiler_params=pltpu.CompilerParams(vmem_limit_bytes=rows * slots_all * 4 + 20 * MIB),
        cost_estimate=pl.CostEstimate(
            flops=2 * rows * slots_all * units, bytes_accessed=10 * rows * units, transcendentals=0
        ),
        name="combine",
    )(*in_hbm([pick, gate, up]), products)


def per_device(
    tokens,
    gate_weight,
    up_weight,
    adapter_down_weight,
    adapter_up_weight,
    row_adapter,
    sorted_rows,
    segment_count,
):
    axis = "tensor"
    size = lax.axis_size(axis)
    me = lax.axis_index(axis).astype(jnp.int32)
    chips = size // CORES
    resident, rank, width = adapter_down_weight.shape
    ranks = resident * rank
    rows = row_adapter.shape[0]
    block = tokens.shape[0]
    me_array = me.reshape(1)
    flips = [(d, d ^ 1) for d in range(size)]

    def other_core(value):
        return lax.ppermute(value, axis, flips)

    most = CORES * resident * ROWS_PER_LIMIT
    sizes = [slots for slots in SLOT_SIZES if slots < most] + [most]
    groups = lax.axis_size("groups")
    own_down = adapter_down_weight.reshape(ranks, width)
    own_maps = adapter_up_weight.reshape(ranks, -1)
    other_down = other_core(own_down)
    counts = [segment_count] + [
        lax.ppermute(segment_count, "groups", [(g, (g + shift) % groups) for g in range(groups)])
        for shift in range(1, groups)
    ]
    other_maps = other_core(own_maps)

    def beside(step, values):
        nonlocal other_down, counts, other_maps
        if step == 1:
            other_down, counts, values[0], values[1] = lax.optimization_barrier((other_down, counts, *values))
        return values

    pieces = ring_gather(tokens, axis, beside)
    own_tokens, own_shrunk, held, choice = shrink(
        me_array, counts, sorted_rows, pieces, own_down, other_down, sizes
    )
    other_shrunk = other_core(own_shrunk)

    order = [half * (chips // 2) + c for c in range(chips // 2) for half in range(2)]
    same_core = [[c * CORES + k for c in order] for k in range(CORES)]

    def finish(slots):
        def branch(own_tokens, own_shrunk, other_shrunk, own_maps, other_maps, held, gate_weight, up_weight):
            products = expand(
                segment_count, me_array, held, own_shrunk, other_shrunk, own_maps, other_maps, order, slots, block
            )
            products = lax.all_to_all(
                products, axis, split_axis=0, concat_axis=0, axis_index_groups=same_core, tiled=True
            )
            held, other_tokens = lax.optimization_barrier((held, other_core(own_tokens)))
            held_rows = jnp.stack([held[c, :slots] for c in order]).reshape(1, chips * slots)
            pick = (jnp.arange(rows, dtype=jnp.int32)[:, None] == held_rows).astype(jnp.bfloat16)
            pick, other_tokens = lax.optimization_barrier((pick, other_tokens))
            gate, up = project(me_array, own_tokens, other_tokens, gate_weight, up_weight, block)
            return combine(pick, gate, up, products)

        return branch

    return lax.switch(
        choice[0],
        [finish(slots) for slots in sizes],
        own_tokens,
        own_shrunk,
        other_shrunk,
        own_maps,
        other_maps,
        held,
        gate_weight,
        up_weight,
    )


def solution(mesh):
    placed = (
        P(("groups", "tensor"), None),
        P(None, "tensor"),
        P(None, "tensor"),
        P(("groups", "tensor"), None, None),
        P(("groups", "tensor"), None, None),
        P("groups"),
        P("groups"),
        P("groups"),
    )
    return jax.shard_map(
        per_device, mesh=mesh, in_specs=placed, out_specs=P("groups", "tensor"), check_vma=False
    )
```

```python
import functools

import jax
import jax.numpy as jnp
from jax import lax
from jax.experimental import pallas as pl
from jax.experimental.pallas import tpu as pltpu
from jax.sharding import PartitionSpec as P

ADAPTER_SCALE = 0.5
ROWS_PER_LIMIT = 64
SLOT_SIZES = (72, 80, 88, 104)
CORES = 2
MIB = 1024 * 1024


def chip_ring(chips):
    return list(range(0, chips, 2)) + list(range(chips - 1, 0, -2))


def ring_chip(me, chips, distance):
    chip = me // CORES
    place = jnp.where(chip % 2 == 0, chip // 2, chips // 2 + (chips - 1 - chip) // 2)
    place = (place + distance + chips) % chips
    return jnp.where(place < chips // 2, 2 * place, chips - 1 - 2 * (place - chips // 2))


def ring_gather(block, axis, beside):
    size = lax.axis_size(axis)
    chips = size // CORES
    ring = chip_ring(chips)

    def moved(value, shift):
        pairs = [
            (ring[p] * CORES + k, ring[(p + shift) % chips] * CORES + k)
            for p in range(chips)
            for k in range(CORES)
        ]
        return lax.ppermute(value, axis, pairs)

    right, left = moved(block, 1), moved(block, -1)
    pieces = [(block, 0, 0), (right, 0, -1), (left, 0, 1)]
    half = block.shape[1] // 2
    far = chips // 2
    columns = (0, half), (half, 0)
    held = [(right[:, a : a + half], left[:, b : b + half]) for a, b in columns]
    held = beside(1, held)
    for step in range(2, far + 1):
        for chain in range(1 if step == far else 2):
            right, left = held[chain]
            held[chain] = moved(right, 1), moved(left, -1)
            for value, column, distance in zip(held[chain], columns[chain], (-step, step)):
                pieces.append((value, column, distance))
        held = beside(step, held)
    return pieces


ANY_SPEC = pl.BlockSpec(memory_space=pl.ANY)


def in_hbm(values):
    return [pltpu.with_memory_space_constraint(value, pltpu.HBM) for value in values]


def run_copies(copies):
    for copy in copies:
        copy.start()
    for copy in copies:
        copy.wait()


def make_plan(sizes, counts, sorted_ref, held_ref, choice_ref):
    chips, most = held_ref.shape
    rows = sorted_ref.shape[1]
    adapters = counts[0].shape[0] // chips

    def total(group, chip):
        return functools.reduce(jnp.add, [counts[group][chip * adapters + a] for a in range(adapters)])

    listed = jnp.broadcast_to(sorted_ref[...], (8, rows))
    slot = lax.broadcasted_iota(jnp.int32, (8, most), 1)
    start = jnp.int32(0)
    for chip in range(chips):
        turned = pltpu.roll(listed, (rows - start) % rows, 1)
        held_ref[chip : chip + 1, :] = jnp.where(slot < total(0, chip), turned[:, :most], -1)[0:1]
        start += total(0, chip)
    largest = functools.reduce(
        jnp.maximum, [total(group, chip) for group in range(len(counts)) for chip in range(chips)]
    )
    choice_ref[0] = functools.reduce(jnp.add, [(largest > size).astype(jnp.int32) for size in sizes[:-1]])


def down_copies(core, own_down_ref, other_down_ref, down_vmem, sems):
    ranks = own_down_ref.shape[0]
    return [
        pltpu.make_async_copy(ref, down_vmem.at[pl.ds(pl.multiple_of(where * ranks, ranks), ranks)], sems.at[i])
        for i, (ref, where) in enumerate(((own_down_ref, core), (other_down_ref, 1 - core)))
    ]


def shrink_near_kernel(sizes, places, groups, me, *refs):
    counts, refs = refs[:groups], refs[groups:]
    sorted_hbm, own_down_ref, other_down_ref = refs[:3]
    refs = refs[3:]
    piece_refs = refs[: len(places)]
    tokens_ref, shrunk_ref, held_ref, choice_ref, sorted_ref, tokens_vmem, down_vmem, sems = refs[len(places) :]
    chips = held_ref.shape[0]
    sorted_copy = pltpu.make_async_copy(sorted_hbm, sorted_ref, sems.at[3 + len(places)])
    sorted_copy.start()
    copies = down_copies(me[0] % CORES, own_down_ref, other_down_ref, down_vmem, sems)
    for ref, (column, distance) in zip(piece_refs, places):
        rows, width = ref.shape
        start = pl.multiple_of(ring_chip(me[0], chips, distance) * rows, rows)
        copies.append(
            pltpu.make_async_copy(
                ref, tokens_vmem.at[pl.ds(start, rows), pl.ds(column, width)], sems.at[len(copies)]
            )
        )
    for copy in copies:
        copy.start()
    sorted_copy.wait()
    make_plan(sizes, counts, sorted_ref, held_ref, choice_ref)
    for copy in copies:
        copy.wait()
    out_copy = pltpu.make_async_copy(tokens_vmem, tokens_ref, sems.at[len(copies)])
    out_copy.start()
    shrunk_ref[...] = lax.dot_general(
        tokens_vmem[...], down_vmem[...], (((1,), (1,)), ((), ())), preferred_element_type=jnp.float32
    ).astype(shrunk_ref.dtype)
    out_copy.wait()


def shrink_far_kernel(places, me, tokens_in, shrunk_in, own_down_ref, other_down_ref, *refs):
    piece_refs = refs[: len(places)]
    tokens_ref, shrunk_ref, far_vmem, down_vmem, sems = refs[len(places) :]
    rows, half = piece_refs[0].shape
    chips = tokens_in.shape[0] // rows
    slots = {distance % chips: i for i, distance in enumerate(range(chips // 2 - 1, chips // 2 + 2))}
    core = me[0] % CORES
    ranks = own_down_ref.shape[0]
    copies = [pltpu.make_async_copy(shrunk_in, shrunk_ref, sems.at[0])]
    halves = []
    for column in (0, half):
        part = pl.ds(column, half)
        ends = [
            (ref.at[:, part], down_vmem.at[pl.ds(pl.multiple_of(where * ranks, ranks), ranks), part])
            for ref, where in ((own_down_ref, core), (other_down_ref, 1 - core))
        ]
        ends += [
            (ref, far_vmem.at[pl.ds(slots[distance % chips] * rows, rows), part])
            for ref, (piece_column, distance) in zip(piece_refs, places)
            if piece_column == column
        ]
        first = len(copies)
        copies += [pltpu.make_async_copy(*end, sems.at[first + i]) for i, end in enumerate(ends)]
        halves.append((column, copies[first:]))
    for copy in copies:
        copy.start()
    turned = jnp.zeros((CORES * ranks, far_vmem.shape[0]), jnp.float32)
    for column, waits in halves:
        for copy in waits:
            copy.wait()
        turned += lax.dot_general(
            down_vmem[:, column : column + half],
            far_vmem[:, column : column + half],
            (((1,), (1,)), ((), ())),
            preferred_element_type=jnp.float32,
        )
    copies[0].wait()
    starts = [pl.multiple_of(ring_chip(me[0], chips, distance) * rows, rows) for distance in slots]
    out_copies = [
        pltpu.make_async_copy(
            far_vmem.at[pl.ds(i * rows, rows)], tokens_ref.at[pl.ds(start, rows)], sems.at[len(copies) + i]
        )
        for i, start in enumerate(starts)
    ]
    for copy in out_copies:
        copy.start()
    shrunk = jnp.transpose(turned).astype(shrunk_ref.dtype)
    for i, start in enumerate(starts):
        shrunk_ref[pl.ds(start, rows), :] = shrunk[i * rows : (i + 1) * rows]
    for copy in out_copies:
        copy.wait()


def shrink(me, counts, sorted_rows, pieces, own_down, other_down, sizes):
    ranks, width = own_down.shape
    rows_all = sorted_rows.shape[0]
    rows = rows_all // CORES
    values = [value for value, _, _ in pieces]
    near = values[:-6]
    block = values[0].shape[0]
    tokens_shape = pltpu.HBM((rows, width), jnp.bfloat16)
    shrunk_shape = jax.ShapeDtypeStruct((rows, CORES * ranks), jnp.bfloat16)
    held_shape = jax.ShapeDtypeStruct((rows // block, sizes[-1]), jnp.int32)

    def whole(shape):
        return pl.BlockSpec(shape, lambda i, *_: (0, 0))

    down_vmem = pltpu.VMEM((CORES * ranks, width), jnp.bfloat16)
    downs = in_hbm([own_down]) + [other_down]
    tokens, shrunk, held, choice = pl.pallas_call(
        functools.partial(shrink_near_kernel, sizes, [place[1:] for place in pieces[:-6]], len(counts)),
        grid_spec=pltpu.PrefetchScalarGridSpec(
            num_scalar_prefetch=1 + len(counts),
            grid=(1,),
            in_specs=[ANY_SPEC] * (3 + len(near)),
            out_specs=[
                ANY_SPEC,
                whole(shrunk_shape.shape),
                whole(held_shape.shape),
                pl.BlockSpec(memory_space=pltpu.SMEM),
            ],
            scratch_shapes=[
                pltpu.VMEM((1, rows_all), jnp.int32),
                pltpu.VMEM((rows, width), jnp.bfloat16),
                down_vmem,
                pltpu.SemaphoreType.DMA((4 + len(near),)),
            ],
        ),
        out_shape=[tokens_shape, shrunk_shape, held_shape, jax.ShapeDtypeStruct((1,), jnp.int32)],
        compiler_params=pltpu.CompilerParams(vmem_limit_bytes=rows * width * 2 + 16 * MIB),
        name="shrink_near",
    )(me, *counts, *in_hbm([sorted_rows.reshape(1, rows_all)]), *downs, *in_hbm(near[:1]), *near[1:])
    tokens, shrunk = pl.pallas_call(
        functools.partial(shrink_far_kernel, [place[1:] for place in pieces[-6:]]),
        grid_spec=pltpu.PrefetchScalarGridSpec(
            num_scalar_prefetch=1,
            grid=(1,),
            in_specs=[ANY_SPEC] * 10,
            out_specs=[ANY_SPEC, whole(shrunk_shape.shape)],
            scratch_shapes=[
                pltpu.VMEM((3 * block, width), jnp.bfloat16),
                down_vmem,
                pltpu.SemaphoreType.DMA((14,)),
            ],
        ),
        out_shape=[tokens_shape, shrunk_shape],
        input_output_aliases={1: 0},
        compiler_params=pltpu.CompilerParams(vmem_limit_bytes=16 * MIB),
        name="shrink_far",
    )(me, *in_hbm([tokens]), shrunk, *downs, *values[-6:])
    return tokens, shrunk, held, choice


def expand_kernel(order, block, counts, me, held_hbm, own_hbm, other_hbm, keep_ref, got_ref, out_ref, *scratch):
    held_ref, own_ref, other_ref, maps_vmem, out_vmem, sems = scratch
    chips, most = held_ref.shape
    slots = out_vmem.shape[0] // chips
    units = out_vmem.shape[1]
    ranks = keep_ref.shape[0]
    adapters = counts.shape[0] // chips
    chip = me[0] // CORES
    core = me[0] % CORES
    copies = []
    for c in range(chips):
        start = pl.multiple_of((order[c] * CORES + core) * units, units)
        for ref, where in ((keep_ref, core), (got_ref, 1 - core)):
            copies.append(
                pltpu.make_async_copy(
                    ref.at[:, pl.ds(start, units)],
                    maps_vmem.at[c, pl.ds(pl.multiple_of(where * ranks, ranks), ranks)],
                    sems.at[len(copies)],
                )
            )
    small = [
        pltpu.make_async_copy(ref, held, sems.at[3 * chips + i])
        for i, (ref, held) in enumerate(((held_hbm, held_ref), (own_hbm, own_ref), (other_hbm, other_ref)))
    ]
    for copy in small + copies:
        copy.start()
    for copy in small:
        copy.wait()

    wanted = held_ref[pl.ds(chip, 1), :]
    index = lax.broadcasted_iota(jnp.int32, (own_ref.shape[0], most), 0)
    row = index // block * (CORES * block) + index % block
    picked = jnp.zeros((most, own_ref.shape[1]), jnp.float32)
    for ref, where in ((own_ref, core), (other_ref, 1 - core)):
        hit = (row + where * block == wanted).astype(jnp.float32).astype(jnp.bfloat16)
        picked += lax.dot_general(hit, ref[...], (((0,), (0,)), ((), ())), preferred_element_type=jnp.float32)
    slot = lax.broadcasted_iota(jnp.int32, picked.shape, 0)
    adapter = lax.broadcasted_iota(jnp.int32, picked.shape, 1) // (picked.shape[1] // adapters)
    mine = jnp.zeros(picked.shape, jnp.int32)
    first = jnp.int32(0)
    for a in range(adapters):
        end = first + counts[chip * adapters + a]
        mine += ((adapter == a) & (slot >= first) & (slot < end)).astype(jnp.int32)
        first = end
    shrunk = jnp.where(mine > 0, ADAPTER_SCALE * picked, 0.0)[:slots].astype(jnp.bfloat16)

    out_copies = []
    for c in range(0, chips, 2):
        products = []
        for i in (c, c + 1):
            copies[2 * i].wait()
            copies[2 * i + 1].wait()
            products.append(jnp.dot(shrunk, maps_vmem[i], preferred_element_type=jnp.float32))
        part = pl.ds(c * slots, 2 * slots)
        out_vmem[part, :] = jnp.concatenate(products, axis=0).astype(out_vmem.dtype)
        out_copies.append(pltpu.make_async_copy(out_vmem.at[part], out_ref.at[part], sems.at[2 * chips + c]))
        out_copies[-1].start()
    for copy in out_copies:
        copy.wait()


def expand(counts, me, held, own_shrunk, other_shrunk, keep, got, order, slots, block):
    ranks, columns = keep.shape
    chips, most = held.shape
    units = columns // chips // CORES
    rows, ranks_all = own_shrunk.shape
    return pl.pallas_call(
        functools.partial(expand_kernel, order, block),
        grid_spec=pltpu.PrefetchScalarGridSpec(
            num_scalar_prefetch=2,
            grid=(1,),
            in_specs=[ANY_SPEC] * 5,
            out_specs=ANY_SPEC,
            scratch_shapes=[
                pltpu.VMEM((chips, most), jnp.int32),
                pltpu.VMEM((rows, ranks_all), jnp.bfloat16),
                pltpu.VMEM((rows, ranks_all), jnp.bfloat16),
                pltpu.VMEM((chips, ranks_all, units), jnp.bfloat16),
                pltpu.VMEM((chips * slots, units), jnp.bfloat16),
                pltpu.SemaphoreType.DMA((3 * chips + 3,)),
            ],
        ),
        out_shape=pltpu.HBM((chips * slots, units), jnp.bfloat16),
        compiler_params=pltpu.CompilerParams(vmem_limit_bytes=16 * MIB),
        cost_estimate=pl.CostEstimate(
            flops=2 * slots * ranks_all * chips * units,
            bytes_accessed=2 * (slots + ranks_all) * chips * units,
            transcendentals=0,
        ),
        name="expand",
    )(counts, me, held, own_shrunk, other_shrunk, *in_hbm([keep, got]))


def project_kernel(block, me, gate_weight_ref, up_weight_ref, own_ref, other_ref, gate_ref, up_ref, tokens_vmem, sems):
    depth = gate_weight_ref.shape[0]
    core = me[0] % CORES
    k = pl.program_id(0)

    @pl.when(k == 0)
    def _():
        copies = []
        for ref, where in ((own_ref, core), (other_ref, 1 - core)):
            for chip in range(ref.shape[0] // block):
                start = pl.multiple_of((chip * CORES + where) * block, block)
                copies.append(
                    pltpu.make_async_copy(
                        ref.at[pl.ds(chip * block, block)], tokens_vmem.at[pl.ds(start, block)], sems.at[len(copies)]
                    )
                )
        run_copies(copies)
        gate_ref[...] = jnp.zeros_like(gate_ref)
        up_ref[...] = jnp.zeros_like(up_ref)

    tokens = tokens_vmem[:, pl.ds(pl.multiple_of(k * depth, depth), depth)]
    gate_ref[...] += jnp.dot(tokens, gate_weight_ref[...], preferred_element_type=jnp.float32)
    up_ref[...] += jnp.dot(tokens, up_weight_ref[...], preferred_element_type=jnp.float32)

    @pl.when(k == pl.num_programs(0) - 1)
    def _():
        gate = gate_ref[...]
        gate_ref[...] = gate / (1.0 + jnp.exp(-gate))


def project(me, own, other, gate_weight, up_weight, block):
    width, units = gate_weight.shape
    rows = CORES * own.shape[0]
    depth = min(1024, width)
    weight_spec = pl.BlockSpec((depth, units), lambda k, s: (k, 0))
    out_spec = pl.BlockSpec((rows, units), lambda k, s: (0, 0))
    out = pltpu.HBM((rows, units), jnp.float32)
    return pl.pallas_call(
        functools.partial(project_kernel, block),
        grid_spec=pltpu.PrefetchScalarGridSpec(
            num_scalar_prefetch=1,
            grid=(width // depth,),
            in_specs=[weight_spec, weight_spec, ANY_SPEC, ANY_SPEC],
            out_specs=[out_spec, out_spec],
            scratch_shapes=[
                pltpu.VMEM((rows, width), jnp.bfloat16),
                pltpu.SemaphoreType.DMA((rows // block,)),
            ],
        ),
        out_shape=[out, out],
        compiler_params=pltpu.CompilerParams(vmem_limit_bytes=rows * width * 2 + 20 * MIB),
        cost_estimate=pl.CostEstimate(
            flops=4 * rows * width * units,
            bytes_accessed=2 * (rows + 2 * units) * width,
            transcendentals=rows * units,
        ),
        name="project",
    )(me, *in_hbm([gate_weight, up_weight, own, other]))


def combine_kernel(pick_ref, gate_ref, up_ref, products_ref, out_ref):
    delta = jnp.dot(pick_ref[...], products_ref[...], preferred_element_type=jnp.float32)
    out_ref[...] = (gate_ref[...] * (up_ref[...] + delta)).astype(out_ref.dtype)


def combine(pick, gate, up, products):
    rows, units = gate.shape
    slots_all = products.shape[0]
    tile = min(512, units)
    column_spec = pl.BlockSpec((rows, tile), lambda n: (0, n))
    return pl.pallas_call(
        combine_kernel,
        grid=(units // tile,),
        in_specs=[
            pl.BlockSpec((rows, slots_all), lambda n: (0, 0)),
            column_spec,
            column_spec,
            pl.BlockSpec((slots_all, tile), lambda n: (0, n)),
        ],
        out_specs=column_spec,
        out_shape=pltpu.HBM((rows, units), jnp.bfloat16),
        compiler_params=pltpu.CompilerParams(vmem_limit_bytes=rows * slots_all * 4 + 20 * MIB),
        cost_estimate=pl.CostEstimate(
            flops=2 * rows * slots_all * units, bytes_accessed=10 * rows * units, transcendentals=0
        ),
        name="combine",
    )(*in_hbm([pick, gate, up]), products)


def per_device(
    tokens,
    gate_weight,
    up_weight,
    adapter_down_weight,
    adapter_up_weight,
    row_adapter,
    sorted_rows,
    segment_count,
):
    axis = "tensor"
    size = lax.axis_size(axis)
    me = lax.axis_index(axis).astype(jnp.int32)
    chips = size // CORES
    resident, rank, width = adapter_down_weight.shape
    ranks = resident * rank
    rows = row_adapter.shape[0]
    block = tokens.shape[0]
    me_array = me.reshape(1)
    flips = [(d, d ^ 1) for d in range(size)]

    def other_core(value):
        return lax.ppermute(value, axis, flips)

    most = CORES * resident * ROWS_PER_LIMIT
    sizes = [slots for slots in SLOT_SIZES if slots < most] + [most]
    groups = lax.axis_size("groups")
    own_down = adapter_down_weight.reshape(ranks, width)
    own_maps = adapter_up_weight.reshape(ranks, -1)
    other_down = other_core(own_down)
    counts = [segment_count] + [
        lax.ppermute(segment_count, "groups", [(g, (g + shift) % groups) for g in range(groups)])
        for shift in range(1, groups)
    ]
    other_maps = other_core(own_maps)

    def beside(step, values):
        nonlocal other_down, counts, other_maps
        if step == 1:
            other_down, counts, values[0], values[1] = lax.optimization_barrier((other_down, counts, *values))
        return values

    pieces = ring_gather(tokens, axis, beside)
    own_tokens, own_shrunk, held, choice = shrink(
        me_array, counts, sorted_rows, pieces, own_down, other_down, sizes
    )
    other_shrunk = other_core(own_shrunk)

    order = [half * (chips // 2) + c for c in range(chips // 2) for half in range(2)]
    same_core = [[c * CORES + k for c in order] for k in range(CORES)]

    def finish(slots):
        def branch(own_tokens, own_shrunk, other_shrunk, own_maps, other_maps, held, gate_weight, up_weight):
            products = expand(
                segment_count, me_array, held, own_shrunk, other_shrunk, own_maps, other_maps, order, slots, block
            )
            products = lax.all_to_all(
                products, axis, split_axis=0, concat_axis=0, axis_index_groups=same_core, tiled=True
            )
            held, other_tokens = lax.optimization_barrier((held, other_core(own_tokens)))
            held_rows = jnp.stack([held[c, :slots] for c in order]).reshape(1, chips * slots)
            pick = (jnp.arange(rows, dtype=jnp.int32)[:, None] == held_rows).astype(jnp.bfloat16)
            pick, other_tokens = lax.optimization_barrier((pick, other_tokens))
            gate, up = project(me_array, own_tokens, other_tokens, gate_weight, up_weight, block)
            return combine(pick, gate, up, products)

        return branch

    return lax.switch(
        choice[0],
        [finish(slots) for slots in sizes],
        own_tokens,
        own_shrunk,
        other_shrunk,
        own_maps,
        other_maps,
        held,
        gate_weight,
        up_weight,
    )


def solution(mesh):
    placed = (
        P(("groups", "tensor"), None),
        P(None, "tensor"),
        P(None, "tensor"),
        P(("groups", "tensor"), None, None),
        P(("groups", "tensor"), None, None),
        P("groups"),
        P("groups"),
        P("groups"),
    )
    return jax.shard_map(
        per_device, mesh=mesh, in_specs=placed, out_specs=P("groups", "tensor"), check_vma=False
    )
```
